128 devices in a mesh: seq: 32 (over z, y, core), tp: 4 (over x).
Axes of the slice: x: 4, y: 4, z: 4, core: 2. Of those that a mesh axis runs over, the one named last changes fastest.
Arguments:
- hidden_in: float32 [8192, 2048], P('seq'), may hold values from -6 to 6
- cotangent: float32 [8192, 2048], P('seq'), may hold values from -6 to 6
- starts: int32 [8192], P('seq'), may hold values from 0 to 1, as said below
- norm_in: float32 [2048], replicated, may hold values from 0.1 to 1.9
- w_in: bfloat16 [3, 2048, 2048], P(None, None, 'tp'), may hold values from -0.125 to 0.125
- short_w: float32 [3, 3, 2048], P(None, None, 'tp'), may hold values from -3.5 to 3.5
- pole_pairs: float32 [2, 16, 2048], P(None, None, 'tp'), may hold values from -1 to 1, as said below
- residues: float32 [2, 16, 2048], P(None, None, 'tp'), may hold values from -1 to 1
- w_out: bfloat16 [2048, 2048], P('tp'), may hold values from -0.125 to 0.125
- norm_mid: float32 [2048], replicated, may hold values from 0.1 to 1.9
- w_gate: bfloat16 [2048, 5632], P(None, 'tp'), may hold values from -0.125 to 0.125
- w_up: bfloat16 [2048, 5632], P(None, 'tp'), may hold values from -0.125 to 0.125
- w_down: bfloat16 [5632, 2048], P('tp'), may hold values from -0.078125 to 0.078125
Outputs:
- result: float32 [8192, 2048], P('seq')
- grad_input: float32 [8192, 2048], P('seq')
- grad_norm_in: float32 [2048], replicated
- grad_w_in: float32 [3, 2048, 2048], P(None, 'seq', 'tp')
- grad_short_w: float32 [3, 3, 2048], P(None, None, 'tp')
- grad_pole_pairs: float32 [2, 16, 2048], P(None, None, 'tp')
- grad_residues: float32 [2, 16, 2048], P(None, None, 'tp')
- grad_w_out: float32 [2048, 2048], P('tp', 'seq')
- grad_norm_mid: float32 [2048], replicated
- grad_w_gate: float32 [2048, 5632], P('seq', 'tp')
- grad_w_up: float32 [2048, 5632], P('seq', 'tp')
- grad_w_down: float32 [5632, 2048], P('tp', 'seq')
The draws below stay inside these ranges and needn't reach their ends.
Inputs may be any that keep to these rules, and one draw needn't show every extreme that they name: `starts`: the first token begins a document. `pole_pairs`: each pole has modulus below 1.
All inputs are finite; a program needn't handle non-finite values.
Results may differ from the reference program's by a relative error of at most 0.0094.
Values sent between devices are 32-bit elements; how exact they have to be, the bound alone decides.
No kernel may reach another device: no remote copies, remote signals or barrier semaphores. Data moves between devices by JAX's collectives and lax.ppermute only.
A program may use at most 448 MiB of HBM per device.

```python
import math
import jax
import jax.numpy as jnp
from jax import lax

D = 2048
FF = 5632
NP = 16
TOK_DEV = 256
TOKENS = 8192


def pole_rates(key, upper):
    lowest = math.log(0.1 / TOKENS)
    return jnp.exp(jax.random.uniform(key, (NP, D), jnp.float32, lowest, math.log(upper)))


def draw_pole_pairs(key, part):
    rates = pole_rates(key, 1.0 / 30.0)
    key = jax.random.fold_in(key, 11)
    angles = jax.random.uniform(key, (NP, D), jnp.float32, -1.0, 1.0)
    radius = jnp.exp(-rates)
    return jnp.stack([radius * jnp.cos(angles), radius * jnp.sin(angles)])


def draw_residues(key, part):
    rates = pole_rates(key, 1.0 / 30.0)
    key = jax.random.fold_in(key, 13)
    amplitude = jnp.sqrt(2.0 * (rates + 1.0 / TOKENS) / NP)
    pairs = jax.random.normal(key, (2, NP, D), jnp.float32)
    return pairs * amplitude


def draw_starts(key, part):
    key = jax.random.fold_in(key, 7)
    draw_keys = jax.random.split(key, 6)
    first_start = jax.random.randint(draw_keys[0], (), 1, TOK_DEV // 2)
    last_start = TOKENS - jax.random.randint(draw_keys[1], (), 1, TOK_DEV // 2)
    first_end = TOKENS // 4 + jax.random.randint(draw_keys[2], (), 0, TOK_DEV // 2)
    second_start = TOKENS // 2 - TOK_DEV - jax.random.randint(draw_keys[3], (), 0, TOK_DEV // 2)
    second_end = 3 * TOKENS // 4 + jax.random.randint(draw_keys[4], (), 0, TOK_DEV // 2)
    positions = jnp.arange(TOKENS, dtype=jnp.int32)
    spacing = min(512, 2 * TOK_DEV)
    scattered = (jax.random.randint(draw_keys[5], (TOKENS,), 0, spacing) == 0).astype(jnp.int32)
    inside = (positions > first_start) & (positions < first_end) | (positions > second_start) & (positions < second_end)
    flags = jnp.where(inside, 0, scattered)
    fixed = (positions == 0) | (positions == first_start) | (positions == first_end) | (positions == second_start) | (positions == second_end) | (positions == last_start)
    return jnp.where(fixed, 1, flags).astype(jnp.int32)


def raised(array, rng, source, target, parts, factor):
    owner, partner = [(jnp.arange(array.shape[position]) // (array.shape[position] // parts)).reshape([-1 if axis == position else 1 for axis in range(array.ndim)]) for position in (source, target)]
    chosen = jax.random.permutation(rng, parts)[partner]
    strong = (owner == chosen) | (owner == (partner + parts // 2) % parts)
    return jnp.where(strong, factor * array, array)


def block_scale(key, shape, shards, low, largest):
    def one(dim, parts):
        draws = jax.random.uniform(jax.random.fold_in(jax.random.fold_in(key, 6), dim), (parts,), jnp.float32, low / len(shards), largest / len(shards))
        return jnp.repeat(jnp.exp(draws), shape[dim] // parts).reshape((-1,) + (1,) * (len(shape) - dim - 1))

    level = one(*shards[0])
    for cut in shards[1:]:
        level = level * one(*cut)
    return level


def centred(key, dims, scale, reach, pieces=(), kind=jnp.bfloat16):
    values = scale * jax.random.normal(key, dims, jnp.float32)
    if pieces:
        values = values * block_scale(key, dims, pieces, -0.22, 0.18)
    return jnp.clip(values, -reach, reach).astype(kind)


def noise_with(own_key, extent, width, limit, cuts, heavy, kind=jnp.bfloat16):
    entries = width * jax.random.normal(own_key, extent, jnp.float32)
    if cuts:
        entries = entries * block_scale(own_key, extent, cuts, -0.22, 0.18)
    return jnp.clip(raised(entries, jax.random.fold_in(own_key, 3), *heavy), -limit, limit).astype(kind)


def setup_inputs(seed: int = 0) -> dict:
    arg_keys = jax.random.split(jax.random.key(seed), 14)
    hidden_in = centred(arg_keys[0], (TOKENS, D), 1.0, 6.0, ((0, 32),), jnp.float32)
    cotangent = noise_with(arg_keys[1], (TOKENS, D), 1.0, 6.0, ((0, 32),), (0, 1, 32, 2.75), jnp.float32)
    starts = draw_starts(jax.random.fold_in(arg_keys[13], 71), 0)
    norm_in = jnp.clip(1.0 + 0.18 * jax.random.normal(arg_keys[3], (D,), jnp.float32), 0.1, 1.9)
    w_in = centred(arg_keys[4], (3, D, D), D ** -0.5, 0.125, ((2, 4),))
    short_w = centred(arg_keys[5], (3, 3, D), 3 ** -0.5, 3.5, ((2, 4),), jnp.float32)
    pole_pairs = draw_pole_pairs(jax.random.fold_in(arg_keys[13], 71), 0)
    residues = draw_residues(jax.random.fold_in(arg_keys[13], 71), 0)
    w_out = centred(arg_keys[8], (D, D), D ** -0.5, 0.125, ((0, 4),))
    norm_mid = jnp.clip(1.0 + 0.18 * jax.random.normal(arg_keys[9], (D,), jnp.float32), 0.1, 1.9)
    w_gate = centred(arg_keys[10], (D, FF), D ** -0.5, 0.125, ((1, 4),))
    w_up = centred(arg_keys[11], (D, FF), D ** -0.5, 0.125, ((1, 4),))
    w_down = centred(arg_keys[12], (FF, D), FF ** -0.5, 0.078125, ((0, 4),))
    return {"hidden_in": hidden_in, "cotangent": cotangent, "starts": starts, "norm_in": norm_in, "w_in": w_in, "short_w": short_w, "pole_pairs": pole_pairs, "residues": residues, "w_out": w_out, "norm_mid": norm_mid, "w_gate": w_gate, "w_up": w_up, "w_down": w_down}


epsilon = 1e-06
highest = lax.Precision.HIGHEST

@jax.custom_vjp
def low(v):
    return lax.optimization_barrier(v.astype(jnp.bfloat16)).astype(jnp.float32)

@jax.custom_vjp
def low_back(v):
    return v

def low_keep(v):
    return (low(v), None)

def low_pass(kept, grad):
    return (grad,)

def back_keep(v):
    return (v, None)

def back_low(kept, grad):
    return (low(grad),)
low.defvjp(low_keep, low_pass)
low_back.defvjp(back_keep, back_low)

def rms_norm(values, norm_gain):
    inverse = lax.rsqrt(lax.optimization_barrier(jnp.mean(values * values, axis=-1, keepdims=True)) + epsilon)
    return values * inverse * norm_gain

def pole_powers(pole_pairs, length):
    radius = 0.5 * jnp.log(pole_pairs[0] * pole_pairs[0] + pole_pairs[1] * pole_pairs[1])
    angles = jnp.arctan2(pole_pairs[1], pole_pairs[0])
    exponent = jnp.arange(length).astype(pole_pairs.dtype)[:, None, None]
    magnitude = jnp.exp(exponent * radius)
    return (magnitude * jnp.cos(exponent * angles), magnitude * jnp.sin(exponent * angles))

def toeplitz_apply(kernel, driven, lag_table, allowed):
    length, channels = driven.shape
    group_size = min(128, channels)
    groups = channels // group_size
    kernel_groups = kernel.reshape(length, groups, group_size).transpose(1, 0, 2)
    driven_groups = driven.reshape(length, groups, group_size).transpose(1, 0, 2)

    def one_group(pair_item):
        kernel_part, source = pair_item
        matrix = kernel_part[lag_table] * allowed[:, :, None]
        return jnp.einsum('tsc,sc->tc', matrix, source, precision=highest)
    output = lax.map(jax.checkpoint(one_group), (kernel_groups, driven_groups))
    return output.transpose(1, 0, 2).reshape(length, channels)

def block_conv(driven, starts, pole_pairs, residues):
    length = driven.shape[0]
    power_re, power_im = pole_powers(pole_pairs, length + 1)
    kernel = lax.optimization_barrier(jnp.sum(residues[0] * power_re[:length] - residues[1] * power_im[:length], axis=1))
    segment = jnp.cumsum(starts).astype(jnp.int32)
    positions = jnp.arange(length, dtype=jnp.int32)
    lag_table = jnp.maximum(positions[:, None] - positions[None, :], 0).astype(jnp.int32)
    allowed = ((positions[:, None] >= positions[None, :]) & (segment[:, None] == segment[None, :])).astype(driven.dtype)
    own_part = toeplitz_apply(kernel, driven, lag_table, allowed)
    tail_rows = (segment == segment[-1]).astype(driven.dtype)
    weighted = driven * tail_rows[:, None]
    back_re = power_re[:length][::-1]
    back_im = power_im[:length][::-1]
    end_re = jnp.einsum('snc,sc->nc', back_re, weighted, precision=highest)
    end_im = jnp.einsum('snc,sc->nc', back_im, weighted, precision=highest)
    open_flag = (segment[-1] == 0).astype(driven.dtype)
    decay_re = power_re[length] * open_flag
    decay_im = power_im[length] * open_flag
    reach_re = residues[0] * power_re[1:] - residues[1] * power_im[1:]
    reach_im = residues[0] * power_im[1:] + residues[1] * power_re[1:]
    return (own_part, end_re, end_im, decay_re, decay_im, reach_re, reach_im)

def long_conv(driven, starts, pole_pairs, residues):
    total_rows, channels = driven.shape
    blocks = total_rows // TOK_DEV

    def step(carried, block_item):
        state_re, state_im = carried
        source, start_marks = block_item
        own_part, end_re, end_im, decay_re, decay_im, reach_re, reach_im = block_conv(source, start_marks, pole_pairs, residues)
        head_rows = (jnp.cumsum(start_marks) == 0).astype(source.dtype)
        from_before = lax.optimization_barrier(jnp.sum(reach_re * state_re - reach_im * state_im, axis=1)) * head_rows[:, None]
        next_re = decay_re * state_re - decay_im * state_im + end_re
        next_im = decay_re * state_im + decay_im * state_re + end_im
        return ((next_re, next_im), own_part + from_before)
    empty_state = jnp.zeros((NP, channels), driven.dtype)
    blocks_in = (driven.reshape(blocks, TOK_DEV, channels), starts.reshape(blocks, TOK_DEV))
    _, signal = lax.scan(jax.checkpoint(step), (empty_state, empty_state), blocks_in)
    return signal.reshape(total_rows, channels)

def short_conv(projected, short_w, keep_one, keep_two):
    total_rows = projected.shape[1]
    padded = jnp.pad(projected, ((0, 0), (2, 0), (0, 0)))
    prev_one = padded[:, 1:total_rows + 1]
    prev_two = padded[:, :total_rows]
    return short_w[:, 0][:, None, :] * projected + short_w[:, 1][:, None, :] * prev_one * keep_one[None, :, None] + short_w[:, 2][:, None, :] * prev_two * keep_two[None, :, None]

def hyena_block(hidden_in, norm_in, w_in, short_w, pole_pairs, residues, w_out, norm_mid, w_gate, w_up, w_down, starts):
    start_marks = starts.astype(hidden_in.dtype)
    keep_one = 1.0 - start_marks
    keep_two = keep_one * (1.0 - jnp.concatenate([jnp.zeros((1,), start_marks.dtype), start_marks[:-1]]))
    normed_in = low(rms_norm(hidden_in, norm_in))
    projected = low_back(jnp.einsum('td,kdc->ktc', normed_in, w_in, precision=highest))
    mixed_rows = short_conv(projected, short_w, keep_one, keep_two)
    driven = mixed_rows[1] * mixed_rows[2]
    signal = long_conv(driven, starts, pole_pairs, residues)
    gated_low = low(mixed_rows[0] * signal)
    branch = low_back(jnp.dot(gated_low, w_out, precision=highest))
    middle = hidden_in + branch
    normed_mid = low(rms_norm(middle, norm_mid))
    gate_pre = low_back(jnp.dot(normed_mid, w_gate, precision=highest))
    up_pre = low_back(jnp.dot(normed_mid, w_up, precision=highest))
    hidden = low(jax.nn.silu(gate_pre) * up_pre)
    return middle + low_back(jnp.dot(hidden, w_down, precision=highest))

def reference(hidden_in, cotangent, starts, norm_in, w_in, short_w, pole_pairs, residues, w_out, norm_mid, w_gate, w_up, w_down):
    weights = (norm_in, w_in.astype(jnp.float32), short_w, pole_pairs, residues, w_out.astype(jnp.float32), norm_mid, w_gate.astype(jnp.float32), w_up.astype(jnp.float32), w_down.astype(jnp.float32))

    def forward(inputs, *params):
        return hyena_block(inputs, *params, starts)
    result, pull_back = jax.vjp(forward, hidden_in, *weights)
    gradients = pull_back(cotangent)
    return (result, gradients[0], gradients[1], gradients[2], gradients[3], gradients[4], gradients[5], gradients[6], gradients[7], gradients[8], gradients[9], gradients[10])
```

```python
import jax
import jax.numpy as jnp
from jax import lax
from jax.experimental import pallas as pl
from jax.experimental.pallas import tpu as pltpu
from jax.sharding import Mesh
from jax.sharding import PartitionSpec as P

SEQ = ("seq_0", "seq_1", "seq_2")
F32 = jnp.float32
BF16 = jnp.bfloat16
epsilon = 1e-06
MIB = 1 << 20
T, C, N, D = 256, 512, 16, 2048
BLOCK = 64
BLOCKS = T // BLOCK
ROWS = 64
VMEM = pl.BlockSpec(memory_space=pltpu.VMEM)
SMEM = pl.BlockSpec(memory_space=pltpu.SMEM)


def whole(*shape):
    return pl.BlockSpec(shape, lambda i: (0,) * len(shape))


def struct(*shape, dtype=F32):
    return jax.ShapeDtypeStruct(shape, dtype)


def token_sum(a, b):
    return lax.dot_general(a, b, (((0,), (0,)), ((), ())), preferred_element_type=F32)


def scan_groups(groups, starts, base, run, carry, reverse):
    def body(step, kept):
        group = groups - 1 - step if reverse else step
        first = base + group * 8
        marks = starts[first]
        for r in range(1, 8):
            marks = marks + starts[first + r]
        return lax.cond(
            marks > 0, lambda c: run(group, c, True), lambda c: run(group, c, False), kept
        )

    return lax.fori_loop(0, groups, body, carry)


def eight(group):
    return pl.ds(pl.multiple_of(group * 8, 8), 8)


def keep_at(starts, token):
    return (1 - starts[token]).astype(F32)


def mix_kernel(proj, taps, keep_one, keep_two, starts, poles, mixed, end, driven):
    one, two = keep_one[...], keep_two[...]
    for k in range(3):
        mixed[k] = (
            taps[3 * k : 3 * k + 1] * proj[k, 8 : 8 + T]
            + taps[3 * k + 1 : 3 * k + 2] * (one * proj[k, 7 : 7 + T])
            + taps[3 * k + 2 : 3 * k + 3] * (two * proj[k, 6 : 6 + T])
        )
    driven[...] = mixed[1] * mixed[2]
    pre, pim = poles[0], poles[1]

    def run(group, state, masked):
        source = driven[eight(group), :]
        re, im = state
        for r in range(8):
            if masked:
                keep = keep_at(starts, group * 8 + r)
                re, im = re * keep, im * keep
            re, im = pre * re - pim * im + source[r : r + 1], pre * im + pim * re
        return re, im

    zero = jnp.zeros((N, C), F32)
    end[0], end[1] = scan_groups(T // 8, starts, 0, run, (zero, zero), False)


def mix(proj, taps, keep_one, keep_two, starts, poles):
    return pl.pallas_call(
        mix_kernel,
        name="mix_and_end_state",
        out_shape=(struct(3, T, C), struct(2, N, C)),
        in_specs=[VMEM, VMEM, VMEM, VMEM, SMEM, VMEM],
        out_specs=(VMEM, VMEM),
        scratch_shapes=[pltpu.VMEM((T, C), F32)],
        compiler_params=pltpu.CompilerParams(vmem_limit_bytes=24 * MIB),
    )(proj, taps, keep_one, keep_two, starts, poles)


def signal_kernel(mixed, starts, poles, residues, first, signal, gated, history, state):
    block = pl.program_id(0)

    @pl.when(block == 0)
    def _():
        state[...] = first[...]

    pre, pim, qre, qim = poles[0], poles[1], residues[0], residues[1]
    base = block * BLOCK

    def run(group, kept, masked):
        source = mixed[1, eight(group), :] * mixed[2, eight(group), :]
        re, im = kept
        for r in range(8):
            if masked:
                keep = keep_at(starts, base + group * 8 + r)
                re, im = re * keep, im * keep
            re, im = pre * re - pim * im + source[r : r + 1], pre * im + pim * re
            history[group * 8 + r, 0] = re
            history[group * 8 + r, 1] = im
            signal[pl.ds(group * 8 + r, 1), :] = jnp.sum(qre * re - qim * im, axis=0, keepdims=True)
        return re, im

    state[0], state[1] = scan_groups(
        BLOCK // 8, starts, base, run, (state[0], state[1]), False
    )
    gated[...] = (mixed[0] * signal[...]).astype(BF16)


def signal_of(mixed, starts, poles, residues, first):
    return pl.pallas_call(
        signal_kernel,
        name="signal",
        grid=(BLOCKS,),
        out_shape=(struct(T, C), struct(T, C, dtype=BF16), struct(T, 2, N, C)),
        in_specs=[
            pl.BlockSpec((3, BLOCK, C), lambda i: (0, i, 0)),
            SMEM,
            whole(2, N, C),
            whole(2, N, C),
            whole(2, N, C),
        ],
        out_specs=(
            pl.BlockSpec((BLOCK, C), lambda i: (i, 0)),
            pl.BlockSpec((BLOCK, C), lambda i: (i, 0)),
            pl.BlockSpec((BLOCK, 2, N, C), lambda i: (i, 0, 0, 0)),
        ),
        scratch_shapes=[pltpu.VMEM((2, N, C), F32)],
        compiler_params=pltpu.CompilerParams(vmem_limit_bytes=56 * MIB),
    )(mixed, starts, poles, residues, first)


def adjoint_kernel(grad_gated, query, starts, poles, residues, out, grads):
    grads[...] = grad_gated[...] * query[0]
    pre, pim, qre, qim = poles[0], poles[1], residues[0], residues[1]

    def run(group, kept, masked):
        source = grads[eight(group), :]
        re, im = kept
        for r in reversed(range(8)):
            row = source[r : r + 1]
            re, im = row * qre + (pre * re + pim * im), (pre * im - pim * re) - row * qim
            if masked:
                keep = keep_at(starts, group * 8 + r)
                re, im = re * keep, im * keep
        return re, im

    zero = jnp.zeros((N, C), F32)
    out[0], out[1] = scan_groups(T // 8, starts, 0, run, (zero, zero), True)


def adjoint_end(grad_gated, mixed, starts, poles, residues):
    return pl.pallas_call(
        adjoint_kernel,
        name="adjoint_end",
        grid=(1,),
        out_shape=struct(2, N, C),
        in_specs=[
            whole(T, C),
            pl.BlockSpec((1, T, C), lambda i: (0, 0, 0)),
            SMEM,
            whole(2, N, C),
            whole(2, N, C),
        ],
        out_specs=whole(2, N, C),
        scratch_shapes=[pltpu.VMEM((T, C), F32)],
        compiler_params=pltpu.CompilerParams(vmem_limit_bytes=24 * MIB),
    )(grad_gated, mixed, starts, poles, residues)


def back_kernel(
    grad_gated,
    mixed,
    signal,
    proj,
    history,
    taps,
    keep_one,
    keep_two,
    starts,
    poles,
    residues,
    first,
    grad_proj,
    rim,
    sums,
    state,
    driven_grad,
    mixed_grad,
):
    step = pl.program_id(0)
    block = BLOCKS - 1 - step

    @pl.when(step == 0)
    def _():
        state[...] = first[...]
        sums[...] = jnp.zeros(sums.shape, F32)

    pre, pim, qre, qim = poles[0], poles[1], residues[0], residues[1]
    base = block * BLOCK

    def run(group, kept, masked):
        rows = pl.ds(pl.multiple_of(base + group * 8, 8), 8)
        source = grad_gated[rows, :] * mixed[0, rows, :]
        re, im = kept
        for r in reversed(range(8)):
            row = source[r : r + 1]
            sre, sim = history[group * 8 + r, 0], history[group * 8 + r, 1]
            sums[0:16] += re * sre + im * sim
            sums[16:32] += im * sre - re * sim
            sums[32:48] += row * sre
            sums[48:64] -= row * sim
            re, im = row * qre + (pre * re + pim * im), (pre * im - pim * re) - row * qim
            driven_grad[pl.ds(base + group * 8 + r, 1), :] = jnp.sum(re, axis=0, keepdims=True)
            if masked:
                keep = keep_at(starts, base + group * 8 + r)
                re, im = re * keep, im * keep
        return re, im

    state[0], state[1] = scan_groups(BLOCK // 8, starts, base, run, (state[0], state[1]), True)

    @pl.when(step == BLOCKS - 1)
    def _():
        one, two = keep_one[...], keep_two[...]
        mixed_grad[0, 0:T] = grad_gated[...] * signal[...]
        mixed_grad[1, 0:T] = driven_grad[...] * mixed[2]
        mixed_grad[2, 0:T] = driven_grad[...] * mixed[1]
        for k in range(3):
            here = mixed_grad[k, 0:T]
            sums[64 + 3 * k : 65 + 3 * k] = jnp.sum(here * proj[k, 8 : 8 + T], axis=0, keepdims=True)
            grad_proj[k] = taps[3 * k : 3 * k + 1] * here
            here = one * mixed_grad[k, 0:T]
            sums[65 + 3 * k : 66 + 3 * k] = jnp.sum(here * proj[k, 7 : 7 + T], axis=0, keepdims=True)
            mixed_grad[k, 0:T] = two * mixed_grad[k, 0:T]
            here = taps[3 * k + 1 : 3 * k + 2] * here
            grad_proj[k, 0 : T - 1] += here[1:T]
            rim[k] = jnp.zeros((8, C), F32)
            rim[k, 1:2] = here[0:1]
            here = mixed_grad[k, 0:T]
            sums[66 + 3 * k : 67 + 3 * k] = jnp.sum(here * proj[k, 6 : 6 + T], axis=0, keepdims=True)
            here = taps[3 * k + 2 : 3 * k + 3] * here
            grad_proj[k, 0 : T - 2] += here[2:T]
            rim[k, 0:2] += here[0:2]


def back(grad_gated, mixed, signal, proj, history, taps, keep_one, keep_two, starts, poles, residues, first):
    return pl.pallas_call(
        back_kernel,
        name="adjoint_and_short_back",
        grid=(BLOCKS,),
        out_shape=(struct(3, T, C), struct(3, 8, C), struct(80, C)),
        in_specs=[
            whole(T, C),
            whole(3, T, C),
            whole(T, C),
            whole(3, T + 8, C),
            pl.BlockSpec((BLOCK, 2, N, C), lambda i: (BLOCKS - 1 - i, 0, 0, 0)),
            whole(9, C),
            whole(T, 1),
            whole(T, 1),
            SMEM,
            whole(2, N, C),
            whole(2, N, C),
            whole(2, N, C),
        ],
        out_specs=(whole(3, T, C), whole(3, 8, C), whole(80, C)),
        scratch_shapes=[
            pltpu.VMEM((2, N, C), F32),
            pltpu.VMEM((T, C), F32),
            pltpu.VMEM((3, T, C), F32),
        ],
        compiler_params=pltpu.CompilerParams(vmem_limit_bytes=40 * MIB),
    )(
        grad_gated,
        mixed,
        signal,
        proj,
        history,
        taps,
        keep_one,
        keep_two,
        starts,
        poles,
        residues,
        first,
    )


def swap(value, axis, mask):
    size = lax.axis_size(axis)
    return lax.ppermute(value, axis, [(i, i ^ mask) for i in range(size)])


def shifted(value, axis, steps):
    count = lax.axis_size(axis)
    first, last = max(0, -steps), min(count, count - steps)
    return lax.ppermute(value, axis, [(i, i + steps) for i in range(first, last)])


def scatter_sum(partial):
    half = partial.shape[1] // 2
    left, right = partial[:, :half], partial[:, half:]
    got_left = swap(left[ROWS : 3 * ROWS], "tp", 1)
    got_right = swap(right[2 * ROWS :], "tp", 3)
    more_left = swap(left[3 * ROWS :] + got_left[ROWS:], "tp", 3)
    more_right = swap(right[ROWS : 2 * ROWS] + got_right[:ROWS], "tp", 1)
    return jnp.concatenate(
        [
            left[:ROWS] + got_left[:ROWS] + more_left,
            right[:ROWS] + got_right[ROWS:] + more_right,
        ],
        axis=1,
    )


def gather_rows(mine):
    half = mine.shape[1] // 2
    left, right = mine[:, :half], mine[:, half:]
    left_3 = swap(left, "tp", 3)
    right_1 = swap(right, "tp", 1)
    left_12 = swap(jnp.concatenate([left, left_3]), "tp", 1)
    right_23 = swap(jnp.concatenate([right_1, right]), "tp", 3)
    return jnp.concatenate(
        [
            jnp.concatenate([left, left_12, left_3]),
            jnp.concatenate([right, right_1, right_23]),
        ],
        axis=1,
    )


def rows_by_owner(x, me, dim=0):
    return jnp.concatenate(
        [lax.dynamic_slice_in_dim(x, (me ^ j) * ROWS, ROWS, dim) for j in range(4)], axis=dim
    )


def times(a, b):
    return a[0] * b[0] - a[1] * b[1], a[0] * b[1] + a[1] * b[0]


def plus(a, b):
    return a[0] + b[0], a[1] + b[1]


def where2(flag, a, b):
    return jnp.where(flag, a[0], b[0]), jnp.where(flag, a[1], b[1])


def scaled(a, factor):
    return a[0] * factor, a[1] * factor


def pack(state, is_open):
    return jnp.concatenate([state[0], state[1], jnp.broadcast_to(is_open, (8, C))])


def unpack(payload):
    return (payload[0:N], payload[N : 2 * N]), payload[2 * N : 2 * N + 1]


def carried_state(end, is_open, powers, reverse):
    by_device, by_chip, by_plane = powers
    core, y = lax.axis_index("seq_2"), lax.axis_index("seq_1")
    z = lax.axis_index("seq_0")
    sign = 1
    if reverse:
        core, y, z, sign = 1 - core, 3 - y, 3 - z, -1
    zero = (jnp.zeros((N, C), F32), jnp.zeros((N, C), F32))
    other, other_open = unpack(swap(pack(end, is_open), "seq_2", 1))
    earlier = where2(core == 1, other, end)
    later = where2(core == 1, end, other)
    later_open = jnp.where(core == 1, is_open, other_open)
    chip = plus(later, times(scaled(by_device, later_open), earlier))
    chip_open = is_open * other_open
    payload = pack(chip, chip_open)

    def cyclic(k):
        return lax.ppermute(payload, "seq_1", [(i, (i + sign * k) % 4) for i in range(4)])

    from_y = {k: unpack(cyclic(k)) for k in (1, 2, 3)}
    in_y, weight = zero, (jnp.ones((N, C), F32), jnp.zeros((N, C), F32))
    for k in (1, 2, 3):
        state, opened = from_y[k]
        before = y >= k
        in_y = where2(before, plus(in_y, times(weight, state)), in_y)
        weight = where2(before, times(weight, scaled(by_chip, opened)), weight)
    plane = plus(chip, times(scaled(by_chip, chip_open), in_y))
    plane_open = chip_open
    for j in (1, 2, 3):
        state, opened = from_y[4 - j]
        plane = where2(y + j <= 3, plus(state, times(scaled(by_chip, opened), plane)), plane)
        plane_open = plane_open * opened
    payload_z = pack(plane, plane_open)
    in_z, weight_z = zero, (jnp.ones((N, C), F32), jnp.zeros((N, C), F32))
    for k in (1, 2, 3):
        state, opened = unpack(shifted(payload_z, "seq_0", sign * k))
        in_z = plus(in_z, times(weight_z, state))
        weight_z = times(weight_z, scaled(by_plane, opened))
    at_chip = plus(in_y, times(weight, in_z))
    at_core = plus(other, times(scaled(by_device, other_open), at_chip))
    return jnp.stack(where2(core == 1, at_core, at_chip))


def sum_over(x, axis):
    if lax.axis_size(axis) == 2:
        return x + swap(x, axis, 1)
    return (x + swap(x, axis, 1)) + (swap(x, axis, 2) + swap(x, axis, 3))


def inverse_rms(values):
    return lax.rsqrt(jnp.mean(values * values, axis=-1, keepdims=True) + epsilon)


def rms_back(values, gain, incoming):
    inverse = inverse_rms(values)
    along = jnp.mean(gain * incoming * values, axis=-1, keepdims=True)
    return inverse * gain * incoming - values * (inverse * inverse * inverse * along)


ANY = pl.BlockSpec(memory_space=pl.ANY)


def nothing(*refs):
    pass


def tie(x, *after):
    return pl.pallas_call(
        nothing,
        name="tie",
        out_shape=struct(*x.shape, dtype=x.dtype),
        in_specs=[ANY] * (1 + len(after)),
        out_specs=ANY,
        input_output_aliases={0: 0},
    )(x, *after)


def wide_sum_kernel(left_a, more_a, left_b, more_b, right_a, wide_a, right_b, wide_b, out, low_a, low_b):
    @pl.when(pl.program_id(0) == 0)
    def _():
        low_a[...] = wide_a[...].astype(BF16)
        low_b[...] = wide_b[...].astype(BF16)

    width = right_a.shape[1]
    out[:, :width] = token_sum(left_a[...], right_a[...]) + token_sum(more_a[...], low_a[...])
    out[:, width:] = token_sum(left_b[...], right_b[...]) + token_sum(
        more_b[...].astype(BF16), low_b[...]
    )


def wide_token_sum(left_a, more_a, left_b, more_b, right_a, wide_a, right_b, wide_b):
    rows = 256
    column = pl.BlockSpec((T, rows), lambda i: (0, i))
    wa, wb = right_a.shape[1], right_b.shape[1]
    return pl.pallas_call(
        wide_sum_kernel,
        name="weight_gradients",
        grid=(D // rows,),
        out_shape=struct(D, wa + wb),
        in_specs=[column] * 4 + [whole(T, wa), whole(T, wa), whole(T, wb), whole(T, wb)],
        out_specs=pl.BlockSpec((rows, wa + wb), lambda i: (i, 0)),
        scratch_shapes=[pltpu.VMEM((T, wa), BF16), pltpu.VMEM((T, wb), BF16)],
        compiler_params=pltpu.CompilerParams(vmem_limit_bytes=40 * MIB),
    )(left_a, more_a, left_b, more_b, right_a, wide_a, right_b, wide_b)


ORDERS = {1: (0, 3, 1, 2), 3: (0, 1, 3, 2)}
STREAMS = (("seq_1", 1), ("seq_1", 3), ("seq_0", 1), ("seq_0", 3))


def chunk_table():
    z, y = lax.axis_index("seq_0"), lax.axis_index("seq_1")
    rows = []
    for axis, mask in STREAMS:
        order = ORDERS[mask]
        for i in range(16):
            first, second = order[i // 4], order[i % 4]
            jy, jz = (first, second) if axis == "seq_1" else (second, first)
            rows.append((z ^ jz) * 4 + (y ^ jy))
    return jnp.stack(rows).astype(jnp.int32)


def stream_sum_kernel(table, *refs):
    lefts, mores = refs[0:4], refs[4:8]
    right_a, wide_a, right_b, wide_b = refs[8:12]
    kept, sent = refs[12:16], refs[16:20]
    low_a, low_b = refs[20:22]
    step = pl.program_id(0)

    @pl.when(step == 0)
    def _():
        low_a[...] = wide_a[...].astype(BF16)
        low_b[...] = wide_b[...].astype(BF16)

    for s in range(4):
        columns = slice(256 * s, 256 * s + 256) if s < 3 else slice(0, 256)
        right, low = (right_a, low_a) if s < 3 else (right_b, low_b)
        total = token_sum(lefts[s][...], right[:, columns]) + token_sum(
            mores[s][...], low[:, columns]
        )

        @pl.when(step < 8)
        def _():
            kept[s][...] = total

        @pl.when(step >= 8)
        def _():
            sent[s][...] = total


def stream_token_sum(table, left_a, more_a, left_b, more_b, right_a, wide_a, right_b, wide_b):
    def column(s):
        return pl.BlockSpec((T, 128), lambda i, table: (0, table[16 * s + i]))

    def fixed(*shape):
        return pl.BlockSpec(shape, lambda i, table: (0,) * len(shape))

    columns = [column(s) for s in range(4)]
    keep = pl.BlockSpec((128, 256), lambda i, table: (jnp.minimum(i, 7), 0))
    send = pl.BlockSpec((128, 256), lambda i, table: (jnp.maximum(i - 8, 0), 0))
    out = pl.pallas_call(
        stream_sum_kernel,
        name="mixer_weight_gradients",
        out_shape=(struct(1024, 256),) * 8,
        grid_spec=pltpu.PrefetchScalarGridSpec(
            num_scalar_prefetch=1,
            grid=(16,),
            in_specs=columns + columns + [fixed(T, 768), fixed(T, 768), fixed(T, 256), fixed(T, 256)],
            out_specs=(keep,) * 4 + (send,) * 4,
            scratch_shapes=[pltpu.VMEM((T, 768), BF16), pltpu.VMEM((T, 256), BF16)],
        ),
        compiler_params=pltpu.CompilerParams(vmem_limit_bytes=32 * MIB),
    )(
        table,
        *([left_a] * 3 + [left_b]),
        *([more_a] * 3 + [more_b]),
        right_a,
        wide_a,
        right_b,
        wide_b,
    )
    return out[:4], out[4:]


def stream_add_kernel(*refs):
    held, got, kept, sent = refs[0:4], refs[4:8], refs[8:12], refs[12:16]
    if not sent:
        for s in range(4):
            kept[s][...] = held[s][...] + got[s][...]
        return
    step, half = pl.program_id(0), pl.num_programs(0) // 2
    for s in range(4):

        @pl.when(step < half)
        def _():
            kept[s][...] = held[s][...] + got[s][...]

        @pl.when(step >= half)
        def _():
            sent[s][...] = held[s][...] + got[s][...]


def stream_add(held, got):
    blocks = held[0].shape[0] // 128
    half = blocks // 2
    row = [pl.BlockSpec((128, x.shape[1]), lambda i: (i, 0)) for x in held]
    keep = [pl.BlockSpec((128, x.shape[1]), lambda i: (jnp.minimum(i, max(half - 1, 0)), 0)) for x in held]
    send = [pl.BlockSpec((128, x.shape[1]), lambda i: (jnp.maximum(i - half, 0), 0)) for x in held]
    shapes = [struct(max(half, 1) * 128, x.shape[1]) for x in held]
    out = pl.pallas_call(
        stream_add_kernel,
        name="stream_add",
        grid=(blocks,),
        out_shape=shapes + shapes if half else shapes,
        in_specs=row + row,
        out_specs=keep + send if half else keep,
        compiler_params=pltpu.CompilerParams(vmem_limit_bytes=32 * MIB),
    )(*held, *got)
    return out[:4], out[4:]


def stream_masks(axis, mask):
    other = "seq_0" if axis == "seq_1" else "seq_1"
    return ((axis, mask), (axis, 4 - mask), (other, mask), (other, 4 - mask))


def sum_streams(kept, sent):
    for step in range(4):
        got = [swap(x, *stream_masks(*STREAMS[s])[step]) for s, x in enumerate(sent)]
        kept, sent = stream_add(kept, got)
    return kept


def dot(a, b):
    return jnp.dot(a, b, preferred_element_type=F32)


def dot_t(a, b):
    return lax.dot_general(a, b, (((1,), (1,)), ((), ())), preferred_element_type=F32)


def per_device(
    hidden_in,
    cotangent,
    starts,
    norm_in,
    w_in,
    short_w,
    pole_pairs,
    residues,
    w_out,
    norm_mid,
    w_gate,
    w_up,
    w_down,
):
    me = lax.axis_index("tp")
    core = lax.axis_index("seq_2")
    first_core = core == 0

    def other_core(x):
        return swap(x, "seq_2", 1)

    hidden_other = other_core(hidden_in)
    cotangent_other = other_core(cotangent)

    marks = starts.astype(F32)
    keep_one = 1.0 - marks
    keep_two = keep_one * (1.0 - jnp.concatenate([jnp.zeros((1,), F32), marks[:-1]]))
    is_open = (jnp.sum(starts) == 0).astype(F32).reshape(1, 1)
    rim_scale = jnp.stack([1.0 - marks[-1], jnp.ones((), F32)])[:, None]
    one_column, two_column = keep_one[:, None], keep_two[:, None]
    taps = short_w.reshape(9, C)

    power = (pole_pairs[0], pole_pairs[1])
    for _ in range(8):
        power = times(power, power)
    by_device = power
    by_chip = times(power, power)
    by_plane = times(by_chip, by_chip)
    by_plane = times(by_plane, by_plane)

    rim_rows = jnp.pad(hidden_in[T - 2 :] * rim_scale, ((6, 0), (0, 0)))
    rim_rows = lax.ppermute(rim_rows, SEQ, [(i, i + 1) for i in range(31)])
    inverse_in = inverse_rms(hidden_in)
    normed_in = (hidden_in * inverse_in * norm_in).astype(BF16)
    normed_rim = (rim_rows * inverse_rms(rim_rows) * norm_in).astype(BF16)
    proj = jnp.einsum(
        "td,kdc->ktc",
        jnp.concatenate([normed_rim, normed_in]),
        w_in,
        preferred_element_type=F32,
    )
    mixed, end = mix(proj, taps, one_column, two_column, starts, pole_pairs)
    entering = carried_state(
        (end[0], end[1]), is_open, (by_device, by_chip, by_plane), False
    )
    signal, gated, history = signal_of(mixed, starts, pole_pairs, residues, entering)

    gated_x = rows_by_owner(gated, me)
    branch = scatter_sum(dot(gated_x, w_out))
    hidden_mine = lax.dynamic_slice_in_dim(hidden_in, me * ROWS, ROWS, 0)
    cotangent_mine = lax.dynamic_slice_in_dim(cotangent, me * ROWS, ROWS, 0)
    middle = hidden_mine + branch
    mid_f = gather_rows(middle * inverse_rms(middle))
    mid_x = (mid_f * norm_mid).astype(BF16)
    mid_other = (other_core(mid_f) * norm_mid).astype(BF16)

    cotangent_x = rows_by_owner(cotangent, me)
    cotangent_other_x = rows_by_owner(cotangent_other, me)
    down_grad = cotangent_x.astype(BF16)
    gate_pre = dot(mid_x, w_gate)
    up_pre = dot(mid_x, w_up)
    sig = jax.nn.sigmoid(gate_pre)
    silu = gate_pre * sig
    hidden = (silu * up_pre).astype(BF16)
    grad_hidden = dot_t(down_grad, w_down)
    grad_gate = (grad_hidden * up_pre * sig * (1.0 + gate_pre * (1.0 - sig))).astype(BF16)
    grad_up = (grad_hidden * silu).astype(BF16)
    mid_terms = dot_t(grad_gate, w_gate) + dot_t(grad_up, w_up)
    grad_normed_mid = scatter_sum(mid_terms)

    def pick(flag, a, b):
        return jnp.where(flag, a, b)

    def gate_up_part(flag):
        return jnp.concatenate(
            [
                pick(flag, grad_gate[:, :768], grad_up[:, 640:]),
                pick(flag, grad_up[:, :640], grad_gate[:, 768:]),
            ],
            axis=1,
        )

    def down_part(flag):
        return pick(flag, hidden[:, :768], hidden[:, 640:])

    ffn_sum = wide_token_sum(
        mid_x,
        mid_other,
        down_grad,
        cotangent_other_x,
        gate_up_part(first_core),
        other_core(gate_up_part(~first_core).astype(F32)),
        down_part(first_core),
        other_core(down_part(~first_core).astype(F32)),
    )
    share_ffn = lax.psum_scatter(ffn_sum, ("seq_0", "seq_1"), scatter_dimension=0, tiled=True)

    through_norm = rms_back(middle, norm_mid, grad_normed_mid)
    grad_middle = cotangent_mine + through_norm
    through_f = gather_rows(through_norm)
    branch_grad = tie((cotangent_x + through_f).astype(BF16), ffn_sum)
    branch_other = (cotangent_other_x + other_core(through_f)).astype(BF16)
    grad_gated = rows_by_owner(dot_t(branch_grad, w_out), me)
    gated_f = gated_x.astype(F32)
    out_right = pick(first_core, gated_x[:, :256], gated_x[:, 256:])
    out_wide = other_core(pick(first_core, gated_f[:, 256:], gated_f[:, :256]))

    ffn = scatter_sum(dot(tie(hidden, grad_gated), w_down))
    leaving = adjoint_end(grad_gated, mixed, starts, pole_pairs, residues)
    conjugate = [(p[0], -p[1]) for p in (by_device, by_chip, by_plane)]
    returning = carried_state((leaving[0], leaving[1]), is_open, conjugate, True)
    grad_proj, rim_grad, sums = back(
        grad_gated,
        mixed,
        signal,
        proj,
        history,
        taps,
        one_column,
        two_column,
        starts,
        pole_pairs,
        residues,
        returning,
    )
    rim_back = lax.ppermute(rim_grad, SEQ, [(i + 1, i) for i in range(31)])
    grad_proj = jnp.concatenate(
        [grad_proj[:, : T - 2], grad_proj[:, T - 2 :] + rim_back[:, :2] * rim_scale], axis=1
    ).astype(BF16)

    grad_proj_x = rows_by_owner(grad_proj, me, 1)
    first_terms = jnp.einsum("ktc,kdc->td", grad_proj_x, w_in, preferred_element_type=F32)
    grad_normed_in = scatter_sum(first_terms)
    normed_other = (hidden_other * inverse_rms(hidden_other) * norm_in).astype(BF16)

    def proj_part(flag):
        return jnp.concatenate(
            [pick(flag, grad_proj[k, :, :256], grad_proj[k, :, 256:]) for k in range(3)], axis=1
        )

    kept, leaving_now = stream_token_sum(
        chunk_table(),
        normed_in,
        normed_other,
        branch_grad,
        branch_other,
        proj_part(first_core),
        other_core(proj_part(~first_core).astype(F32)),
        out_right,
        out_wide,
    )
    share_mixer = sum_streams(kept, leaving_now)
    result = rows_by_owner(gather_rows(middle + ffn), me)
    grad_input = grad_middle + rms_back(hidden_mine, norm_in, grad_normed_in)
    grad_input = rows_by_owner(gather_rows(grad_input), me)

    gain_mid = jnp.sum(grad_normed_mid * middle * inverse_rms(middle), axis=0)
    gain_in = jnp.sum(grad_normed_in * hidden_mine * inverse_rms(hidden_mine), axis=0)
    gains = sum_over(jnp.concatenate([gain_in.reshape(4, C), gain_mid.reshape(4, C)]), "tp")
    small = jnp.concatenate([sums, gains])
    for axis in ("seq_2", "seq_1", "seq_0"):
        small = sum_over(small, axis)

    def joined(share):
        low, high = share[:64], share[64:]
        kept = jnp.where(first_core, low, high)
        got = other_core(jnp.where(first_core, high, low))
        return jnp.where(first_core, kept, got), jnp.where(first_core, got, kept)

    a, b = joined(share_ffn)
    share_gate = jnp.concatenate([a[:, :768], b[:, 768:1408]], axis=1)
    share_up = jnp.concatenate([a[:, 768:1408], b[:, :768]], axis=1)
    share_down = jnp.concatenate([a[:, 1408:], b[:, 1408 + 128 :]], axis=1).T
    a, b = joined(jnp.concatenate(share_mixer, axis=1))
    share_in = jnp.stack(
        [
            jnp.concatenate([a[:, 256 * k : 256 * k + 256], b[:, 256 * k : 256 * k + 256]], axis=1)
            for k in range(3)
        ]
    )
    share_out = jnp.concatenate([a[:, 768:], b[:, 768:]], axis=1).T
    return (
        result,
        grad_input,
        small[80:84].reshape(D),
        share_in,
        small[64:73].reshape(3, 3, C),
        small[0:32].reshape(2, N, C),
        small[32:64].reshape(2, N, C),
        share_out,
        small[84:88].reshape(D),
        share_gate,
        share_up,
        share_down,
    )


def solution(mesh):
    split = Mesh(mesh.devices.reshape(4, 4, 2, mesh.shape["tp"]), ("seq_0", "seq_1", "seq_2", "tp"))
    in_specs = (
        P(SEQ, None),
        P(SEQ, None),
        P(SEQ),
        P(),
        P(None, None, "tp"),
        P(None, None, "tp"),
        P(None, None, "tp"),
        P(None, None, "tp"),
        P("tp", None),
        P(),
        P(None, "tp"),
        P(None, "tp"),
        P("tp", None),
    )
    out_specs = (
        P(SEQ, None),
        P(SEQ, None),
        P(),
        P(None, SEQ, "tp"),
        P(None, None, "tp"),
        P(None, None, "tp"),
        P(None, None, "tp"),
        P("tp", SEQ),
        P(),
        P(SEQ, "tp"),
        P(SEQ, "tp"),
        P("tp", SEQ),
    )
    return jax.shard_map(
        per_device, mesh=split, in_specs=in_specs, out_specs=out_specs, check_vma=False
    )
```

```python
import functools

import jax
import jax.numpy as jnp
from jax import lax
from jax.experimental import pallas as pl
from jax.experimental.pallas import tpu as pltpu
from jax.sharding import Mesh
from jax.sharding import PartitionSpec as P

SEQ = ("seq_0", "seq_1", "seq_2")
F32 = jnp.float32
BF16 = jnp.bfloat16
epsilon = 1e-06
MIB = 1 << 20
T, C, N, D = 256, 512, 16, 2048
BLOCK = 32
BLOCKS = T // BLOCK
ROWS = 64
VMEM = pl.BlockSpec(memory_space=pltpu.VMEM)
SMEM = pl.BlockSpec(memory_space=pltpu.SMEM)
ANY = pl.BlockSpec(memory_space=pl.ANY)


def in_hbm(x):
    return pltpu.with_memory_space_constraint(x, pltpu.HBM)


def taking(microseconds):
    return pl.CostEstimate(flops=0, bytes_accessed=int(microseconds * 3.0e6), transcendentals=0)


def whole(*shape):
    return pl.BlockSpec(shape, lambda i: (0,) * len(shape))


def struct(*shape, dtype=F32):
    return jax.ShapeDtypeStruct(shape, dtype)


def times(a, b):
    return a[0] * b[0] - a[1] * b[1], a[0] * b[1] + a[1] * b[0]


def plus(a, b):
    return a[0] + b[0], a[1] + b[1]


def where2(flag, a, b):
    return jnp.where(flag, a[0], b[0]), jnp.where(flag, a[1], b[1])


def scaled(a, factor):
    return a[0] * factor, a[1] * factor


def token_sum(a, b):
    return lax.dot_general(a, b, (((0,), (0,)), ((), ())), preferred_element_type=F32)


def dot(a, b):
    return jnp.dot(a, b, preferred_element_type=F32)


def dot_t(a, b):
    return lax.dot_general(a, b, (((1,), (1,)), ((), ())), preferred_element_type=F32)


def scan_groups(groups, starts, base, run, carry, reverse):
    def body(step, kept):
        group = groups - 1 - step if reverse else step
        first = base + group * 8
        marks = starts[first]
        for r in range(1, 8):
            marks = marks + starts[first + r]
        return lax.cond(
            marks > 0, lambda c: run(group, c, True), lambda c: run(group, c, False), kept
        )

    return lax.fori_loop(0, groups, body, carry)


def quarter_rows(quarter):
    return pl.ds(pl.multiple_of(quarter * ROWS, ROWS), ROWS)


def eight(group):
    return pl.ds(pl.multiple_of(group * 8, 8), 8)


def keep_at(starts, token):
    return (1 - starts[token]).astype(F32)


def with_rim(proj, rim, k, rows):
    rows[0:8] = rim[k]
    rows[8:] = proj[k]


def keeps_of(column):
    marks = column[...].astype(F32)
    one = 1.0 - marks
    two = one * jnp.concatenate([jnp.ones((1, 1), F32), one[: T - 1]])
    return one, two, 1.0 - jnp.max(marks, axis=0, keepdims=True)


def mix_kernel(proj, rim, taps, column, starts, poles, mixed, end, powers, rows, driven):
    one, two, is_open = keeps_of(column)
    for k in range(3):
        with_rim(proj, rim, k, rows)
        mixed[k] = (
            taps[k, 0:1] * proj[k]
            + taps[k, 1:2] * (one * rows[7 : 7 + T])
            + taps[k, 2:3] * (two * rows[6 : 6 + T])
        )
    driven[...] = mixed[1] * mixed[2]
    pre, pim = poles[0], poles[1]

    def run(group, state, masked):
        source = driven[eight(group), :]
        re, im = state
        for r in range(8):
            if masked:
                keep = keep_at(starts, group * 8 + r)
                re, im = re * keep, im * keep
            re, im = pre * re - pim * im + source[r : r + 1], pre * im + pim * re
        return re, im

    zero = jnp.zeros((N, C), F32)
    end[0:N], end[N : 2 * N] = scan_groups(T // 8, starts, 0, run, (zero, zero), False)
    end[2 * N :] = jnp.broadcast_to(is_open, (8, C))
    power = (pre, pim)
    for n in range(1, 12):
        power = times(power, power)
        if n in (8, 9, 11):
            at = {8: 0, 9: 2, 11: 4}[n]
            powers[at], powers[at + 1] = power


def mix(proj, rim, taps, column, starts, poles):
    return pl.pallas_call(
        mix_kernel,
        name="mix_and_end_state",
        cost_estimate=taking(4),
        out_shape=(pltpu.HBM((3, T, C), F32), struct(2 * N + 8, C), struct(6, N, C)),
        in_specs=[VMEM] * 4 + [SMEM, VMEM],
        out_specs=(VMEM,) * 3,
        scratch_shapes=[pltpu.VMEM((T + 8, C), F32), pltpu.VMEM((T, C), F32)],
        compiler_params=pltpu.CompilerParams(vmem_limit_bytes=10 * MIB),
    )(proj, rim, taps, column, starts, poles)


def forward_rows(mixed, starts, poles, block, state, visit):
    pre, pim = poles[0], poles[1]
    base = block * BLOCK

    def run(group, kept, masked):
        source = mixed[1, eight(group), :] * mixed[2, eight(group), :]
        re, im = kept
        for r in range(8):
            if masked:
                keep = keep_at(starts, base + group * 8 + r)
                re, im = re * keep, im * keep
            re, im = pre * re - pim * im + source[r : r + 1], pre * im + pim * re
            visit(group * 8 + r, re, im)
        return re, im

    state[0], state[1] = scan_groups(BLOCK // 8, starts, base, run, (state[0], state[1]), False)


def signal_kernel(mixed, starts, poles, residues, first, signal, gated, state):
    block = pl.program_id(0)

    @pl.when(block == 0)
    def _():
        state[...] = first[...]

    qre, qim = residues[0], residues[1]

    def visit(row, re, im):
        signal[pl.ds(row, 1), :] = jnp.sum(qre * re - qim * im, axis=0, keepdims=True)

    forward_rows(mixed, starts, poles, block, state, visit)
    gated[...] = (mixed[0] * signal[...]).astype(BF16)


def history_kernel(mixed, starts, poles, first, *rest):
    h0, h1, h2, h3, token, state = rest[-6:]
    block = pl.program_id(0)
    token[...] = jnp.zeros(token.shape, F32)

    @pl.when(block == 0)
    def _():
        state[...] = first[...]

    def visit(row, re, im):
        h0[row], h1[row] = re[:8], re[8:]
        h2[row], h3[row] = im[:8], im[8:]

    forward_rows(mixed, starts, poles, block, state, visit)


def signal_of(mixed, starts, poles, residues, first):
    return pl.pallas_call(
        signal_kernel,
        name="signal",
        cost_estimate=taking(6),
        grid=(BLOCKS,),
        out_shape=(struct(T, C), struct(T, C, dtype=BF16)),
        in_specs=[
            pl.BlockSpec((3, BLOCK, C), lambda i: (0, i, 0)),
            SMEM,
            whole(2, N, C),
            whole(2, N, C),
            whole(2, N, C),
        ],
        out_specs=(pl.BlockSpec((BLOCK, C), lambda i: (i, 0)),) * 2,
        scratch_shapes=[pltpu.VMEM((2, N, C), F32)],
        compiler_params=pltpu.CompilerParams(vmem_limit_bytes=8 * MIB),
    )(mixed, starts, poles, residues, first)


def history_of(mixed, starts, poles, first, *after):
    return pl.pallas_call(
        history_kernel,
        name="state_history",
        cost_estimate=taking(8),
        grid=(BLOCKS,),
        out_shape=(pltpu.HBM((T, 8, C), F32),) * 4 + (struct(8, 128),),
        in_specs=[
            pl.BlockSpec((3, BLOCK, C), lambda i: (0, i, 0)),
            SMEM,
            whole(2, N, C),
            whole(2, N, C),
        ]
        + [ANY] * len(after),
        out_specs=(pl.BlockSpec((BLOCK, 8, C), lambda i: (i, 0, 0)),) * 4 + (whole(8, 128),),
        scratch_shapes=[pltpu.VMEM((2, N, C), F32)],
        compiler_params=pltpu.CompilerParams(vmem_limit_bytes=11 * MIB),
    )(in_hbm(mixed), starts, poles, first, *after)


def adjoint_kernel(grad_gated, query, column, starts, poles, residues, out, grads):
    grads[...] = grad_gated[...] * query[0]
    pre, pim, qre, qim = poles[0], poles[1], residues[0], residues[1]

    def run(group, kept, masked):
        source = grads[eight(group), :]
        re, im = kept
        for r in reversed(range(8)):
            row = source[r : r + 1]
            re, im = row * qre + (pre * re + pim * im), (pre * im - pim * re) - row * qim
            if masked:
                keep = keep_at(starts, group * 8 + r)
                re, im = re * keep, im * keep
        return re, im

    zero = jnp.zeros((N, C), F32)
    out[0:N], out[N : 2 * N] = scan_groups(T // 8, starts, 0, run, (zero, zero), True)
    out[2 * N :] = jnp.broadcast_to(keeps_of(column)[2], (8, C))


def adjoint_end(grad_gated, mixed, column, starts, poles, residues):
    return pl.pallas_call(
        adjoint_kernel,
        name="adjoint_end",
        cost_estimate=taking(4),
        grid=(1,),
        out_shape=struct(2 * N + 8, C),
        in_specs=[
            whole(T, C),
            pl.BlockSpec((1, T, C), lambda i: (0, 0, 0)),
            whole(T, 1),
            SMEM,
            whole(2, N, C),
            whole(2, N, C),
        ],
        out_specs=whole(2 * N + 8, C),
        scratch_shapes=[pltpu.VMEM((T, C), F32)],
        compiler_params=pltpu.CompilerParams(vmem_limit_bytes=9 * MIB),
    )(grad_gated, mixed, column, starts, poles, residues)


def back_kernel(
    grad_gated,
    mixed,
    signal,
    proj,
    proj_rim,
    h0,
    h1,
    h2,
    h3,
    taps,
    column,
    starts,
    poles,
    residues,
    first,
    *rest,
):
    grad_proj, rim, sums, state, driven_grad, mixed_grad, rows_before = rest[-7:]
    step = pl.program_id(0)
    block = BLOCKS - 1 - step

    @pl.when(step == 0)
    def _():
        state[...] = first[...]
        sums[...] = jnp.zeros(sums.shape, F32)

    pre, pim, qre, qim = poles[0], poles[1], residues[0], residues[1]
    base = block * BLOCK

    def run(group, kept, masked):
        rows = pl.ds(pl.multiple_of(base + group * 8, 8), 8)
        source = grad_gated[rows, :] * mixed[0, rows, :]
        re, im = kept
        for r in reversed(range(8)):
            row = source[r : r + 1]
            token = group * 8 + r
            sre = jnp.concatenate([h0[token], h1[token]])
            sim = jnp.concatenate([h2[token], h3[token]])
            sums[0:16] += re * sre + im * sim
            sums[16:32] += im * sre - re * sim
            sums[32:48] += row * sre
            sums[48:64] -= row * sim
            re, im = row * qre + (pre * re + pim * im), (pre * im - pim * re) - row * qim
            driven_grad[pl.ds(base + group * 8 + r, 1), :] = jnp.sum(re, axis=0, keepdims=True)
            if masked:
                keep = keep_at(starts, base + group * 8 + r)
                re, im = re * keep, im * keep
        return re, im

    state[0], state[1] = scan_groups(BLOCK // 8, starts, base, run, (state[0], state[1]), True)

    @pl.when(step == BLOCKS - 1)
    def _():
        one, two, _ = keeps_of(column)
        mixed_grad[0, 0:T] = grad_gated[...] * signal[...]
        mixed_grad[1, 0:T] = driven_grad[...] * mixed[2]
        mixed_grad[2, 0:T] = driven_grad[...] * mixed[1]
        for k in range(3):
            with_rim(proj, proj_rim, k, rows_before)
            here = mixed_grad[k, 0:T]
            sums[64 + 3 * k : 65 + 3 * k] = jnp.sum(here * proj[k], axis=0, keepdims=True)
            grad_proj[k] = taps[k, 0:1] * here
            here = one * mixed_grad[k, 0:T]
            sums[65 + 3 * k : 66 + 3 * k] = jnp.sum(here * rows_before[7 : 7 + T], axis=0, keepdims=True)
            mixed_grad[k, 0:T] = two * mixed_grad[k, 0:T]
            here = taps[k, 1:2] * here
            grad_proj[k, 0 : T - 1] += here[1:T]
            rim[k] = jnp.zeros((8, C), F32)
            rim[k, 1:2] = here[0:1]
            here = mixed_grad[k, 0:T]
            sums[66 + 3 * k : 67 + 3 * k] = jnp.sum(here * rows_before[6 : 6 + T], axis=0, keepdims=True)
            here = taps[k, 2:3] * here
            grad_proj[k, 0 : T - 2] += here[2:T]
            rim[k, 0:2] += here[0:2]


def back(grad_gated, mixed, signal, proj, proj_rim, history, taps, column, starts, poles, residues, first, *after):
    return pl.pallas_call(
        back_kernel,
        name="adjoint_and_short_back",
        cost_estimate=taking(13),
        grid=(BLOCKS,),
        out_shape=(struct(3, T, C), struct(3, 8, C), struct(80, C)),
        in_specs=[
            whole(T, C),
            whole(3, T, C),
            whole(T, C),
            whole(3, T, C),
            whole(3, 8, C),
        ]
        + [pl.BlockSpec((BLOCK, 8, C), lambda i: (BLOCKS - 1 - i, 0, 0))] * 4
        + [
            whole(3, 3, C),
            whole(T, 1),
            SMEM,
            whole(2, N, C),
            whole(2, N, C),
            whole(2, N, C),
        ]
        + [ANY] * len(after),
        out_specs=(whole(3, T, C), whole(3, 8, C), whole(80, C)),
        scratch_shapes=[
            pltpu.VMEM((2, N, C), F32),
            pltpu.VMEM((T, C), F32),
            pltpu.VMEM((3, T, C), F32),
            pltpu.VMEM((T + 8, C), F32),
        ],
        compiler_params=pltpu.CompilerParams(vmem_limit_bytes=25 * MIB),
    )(
        grad_gated,
        mixed,
        signal,
        proj,
        proj_rim,
        *history,
        taps,
        column,
        starts,
        poles,
        residues,
        first,
        *after,
    )


def swap(value, axis, mask):
    size = lax.axis_size(axis)
    return lax.ppermute(value, axis, [(i, i ^ mask) for i in range(size)])


def shifted(value, axis, steps):
    count = lax.axis_size(axis)
    first, last = max(0, -steps), min(count, count - steps)
    return lax.ppermute(value, axis, [(i, i + steps) for i in range(first, last)])


def pair_add_kernel(left, got_left, right, got_right, *rest):
    left_own, left_next, right_own, right_next = rest[-4:]
    left_own[...] = left[:ROWS] + got_left[:ROWS]
    left_next[...] = left[ROWS:] + got_left[ROWS:]
    right_own[...] = right[:ROWS] + got_right[:ROWS]
    right_next[...] = right[ROWS:] + got_right[ROWS:]


def pair_call(name, kernel, shapes, operands, after):
    return pl.pallas_call(
        kernel,
        name=name,
        cost_estimate=taking(0.8),
        out_shape=shapes,
        in_specs=[VMEM] * len(operands) + [ANY] * len(after),
        out_specs=[VMEM] * len(shapes),
        compiler_params=pltpu.CompilerParams(vmem_limit_bytes=10 * MIB),
    )(*operands, *after)


def scatter_end(pieces, got_left, got_right, *after):
    left_own, left_next, right_own, right_next = pair_call(
        "pair_add",
        pair_add_kernel,
        [struct(ROWS, HALF)] * 4,
        (pieces[0], got_left, pieces[2], got_right),
        after,
    )
    return left_own, swap(left_next, "tp", 3), right_own, swap(right_next, "tp", 1)


def scatter_start(pieces):
    return swap(pieces[1], "tp", 1), swap(pieces[3], "tp", 3)


def scatter_sum(pieces, *after):
    return scatter_end(pieces, *scatter_start(pieces), *after)


def pair_join_kernel(left, left_3, right, right_1, *rest):
    left_03, right_10 = rest[-2:]
    rows = left.shape[0]
    left_03[:rows], left_03[rows:] = left[...], left_3[...]
    right_10[:rows], right_10[rows:] = right_1[...], right[...]


def gather_joined(left, right, *after):
    left_3 = swap(left, "tp", 3)
    right_1 = swap(right, "tp", 1)
    left_03, right_10 = pair_call(
        "pair_join",
        pair_join_kernel,
        [struct(2 * left.shape[0], HALF)] * 2,
        (left, left_3, right, right_1),
        after,
    )
    parts = left, swap(left_03, "tp", 1), left_3, right, right_1, swap(right_10, "tp", 3)
    return parts, (left_03, right_10)


def gather_parts(left, right, *after):
    return gather_joined(left, right, *after)[0]


def quarters_of(parts):
    left, left_12, left_3, right, right_1, right_23 = parts
    rows = left.shape[0]
    return (
        (left[:rows], right[:rows]),
        (left_12[:rows], right_1[:rows]),
        (left_12[rows:], right_23[:rows]),
        (left_3[:rows], right_23[rows:]),
    )


def of_payload(ref):
    return (ref[0:N], ref[N : 2 * N]), ref[2 * N : 2 * N + 1]


def to_payload(ref, state, is_open):
    ref[0:N], ref[N : 2 * N] = state
    ref[2 * N :] = jnp.broadcast_to(is_open, (8, C))


def power_of(powers, at, reverse):
    return powers[at], -powers[at + 1] if reverse else powers[at + 1]


def chip_kernel(reverse, place, mine, other, powers, out):
    (state, is_open), (state_other, open_other) = of_payload(mine), of_payload(other)
    by_device = power_of(powers, 0, reverse)
    last = place[1] == (0 if reverse else 1)
    earlier = where2(last, state_other, state)
    later = where2(last, state, state_other)
    later_open = jnp.where(last, is_open, open_other)
    chip = plus(later, times(scaled(by_device, later_open), earlier))
    to_payload(out, chip, is_open * open_other)


def plane_kernel(reverse, place, mine, got_1, got_2, got_3, powers, *rest):
    out, before = rest[-2:]
    chip, is_open = of_payload(mine)
    by_chip = power_of(powers, 2, reverse)
    got = {1: of_payload(got_1), 2: of_payload(got_2), 3: of_payload(got_3)}
    y = 3 - place[2] if reverse else place[2]
    one, zero = jnp.ones((N, C), F32), jnp.zeros((N, C), F32)
    entering, weight = (zero, zero), (one, zero)
    for k in (1, 2, 3):
        state, opened = got[k]
        entering = where2(y >= k, plus(entering, times(weight, state)), entering)
        weight = where2(y >= k, times(weight, scaled(by_chip, opened)), weight)
    plane = plus(chip, times(scaled(by_chip, is_open), entering))
    for j in (1, 2, 3):
        state, opened = got[4 - j]
        plane = where2(y + j <= 3, plus(state, times(scaled(by_chip, opened), plane)), plane)
        is_open = is_open * opened
    to_payload(out, plane, is_open)
    before[0], before[1] = entering
    before[2], before[3] = weight


def enter_kernel(reverse, place, before, got_1, got_2, got_3, other, powers, *rest):
    out = rest[-1]
    by_device, by_plane = power_of(powers, 0, reverse), power_of(powers, 4, reverse)
    one, zero = jnp.ones((N, C), F32), jnp.zeros((N, C), F32)
    entering, weight = (zero, zero), (one, zero)
    for ref in (got_1, got_2, got_3):
        state, opened = of_payload(ref)
        entering = plus(entering, times(weight, state))
        weight = times(weight, scaled(by_plane, opened))
    at_chip = plus((before[0], before[1]), times((before[2], before[3]), entering))
    state, opened = of_payload(other)
    at_core = plus(state, times(scaled(by_device, opened), at_chip))
    out[0], out[1] = where2(place[1] == (0 if reverse else 1), at_core, at_chip)


def small_call(name, kernel, reverse, shapes, operands, after=()):
    return pl.pallas_call(
        functools.partial(kernel, reverse),
        name=name,
        cost_estimate=taking(1.6),
        out_shape=shapes,
        in_specs=[SMEM] + [VMEM] * (len(operands) - 1) + [ANY] * len(after),
        out_specs=jax.tree.map(lambda _: VMEM, shapes),
        compiler_params=pltpu.CompilerParams(vmem_limit_bytes=8 * MIB),
    )(*operands, *after)


def carried_state(place, mine, powers, reverse, after=(), late=()):
    sign = -1 if reverse else 1
    payload = struct(2 * N + 8, C)
    other = swap(mine, "seq_2", 1)
    chip = small_call("chip_state", chip_kernel, reverse, payload, (place, mine, other, powers))
    got = [
        lax.ppermute(chip, "seq_1", [(i, (i + sign * k) % 4) for i in range(4)]) for k in (1, 2, 3)
    ]
    plane, before = small_call(
        "plane_state",
        plane_kernel,
        reverse,
        (payload, struct(4, N, C)),
        (place, chip, *got, powers),
        after,
    )
    got = [shifted(plane, "seq_0", sign * k) for k in (1, 2, 3)]
    entering = small_call(
        "entering_state",
        enter_kernel,
        reverse,
        struct(2, N, C),
        (place, before, *got, other, powers),
        late,
    )
    return entering, plane


def sum_over(x, axis, *after):
    if lax.axis_size(axis) == 2:
        return x + swap(x, axis, 1)
    got = [swap(x, axis, k) for k in (1, 2, 3)]
    if after:
        got = [tie(g, *after) for g in got]
    return (x + got[0]) + (got[1] + got[2])


def inverse_rms(values):
    return lax.rsqrt(jnp.mean(values * values, axis=-1, keepdims=True) + epsilon)


def nothing(*refs):
    pass


def tie(x, *after, hbm=False):
    shape = struct(*x.shape, dtype=x.dtype)
    if hbm:
        x, shape = in_hbm(x), pltpu.HBM(x.shape, x.dtype)
    return pl.pallas_call(
        nothing,
        name="tie",
        out_shape=shape,
        in_specs=[ANY] * (1 + len(after)),
        out_specs=ANY,
        input_output_aliases={0: 0},
        compiler_params=pltpu.CompilerParams(vmem_limit_bytes=6 * MIB),
    )(x, *after)


WIDE = 1408


def wide_sum_kernel(left_a, l03, r10, l12, r23, left_b, more_b, right, wide, gain, out, token, low, mid):
    step = pl.program_id(0)

    @pl.when(step == 0)
    def _():
        low[...] = wide[...].astype(BF16)
        token[...] = jnp.zeros(token.shape, F32)

    def put(*quarters):
        mid[...] = (jnp.concatenate(quarters) * gain[...]).astype(BF16)

    pl.when(step < 4)(lambda: put(l03[:ROWS], l12[:ROWS], l12[ROWS:], l03[ROWS:]))
    pl.when(step >= 4)(lambda: put(r10[ROWS:], r10[:ROWS], r23[:ROWS], r23[ROWS:]))
    out[:, :WIDE] = token_sum(left_a[...], right[:, :WIDE]) + token_sum(mid[...], low[:, :WIDE])
    out[:, WIDE:] = token_sum(left_b[...], right[:, WIDE:]) + token_sum(more_b[...], low[:, WIDE:])


def wide_token_sum(left_a, more_a, left_b, more_b, right, wide, gain):
    rows = 256
    column = pl.BlockSpec((T, rows), lambda i: (0, i))
    low = pl.BlockSpec((2 * ROWS, rows), lambda i: (0, jnp.minimum(i, 3)))
    high = pl.BlockSpec((2 * ROWS, rows), lambda i: (0, jnp.maximum(i - 4, 0)))
    width = right.shape[1]
    return pl.pallas_call(
        wide_sum_kernel,
        name="weight_gradients",
        cost_estimate=taking(10),
        grid=(D // rows,),
        out_shape=(pltpu.HBM((D, width), F32), struct(8, 128)),
        in_specs=[column, low, high, low, high, column, column]
        + [whole(T, width), whole(T, width), pl.BlockSpec((1, rows), lambda i: (0, i))],
        out_specs=(pl.BlockSpec((rows, width), lambda i: (i, 0)), whole(8, 128)),
        scratch_shapes=[pltpu.VMEM((T, width), BF16), pltpu.VMEM((T, rows), BF16)],
        compiler_params=pltpu.CompilerParams(vmem_limit_bytes=22 * MIB),
    )(left_a, *more_a, left_b, more_b, right, wide, gain)


ORDERS = {1: (0, 3, 1, 2), 3: (0, 1, 3, 2)}
STREAMS = (("seq_1", 1), ("seq_1", 3), ("seq_0", 1), ("seq_0", 3))


def stream_places(step):
    jz, jy = divmod(step, 4)
    places = []
    for axis, mask in STREAMS:
        order = ORDERS[mask]
        first, second = (jy, jz) if axis == "seq_1" else (jz, jy)
        places.append(order.index(first) * 4 + order.index(second))
    return places


def stream_sum_kernel(
    place,
    left_a,
    more_a,
    left_b,
    more_b,
    right_a,
    wide_a,
    right_b,
    wide_b,
    sums,
    gains_a,
    gains_b,
    *rest,
):
    kept, sent, token, turned = rest[-10:-6], rest[-6:-2], rest[-2], rest[-1]
    token[...] = jnp.zeros(token.shape, F32)
    for s in range(4):
        kept[s][2048 : 2048 + 80] = sums[:, 128 * s : 128 * s + 128]
        for n in range(8):
            row = (gains_a, gains_b)[n // 4]
            at = C * (n % 4) + 128 * s
            kept[s][2128 + n : 2129 + n] = row[:, at : at + 128]
        sent[s][2048:] = kept[s][2048:]
    turned[0:768, 0:T] = right_a[...].T
    turned[768:, 0:T] = right_b[...].T
    turned[0:768, T:] = wide_a[...].astype(BF16).T
    turned[768:, T:] = wide_b[...].astype(BF16).T
    y, z = place[2], place[3]
    for step in range(16):
        jz, jy = divmod(step, 4)
        chunk = (z ^ jz) * 4 + (y ^ jy)
        columns = pl.ds(pl.multiple_of(chunk * 128, 128), 128)
        total_a = dot(turned[0:768, 0:T], left_a[:, columns]) + dot(turned[0:768, T:], more_a[:, columns])
        total_b = dot(turned[768:, 0:T], left_b[:, columns]) + dot(turned[768:, T:], more_b[:, columns])
        for s, at in enumerate(stream_places(step)):
            target = kept[s] if at < 8 else sent[s]
            rows = slice((at % 8) * 256, (at % 8) * 256 + 256)
            target[rows] = total_a[256 * s : 256 * s + 256] if s < 3 else total_b


def stream_token_sum(place, *operands):
    out = pl.pallas_call(
        stream_sum_kernel,
        name="mixer_weight_gradients",
        cost_estimate=taking(7),
        out_shape=(struct(2048 + SMALL, 128),) * 8 + (struct(8, 128),),
        in_specs=[SMEM] + [VMEM] * 11 + [ANY] * (len(operands) - 11),
        out_specs=(VMEM,) * 9,
        scratch_shapes=[pltpu.VMEM((1024, 2 * T), BF16)],
        compiler_params=pltpu.CompilerParams(vmem_limit_bytes=8 * MIB),
    )(place, *operands)
    return out[:4], out[4:8], out[8]


SMALL = 88


def stream_add_kernel(*refs):
    held, got, kept, sent = refs[0:4], refs[4:8], refs[-8:-4], refs[-4:]
    for s in range(4):
        rows = held[s].shape[0] - SMALL
        low = rows // 2
        small = held[s][rows:] + got[s][rows:]
        kept[s][0:low] = held[s][0:low] + got[s][0:low]
        kept[s][low:] = small
        sent[s][0:low] = held[s][low:rows] + got[s][low:rows]
        sent[s][low:] = small


def stream_add(held, got, *after):
    rows = held[0].shape[0] - SMALL
    shape = struct(rows // 2 + SMALL, 128)
    out = pl.pallas_call(
        stream_add_kernel,
        name="stream_add",
        cost_estimate=taking(0.7 + rows / 1000),
        out_shape=[shape] * 8,
        in_specs=[VMEM] * 8 + [ANY] * len(after),
        out_specs=[VMEM] * 8,
        compiler_params=pltpu.CompilerParams(vmem_limit_bytes=6 * MIB),
    )(*held, *got, *after)
    return out[:4], out[4:]


def stream_last_kernel(place, *refs):
    held, got, (own, send, small) = refs[0:4], refs[4:8], refs[-3:]
    first = place[1] == 0
    for s in range(4):
        total = (held[s][0:256] + got[s][0:256]).T
        columns = slice(256 * s, 256 * s + 256)
        own[:, columns] = jnp.where(first, total[:64], total[64:])
        send[:, columns] = jnp.where(first, total[64:], total[:64])
        small[:, 128 * s : 128 * s + 128] = held[s][256:] + got[s][256:]


def stream_last(place, held, got, *after):
    return pl.pallas_call(
        stream_last_kernel,
        name="stream_last",
        cost_estimate=taking(1.5),
        out_shape=(struct(64, 1024), struct(64, 1024), struct(SMALL, C)),
        in_specs=[SMEM] + [VMEM] * 8 + [ANY] * len(after),
        out_specs=[VMEM] * 3,
        compiler_params=pltpu.CompilerParams(vmem_limit_bytes=6 * MIB),
    )(place, *held, *got, *after)


def stream_masks(axis, mask):
    other = "seq_0" if axis == "seq_1" else "seq_1"
    return ((axis, mask), (axis, 4 - mask), (other, mask), (other, 4 - mask))


def stream_swap(sent, step):
    return [swap(x, *stream_masks(*STREAMS[s])[step]) for s, x in enumerate(sent)]


def mixer_shares_kernel(place, own, got, small, small_got, grad_in, grad_out, small_sum, gains):
    first = place[1] == 0
    low = jnp.where(first, own[...], got[...])
    high = jnp.where(first, got[...], own[...])
    for k in range(3):
        columns = slice(256 * k, 256 * k + 256)
        grad_in[k, :, :256], grad_in[k, :, 256:] = low[:, columns], high[:, columns]
    grad_out[:, :256], grad_out[:, 256:] = low[:, 768:], high[:, 768:]
    total = small[...] + small_got[...]
    small_sum[...], gains[...] = total[:80], total[80:]


def mixer_shares(place, own, got, small, small_got):
    return pl.pallas_call(
        mixer_shares_kernel,
        name="mixer_shares",
        cost_estimate=taking(1.5),
        out_shape=(struct(3, 64, C), struct(64, C), struct(80, C), struct(8, C)),
        in_specs=[SMEM] + [VMEM] * 4,
        out_specs=[VMEM] * 4,
        compiler_params=pltpu.CompilerParams(vmem_limit_bytes=6 * MIB),
    )(place, own, got, small, small_got)


def ffn_send_kernel(place, share, *rest):
    own, send = rest[-2:]
    first = place[1] == 0
    low, high = share[:64], share[64:]
    own[...] = jnp.where(first, low, high)
    send[...] = jnp.where(first, high, low)


def ffn_shares_kernel(place, own, got, gate, up, down, token):
    first = place[1] == 0
    low = jnp.where(first, own[...], got[...])
    high = jnp.where(first, got[...], own[...])
    gate[:, :768], gate[:, 768:] = low[:, :768], high[:, 768:1408]
    up[:, :640], up[:, 640:] = low[:, 768:1408], high[:, :768]
    down[:, :768], down[:, 768:] = low[:, 1408:], high[:, 1408 + 128 :]
    token[...] = jnp.zeros(token.shape, F32)


def ffn_shares(place, share, other_core, *after):
    own, send = pl.pallas_call(
        ffn_send_kernel,
        name="ffn_send",
        cost_estimate=taking(1),
        out_shape=(struct(64, 2176),) * 2,
        in_specs=[SMEM, VMEM] + [ANY] * len(after),
        out_specs=[VMEM] * 2,
        compiler_params=pltpu.CompilerParams(vmem_limit_bytes=6 * MIB),
    )(place, share, *after)
    return pl.pallas_call(
        ffn_shares_kernel,
        name="ffn_shares",
        cost_estimate=taking(2),
        out_shape=(struct(64, 1408),) * 3 + (struct(8, 128),),
        in_specs=[SMEM, VMEM, VMEM],
        out_specs=[VMEM] * 4,
        compiler_params=pltpu.CompilerParams(vmem_limit_bytes=7 * MIB),
    )(place, own, other_core(send))


def outputs_kernel(place, *refs):
    *parts, result, grad_input = refs
    for q, (left, right) in enumerate(quarters_of(parts)):
        rows = quarter_rows(place[0] ^ q)
        for n, out in enumerate((result, grad_input)):
            out[rows, :HALF] = left[ROWS * n : ROWS * n + ROWS]
            out[rows, HALF:] = right[ROWS * n : ROWS * n + ROWS]


def outputs_of(place, parts):
    return pl.pallas_call(
        outputs_kernel,
        name="outputs",
        cost_estimate=taking(2),
        out_shape=(struct(T, D),) * 2,
        in_specs=[SMEM] + [VMEM] * 6,
        out_specs=[VMEM] * 2,
        compiler_params=pltpu.CompilerParams(vmem_limit_bytes=9 * MIB),
    )(place, *parts)


def norm_kernel(values, gain, *rest):
    out, inverse = rest[-2:]
    v = values[...]
    inverse[...] = inverse_rms(v)
    out[...] = (v * inverse[...] * gain[...]).astype(BF16)


def normed(values, gain, *after):
    rows = 128
    row = pl.BlockSpec((rows, D), lambda i: (i, 0))
    return pl.pallas_call(
        norm_kernel,
        name="normed_in",
        cost_estimate=taking(1.8),
        grid=(values.shape[0] // rows,),
        out_shape=(struct(*values.shape, dtype=BF16), struct(values.shape[0], 1)),
        in_specs=[row, whole(1, D)] + [ANY] * len(after),
        out_specs=(row, pl.BlockSpec((rows, 1), lambda i: (i, 0))),
        compiler_params=pltpu.CompilerParams(vmem_limit_bytes=11 * MIB),
    )(values, gain, *after)


HALF = D // 2


def rows_by_quarter(place, ref):
    return jnp.concatenate([ref[quarter_rows(place[0] ^ q), :] for q in range(4)])


def cotangent_kernel(place, cotangent, w_down, *rest):
    low, grad_hidden = rest[-2:]

    @pl.when(pl.program_id(0) == 0)
    def _():
        for q in range(4):
            low[ROWS * q : ROWS * q + ROWS] = cotangent[quarter_rows(place[0] ^ q), :].astype(BF16)

    grad_hidden[...] = dot_t(low[...], w_down[...])


def cotangent_part(place, cotangent, w_down, *after):
    wide = w_down.shape[0]
    return pl.pallas_call(
        cotangent_kernel,
        name="cotangent_part",
        cost_estimate=taking(4),
        grid=(6,),
        out_shape=(struct(T, D, dtype=BF16), struct(T, wide)),
        in_specs=[SMEM, VMEM, pl.BlockSpec((256, D), lambda i: (i, 0))] + [ANY] * len(after),
        out_specs=(VMEM, pl.BlockSpec((T, 256), lambda i: (0, i))),
        compiler_params=pltpu.CompilerParams(vmem_limit_bytes=9 * MIB),
    )(place, cotangent, w_down, *after)


def out_parts_kernel(place, gated, *rest):
    own, send = rest[-2:]
    first = place[1] == 0
    rows = rows_by_quarter(place, gated).astype(F32)
    low, high = rows[:, :256], rows[:, 256:]
    own[...] = jnp.where(first, low, high).astype(BF16)
    send[...] = jnp.where(first, high, low)


def out_parts(place, gated, *after):
    return pl.pallas_call(
        out_parts_kernel,
        name="out_parts",
        cost_estimate=taking(1),
        out_shape=(struct(T, 256, dtype=BF16), struct(T, 256)),
        in_specs=[SMEM, VMEM] + [ANY] * len(after),
        out_specs=[VMEM] * 2,
        compiler_params=pltpu.CompilerParams(vmem_limit_bytes=7 * MIB),
    )(place, gated, *after)


def owner_kernel(place, rows, *rest):
    rest[-1][...] = rows[...].astype(BF16)


def owner_rows(place, x, *after):
    row = pl.BlockSpec((ROWS, D), lambda i, place: (place[0] ^ i, 0))
    out = pl.BlockSpec((ROWS, D), lambda i, place: (i, 0))
    return pl.pallas_call(
        owner_kernel,
        name="owner_rows",
        cost_estimate=taking(2),
        out_shape=pltpu.HBM((T, D), BF16),
        grid_spec=pltpu.PrefetchScalarGridSpec(
            num_scalar_prefetch=1, grid=(4,), in_specs=[row] + [ANY] * len(after), out_specs=out
        ),
        compiler_params=pltpu.CompilerParams(vmem_limit_bytes=9 * MIB),
    )(place, in_hbm(x), *after)


def branch_other_kernel(place, cotangent, through, out):
    out[...] = (cotangent[...] + through[...]).astype(BF16)


def branch_other_of(place, cotangent, through):
    row = pl.BlockSpec((ROWS, D), lambda i, place: (i, 0))
    return pl.pallas_call(
        branch_other_kernel,
        name="branch_other",
        cost_estimate=taking(2),
        out_shape=struct(T, D, dtype=BF16),
        grid_spec=pltpu.PrefetchScalarGridSpec(
            num_scalar_prefetch=1,
            grid=(4,),
            in_specs=[pl.BlockSpec((ROWS, D), lambda i, place: (place[0] ^ i, 0)), row],
            out_specs=row,
        ),
        compiler_params=pltpu.CompilerParams(vmem_limit_bytes=9 * MIB),
    )(place, in_hbm(cotangent), through)


def middle_kernel(place, left, left_more, right, right_more, hidden, middle, out_left, out_right):
    low = hidden[:, :HALF] + (left[...] + left_more[...])
    high = hidden[:, HALF:] + (right[...] + right_more[...])
    square = jnp.sum(low * low, axis=-1, keepdims=True) + jnp.sum(high * high, axis=-1, keepdims=True)
    inverse = lax.rsqrt(square * (1.0 / D) + epsilon)
    middle[:, :HALF], middle[:, HALF:] = low, high
    out_left[...], out_right[...] = low * inverse, high * inverse


def norm_back_parts(left, left_more, right, right_more, values, gain):
    grads = (left[...] + left_more[...], right[...] + right_more[...])
    v = (values[:, :HALF], values[:, HALF:])
    g = (gain[:, :HALF], gain[:, HALF:])
    square = sum(jnp.sum(x * x, axis=-1, keepdims=True) for x in v)
    inverse = lax.rsqrt(square * (1.0 / D) + epsilon)
    along = sum(jnp.sum(a * b * c, axis=-1, keepdims=True) for a, b, c in zip(g, grads, v))
    along = inverse * inverse * inverse * (along * (1.0 / D))
    back = [inverse * g[n] * grads[n] - v[n] * along for n in (0, 1)]
    return back, [grads[n] * (v[n] * inverse) for n in (0, 1)]


def norm_back_kernel(left, left_more, right, right_more, values, gain, *rest):
    out_left, out_right, gains = rest[-3:]
    back, weighed = norm_back_parts(left, left_more, right, right_more, values, gain)
    out_left[...], out_right[...] = back
    for n in (0, 1):
        gains[:, HALF * n : HALF * n + HALF] = jnp.sum(weighed[n], axis=0, keepdims=True)


def last_back_kernel(place, *refs):
    pieces, (hidden, gain, cotangent), through, (middle, *ffn), outs = (
        refs[0:4],
        refs[4:7],
        refs[7:9],
        refs[9:14],
        refs[14:16],
    )
    back, _ = norm_back_parts(*pieces, hidden, gain)
    for n in (0, 1):
        columns = slice(HALF * n, HALF * n + HALF)
        outs[n][:ROWS] = middle[:, columns] + (ffn[2 * n][...] + ffn[2 * n + 1][...])
        outs[n][ROWS:] = cotangent[:, columns] + through[n][...] + back[n]


def by_owner_grid(in_specs, out_specs):
    return pltpu.PrefetchScalarGridSpec(
        num_scalar_prefetch=1, grid=(1,), in_specs=in_specs, out_specs=out_specs
    )


MINE = pl.BlockSpec((ROWS, D), lambda i, place: (place[0], 0))


def after_middle(place, pieces, hidden):
    return pl.pallas_call(
        middle_kernel,
        name="middle_and_norm",
        cost_estimate=taking(1.5),
        out_shape=(struct(ROWS, D), struct(ROWS, HALF), struct(ROWS, HALF)),
        grid_spec=by_owner_grid([VMEM] * 4 + [MINE], (VMEM,) * 3),
        compiler_params=pltpu.CompilerParams(vmem_limit_bytes=8 * MIB),
    )(place, *pieces, in_hbm(hidden))


def norm_back(pieces, values, gain, *after):
    return pl.pallas_call(
        norm_back_kernel,
        name="norm_back",
        cost_estimate=taking(2),
        out_shape=(struct(ROWS, HALF), struct(ROWS, HALF), struct(1, D)),
        in_specs=[VMEM] * 6 + [ANY] * len(after),
        out_specs=(VMEM,) * 3,
        compiler_params=pltpu.CompilerParams(vmem_limit_bytes=7 * MIB),
    )(*pieces, values, gain, *after)


def last_back(place, pieces, hidden, gain, cotangent, through, middle, ffn):
    return pl.pallas_call(
        last_back_kernel,
        name="last_back",
        cost_estimate=taking(2),
        out_shape=(struct(2 * ROWS, HALF),) * 2,
        grid_spec=by_owner_grid([VMEM] * 4 + [MINE, VMEM, MINE] + [VMEM] * 7, (VMEM,) * 2),
        compiler_params=pltpu.CompilerParams(vmem_limit_bytes=9 * MIB),
    )(place, *pieces, in_hbm(hidden), gain, in_hbm(cotangent), *through, middle, *ffn)


def rim_kernel(starts, rows, *rest):
    out = rest[-1]
    at = lax.broadcasted_iota(jnp.int32, (8, D), 0)
    out[...] = jnp.where(at == 6, rows[...] * keep_at(starts, T - 1), rows[...])


def rim_rows_of(starts, hidden, *after):
    return pl.pallas_call(
        rim_kernel,
        name="rim_rows",
        cost_estimate=taking(1),
        grid=(1,),
        out_shape=struct(8, D),
        in_specs=[SMEM, pl.BlockSpec((8, D), lambda i: (T // 8 - 1, 0))] + [ANY] * len(after),
        out_specs=whole(8, D),
        compiler_params=pltpu.CompilerParams(vmem_limit_bytes=6 * MIB),
    )(starts, in_hbm(hidden), *after)


def project_kernel(rows, rim, gain, weights, proj, proj_rim, left):
    part = pl.program_id(1)

    @pl.when((pl.program_id(0) == 0) & (part == 0))
    def _():
        v = rim[...]
        v = (v * inverse_rms(v) * gain[...]).astype(BF16)
        for n in (0, 1):
            columns = slice(HALF * n, HALF * n + HALF)
            left[n, 0:T] = rows[:, columns]
            left[n, T:] = jnp.concatenate([v[:, columns], v[:, columns]])

    out = dot(left[part], weights[0])

    @pl.when(part == 0)
    def _():
        proj[0], proj_rim[0] = out[:T], out[T : T + 8]

    @pl.when(part == 1)
    def _():
        proj[0] += out[:T]
        proj_rim[0] += out[T : T + 8]


def project(rows, rim, gain, weights):
    return pl.pallas_call(
        project_kernel,
        name="project",
        cost_estimate=taking(3),
        grid=(3, 2),
        out_shape=(struct(3, T, C), struct(3, 8, C)),
        in_specs=[
            pl.BlockSpec((T, D), lambda k, j: (0, 0)),
            pl.BlockSpec((8, D), lambda k, j: (0, 0)),
            pl.BlockSpec((1, D), lambda k, j: (0, 0)),
            pl.BlockSpec((1, HALF, C), lambda k, j: (k, j, 0)),
        ],
        out_specs=(
            pl.BlockSpec((1, T, C), lambda k, j: (k, 0, 0)),
            pl.BlockSpec((1, 8, C), lambda k, j: (k, 0, 0)),
        ),
        scratch_shapes=[pltpu.VMEM((2, T + 16, HALF), BF16)],
        compiler_params=pltpu.CompilerParams(vmem_limit_bytes=13 * MIB),
    )(rows, rim, gain, in_hbm(weights))


PIECES = ((0, 3), (1, 2), (0, 1), (3, 2))


def put_pieces(place, total, outs, by_owner=False):
    step = pl.program_id(0)

    def put(which):
        for out, quarters in zip(outs[2 * which : 2 * which + 2], PIECES[2 * which : 2 * which + 2]):
            for n, q in enumerate(quarters):
                rows = slice(ROWS * q, ROWS * q + ROWS) if by_owner else quarter_rows(place[0] ^ q)
                out[ROWS * n : ROWS * n + ROWS] = total[rows, :]

    pl.when(step < 2)(functools.partial(put, 0))
    pl.when(step >= 2)(functools.partial(put, 1))


def split_kernel(compute, by_owner, count, place, *refs):
    lk, ls, rk, rs, total = refs[-5:]
    total[...] = compute(*refs[:count])
    put_pieces(place, total, (lk, ls, rk, rs), by_owner)


def block_specs(operands):
    return [pl.BlockSpec(shape, index) if shape else VMEM for _, shape, index in operands]


PIECE_SHAPES = (struct(2 * ROWS, HALF),) * 4
PIECE_SPECS = (pl.BlockSpec((2 * ROWS, 512), lambda i: (0, jnp.minimum(i, 1))),) * 2 + (
    pl.BlockSpec((2 * ROWS, 512), lambda i: (0, jnp.maximum(i - 2, 0))),
) * 2


def split_dot(name, compute, by_owner, place, *operands, after=()):
    return pl.pallas_call(
        functools.partial(split_kernel, compute, by_owner, len(operands)),
        name=name,
        cost_estimate=taking(2.5),
        grid=(4,),
        out_shape=PIECE_SHAPES,
        in_specs=[SMEM] + block_specs(operands) + [ANY] * len(after),
        out_specs=PIECE_SPECS,
        scratch_shapes=[pltpu.VMEM((T, 512), F32)],
        compiler_params=pltpu.CompilerParams(vmem_limit_bytes=18 * MIB),
    )(place, *[a for a, _, _ in operands], *after)


def ffn_kernel(place, *refs):
    parts, refs = refs[:6], refs[6:]
    gain, w_gate, w_up, grad_hidden = refs[:4]
    mid_x, hidden, grad_gate, grad_up, own_all, send_all = refs[-9:-3]
    kept_hidden, kept_gate, kept_up = refs[-3:]
    step = pl.program_id(0)

    @pl.when(step == 0)
    def _():
        for q, (left, right) in enumerate(quarters_of(parts)):
            rows = slice(ROWS * q, ROWS * q + ROWS)
            mid_x[rows, :HALF] = (left * gain[:, :HALF]).astype(BF16)
            mid_x[rows, HALF:] = (right * gain[:, HALF:]).astype(BF16)

    gate = dot(mid_x[...], w_gate[...])
    up = dot(mid_x[...], w_up[...])
    sig = 1.0 / (1.0 + jnp.exp(-gate))
    silu = gate * sig
    incoming = grad_hidden[...]
    columns = pl.ds(pl.multiple_of(step * 256, 256), 256)
    kept_hidden[:, columns] = (silu * up).astype(BF16)
    kept_gate[:, columns] = (incoming * up * sig * (1.0 + gate * (1.0 - sig))).astype(BF16)
    kept_up[:, columns] = (incoming * silu).astype(BF16)

    @pl.when(step == pl.num_programs(0) - 1)
    def _():
        hidden[...] = kept_hidden[:, :1408]
        grad_gate[...] = kept_gate[:, :1408]
        grad_up[...] = kept_up[:, :1408]
        first = place[1] == 0

        def halves(columns, low, high):
            a, b = low.astype(F32), high.astype(F32)
            own_all[:, columns] = jnp.where(first, a, b).astype(BF16)
            send_all[:, columns] = jnp.where(first, b, a)

        halves(slice(0, 768), kept_gate[:, :768], kept_up[:, 640:1408])
        halves(slice(768, 1408), kept_up[:, :640], kept_gate[:, 768:1408])
        halves(slice(1408, 2176), kept_hidden[:, :768], kept_hidden[:, 640:1408])


def feed_forward(place, parts, gain, w_gate, w_up, grad_hidden, *after):
    wide = w_gate.shape[1]
    column = pl.BlockSpec((D, 256), lambda i: (0, i))
    low = struct(T, wide, dtype=BF16)
    return pl.pallas_call(
        ffn_kernel,
        name="feed_forward",
        cost_estimate=taking(8),
        grid=(6,),
        out_shape=(
            struct(T, D, dtype=BF16),
            low,
            low,
            low,
            struct(T, wide + 768, dtype=BF16),
            struct(T, wide + 768),
        ),
        in_specs=[SMEM]
        + [VMEM] * 7
        + [column, column, pl.BlockSpec((T, 256), lambda i: (0, i))]
        + [ANY] * len(after),
        out_specs=(VMEM,) * 6,
        scratch_shapes=[pltpu.VMEM((T, 1536), BF16)] * 3,
        compiler_params=pltpu.CompilerParams(vmem_limit_bytes=14 * MIB),
    )(place, *parts, gain, w_gate, w_up, grad_hidden, *after)


def branch_back_kernel(place, *refs):
    parts, cotangent, w_out = refs[:6], *refs[6:8]
    through, branch, grad_gated = refs[-3:]
    for q, (left, right) in enumerate(quarters_of(parts)):
        rows = slice(ROWS * q, ROWS * q + ROWS)
        through[rows, :HALF], through[rows, HALF:] = left, right
    branch[...] = (rows_by_quarter(place, cotangent) + through[...]).astype(BF16)
    back = dot_t(branch[...], w_out[...])
    for q in range(4):
        grad_gated[quarter_rows(place[0] ^ q), :] = back[ROWS * q : ROWS * q + ROWS]


def branch_back(place, parts, cotangent, w_out, *after):
    return pl.pallas_call(
        branch_back_kernel,
        name="branch_back",
        cost_estimate=taking(3),
        out_shape=(struct(T, D), pltpu.HBM((T, D), BF16), struct(T, C)),
        in_specs=[SMEM] + [VMEM] * 8 + [ANY] * len(after),
        out_specs=(VMEM,) * 3,
        compiler_params=pltpu.CompilerParams(vmem_limit_bytes=8 * MIB),
    )(place, *parts, cotangent, w_out, *after)


def finish_kernel(place, starts, grads, rim, *rest):
    low, own, send = rest[-3:]
    first = place[1] == 0
    at = lax.broadcasted_iota(jnp.int32, (8, C), 0)
    for k in range(3):
        turned = jnp.concatenate([jnp.zeros((6, C), F32), rim[k, 0:2]])
        turned = jnp.where(at == 6, turned * keep_at(starts, T - 1), turned)
        low[k, : T - 16] = grads[k, : T - 16].astype(BF16)
        low[k, T - 16 :] = jnp.concatenate(
            [grads[k, T - 16 : T - 8], grads[k, T - 8 :] + turned]
        ).astype(BF16)
        a, b = low[k, :, :256].astype(F32), low[k, :, 256:].astype(F32)
        columns = slice(256 * k, 256 * k + 256)
        own[:, columns] = jnp.where(first, a, b).astype(BF16)
        send[:, columns] = jnp.where(first, b, a)


def finish_projected(place, starts, grads, rim, *after):
    return pl.pallas_call(
        finish_kernel,
        name="finish_projected",
        cost_estimate=taking(1.5),
        out_shape=(struct(3, T, C, dtype=BF16), struct(T, 768, dtype=BF16), struct(T, 768)),
        in_specs=[SMEM, SMEM, VMEM, VMEM] + [ANY] * len(after),
        out_specs=(VMEM,) * 3,
        compiler_params=pltpu.CompilerParams(vmem_limit_bytes=7 * MIB),
    )(place, starts, grads, rim, *after)


def first_kernel(place, grads, hidden, inverse, w_in, lk, ls, rk, rs, gains, total):
    total[...] = sum(dot_t(grads[k], w_in[k]) for k in range(3))
    gains[...] = jnp.sum(total[...] * (hidden[...] * inverse[...]), axis=0, keepdims=True)
    put_pieces(place, total, (lk, ls, rk, rs))


def first_back(place, grads, hidden, inverse, w_in):
    return pl.pallas_call(
        first_kernel,
        name="first_back",
        cost_estimate=taking(3),
        grid=(4,),
        out_shape=PIECE_SHAPES + (struct(1, D),),
        in_specs=[
            SMEM,
            whole(3, T, C),
            pl.BlockSpec((T, 512), lambda i: (0, i)),
            whole(T, 1),
            pl.BlockSpec((3, 512, C), lambda i: (0, i, 0)),
        ],
        out_specs=PIECE_SPECS + (pl.BlockSpec((1, 512), lambda i: (0, i)),),
        scratch_shapes=[pltpu.VMEM((T, 512), F32)],
        compiler_params=pltpu.CompilerParams(vmem_limit_bytes=15 * MIB),
    )(place, grads, in_hbm(hidden), inverse, w_in)


def per_device(
    hidden_in,
    cotangent,
    starts,
    norm_in,
    w_in,
    short_w,
    pole_pairs,
    residues,
    w_out,
    norm_mid,
    w_gate,
    w_up,
    w_down,
):
    place = jnp.stack(
        [lax.axis_index(axis) for axis in ("tp", "seq_2", "seq_1", "seq_0")]
    ).astype(jnp.int32)
    column = starts[:, None]
    gain_in, gain_mid = norm_in[None], norm_mid[None]

    def other_core(x):
        return swap(x, "seq_2", 1)

    rim_rows = rim_rows_of(starts, hidden_in, place, column)
    rim_rows = lax.ppermute(rim_rows, SEQ, [(i, i + 1) for i in range(31)])
    hidden_other = other_core(hidden_in)
    cotangent_other = other_core(cotangent)
    normed_in, inverse_in = normed(hidden_in, gain_in)
    proj, rim = project(normed_in, rim_rows, gain_in, w_in)
    mixed, end, powers = mix(proj, rim, short_w, column, starts, pole_pairs)

    down_grad, grad_hidden = cotangent_part(place, cotangent, w_down, end)
    entering, _ = carried_state(place, end, powers, False, late=(grad_hidden,))
    signal, gated = signal_of(mixed, starts, pole_pairs, residues, entering)

    branch = split_dot(
        "branch",
        lambda a, b: dot(a[...], b[...]),
        False,
        place,
        (gated, None, None),
        (w_out, (C, 512), lambda i: (0, i)),
    )
    *history, history_token = history_of(mixed, starts, pole_pairs, entering, branch[1])
    out_right, out_send = out_parts(place, gated, branch[1])
    middle, mid_left, mid_right = after_middle(
        place,
        scatter_sum(branch, history_token, out_send),
        hidden_in,
    )

    normed_other, _ = normed(hidden_other, gain_in, mid_left)
    down_other = owner_rows(place, cotangent_other, mid_left)
    parts, joined = gather_joined(mid_left, mid_right, in_hbm(normed_other), in_hbm(down_other))
    mid_other = [other_core(x) for x in joined]
    mid_x, hidden, grad_gate, grad_up, own_all, send_all = feed_forward(
        place,
        parts,
        gain_mid,
        w_gate,
        w_up,
        grad_hidden,
        *mid_other,
    )
    mid_other += [other_core(parts[1]), other_core(parts[5])]
    mid_terms = split_dot(
        "mid_terms",
        lambda a, b, c, d: dot_t(a[...], c[...]) + dot_t(b[...], d[...]),
        True,
        place,
        (grad_gate, None, None),
        (grad_up, None, None),
        (w_gate, (512, w_gate.shape[1]), lambda i: (i, 0)),
        (w_up, (512, w_up.shape[1]), lambda i: (i, 0)),
        after=mid_other[2:],
    )

    ffn_sum, ffn_token = wide_token_sum(
        mid_x,
        mid_other,
        down_grad,
        down_other,
        own_all,
        other_core(tie(send_all, mid_terms[1])),
        gain_mid,
    )

    pieces = scatter_sum(mid_terms, ffn_token)
    share_ffn = lax.psum_scatter(
        tie(ffn_sum, pieces[0], hbm=True), ("seq_0", "seq_1"), scatter_dimension=0, tiled=True
    )
    through_left, through_right, gains_mid = norm_back(pieces, middle, gain_mid)
    ffn = split_dot(
        "ffn",
        lambda a, b, after: dot(a[...], b[...]),
        True,
        place,
        (hidden, None, None),
        (w_down, (w_down.shape[0], 512), lambda i: (0, i)),
        (gains_mid, None, None),
    )
    through_f, branch_grad, grad_gated = branch_back(
        place, gather_parts(through_left, through_right), cotangent, w_out, ffn[1]
    )

    leaving = adjoint_end(grad_gated, mixed, column, starts, pole_pairs, residues)
    branch_other = branch_other_of(place, cotangent_other, other_core(through_f))
    returning, plane = carried_state(place, leaving, powers, True, after=(in_hbm(branch_other),))
    ffn = scatter_sum((ffn[0], tie(ffn[1], plane), ffn[2], tie(ffn[3], plane)), returning)
    grad_proj, rim_grad, sums = back(
        grad_gated,
        mixed,
        signal,
        proj,
        rim,
        history,
        short_w,
        column,
        starts,
        pole_pairs,
        residues,
        returning,
        ffn[0],
    )
    rim_back = lax.ppermute(rim_grad, SEQ, [(i + 1, i) for i in range(31)])

    projected_low, proj_own, proj_send = finish_projected(
        place, starts, grad_proj, rim_back, ffn[1], ffn[3]
    )
    proj_wide = other_core(proj_send)
    *first_terms, gains_in = first_back(place, projected_low, hidden_in, inverse_in, w_in)
    kept, leaving_now, mixer_token = stream_token_sum(
        place,
        normed_in,
        normed_other,
        branch_grad,
        branch_other,
        proj_own,
        proj_wide,
        out_right,
        other_core(out_send),
        sums,
        gains_in,
        gains_mid,
    )
    pieces = scatter_sum(first_terms, mixer_token)
    got = stream_swap([tie(x, pieces[0]) for x in leaving_now], 0)
    both_left, both_right = last_back(
        place,
        pieces,
        hidden_in,
        gain_in,
        cotangent,
        (through_left, through_right),
        middle,
        ffn,
    )
    kept, leaving_now = stream_add(kept, got, both_left)
    got = stream_swap(leaving_now, 1)
    parts = gather_parts(both_left, both_right, kept[0])
    kept, leaving_now = stream_add(kept, got)
    got = stream_swap(leaving_now, 2)
    kept, leaving_now = stream_add(kept, got)
    got = stream_swap(leaving_now, 3)
    share_gate, share_up, share_down, shares_token = ffn_shares(
        place, share_ffn, other_core, kept[0]
    )
    result, grad_input = outputs_of(place, parts)
    own, send, small = stream_last(place, kept, got, shares_token)
    share_in, share_out, small, gains = mixer_shares(
        place, own, other_core(send), small, other_core(small)
    )
    gains = sum_over(gains, "tp")
    return (
        result,
        grad_input,
        gains[0:4].reshape(D),
        share_in,
        small[64:73].reshape(3, 3, C),
        small[0:32].reshape(2, N, C),
        small[32:64].reshape(2, N, C),
        share_out.T,
        gains[4:8].reshape(D),
        share_gate,
        share_up,
        share_down.T,
    )


def solution(mesh):
    split = Mesh(mesh.devices.reshape(4, 4, 2, mesh.shape["tp"]), ("seq_0", "seq_1", "seq_2", "tp"))
    in_specs = (
        P(SEQ, None),
        P(SEQ, None),
        P(SEQ),
        P(),
        P(None, None, "tp"),
        P(None, None, "tp"),
        P(None, None, "tp"),
        P(None, None, "tp"),
        P("tp", None),
        P(),
        P(None, "tp"),
        P(None, "tp"),
        P("tp", None),
    )
    out_specs = (
        P(SEQ, None),
        P(SEQ, None),
        P(),
        P(None, SEQ, "tp"),
        P(None, None, "tp"),
        P(None, None, "tp"),
        P(None, None, "tp"),
        P("tp", SEQ),
        P(),
        P(SEQ, "tp"),
        P(SEQ, "tp"),
        P("tp", SEQ),
    )
    return jax.shard_map(
        per_device, mesh=split, in_specs=in_specs, out_specs=out_specs, check_vma=False
    )
```

```python
import functools

import jax
import jax.numpy as jnp
from jax import lax
from jax.experimental import pallas as pl
from jax.experimental.pallas import tpu as pltpu
from jax.sharding import Mesh
from jax.sharding import PartitionSpec as P

SEQ = ("seq_0", "seq_1", "seq_2")
F32 = jnp.float32
BF16 = jnp.bfloat16
epsilon = 1e-06
MIB = 1 << 20
T, C, N, D = 256, 512, 16, 2048
BLOCK = 32
BLOCKS = T // BLOCK
ROWS = 64
VMEM = pl.BlockSpec(memory_space=pltpu.VMEM)
SMEM = pl.BlockSpec(memory_space=pltpu.SMEM)
ANY = pl.BlockSpec(memory_space=pl.ANY)


def in_hbm(x):
    return pltpu.with_memory_space_constraint(x, pltpu.HBM)


def taking(microseconds):
    return pl.CostEstimate(flops=0, bytes_accessed=int(microseconds * 3.0e6), transcendentals=0)


def whole(*shape):
    return pl.BlockSpec(shape, lambda i: (0,) * len(shape))


def struct(*shape, dtype=F32):
    return jax.ShapeDtypeStruct(shape, dtype)


def times(a, b):
    return a[0] * b[0] - a[1] * b[1], a[0] * b[1] + a[1] * b[0]


def plus(a, b):
    return a[0] + b[0], a[1] + b[1]


def where2(flag, a, b):
    return jnp.where(flag, a[0], b[0]), jnp.where(flag, a[1], b[1])


def scaled(a, factor):
    return a[0] * factor, a[1] * factor


def token_sum(a, b):
    return lax.dot_general(a, b, (((0,), (0,)), ((), ())), preferred_element_type=F32)


def dot(a, b):
    return jnp.dot(a, b, preferred_element_type=F32)


def dot_t(a, b):
    return lax.dot_general(a, b, (((1,), (1,)), ((), ())), preferred_element_type=F32)


def scan_groups(groups, starts, base, run, carry, reverse):
    def body(step, kept):
        group = groups - 1 - step if reverse else step
        first = base + group * 8
        marks = starts[first]
        for r in range(1, 8):
            marks = marks + starts[first + r]
        return lax.cond(
            marks > 0, lambda c: run(group, c, True), lambda c: run(group, c, False), kept
        )

    return lax.fori_loop(0, groups, body, carry)


def quarter_rows(quarter):
    return pl.ds(pl.multiple_of(quarter * ROWS, ROWS), ROWS)


def eight(group):
    return pl.ds(pl.multiple_of(group * 8, 8), 8)


def keep_at(starts, token):
    return (1 - starts[token]).astype(F32)


def with_rim(proj, rim, k, rows):
    rows[0:8] = rim[k]
    rows[8:] = proj[k]


def keeps_of(column):
    marks = column[...].astype(F32)
    one = 1.0 - marks
    two = one * jnp.concatenate([jnp.ones((1, 1), F32), one[: T - 1]])
    return one, two, 1.0 - jnp.max(marks, axis=0, keepdims=True)


def mix_kernel(rows, rim, gain, *refs):
    weights, (taps, column, starts, poles), refs = refs[:4], refs[4:8], refs[8:]
    proj, proj_rim, mixed, end, powers, left, kept, shifted_rows, driven = refs
    k = pl.program_id(0)
    quarter = D // 4

    @pl.when(k == 0)
    def _():
        v = rim[...]
        v = (v * inverse_rms(v) * gain[...]).astype(BF16)
        for n in range(4):
            columns = slice(quarter * n, quarter * n + quarter)
            left[n, 0:T] = rows[:, columns]
            left[n, T:] = jnp.concatenate([v[:, columns], v[:, columns]])

    out = sum(dot(left[n], weights[n][0]) for n in range(4))
    proj[0], proj_rim[0] = out[:T], out[T : T + 8]
    kept[k] = out[: T + 8]
    pl.when(k == 2)(
        functools.partial(mix_end, kept, taps, column, starts, poles, mixed, end, powers, shifted_rows, driven)
    )


def mix_end(kept, taps, column, starts, poles, mixed, end, powers, rows, driven):
    one, two, is_open = keeps_of(column)
    for k in range(3):
        rows[0:8], rows[8:] = kept[k, T:], kept[k, :T]
        mixed[k] = (
            taps[k, 0:1] * kept[k, :T]
            + taps[k, 1:2] * (one * rows[7 : 7 + T])
            + taps[k, 2:3] * (two * rows[6 : 6 + T])
        )
    driven[...] = mixed[1] * mixed[2]
    pre, pim = poles[0], poles[1]

    def run(group, state, masked):
        source = driven[eight(group), :]
        re, im = state
        for r in range(8):
            if masked:
                keep = keep_at(starts, group * 8 + r)
                re, im = re * keep, im * keep
            re, im = pre * re - pim * im + source[r : r + 1], pre * im + pim * re
        return re, im

    zero = jnp.zeros((N, C), F32)
    end[0:N], end[N : 2 * N] = scan_groups(T // 8, starts, 0, run, (zero, zero), False)
    end[2 * N :] = jnp.broadcast_to(is_open, (8, C))
    power = (pre, pim)
    for n in range(1, 12):
        power = times(power, power)
        if n in (8, 9, 11):
            at = {8: 0, 9: 2, 11: 4}[n]
            powers[at], powers[at + 1] = power


def project_and_mix(rows, rim, gain, weights, taps, column, starts, poles):
    depth = D // 4

    def part(n):
        return pl.BlockSpec((1, depth, C), lambda k: (k, n, 0))

    weights = in_hbm(weights)
    return pl.pallas_call(
        mix_kernel,
        name="project_and_mix",
        cost_estimate=taking(8),
        grid=(3,),
        out_shape=(
            pltpu.HBM((3, T, C), F32),
            struct(3, 8, C),
            pltpu.HBM((3, T, C), F32),
            struct(2 * N + 8, C),
            struct(6, N, C),
        ),
        in_specs=[VMEM, VMEM, VMEM]
        + [part(n) for n in range(4)]
        + [VMEM, VMEM, SMEM, VMEM],
        out_specs=(
            pl.BlockSpec((1, T, C), lambda k: (k, 0, 0)),
            pl.BlockSpec((1, 8, C), lambda k: (k, 0, 0)),
            whole(3, T, C),
            VMEM,
            VMEM,
        ),
        scratch_shapes=[
            pltpu.VMEM((4, T + 16, depth), BF16),
            pltpu.VMEM((3, T + 8, C), F32),
            pltpu.VMEM((T + 8, C), F32),
            pltpu.VMEM((T, C), F32),
        ],
        compiler_params=pltpu.CompilerParams(vmem_limit_bytes=22 * MIB),
    )(rows, rim, gain, *[weights] * 4, taps, column, starts, poles)


def forward_rows(mixed, starts, poles, block, state, visit):
    pre, pim = poles[0], poles[1]
    base = block * BLOCK

    def run(group, kept, masked):
        source = mixed[1, eight(group), :] * mixed[2, eight(group), :]
        re, im = kept
        for r in range(8):
            if masked:
                keep = keep_at(starts, base + group * 8 + r)
                re, im = re * keep, im * keep
            re, im = pre * re - pim * im + source[r : r + 1], pre * im + pim * re
            visit(group * 8 + r, re, im)
        return re, im

    state[0], state[1] = scan_groups(BLOCK // 8, starts, base, run, (state[0], state[1]), False)


def signal_kernel(mixed, starts, poles, residues, first, signal, gated, state):
    block = pl.program_id(0)

    @pl.when(block == 0)
    def _():
        state[...] = first[...]

    qre, qim = residues[0], residues[1]

    def visit(row, re, im):
        signal[pl.ds(row, 1), :] = jnp.sum(qre * re - qim * im, axis=0, keepdims=True)

    forward_rows(mixed, starts, poles, block, state, visit)
    gated[...] = (mixed[0] * signal[...]).astype(BF16)


def history_kernel(mixed, starts, poles, first, *rest):
    h0, h1, h2, h3, token, state = rest[-6:]
    block = pl.program_id(0)
    token[...] = jnp.zeros(token.shape, F32)

    @pl.when(block == 0)
    def _():
        state[...] = first[...]

    def visit(row, re, im):
        h0[row], h1[row] = re[:8], re[8:]
        h2[row], h3[row] = im[:8], im[8:]

    forward_rows(mixed, starts, poles, block, state, visit)


def signal_of(mixed, starts, poles, residues, first):
    return pl.pallas_call(
        signal_kernel,
        name="signal",
        cost_estimate=taking(6),
        grid=(BLOCKS,),
        out_shape=(struct(T, C), struct(T, C, dtype=BF16)),
        in_specs=[
            pl.BlockSpec((3, BLOCK, C), lambda i: (0, i, 0)),
            SMEM,
            whole(2, N, C),
            whole(2, N, C),
            whole(2, N, C),
        ],
        out_specs=(pl.BlockSpec((BLOCK, C), lambda i: (i, 0)),) * 2,
        scratch_shapes=[pltpu.VMEM((2, N, C), F32)],
        compiler_params=pltpu.CompilerParams(vmem_limit_bytes=8 * MIB),
    )(mixed, starts, poles, residues, first)


def history_of(mixed, starts, poles, first, *after):
    return pl.pallas_call(
        history_kernel,
        name="state_history",
        cost_estimate=taking(8),
        grid=(BLOCKS,),
        out_shape=(pltpu.HBM((T, 8, C), F32),) * 4 + (struct(8, 128),),
        in_specs=[
            pl.BlockSpec((3, BLOCK, C), lambda i: (0, i, 0)),
            SMEM,
            whole(2, N, C),
            whole(2, N, C),
        ]
        + [ANY] * len(after),
        out_specs=(pl.BlockSpec((BLOCK, 8, C), lambda i: (i, 0, 0)),) * 4 + (whole(8, 128),),
        scratch_shapes=[pltpu.VMEM((2, N, C), F32)],
        compiler_params=pltpu.CompilerParams(vmem_limit_bytes=11 * MIB),
    )(in_hbm(mixed), starts, poles, first, *after)


def adjoint_kernel(grad_gated, query, column, starts, poles, residues, out, grads):
    grads[...] = grad_gated[...] * query[0]
    pre, pim, qre, qim = poles[0], poles[1], residues[0], residues[1]

    def run(group, kept, masked):
        source = grads[eight(group), :]
        re, im = kept
        for r in reversed(range(8)):
            row = source[r : r + 1]
            re, im = row * qre + (pre * re + pim * im), (pre * im - pim * re) - row * qim
            if masked:
                keep = keep_at(starts, group * 8 + r)
                re, im = re * keep, im * keep
        return re, im

    zero = jnp.zeros((N, C), F32)
    out[0:N], out[N : 2 * N] = scan_groups(T // 8, starts, 0, run, (zero, zero), True)
    out[2 * N :] = jnp.broadcast_to(keeps_of(column)[2], (8, C))


def adjoint_end(grad_gated, mixed, column, starts, poles, residues):
    return pl.pallas_call(
        adjoint_kernel,
        name="adjoint_end",
        cost_estimate=taking(4),
        grid=(1,),
        out_shape=struct(2 * N + 8, C),
        in_specs=[
            whole(T, C),
            pl.BlockSpec((1, T, C), lambda i: (0, 0, 0)),
            whole(T, 1),
            SMEM,
            whole(2, N, C),
            whole(2, N, C),
        ],
        out_specs=whole(2 * N + 8, C),
        scratch_shapes=[pltpu.VMEM((T, C), F32)],
        compiler_params=pltpu.CompilerParams(vmem_limit_bytes=9 * MIB),
    )(grad_gated, mixed, column, starts, poles, residues)


def back_kernel(
    grad_gated,
    mixed,
    signal,
    proj,
    proj_rim,
    h0,
    h1,
    h2,
    h3,
    taps,
    column,
    starts,
    poles,
    residues,
    first,
    *rest,
):
    grad_proj, rim, sums, state, driven_grad, mixed_grad, rows_before = rest[-7:]
    step = pl.program_id(0)
    block = BLOCKS - 1 - step

    @pl.when(step == 0)
    def _():
        state[...] = first[...]
        sums[...] = jnp.zeros(sums.shape, F32)

    pre, pim, qre, qim = poles[0], poles[1], residues[0], residues[1]
    base = block * BLOCK

    def run(group, kept, masked):
        rows = pl.ds(pl.multiple_of(base + group * 8, 8), 8)
        source = grad_gated[rows, :] * mixed[0, rows, :]
        re, im = kept
        for r in reversed(range(8)):
            row = source[r : r + 1]
            token = group * 8 + r
            sre = jnp.concatenate([h0[token], h1[token]])
            sim = jnp.concatenate([h2[token], h3[token]])
            sums[0:16] += re * sre + im * sim
            sums[16:32] += im * sre - re * sim
            sums[32:48] += row * sre
            sums[48:64] -= row * sim
            re, im = row * qre + (pre * re + pim * im), (pre * im - pim * re) - row * qim
            driven_grad[pl.ds(base + group * 8 + r, 1), :] = jnp.sum(re, axis=0, keepdims=True)
            if masked:
                keep = keep_at(starts, base + group * 8 + r)
                re, im = re * keep, im * keep
        return re, im

    state[0], state[1] = scan_groups(BLOCK // 8, starts, base, run, (state[0], state[1]), True)

    @pl.when(step == BLOCKS - 1)
    def _():
        one, two, _ = keeps_of(column)
        mixed_grad[0, 0:T] = grad_gated[...] * signal[...]
        mixed_grad[1, 0:T] = driven_grad[...] * mixed[2]
        mixed_grad[2, 0:T] = driven_grad[...] * mixed[1]
        for k in range(3):
            with_rim(proj, proj_rim, k, rows_before)
            here = mixed_grad[k, 0:T]
            sums[64 + 3 * k : 65 + 3 * k] = jnp.sum(here * proj[k], axis=0, keepdims=True)
            grad_proj[k] = taps[k, 0:1] * here
            here = one * mixed_grad[k, 0:T]
            sums[65 + 3 * k : 66 + 3 * k] = jnp.sum(here * rows_before[7 : 7 + T], axis=0, keepdims=True)
            mixed_grad[k, 0:T] = two * mixed_grad[k, 0:T]
            here = taps[k, 1:2] * here
            grad_proj[k, 0 : T - 1] += here[1:T]
            rim[k] = jnp.zeros((8, C), F32)
            rim[k, 1:2] = here[0:1]
            here = mixed_grad[k, 0:T]
            sums[66 + 3 * k : 67 + 3 * k] = jnp.sum(here * rows_before[6 : 6 + T], axis=0, keepdims=True)
            here = taps[k, 2:3] * here
            grad_proj[k, 0 : T - 2] += here[2:T]
            rim[k, 0:2] += here[0:2]


def back(grad_gated, mixed, signal, proj, proj_rim, history, taps, column, starts, poles, residues, first, *after):
    return pl.pallas_call(
        back_kernel,
        name="adjoint_and_short_back",
        cost_estimate=taking(13),
        grid=(BLOCKS,),
        out_shape=(struct(3, T, C), struct(3, 8, C), struct(80, C)),
        in_specs=[
            whole(T, C),
            whole(3, T, C),
            whole(T, C),
            whole(3, T, C),
            whole(3, 8, C),
        ]
        + [pl.BlockSpec((BLOCK, 8, C), lambda i: (BLOCKS - 1 - i, 0, 0))] * 4
        + [
            whole(3, 3, C),
            whole(T, 1),
            SMEM,
            whole(2, N, C),
            whole(2, N, C),
            whole(2, N, C),
        ]
        + [ANY] * len(after),
        out_specs=(whole(3, T, C), whole(3, 8, C), whole(80, C)),
        scratch_shapes=[
            pltpu.VMEM((2, N, C), F32),
            pltpu.VMEM((T, C), F32),
            pltpu.VMEM((3, T, C), F32),
            pltpu.VMEM((T + 8, C), F32),
        ],
        compiler_params=pltpu.CompilerParams(vmem_limit_bytes=25 * MIB),
    )(
        grad_gated,
        mixed,
        signal,
        proj,
        proj_rim,
        *history,
        taps,
        column,
        starts,
        poles,
        residues,
        first,
        *after,
    )


def swap(value, axis, mask):
    size = lax.axis_size(axis)
    return lax.ppermute(value, axis, [(i, i ^ mask) for i in range(size)])


def shifted(value, axis, steps):
    count = lax.axis_size(axis)
    first, last = max(0, -steps), min(count, count - steps)
    return lax.ppermute(value, axis, [(i, i + steps) for i in range(first, last)])


def pair_add_kernel(left, got_left, right, got_right, *rest):
    left_own, left_next, right_own, right_next = rest[-4:]
    left_own[...] = left[:ROWS] + got_left[:ROWS]
    left_next[...] = left[ROWS:] + got_left[ROWS:]
    right_own[...] = right[:ROWS] + got_right[:ROWS]
    right_next[...] = right[ROWS:] + got_right[ROWS:]


def pair_call(name, kernel, shapes, operands, after):
    return pl.pallas_call(
        kernel,
        name=name,
        cost_estimate=taking(0.8),
        out_shape=shapes,
        in_specs=[VMEM] * len(operands) + [ANY] * len(after),
        out_specs=[VMEM] * len(shapes),
        compiler_params=pltpu.CompilerParams(vmem_limit_bytes=10 * MIB),
    )(*operands, *after)


def scatter_end(pieces, got_left, got_right, *after):
    left_own, left_next, right_own, right_next = pair_call(
        "pair_add",
        pair_add_kernel,
        [struct(ROWS, HALF)] * 4,
        (pieces[0], got_left, pieces[2], got_right),
        after,
    )
    return left_own, swap(left_next, "tp", 3), right_own, swap(right_next, "tp", 1)


def scatter_start(pieces):
    return swap(pieces[1], "tp", 1), swap(pieces[3], "tp", 3)


def scatter_sum(pieces, *after):
    return scatter_end(pieces, *scatter_start(pieces), *after)


def pair_join_kernel(left, left_3, right, right_1, *rest):
    left_03, right_10 = rest[-2:]
    rows = left.shape[0]
    left_03[:rows], left_03[rows:] = left[...], left_3[...]
    right_10[:rows], right_10[rows:] = right_1[...], right[...]


def gather_joined(left, right, *after):
    return joined_parts(left, swap(left, "tp", 3), right, swap(right, "tp", 1), *after)


def joined_parts(left, left_3, right, right_1, *after):
    left_03, right_10 = pair_call(
        "pair_join",
        pair_join_kernel,
        [struct(2 * left.shape[0], HALF)] * 2,
        (left, left_3, right, right_1),
        after,
    )
    parts = left, swap(left_03, "tp", 1), left_3, right, right_1, swap(right_10, "tp", 3)
    return parts, (left_03, right_10)


def gather_parts(left, right, *after):
    return gather_joined(left, right, *after)[0]


def quarters_of(parts):
    left, left_12, left_3, right, right_1, right_23 = parts
    rows = left.shape[0]
    return (
        (left[:rows], right[:rows]),
        (left_12[:rows], right_1[:rows]),
        (left_12[rows:], right_23[:rows]),
        (left_3[:rows], right_23[rows:]),
    )


def of_payload(ref):
    return (ref[0:N], ref[N : 2 * N]), ref[2 * N : 2 * N + 1]


def to_payload(ref, state, is_open):
    ref[0:N], ref[N : 2 * N] = state
    ref[2 * N :] = jnp.broadcast_to(is_open, (8, C))


def power_of(powers, at, reverse):
    return powers[at], -powers[at + 1] if reverse else powers[at + 1]


def chip_kernel(reverse, place, mine, other, powers, out):
    (state, is_open), (state_other, open_other) = of_payload(mine), of_payload(other)
    by_device = power_of(powers, 0, reverse)
    last = place[1] == (0 if reverse else 1)
    earlier = where2(last, state_other, state)
    later = where2(last, state, state_other)
    later_open = jnp.where(last, is_open, open_other)
    chip = plus(later, times(scaled(by_device, later_open), earlier))
    to_payload(out, chip, is_open * open_other)


def plane_kernel(reverse, place, mine, got_1, got_2, got_3, powers, *rest):
    out, before = rest[-2:]
    chip, is_open = of_payload(mine)
    by_chip = power_of(powers, 2, reverse)
    got = {1: of_payload(got_1), 2: of_payload(got_2), 3: of_payload(got_3)}
    y = 3 - place[2] if reverse else place[2]
    one, zero = jnp.ones((N, C), F32), jnp.zeros((N, C), F32)
    entering, weight = (zero, zero), (one, zero)
    for k in (1, 2, 3):
        state, opened = got[k]
        entering = where2(y >= k, plus(entering, times(weight, state)), entering)
        weight = where2(y >= k, times(weight, scaled(by_chip, opened)), weight)
    plane = plus(chip, times(scaled(by_chip, is_open), entering))
    for j in (1, 2, 3):
        state, opened = got[4 - j]
        plane = where2(y + j <= 3, plus(state, times(scaled(by_chip, opened), plane)), plane)
        is_open = is_open * opened
    to_payload(out, plane, is_open)
    before[0], before[1] = entering
    before[2], before[3] = weight


def enter_kernel(reverse, place, before, got_1, got_2, got_3, other, powers, *rest):
    out = rest[-1]
    by_device, by_plane = power_of(powers, 0, reverse), power_of(powers, 4, reverse)
    one, zero = jnp.ones((N, C), F32), jnp.zeros((N, C), F32)
    entering, weight = (zero, zero), (one, zero)
    for ref in (got_1, got_2, got_3):
        state, opened = of_payload(ref)
        entering = plus(entering, times(weight, state))
        weight = times(weight, scaled(by_plane, opened))
    at_chip = plus((before[0], before[1]), times((before[2], before[3]), entering))
    state, opened = of_payload(other)
    at_core = plus(state, times(scaled(by_device, opened), at_chip))
    out[0], out[1] = where2(place[1] == (0 if reverse else 1), at_core, at_chip)


def small_call(name, kernel, reverse, shapes, operands, after=()):
    return pl.pallas_call(
        functools.partial(kernel, reverse),
        name=name,
        cost_estimate=taking(1.6),
        out_shape=shapes,
        in_specs=[SMEM] + [VMEM] * (len(operands) - 1) + [ANY] * len(after),
        out_specs=jax.tree.map(lambda _: VMEM, shapes),
        compiler_params=pltpu.CompilerParams(vmem_limit_bytes=8 * MIB),
    )(*operands, *after)


def carried_state(place, mine, powers, reverse, after=(), late=()):
    sign = -1 if reverse else 1
    payload = struct(2 * N + 8, C)
    other = swap(mine, "seq_2", 1)
    chip = small_call("chip_state", chip_kernel, reverse, payload, (place, mine, other, powers))
    got = [
        lax.ppermute(chip, "seq_1", [(i, (i + sign * k) % 4) for i in range(4)]) for k in (1, 2, 3)
    ]
    plane, before = small_call(
        "plane_state",
        plane_kernel,
        reverse,
        (payload, struct(4, N, C)),
        (place, chip, *got, powers),
        after,
    )
    got = [shifted(plane, "seq_0", sign * k) for k in (1, 2, 3)]
    entering = small_call(
        "entering_state",
        enter_kernel,
        reverse,
        struct(2, N, C),
        (place, before, *got, other, powers),
        late,
    )
    return entering


def sum_over(x, axis, *after):
    if lax.axis_size(axis) == 2:
        return x + swap(x, axis, 1)
    got = [swap(x, axis, k) for k in (1, 2, 3)]
    if after:
        got = [tie(g, *after) for g in got]
    return (x + got[0]) + (got[1] + got[2])


def inverse_rms(values):
    return lax.rsqrt(jnp.mean(values * values, axis=-1, keepdims=True) + epsilon)


def nothing(*refs):
    pass


def tie(x, *after, hbm=False):
    shape = struct(*x.shape, dtype=x.dtype)
    if hbm:
        x, shape = in_hbm(x), pltpu.HBM(x.shape, x.dtype)
    return pl.pallas_call(
        nothing,
        name="tie",
        out_shape=shape,
        in_specs=[ANY] * (1 + len(after)),
        out_specs=ANY,
        input_output_aliases={0: 0},
        compiler_params=pltpu.CompilerParams(vmem_limit_bytes=6 * MIB),
    )(x, *after)


WIDE = 1408


def wide_sum_kernel(left_a, l03, r10, l12, r23, left_b, more_b, right, wide, gain, out, token, both, rows_a, rows_b):
    step = pl.program_id(0)

    @pl.when(step == 0)
    def _():
        both[:T] = right[...]
        both[T:] = wide[...].astype(BF16)
        token[...] = jnp.zeros(token.shape, F32)

    def put(*quarters):
        rows_a[T:] = (jnp.concatenate(quarters) * gain[...]).astype(BF16)

    pl.when(step < 4)(lambda: put(l03[:ROWS], l12[:ROWS], l12[ROWS:], l03[ROWS:]))
    pl.when(step >= 4)(lambda: put(r10[ROWS:], r10[:ROWS], r23[:ROWS], r23[ROWS:]))
    rows_a[:T], rows_b[:T], rows_b[T:] = left_a[...], left_b[...], more_b[...]
    out[:, :WIDE] = token_sum(rows_a[...], both[:, :WIDE])
    out[:, WIDE:] = token_sum(rows_b[...], both[:, WIDE:])


def wide_token_sum(left_a, more_a, left_b, more_b, right, wide, gain):
    rows = 256
    column = pl.BlockSpec((T, rows), lambda i: (0, i))
    low = pl.BlockSpec((2 * ROWS, rows), lambda i: (0, jnp.minimum(i, 3)))
    high = pl.BlockSpec((2 * ROWS, rows), lambda i: (0, jnp.maximum(i - 4, 0)))
    width = right.shape[1]
    return pl.pallas_call(
        wide_sum_kernel,
        name="weight_gradients",
        cost_estimate=taking(10),
        grid=(D // rows,),
        out_shape=(pltpu.HBM((D, width), F32), struct(8, 128)),
        in_specs=[column, low, high, low, high, column, column]
        + [VMEM, VMEM, pl.BlockSpec((1, rows), lambda i: (0, i))],
        out_specs=(pl.BlockSpec((rows, width), lambda i: (i, 0)), whole(8, 128)),
        scratch_shapes=[
            pltpu.VMEM((2 * T, width), BF16),
            pltpu.VMEM((2 * T, rows), BF16),
            pltpu.VMEM((2 * T, rows), BF16),
        ],
        compiler_params=pltpu.CompilerParams(vmem_limit_bytes=20 * MIB),
    )(left_a, *more_a, left_b, more_b, right, wide, gain)


ORDERS = {1: (0, 3, 1, 2), 3: (0, 1, 3, 2)}
STREAMS = (("seq_1", 1), ("seq_1", 3), ("seq_0", 1), ("seq_0", 3))


def stream_places(step):
    jz, jy = divmod(step, 4)
    places = []
    for axis, mask in STREAMS:
        order = ORDERS[mask]
        first, second = (jy, jz) if axis == "seq_1" else (jz, jy)
        places.append(order.index(first) * 4 + order.index(second))
    return places


def stream_sum_kernel(
    place,
    left_a,
    more_a,
    left_b,
    more_b,
    right_a,
    wide_a,
    right_b,
    wide_b,
    sums,
    gains_a,
    gains_b,
    *rest,
):
    kept, sent, token, turned = rest[-10:-6], rest[-6:-2], rest[-2], rest[-1]
    token[...] = jnp.zeros(token.shape, F32)
    for s in range(4):
        kept[s][2048 : 2048 + 80] = sums[:, 128 * s : 128 * s + 128]
        for n in range(8):
            row = (gains_a, gains_b)[n // 4]
            at = C * (n % 4) + 128 * s
            kept[s][2128 + n : 2129 + n] = row[:, at : at + 128]
        sent[s][2048:] = kept[s][2048:]
    turned[0:768, 0:T] = right_a[...].T
    turned[768:, 0:T] = right_b[...].T
    turned[0:768, T:] = wide_a[...].astype(BF16).T
    turned[768:, T:] = wide_b[...].astype(BF16).T
    y, z = place[2], place[3]
    for step in range(16):
        jz, jy = divmod(step, 4)
        chunk = (z ^ jz) * 4 + (y ^ jy)
        columns = pl.ds(pl.multiple_of(chunk * 128, 128), 128)
        total_a = dot(turned[0:768, 0:T], left_a[:, columns]) + dot(turned[0:768, T:], more_a[:, columns])
        total_b = dot(turned[768:, 0:T], left_b[:, columns]) + dot(turned[768:, T:], more_b[:, columns])
        for s, at in enumerate(stream_places(step)):
            target = kept[s] if at < 8 else sent[s]
            rows = slice((at % 8) * 256, (at % 8) * 256 + 256)
            target[rows] = total_a[256 * s : 256 * s + 256] if s < 3 else total_b


def stream_token_sum(place, *operands):
    out = pl.pallas_call(
        stream_sum_kernel,
        name="mixer_weight_gradients",
        cost_estimate=taking(7),
        out_shape=(struct(2048 + SMALL, 128),) * 8 + (struct(8, 128),),
        in_specs=[SMEM] + [VMEM] * 11 + [ANY] * (len(operands) - 11),
        out_specs=(VMEM,) * 9,
        scratch_shapes=[pltpu.VMEM((1024, 2 * T), BF16)],
        compiler_params=pltpu.CompilerParams(vmem_limit_bytes=8 * MIB),
    )(place, *operands)
    return out[:4], out[4:8], out[8]


SMALL = 88


def stream_add_kernel(*refs):
    held, got, kept, sent = refs[0:4], refs[4:8], refs[-8:-4], refs[-4:]
    for s in range(4):
        rows = held[s].shape[0] - SMALL
        low = rows // 2
        small = held[s][rows:] + got[s][rows:]
        kept[s][0:low] = held[s][0:low] + got[s][0:low]
        kept[s][low:] = small
        sent[s][0:low] = held[s][low:rows] + got[s][low:rows]
        sent[s][low:] = small


def stream_add(held, got, *after):
    rows = held[0].shape[0] - SMALL
    shape = struct(rows // 2 + SMALL, 128)
    out = pl.pallas_call(
        stream_add_kernel,
        name="stream_add",
        cost_estimate=taking(0.7 + rows / 1000),
        out_shape=[shape] * 8,
        in_specs=[VMEM] * 8 + [ANY] * len(after),
        out_specs=[VMEM] * 8,
        compiler_params=pltpu.CompilerParams(vmem_limit_bytes=6 * MIB),
    )(*held, *got, *after)
    return out[:4], out[4:]


def stream_last_kernel(place, *refs):
    held, got, (own, send, small, gains) = refs[0:4], refs[4:8], refs[-4:]
    first = place[1] == 0
    for s in range(4):
        total = (held[s][0:256] + got[s][0:256]).T
        columns = slice(256 * s, 256 * s + 256)
        own[:, columns] = jnp.where(first, total[:64], total[64:])
        send[:, columns] = jnp.where(first, total[64:], total[:64])
        total = held[s][256:] + got[s][256:]
        small[:, 128 * s : 128 * s + 128] = total[:80]
        gains[:, 128 * s : 128 * s + 128] = total[80:]


def stream_last(place, held, got, *after):
    return pl.pallas_call(
        stream_last_kernel,
        name="stream_last",
        cost_estimate=taking(1.5),
        out_shape=(struct(64, 1024), struct(64, 1024), struct(80, C), struct(8, C)),
        in_specs=[SMEM] + [VMEM] * 8 + [ANY] * len(after),
        out_specs=[VMEM] * 4,
        compiler_params=pltpu.CompilerParams(vmem_limit_bytes=6 * MIB),
    )(place, *held, *got, *after)


def stream_masks(axis, mask):
    other = "seq_0" if axis == "seq_1" else "seq_1"
    return ((axis, mask), (axis, 4 - mask), (other, mask), (other, 4 - mask))


def stream_swap(sent, step):
    return [swap(x, *stream_masks(*STREAMS[s])[step]) for s, x in enumerate(sent)]


def mixer_shares_kernel(place, own, got, small, small_got, *rest):
    grad_in, grad_out, small_sum = rest[-3:]
    first = place[1] == 0
    low = jnp.where(first, own[...], got[...])
    high = jnp.where(first, got[...], own[...])
    for k in range(3):
        columns = slice(256 * k, 256 * k + 256)
        grad_in[k, :, :256], grad_in[k, :, 256:] = low[:, columns], high[:, columns]
    grad_out[:, :256], grad_out[:, 256:] = low[:, 768:], high[:, 768:]
    small_sum[...] = small[...] + small_got[...]


def mixer_shares(place, own, got, small, small_got, *after):
    return pl.pallas_call(
        mixer_shares_kernel,
        name="mixer_shares",
        cost_estimate=taking(1.5),
        out_shape=(struct(3, 64, C), struct(64, C), struct(80, C)),
        in_specs=[SMEM] + [VMEM] * 4 + [ANY] * len(after),
        out_specs=[VMEM] * 3,
        compiler_params=pltpu.CompilerParams(vmem_limit_bytes=6 * MIB),
    )(place, own, got, small, small_got, *after)


def ffn_send_kernel(place, share, *rest):
    own, send = rest[-2:]
    first = place[1] == 0
    low, high = share[:64], share[64:]
    own[...] = jnp.where(first, low, high)
    send[...] = jnp.where(first, high, low)


def ffn_shares_kernel(place, own, got, *rest):
    gate, up, down, token = rest[-4:]
    first = place[1] == 0
    low = jnp.where(first, own[...], got[...])
    high = jnp.where(first, got[...], own[...])
    gate[:, :768], gate[:, 768:] = low[:, :768], high[:, 768:1408]
    up[:, :640], up[:, 640:] = low[:, 768:1408], high[:, :768]
    down[:, :768], down[:, 768:] = low[:, 1408:], high[:, 1408 + 128 :]
    token[...] = jnp.zeros(token.shape, F32)


def ffn_halves(place, share, *after):
    return pl.pallas_call(
        ffn_send_kernel,
        name="ffn_send",
        cost_estimate=taking(1),
        out_shape=(struct(64, 2176),) * 2,
        in_specs=[SMEM, VMEM] + [ANY] * len(after),
        out_specs=[VMEM] * 2,
        compiler_params=pltpu.CompilerParams(vmem_limit_bytes=6 * MIB),
    )(place, share, *after)


def ffn_shares(place, own, got, *after):
    return pl.pallas_call(
        ffn_shares_kernel,
        name="ffn_shares",
        cost_estimate=taking(2),
        out_shape=(struct(64, 1408),) * 3 + (struct(8, 128),),
        in_specs=[SMEM, VMEM, VMEM] + [ANY] * len(after),
        out_specs=[VMEM] * 4,
        compiler_params=pltpu.CompilerParams(vmem_limit_bytes=8 * MIB),
    )(place, own, got, *after)


def norm_kernel(values, gain, *rest):
    out, inverse = rest[-2:]
    v = values[...]
    inverse[...] = inverse_rms(v)
    out[...] = (v * inverse[...] * gain[...]).astype(BF16)


def normed(values, gain, *after):
    rows = 128
    row = pl.BlockSpec((rows, D), lambda i: (i, 0))
    return pl.pallas_call(
        norm_kernel,
        name="normed_in",
        cost_estimate=taking(1.8),
        grid=(values.shape[0] // rows,),
        out_shape=(struct(*values.shape, dtype=BF16), struct(values.shape[0], 1)),
        in_specs=[row, whole(1, D)] + [ANY] * len(after),
        out_specs=(row, pl.BlockSpec((rows, 1), lambda i: (i, 0))),
        compiler_params=pltpu.CompilerParams(vmem_limit_bytes=11 * MIB),
    )(values, gain, *after)


HALF = D // 2


def rows_by_quarter(place, ref):
    return jnp.concatenate([ref[quarter_rows(place[0] ^ q), :] for q in range(4)])


def cotangent_kernel(place, cotangent, w_down, *rest):
    low, grad_hidden = rest[-2:]

    @pl.when(pl.program_id(0) == 0)
    def _():
        for q in range(4):
            low[ROWS * q : ROWS * q + ROWS] = cotangent[quarter_rows(place[0] ^ q), :].astype(BF16)

    grad_hidden[...] = dot_t(low[...], w_down[...])


def cotangent_part(place, cotangent, w_down, *after):
    wide = w_down.shape[0]
    return pl.pallas_call(
        cotangent_kernel,
        name="cotangent_part",
        cost_estimate=taking(4),
        grid=(6,),
        out_shape=(struct(T, D, dtype=BF16), struct(T, wide)),
        in_specs=[SMEM, VMEM, pl.BlockSpec((256, D), lambda i: (i, 0))] + [ANY] * len(after),
        out_specs=(VMEM, pl.BlockSpec((T, 256), lambda i: (0, i))),
        compiler_params=pltpu.CompilerParams(vmem_limit_bytes=9 * MIB),
    )(place, cotangent, w_down, *after)


def out_parts_kernel(place, gated, *rest):
    own, send = rest[-2:]
    first = place[1] == 0
    rows = rows_by_quarter(place, gated).astype(F32)
    low, high = rows[:, :256], rows[:, 256:]
    own[...] = jnp.where(first, low, high).astype(BF16)
    send[...] = jnp.where(first, high, low)


def out_parts(place, gated, *after):
    return pl.pallas_call(
        out_parts_kernel,
        name="out_parts",
        cost_estimate=taking(1),
        out_shape=(struct(T, 256, dtype=BF16), struct(T, 256)),
        in_specs=[SMEM, VMEM] + [ANY] * len(after),
        out_specs=[VMEM] * 2,
        compiler_params=pltpu.CompilerParams(vmem_limit_bytes=7 * MIB),
    )(place, gated, *after)


def owner_kernel(place, rows, *rest):
    rest[-1][...] = rows[...].astype(BF16)


def owner_rows(place, x, *after):
    row = pl.BlockSpec((ROWS, D), lambda i, place: (place[0] ^ i, 0))
    out = pl.BlockSpec((ROWS, D), lambda i, place: (i, 0))
    return pl.pallas_call(
        owner_kernel,
        name="owner_rows",
        cost_estimate=taking(2),
        out_shape=pltpu.HBM((T, D), BF16),
        grid_spec=pltpu.PrefetchScalarGridSpec(
            num_scalar_prefetch=1, grid=(4,), in_specs=[row] + [ANY] * len(after), out_specs=out
        ),
        compiler_params=pltpu.CompilerParams(vmem_limit_bytes=9 * MIB),
    )(place, in_hbm(x), *after)


def branch_other_kernel(place, cotangent, through, out):
    out[...] = (cotangent[...] + through[...]).astype(BF16)


def branch_other_of(place, cotangent, through):
    row = pl.BlockSpec((ROWS, D), lambda i, place: (i, 0))
    return pl.pallas_call(
        branch_other_kernel,
        name="branch_other",
        cost_estimate=taking(2),
        out_shape=struct(T, D, dtype=BF16),
        grid_spec=pltpu.PrefetchScalarGridSpec(
            num_scalar_prefetch=1,
            grid=(4,),
            in_specs=[pl.BlockSpec((ROWS, D), lambda i, place: (place[0] ^ i, 0)), row],
            out_specs=row,
        ),
        compiler_params=pltpu.CompilerParams(vmem_limit_bytes=9 * MIB),
    )(place, in_hbm(cotangent), through)


def middle_kernel(place, left, left_more, right, right_more, hidden, middle, out_left, out_right):
    low = hidden[:, :HALF] + (left[...] + left_more[...])
    high = hidden[:, HALF:] + (right[...] + right_more[...])
    square = jnp.sum(low * low, axis=-1, keepdims=True) + jnp.sum(high * high, axis=-1, keepdims=True)
    inverse = lax.rsqrt(square * (1.0 / D) + epsilon)
    middle[:, :HALF], middle[:, HALF:] = low, high
    out_left[...], out_right[...] = low * inverse, high * inverse


def norm_back_parts(left, left_more, right, right_more, values, gain):
    grads = (left[...] + left_more[...], right[...] + right_more[...])
    v = (values[:, :HALF], values[:, HALF:])
    g = (gain[:, :HALF], gain[:, HALF:])
    square = sum(jnp.sum(x * x, axis=-1, keepdims=True) for x in v)
    inverse = lax.rsqrt(square * (1.0 / D) + epsilon)
    along = sum(jnp.sum(a * b * c, axis=-1, keepdims=True) for a, b, c in zip(g, grads, v))
    along = inverse * inverse * inverse * (along * (1.0 / D))
    back = [inverse * g[n] * grads[n] - v[n] * along for n in (0, 1)]
    return back, [grads[n] * (v[n] * inverse) for n in (0, 1)]


def norm_back_kernel(left, left_more, right, right_more, values, gain, *rest):
    out_left, out_right, gains = rest[-3:]
    back, weighed = norm_back_parts(left, left_more, right, right_more, values, gain)
    out_left[...], out_right[...] = back
    for n in (0, 1):
        gains[:, HALF * n : HALF * n + HALF] = jnp.sum(weighed[n], axis=0, keepdims=True)


def by_owner_grid(in_specs, out_specs):
    return pltpu.PrefetchScalarGridSpec(
        num_scalar_prefetch=1, grid=(1,), in_specs=in_specs, out_specs=out_specs
    )


MINE = pl.BlockSpec((ROWS, D), lambda i, place: (place[0], 0))


def after_middle(place, pieces, hidden):
    return pl.pallas_call(
        middle_kernel,
        name="middle_and_norm",
        cost_estimate=taking(1.5),
        out_shape=(struct(ROWS, D), struct(ROWS, HALF), struct(ROWS, HALF)),
        grid_spec=by_owner_grid([VMEM] * 4 + [MINE], (VMEM,) * 3),
        compiler_params=pltpu.CompilerParams(vmem_limit_bytes=8 * MIB),
    )(place, *pieces, in_hbm(hidden))


def norm_back(pieces, values, gain, *after):
    return pl.pallas_call(
        norm_back_kernel,
        name="norm_back",
        cost_estimate=taking(2),
        out_shape=(struct(ROWS, HALF), struct(ROWS, HALF), struct(1, D)),
        grid=(1,),
        in_specs=[whole(ROWS, HALF)] * 4 + [whole(ROWS, D), whole(1, D)] + [ANY] * len(after),
        out_specs=(VMEM,) * 3,
        compiler_params=pltpu.CompilerParams(vmem_limit_bytes=9 * MIB),
    )(*pieces, values, gain, *after)


def rim_kernel(starts, rows, *rest):
    out = rest[-1]
    at = lax.broadcasted_iota(jnp.int32, (8, D), 0)
    out[...] = jnp.where(at == 6, rows[...] * keep_at(starts, T - 1), rows[...])


def rim_rows_of(starts, hidden, *after):
    return pl.pallas_call(
        rim_kernel,
        name="rim_rows",
        cost_estimate=taking(1),
        grid=(1,),
        out_shape=struct(8, D),
        in_specs=[SMEM, pl.BlockSpec((8, D), lambda i: (T // 8 - 1, 0))] + [ANY] * len(after),
        out_specs=whole(8, D),
        compiler_params=pltpu.CompilerParams(vmem_limit_bytes=6 * MIB),
    )(starts, in_hbm(hidden), *after)


PIECES = ((0, 3), (1, 2), (0, 1), (3, 2))
PIECE_SHAPES = (struct(2 * ROWS, HALF),) * 4


def put_pieces(place, block, total, outs, by_owner=False):
    which, columns = block // 2, slice(512 * (block % 2), 512 * (block % 2) + 512)
    for n in (0, 1):
        out, quarters = outs[2 * which + n], PIECES[2 * which + n]
        for m, q in enumerate(quarters):
            rows = slice(ROWS * q, ROWS * q + ROWS) if by_owner else quarter_rows(place[0] ^ q)
            out[ROWS * m : ROWS * m + ROWS, columns] = total[rows, :]


def split_kernel(compute, by_owner, count, place, *refs):
    *outs, total = refs[-5:]
    for block in range(4):
        total[...] = compute(slice(512 * block, 512 * block + 512), *refs[:count])
        put_pieces(place, block, total, outs, by_owner)


def split_dot(name, compute, by_owner, place, *operands, after=()):
    return pl.pallas_call(
        functools.partial(split_kernel, compute, by_owner, len(operands)),
        name=name,
        cost_estimate=taking(2.5),
        out_shape=PIECE_SHAPES,
        in_specs=[SMEM] + [VMEM] * len(operands) + [ANY] * len(after),
        out_specs=[VMEM] * 4,
        scratch_shapes=[pltpu.VMEM((T, 512), F32)],
        compiler_params=pltpu.CompilerParams(vmem_limit_bytes=8 * MIB),
    )(place, *operands, *after)


def result_kernel(place, hidden, w_down, middle, *rest):
    out, token = rest[-2:]
    token[...] = jnp.zeros(token.shape, F32)
    for block in range(4):
        columns = slice(512 * block, 512 * block + 512)
        total = dot(hidden[...], w_down[:, columns])
        for q in range(4):
            rows = total[ROWS * q : ROWS * q + ROWS]
            out[quarter_rows(place[0] ^ q), columns] = rows + middle[:, columns] if q == 0 else rows


def result_part(place, hidden, w_down, middle, *after):
    return pl.pallas_call(
        result_kernel,
        name="result_part",
        cost_estimate=taking(2.5),
        out_shape=(pltpu.HBM((T, D), F32), struct(8, 128)),
        in_specs=[SMEM] + [VMEM] * 3 + [ANY] * len(after),
        out_specs=(VMEM, VMEM),
        compiler_params=pltpu.CompilerParams(vmem_limit_bytes=10 * MIB),
    )(place, hidden, w_down, middle, *after)


def ffn_kernel(place, *refs):
    parts, refs = refs[:6], refs[6:]
    gain, w_gate, w_up, grad_hidden = refs[:4]
    mid_x, hidden, grad_gate, grad_up, own_all, send_all = refs[-6:]
    for q, (left, right) in enumerate(quarters_of(parts)):
        rows = slice(ROWS * q, ROWS * q + ROWS)
        mid_x[rows, :HALF] = (left * gain[:, :HALF]).astype(BF16)
        mid_x[rows, HALF:] = (right * gain[:, HALF:]).astype(BF16)
    wide = w_gate.shape[1]
    for start in range(0, wide, 256):
        columns = slice(start, min(start + 256, wide))
        gate = dot(mid_x[...], w_gate[:, columns])
        up = dot(mid_x[...], w_up[:, columns])
        sig = 1.0 / (1.0 + jnp.exp(-gate))
        silu = gate * sig
        incoming = grad_hidden[:, columns]
        hidden[:, columns] = (silu * up).astype(BF16)
        grad_gate[:, columns] = (incoming * up * sig * (1.0 + gate * (1.0 - sig))).astype(BF16)
        grad_up[:, columns] = (incoming * silu).astype(BF16)
    first = place[1] == 0

    def halves(columns, low, high):
        a, b = low.astype(F32), high.astype(F32)
        own_all[:, columns] = jnp.where(first, a, b).astype(BF16)
        send_all[:, columns] = jnp.where(first, b, a)

    halves(slice(0, 768), grad_gate[:, :768], grad_up[:, 640:1408])
    halves(slice(768, 1408), grad_up[:, :640], grad_gate[:, 768:1408])
    halves(slice(1408, 2176), hidden[:, :768], hidden[:, 640:1408])


def feed_forward(place, parts, gain, w_gate, w_up, grad_hidden, *after):
    wide = w_gate.shape[1]
    low = struct(T, wide, dtype=BF16)
    return pl.pallas_call(
        ffn_kernel,
        name="feed_forward",
        cost_estimate=taking(7),
        out_shape=(
            struct(T, D, dtype=BF16),
            low,
            low,
            low,
            struct(T, wide + 768, dtype=BF16),
            struct(T, wide + 768),
        ),
        in_specs=[SMEM] + [VMEM] * 10 + [ANY] * len(after),
        out_specs=(VMEM,) * 6,
        compiler_params=pltpu.CompilerParams(vmem_limit_bytes=10 * MIB),
    )(place, *parts, gain, w_gate, w_up, grad_hidden, *after)


def branch_back_kernel(place, *refs):
    parts, cotangent, w_out = refs[:6], *refs[6:8]
    through, branch, grad_gated = refs[-3:]
    for q, (left, right) in enumerate(quarters_of(parts)):
        rows = slice(ROWS * q, ROWS * q + ROWS)
        through[rows, :HALF], through[rows, HALF:] = left, right
    branch[...] = (rows_by_quarter(place, cotangent) + through[...]).astype(BF16)
    back = dot_t(branch[...], w_out[...])
    for q in range(4):
        grad_gated[quarter_rows(place[0] ^ q), :] = back[ROWS * q : ROWS * q + ROWS]


def branch_back(place, parts, cotangent, w_out, *after):
    return pl.pallas_call(
        branch_back_kernel,
        name="branch_back",
        cost_estimate=taking(3),
        out_shape=(struct(T, D), pltpu.HBM((T, D), BF16), struct(T, C)),
        in_specs=[SMEM] + [VMEM] * 8 + [ANY] * len(after),
        out_specs=(VMEM,) * 3,
        compiler_params=pltpu.CompilerParams(vmem_limit_bytes=8 * MIB),
    )(place, *parts, cotangent, w_out, *after)


def finish_kernel(place, starts, grads, rim, *rest):
    low, own, send = rest[-3:]
    first = place[1] == 0
    at = lax.broadcasted_iota(jnp.int32, (8, C), 0)
    for k in range(3):
        turned = jnp.concatenate([jnp.zeros((6, C), F32), rim[k, 0:2]])
        turned = jnp.where(at == 6, turned * keep_at(starts, T - 1), turned)
        low[k, : T - 16] = grads[k, : T - 16].astype(BF16)
        low[k, T - 16 :] = jnp.concatenate(
            [grads[k, T - 16 : T - 8], grads[k, T - 8 :] + turned]
        ).astype(BF16)
        a, b = low[k, :, :256].astype(F32), low[k, :, 256:].astype(F32)
        columns = slice(256 * k, 256 * k + 256)
        own[:, columns] = jnp.where(first, a, b).astype(BF16)
        send[:, columns] = jnp.where(first, b, a)


def finish_projected(place, starts, grads, rim, *after):
    return pl.pallas_call(
        finish_kernel,
        name="finish_projected",
        cost_estimate=taking(1.5),
        out_shape=(struct(3, T, C, dtype=BF16), struct(T, 768, dtype=BF16), struct(T, 768)),
        in_specs=[SMEM, SMEM, VMEM, VMEM] + [ANY] * len(after),
        out_specs=(VMEM,) * 3,
        compiler_params=pltpu.CompilerParams(vmem_limit_bytes=7 * MIB),
    )(place, starts, grads, rim, *after)


def first_kernel(place, grads, hidden, inverse, gain, w_in, cotangent, left, right, *rest):
    out, gains, total = rest[-3:]
    along = jnp.zeros((T, 1), F32)
    for block in range(4):
        columns = slice(512 * block, 512 * block + 512)
        part = sum(dot_t(grads[k], w_in[k, columns, :]) for k in range(3))
        weighed = part * (hidden[:, columns] * inverse[...])
        gains[:, columns] = jnp.sum(weighed, axis=0, keepdims=True)
        along += jnp.sum(weighed * gain[:, columns], axis=1, keepdims=True)
        total[:, columns] = part
    along = inverse[...] * inverse[...] * (along * (1.0 / D))
    mine = quarter_rows(place[0])
    for block in range(4):
        columns = slice(512 * block, 512 * block + 512)
        out[:, columns] = inverse[...] * (gain[:, columns] * total[:, columns]) - hidden[:, columns] * along
        side, own = (left, right)[block // 2], slice(512 * (block % 2), 512 * (block % 2) + 512)
        out[mine, columns] += cotangent[mine, columns] + side[:, own]


def first_back(place, grads, hidden, inverse, gain, w_in, cotangent, left, right, *after):
    return pl.pallas_call(
        first_kernel,
        name="first_back",
        cost_estimate=taking(4),
        out_shape=(pltpu.HBM((T, D), F32), struct(1, D)),
        in_specs=[SMEM] + [VMEM] * 8 + [ANY] * len(after),
        out_specs=[VMEM] * 2,
        scratch_shapes=[pltpu.VMEM((T, D), F32)],
        compiler_params=pltpu.CompilerParams(vmem_limit_bytes=14 * MIB),
    )(place, grads, hidden, inverse, gain, w_in, cotangent, left, right, *after)


def emit_kernel(first, second, *rest):
    first_out, second_out, token = rest[-3:]
    token[...] = jnp.zeros(token.shape, F32)
    first_out[...], second_out[...] = first[...], second[...]


def emit(first, second, *after):
    row = pl.BlockSpec((ROWS, D), lambda i: (i, 0))
    return pl.pallas_call(
        emit_kernel,
        name="emit",
        cost_estimate=taking(3),
        grid=(4,),
        out_shape=(struct(T, D), struct(T, D), struct(8, 128)),
        in_specs=[row, row] + [ANY] * len(after),
        out_specs=(row, row, whole(8, 128)),
        compiler_params=pltpu.CompilerParams(vmem_limit_bytes=9 * MIB),
    )(in_hbm(first), in_hbm(second), *after)


def per_device(
    hidden_in,
    cotangent,
    starts,
    norm_in,
    w_in,
    short_w,
    pole_pairs,
    residues,
    w_out,
    norm_mid,
    w_gate,
    w_up,
    w_down,
):
    place = jnp.stack(
        [lax.axis_index(axis) for axis in ("tp", "seq_2", "seq_1", "seq_0")]
    ).astype(jnp.int32)
    column = starts[:, None]
    gain_in, gain_mid = norm_in[None], norm_mid[None]

    def other_core(x):
        return swap(x, "seq_2", 1)

    rim_rows = rim_rows_of(starts, hidden_in, place, column)
    rim_rows = lax.ppermute(rim_rows, SEQ, [(i, i + 1) for i in range(31)])
    hidden_other = other_core(hidden_in)
    cotangent_other = other_core(cotangent)
    normed_in, inverse_in = normed(hidden_in, gain_in)
    proj, rim, mixed, end, powers = project_and_mix(
        normed_in, rim_rows, gain_in, w_in, short_w, column, starts, pole_pairs
    )

    down_grad, grad_hidden = cotangent_part(place, cotangent, w_down, end)
    entering = carried_state(place, end, powers, False, late=(grad_hidden,))
    signal, gated = signal_of(mixed, starts, pole_pairs, residues, entering)

    branch = split_dot(
        "branch",
        lambda columns, a, b: dot(a[...], b[:, columns]),
        False,
        place,
        gated,
        w_out,
    )
    *history, history_token = history_of(mixed, starts, pole_pairs, entering, branch[1])
    out_right, out_send = out_parts(place, gated, branch[1])
    middle, mid_left, mid_right = after_middle(
        place,
        scatter_sum(branch, history_token, out_send),
        hidden_in,
    )

    normed_other, _ = normed(hidden_other, gain_in, mid_left)
    down_other = owner_rows(place, cotangent_other, mid_left)
    parts, joined = gather_joined(mid_left, mid_right, in_hbm(normed_other), in_hbm(down_other))
    mid_other = [other_core(x) for x in joined]
    mid_x, hidden, grad_gate, grad_up, own_all, send_all = feed_forward(
        place,
        parts,
        gain_mid,
        w_gate,
        w_up,
        grad_hidden,
        *mid_other,
    )
    mid_other += [other_core(parts[1]), other_core(parts[5])]
    mid_terms = split_dot(
        "mid_terms",
        lambda columns, a, b, c, d: dot_t(a[...], c[columns, :]) + dot_t(b[...], d[columns, :]),
        True,
        place,
        grad_gate,
        grad_up,
        w_gate,
        w_up,
        after=mid_other[2:],
    )

    ffn_sum, ffn_token = wide_token_sum(
        mid_x,
        mid_other,
        down_grad,
        down_other,
        own_all,
        other_core(tie(send_all, mid_terms[1])),
        gain_mid,
    )

    pieces = scatter_sum(mid_terms, ffn_token)
    share_ffn = lax.psum_scatter(
        tie(ffn_sum, pieces[0], hbm=True), ("seq_0", "seq_1"), scatter_dimension=0, tiled=True
    )
    through_left, through_right, gains_mid = norm_back(pieces, middle, gain_mid)
    result, part_token = result_part(place, hidden, w_down, middle, gains_mid)
    through_f, branch_grad, grad_gated = branch_back(
        place, gather_parts(through_left, through_right), cotangent, w_out, part_token
    )

    leaving = adjoint_end(grad_gated, mixed, column, starts, pole_pairs, residues)
    branch_other = branch_other_of(place, cotangent_other, other_core(through_f))
    returning = carried_state(place, leaving, powers, True, after=(in_hbm(branch_other),))
    grad_proj, rim_grad, sums = back(
        grad_gated,
        mixed,
        signal,
        proj,
        rim,
        history,
        short_w,
        column,
        starts,
        pole_pairs,
        residues,
        returning,
    )
    rim_back = lax.ppermute(rim_grad, SEQ, [(i + 1, i) for i in range(31)])

    projected_low, proj_own, proj_send = finish_projected(
        place, starts, grad_proj, rim_back
    )
    proj_wide = other_core(proj_send)
    grad_input, gains_in = first_back(
        place,
        projected_low,
        hidden_in,
        inverse_in,
        gain_in,
        w_in,
        cotangent,
        through_left,
        through_right,
    )
    result, grad_input = lax.psum((result, grad_input), "tp")
    kept, leaving_now, mixer_token = stream_token_sum(
        place,
        normed_in,
        normed_other,
        branch_grad,
        branch_other,
        proj_own,
        proj_wide,
        out_right,
        other_core(out_send),
        sums,
        gains_in,
        gains_mid,
    )
    got = stream_swap(leaving_now, 0)
    kept, leaving_now = stream_add(kept, got)
    got = stream_swap(leaving_now, 1)
    kept, leaving_now = stream_add(kept, got)
    got = stream_swap(leaving_now, 2)
    kept, leaving_now = stream_add(kept, got)
    got = stream_swap(leaving_now, 3)
    ffn_own, ffn_out = ffn_halves(place, share_ffn, kept[0])
    share_gate, share_up, share_down, shares_token = ffn_shares(place, ffn_own, other_core(ffn_out))
    result, grad_input, output_token = emit(result, grad_input, ffn_own)
    own, send, small, gains = stream_last(place, kept, got, shares_token)
    share_in, share_out, small = mixer_shares(
        place, own, other_core(send), small, other_core(small), output_token
    )
    gains = sum_over(sum_over(gains, "tp", output_token), "seq_2")
    return (
        result,
        grad_input,
        gains[0:4].reshape(D),
        share_in,
        small[64:73].reshape(3, 3, C),
        small[0:32].reshape(2, N, C),
        small[32:64].reshape(2, N, C),
        share_out.T,
        gains[4:8].reshape(D),
        share_gate,
        share_up,
        share_down.T,
    )


def solution(mesh):
    split = Mesh(mesh.devices.reshape(4, 4, 2, mesh.shape["tp"]), ("seq_0", "seq_1", "seq_2", "tp"))
    in_specs = (
        P(SEQ, None),
        P(SEQ, None),
        P(SEQ),
        P(),
        P(None, None, "tp"),
        P(None, None, "tp"),
        P(None, None, "tp"),
        P(None, None, "tp"),
        P("tp", None),
        P(),
        P(None, "tp"),
        P(None, "tp"),
        P("tp", None),
    )
    out_specs = (
        P(SEQ, None),
        P(SEQ, None),
        P(),
        P(None, SEQ, "tp"),
        P(None, None, "tp"),
        P(None, None, "tp"),
        P(None, None, "tp"),
        P("tp", SEQ),
        P(),
        P(SEQ, "tp"),
        P(SEQ, "tp"),
        P("tp", SEQ),
    )
    return jax.shard_map(
        per_device, mesh=split, in_specs=in_specs, out_specs=out_specs, check_vma=False
    )
```

```python
import functools

import jax
import jax.numpy as jnp
from jax import lax
from jax.experimental import pallas as pl
from jax.experimental.pallas import tpu as pltpu
from jax.sharding import Mesh
from jax.sharding import PartitionSpec as P

SEQ = ("seq_0", "seq_1", "seq_2")
F32 = jnp.float32
BF16 = jnp.bfloat16
epsilon = 1e-06
MIB = 1 << 20
T, C, N, D = 256, 512, 16, 2048
BLOCK = 32
BLOCKS = T // BLOCK
PARTS = 1
ROWS = 64
VMEM = pl.BlockSpec(memory_space=pltpu.VMEM)
SMEM = pl.BlockSpec(memory_space=pltpu.SMEM)
ANY = pl.BlockSpec(memory_space=pl.ANY)


def in_hbm(x):
    return pltpu.with_memory_space_constraint(x, pltpu.HBM)


def taking(microseconds):
    return pl.CostEstimate(flops=0, bytes_accessed=int(microseconds * 3.0e6), transcendentals=0)


def whole(*shape):
    return pl.BlockSpec(shape, lambda i: (0,) * len(shape))


def struct(*shape, dtype=F32):
    return jax.ShapeDtypeStruct(shape, dtype)


def times(a, b):
    return a[0] * b[0] - a[1] * b[1], a[0] * b[1] + a[1] * b[0]


def plus(a, b):
    return a[0] + b[0], a[1] + b[1]


def where2(flag, a, b):
    return jnp.where(flag, a[0], b[0]), jnp.where(flag, a[1], b[1])


def scaled(a, factor):
    return a[0] * factor, a[1] * factor


def token_sum(a, b):
    return lax.dot_general(a, b, (((0,), (0,)), ((), ())), preferred_element_type=F32)


def dot(a, b):
    return jnp.dot(a, b, preferred_element_type=F32)


def dot_t(a, b):
    return lax.dot_general(a, b, (((1,), (1,)), ((), ())), preferred_element_type=F32)


def scan_groups(groups, starts, base, run, carry, reverse):
    def body(step, kept):
        group = groups - 1 - step if reverse else step
        first = base + group * 8
        marks = starts[first]
        for r in range(1, 8):
            marks = marks + starts[first + r]
        return lax.cond(
            marks > 0, lambda c: run(group, c, True), lambda c: run(group, c, False), kept
        )

    return lax.fori_loop(0, groups, body, carry)


def quarter_rows(quarter):
    return pl.ds(pl.multiple_of(quarter * ROWS, ROWS), ROWS)


def eight(group):
    return pl.ds(pl.multiple_of(group * 8, 8), 8)


def fold(x, y, step):
    at = lax.broadcasted_iota(jnp.int32, x.shape, 0)
    of_x = (at & step) == 0
    return jnp.where(of_x, x, y) + pltpu.roll(jnp.where(of_x, y, x), 8 - step, 0)


def row_sums(parts):
    for step in (1, 2, 4):
        parts = [fold(parts[n], parts[n + 1], step) for n in range(0, len(parts), 2)]
    return parts[0]


def keep_at(starts, token):
    return (1 - starts[token]).astype(F32)


def with_rim(proj, rim, k, rows):
    rows[0:8] = rim[k]
    rows[8:] = proj[k]


def keeps_of(column):
    marks = column[...].astype(F32)
    one = 1.0 - marks
    two = one * jnp.concatenate([jnp.ones((1, 1), F32), one[: T - 1]])
    return one, two, 1.0 - jnp.max(marks, axis=0, keepdims=True)


def mix_kernel(rows, rim, gain, *refs):
    weights, (taps, column, starts, poles), refs = refs[:4], refs[4:8], refs[8:]
    proj, proj_rim, mixed, end, powers, left, kept, shifted_rows, driven = refs
    k = pl.program_id(0)
    quarter = D // 4

    @pl.when(k == 0)
    def _():
        v = rim[...]
        v = (v * inverse_rms(v) * gain[...]).astype(BF16)
        for n in range(4):
            columns = slice(quarter * n, quarter * n + quarter)
            left[n, 0:T] = rows[:, columns]
            left[n, T:] = jnp.concatenate([v[:, columns], v[:, columns]])

    out = sum(dot(left[n], weights[n][0]) for n in range(4))
    proj[0], proj_rim[0] = out[:T], out[T : T + 8]
    kept[k] = out[: T + 8]
    pl.when(k == 2)(
        functools.partial(mix_end, kept, taps, column, starts, poles, mixed, end, powers, shifted_rows, driven)
    )


def mix_end(kept, taps, column, starts, poles, mixed, end, powers, rows, driven):
    one, two, is_open = keeps_of(column)
    for k in range(3):
        rows[0:8], rows[8:] = kept[k, T:], kept[k, :T]
        mixed[k] = (
            taps[k, 0:1] * kept[k, :T]
            + taps[k, 1:2] * (one * rows[7 : 7 + T])
            + taps[k, 2:3] * (two * rows[6 : 6 + T])
        )
    driven[...] = mixed[1] * mixed[2]
    pre, pim = poles[0], poles[1]

    def run(group, state, masked):
        source = driven[eight(group), :]
        re, im = state
        for r in range(8):
            if masked:
                keep = keep_at(starts, group * 8 + r)
                re, im = re * keep, im * keep
            re, im = pre * re - pim * im + source[r : r + 1], pre * im + pim * re
        return re, im

    zero = jnp.zeros((N, C), F32)
    end[0:N], end[N : 2 * N] = scan_groups(T // 8, starts, 0, run, (zero, zero), False)
    end[2 * N :] = jnp.broadcast_to(is_open, (8, C))
    power = (pre, pim)
    for n in range(1, 12):
        power = times(power, power)
        if n in (8, 9, 11):
            at = {8: 0, 9: 2, 11: 4}[n]
            powers[at], powers[at + 1] = power


def project_and_mix(rows, rim, gain, weights, taps, column, starts, poles):
    depth = D // 4

    def part(n):
        return pl.BlockSpec((1, depth, C), lambda k: (k, n, 0))

    weights = in_hbm(weights)
    return pl.pallas_call(
        mix_kernel,
        name="project_and_mix",
        cost_estimate=taking(8),
        grid=(3,),
        out_shape=(
            pltpu.HBM((3, T, C), F32),
            struct(3, 8, C),
            pltpu.HBM((3, T, C), F32),
            struct(2 * N + 8, C),
            struct(6, N, C),
        ),
        in_specs=[VMEM, VMEM, VMEM]
        + [part(n) for n in range(4)]
        + [VMEM, VMEM, SMEM, VMEM],
        out_specs=(
            pl.BlockSpec((1, T, C), lambda k: (k, 0, 0)),
            pl.BlockSpec((1, 8, C), lambda k: (k, 0, 0)),
            whole(3, T, C),
            VMEM,
            VMEM,
        ),
        scratch_shapes=[
            pltpu.VMEM((4, T + 16, depth), BF16),
            pltpu.VMEM((3, T + 8, C), F32),
            pltpu.VMEM((T + 8, C), F32),
            pltpu.VMEM((T, C), F32),
        ],
        compiler_params=pltpu.CompilerParams(vmem_limit_bytes=22 * MIB),
    )(rows, rim, gain, *[weights] * 4, taps, column, starts, poles)


def forward_rows(mixed, starts, poles, block, state, visit, finish=None):
    pre, pim = poles[0], poles[1]
    base = block * BLOCK

    def run(group, kept, masked):
        source = mixed[1, eight(group), :] * mixed[2, eight(group), :]
        re, im = kept
        seen = []
        for r in range(8):
            if masked:
                keep = keep_at(starts, base + group * 8 + r)
                re, im = re * keep, im * keep
            re, im = pre * re - pim * im + source[r : r + 1], pre * im + pim * re
            seen.append(visit(group * 8 + r, re, im))
        if finish:
            finish(group, seen)
        return re, im

    state[0], state[1] = scan_groups(BLOCK // 8, starts, base, run, (state[0], state[1]), False)


def signal_kernel(mixed, starts, poles, residues, first, signal, gated, state):
    block = pl.program_id(0)

    @pl.when(block == 0)
    def _():
        state[...] = first[...]

    qre, qim = residues[0], residues[1]

    def visit(row, re, im):
        weighed = qre * re - qim * im
        return weighed[:8] + weighed[8:]

    def finish(group, seen):
        signal[eight(group), :] = row_sums(seen)

    forward_rows(mixed, starts, poles, block, state, visit, finish)
    gated[...] = (mixed[0] * signal[...]).astype(BF16)


def history_kernel(mixed, starts, poles, first, *rest):
    h0, h1, h2, h3, token, state = rest[-6:]
    block = pl.program_id(0)
    token[...] = jnp.zeros(token.shape, F32)

    @pl.when(block == 0)
    def _():
        state[...] = first[...]

    def visit(row, re, im):
        h0[row], h1[row] = re[:8], re[8:]
        h2[row], h3[row] = im[:8], im[8:]

    forward_rows(mixed, starts, poles, block, state, visit)


def signal_of(mixed, starts, poles, residues, first):
    return pl.pallas_call(
        signal_kernel,
        name="signal",
        cost_estimate=taking(6),
        grid=(BLOCKS,),
        out_shape=(struct(T, C), struct(T, C, dtype=BF16)),
        in_specs=[
            pl.BlockSpec((3, BLOCK, C), lambda i: (0, i, 0)),
            SMEM,
            whole(2, N, C),
            whole(2, N, C),
            whole(2, N, C),
        ],
        out_specs=(pl.BlockSpec((BLOCK, C), lambda i: (i, 0)),) * 2,
        scratch_shapes=[pltpu.VMEM((2, N, C), F32)],
        compiler_params=pltpu.CompilerParams(vmem_limit_bytes=8 * MIB),
    )(mixed, starts, poles, residues, first)


def history_of(mixed, starts, poles, first, *after):
    return pl.pallas_call(
        history_kernel,
        name="state_history",
        cost_estimate=taking(8),
        grid=(BLOCKS,),
        out_shape=(pltpu.HBM((T, 8, C), F32),) * 4 + (struct(8, 128),),
        in_specs=[
            pl.BlockSpec((3, BLOCK, C), lambda i: (0, i, 0)),
            SMEM,
            whole(2, N, C),
            whole(2, N, C),
        ]
        + [ANY] * len(after),
        out_specs=(pl.BlockSpec((BLOCK, 8, C), lambda i: (i, 0, 0)),) * 4 + (whole(8, 128),),
        scratch_shapes=[pltpu.VMEM((2, N, C), F32)],
        compiler_params=pltpu.CompilerParams(vmem_limit_bytes=11 * MIB),
    )(in_hbm(mixed), starts, poles, first, *after)


def adjoint_kernel(grad_gated, query, column, starts, poles, residues, out, grads):
    grads[...] = grad_gated[...] * query[0]
    pre, pim, qre, qim = poles[0], poles[1], residues[0], residues[1]

    def run(group, kept, masked):
        source = grads[eight(group), :]
        re, im = kept
        for r in reversed(range(8)):
            row = source[r : r + 1]
            re, im = row * qre + (pre * re + pim * im), (pre * im - pim * re) - row * qim
            if masked:
                keep = keep_at(starts, group * 8 + r)
                re, im = re * keep, im * keep
        return re, im

    zero = jnp.zeros((N, C), F32)
    out[0:N], out[N : 2 * N] = scan_groups(T // 8, starts, 0, run, (zero, zero), True)
    out[2 * N :] = jnp.broadcast_to(keeps_of(column)[2], (8, C))


def adjoint_end(grad_gated, mixed, column, starts, poles, residues):
    return pl.pallas_call(
        adjoint_kernel,
        name="adjoint_end",
        cost_estimate=taking(4),
        grid=(1,),
        out_shape=struct(2 * N + 8, C),
        in_specs=[
            whole(T, C),
            pl.BlockSpec((1, T, C), lambda i: (0, 0, 0)),
            whole(T, 1),
            SMEM,
            whole(2, N, C),
            whole(2, N, C),
        ],
        out_specs=whole(2 * N + 8, C),
        scratch_shapes=[pltpu.VMEM((T, C), F32)],
        compiler_params=pltpu.CompilerParams(vmem_limit_bytes=9 * MIB),
    )(grad_gated, mixed, column, starts, poles, residues)


def back_kernel(
    grad_gated,
    mixed,
    signal,
    proj,
    proj_rim,
    h0,
    h1,
    h2,
    h3,
    taps,
    column,
    starts,
    poles,
    residues,
    first,
    *rest,
):
    grad_proj, rim, sums, state, driven_grad, mixed_grad, rows_before = rest[-7:]
    step = pl.program_id(0)
    block = BLOCKS - 1 - step

    @pl.when(step == 0)
    def _():
        state[...] = first[...]
        sums[...] = jnp.zeros(sums.shape, F32)

    base = block * BLOCK
    for part in range(PARTS):
        columns = slice(C // PARTS * part, C // PARTS * (part + 1))
        pre, pim = poles[0, :, columns], poles[1, :, columns]
        qre, qim = residues[0, :, columns], residues[1, :, columns]

        def run(group, kept, masked):
            rows = pl.ds(pl.multiple_of(base + group * 8, 8), 8)
            source = grad_gated[rows, columns] * mixed[0, rows, columns]
            re, im, pole_re, pole_im, res_re, res_im = kept
            seen = [None] * 8
            for r in reversed(range(8)):
                row = source[r : r + 1]
                token = group * 8 + r
                sre = jnp.concatenate([h0[token, :, columns], h1[token, :, columns]])
                sim = jnp.concatenate([h2[token, :, columns], h3[token, :, columns]])
                pole_re += re * sre + im * sim
                pole_im += im * sre - re * sim
                res_re += row * sre
                res_im -= row * sim
                re, im = row * qre + (pre * re + pim * im), (pre * im - pim * re) - row * qim
                seen[r] = re[:8] + re[8:]
                if masked:
                    keep = keep_at(starts, base + group * 8 + r)
                    re, im = re * keep, im * keep
            driven_grad[rows, columns] = row_sums(seen)
            return re, im, pole_re, pole_im, res_re, res_im

        zero = jnp.zeros((N, C // PARTS), F32)
        kept = (state[0, :, columns], state[1, :, columns], zero, zero, zero, zero)
        kept = scan_groups(BLOCK // 8, starts, base, run, kept, True)
        state[0, :, columns], state[1, :, columns] = kept[:2]
        for n in range(4):
            sums[N * n : N * n + N, columns] += kept[2 + n]

    @pl.when(step == BLOCKS - 1)
    def _():
        one, two, _ = keeps_of(column)
        mixed_grad[0, 0:T] = grad_gated[...] * signal[...]
        mixed_grad[1, 0:T] = driven_grad[...] * mixed[2]
        mixed_grad[2, 0:T] = driven_grad[...] * mixed[1]
        for k in range(3):
            with_rim(proj, proj_rim, k, rows_before)
            here = mixed_grad[k, 0:T]
            sums[64 + 3 * k : 65 + 3 * k] = jnp.sum(here * proj[k], axis=0, keepdims=True)
            grad_proj[k] = taps[k, 0:1] * here
            here = one * mixed_grad[k, 0:T]
            sums[65 + 3 * k : 66 + 3 * k] = jnp.sum(here * rows_before[7 : 7 + T], axis=0, keepdims=True)
            mixed_grad[k, 0:T] = two * mixed_grad[k, 0:T]
            here = taps[k, 1:2] * here
            grad_proj[k, 0 : T - 1] += here[1:T]
            rim[k] = jnp.zeros((8, C), F32)
            rim[k, 1:2] = here[0:1]
            here = mixed_grad[k, 0:T]
            sums[66 + 3 * k : 67 + 3 * k] = jnp.sum(here * rows_before[6 : 6 + T], axis=0, keepdims=True)
            here = taps[k, 2:3] * here
            grad_proj[k, 0 : T - 2] += here[2:T]
            rim[k, 0:2] += here[0:2]


def back(grad_gated, mixed, signal, proj, proj_rim, history, taps, column, starts, poles, residues, first, *after):
    return pl.pallas_call(
        back_kernel,
        name="adjoint_and_short_back",
        cost_estimate=taking(13),
        grid=(BLOCKS,),
        out_shape=(struct(3, T, C), struct(3, 8, C), struct(80, C)),
        in_specs=[
            whole(T, C),
            whole(3, T, C),
            whole(T, C),
            whole(3, T, C),
            whole(3, 8, C),
        ]
        + [pl.BlockSpec((BLOCK, 8, C), lambda i: (BLOCKS - 1 - i, 0, 0))] * 4
        + [
            whole(3, 3, C),
            whole(T, 1),
            SMEM,
            whole(2, N, C),
            whole(2, N, C),
            whole(2, N, C),
        ]
        + [ANY] * len(after),
        out_specs=(whole(3, T, C), whole(3, 8, C), whole(80, C)),
        scratch_shapes=[
            pltpu.VMEM((2, N, C), F32),
            pltpu.VMEM((T, C), F32),
            pltpu.VMEM((3, T, C), F32),
            pltpu.VMEM((T + 8, C), F32),
        ],
        compiler_params=pltpu.CompilerParams(vmem_limit_bytes=25 * MIB),
    )(
        grad_gated,
        mixed,
        signal,
        proj,
        proj_rim,
        *history,
        taps,
        column,
        starts,
        poles,
        residues,
        first,
        *after,
    )


def swap(value, axis, mask):
    size = lax.axis_size(axis)
    return lax.ppermute(value, axis, [(i, i ^ mask) for i in range(size)])


def shifted(value, axis, steps):
    count = lax.axis_size(axis)
    first, last = max(0, -steps), min(count, count - steps)
    return lax.ppermute(value, axis, [(i, i + steps) for i in range(first, last)])


def pair_add_kernel(left, got_left, right, got_right, *rest):
    left_own, left_next, right_own, right_next = rest[-4:]
    left_own[...] = left[:ROWS] + got_left[:ROWS]
    left_next[...] = left[ROWS:] + got_left[ROWS:]
    right_own[...] = right[:ROWS] + got_right[:ROWS]
    right_next[...] = right[ROWS:] + got_right[ROWS:]


def pair_call(name, kernel, shapes, operands, after):
    return pl.pallas_call(
        kernel,
        name=name,
        cost_estimate=taking(0.8),
        out_shape=shapes,
        in_specs=[VMEM] * len(operands) + [ANY] * len(after),
        out_specs=[VMEM] * len(shapes),
        compiler_params=pltpu.CompilerParams(vmem_limit_bytes=10 * MIB),
    )(*operands, *after)


def scatter_end(pieces, got_left, got_right, *after, shape=struct):
    left_own, left_next, right_own, right_next = pair_call(
        "pair_add",
        pair_add_kernel,
        [shape(ROWS, HALF)] * 4,
        (pieces[0], got_left, pieces[2], got_right),
        after,
    )
    return left_own, swap(left_next, "tp", 3), right_own, swap(right_next, "tp", 1)


def scatter_start(pieces):
    return swap(pieces[1], "tp", 1), swap(pieces[3], "tp", 3)


def in_hbm_struct(*shape):
    return pltpu.HBM(shape, F32)


def scatter_sum(pieces, *after, shape=struct):
    return scatter_end(pieces, *scatter_start(pieces), *after, shape=shape)


def pair_join_kernel(left, left_3, right, right_1, *rest):
    left_03, right_10 = rest[-2:]
    rows = left.shape[0]
    left_03[:rows], left_03[rows:] = left[...], left_3[...]
    right_10[:rows], right_10[rows:] = right_1[...], right[...]


def gather_joined(left, right, *after):
    return joined_parts(left, swap(left, "tp", 3), right, swap(right, "tp", 1), *after)


def joined_parts(left, left_3, right, right_1, *after):
    left_03, right_10 = pair_call(
        "pair_join",
        pair_join_kernel,
        [struct(2 * left.shape[0], HALF)] * 2,
        (left, left_3, right, right_1),
        after,
    )
    parts = left, swap(left_03, "tp", 1), left_3, right, right_1, swap(right_10, "tp", 3)
    return parts, (left_03, right_10)


def gather_parts(left, right, *after):
    return gather_joined(left, right, *after)[0]


def quarters_of(parts):
    left, left_12, left_3, right, right_1, right_23 = parts
    rows = left.shape[0]
    return (
        (left[:rows], right[:rows]),
        (left_12[:rows], right_1[:rows]),
        (left_12[rows:], right_23[:rows]),
        (left_3[:rows], right_23[rows:]),
    )


def of_payload(ref):
    return (ref[0:N], ref[N : 2 * N]), ref[2 * N : 2 * N + 1]


def to_payload(ref, state, is_open):
    ref[0:N], ref[N : 2 * N] = state
    ref[2 * N :] = jnp.broadcast_to(is_open, (8, C))


def power_of(powers, at, reverse):
    return powers[at], -powers[at + 1] if reverse else powers[at + 1]


def chip_kernel(reverse, place, mine, other, powers, out):
    (state, is_open), (state_other, open_other) = of_payload(mine), of_payload(other)
    by_device = power_of(powers, 0, reverse)
    last = place[1] == (0 if reverse else 1)
    earlier = where2(last, state_other, state)
    later = where2(last, state, state_other)
    later_open = jnp.where(last, is_open, open_other)
    chip = plus(later, times(scaled(by_device, later_open), earlier))
    to_payload(out, chip, is_open * open_other)


def plane_kernel(reverse, place, mine, got_1, got_2, got_3, powers, *rest):
    out, before = rest[-2:]
    chip, is_open = of_payload(mine)
    by_chip = power_of(powers, 2, reverse)
    got = {1: of_payload(got_1), 2: of_payload(got_2), 3: of_payload(got_3)}
    y = 3 - place[2] if reverse else place[2]
    one, zero = jnp.ones((N, C), F32), jnp.zeros((N, C), F32)
    entering, weight = (zero, zero), (one, zero)
    for k in (1, 2, 3):
        state, opened = got[k]
        entering = where2(y >= k, plus(entering, times(weight, state)), entering)
        weight = where2(y >= k, times(weight, scaled(by_chip, opened)), weight)
    plane = plus(chip, times(scaled(by_chip, is_open), entering))
    for j in (1, 2, 3):
        state, opened = got[4 - j]
        plane = where2(y + j <= 3, plus(state, times(scaled(by_chip, opened), plane)), plane)
        is_open = is_open * opened
    to_payload(out, plane, is_open)
    before[0], before[1] = entering
    before[2], before[3] = weight


def enter_kernel(reverse, place, before, got_1, got_2, got_3, other, powers, *rest):
    out = rest[-1]
    by_device, by_plane = power_of(powers, 0, reverse), power_of(powers, 4, reverse)
    one, zero = jnp.ones((N, C), F32), jnp.zeros((N, C), F32)
    entering, weight = (zero, zero), (one, zero)
    for ref in (got_1, got_2, got_3):
        state, opened = of_payload(ref)
        entering = plus(entering, times(weight, state))
        weight = times(weight, scaled(by_plane, opened))
    at_chip = plus((before[0], before[1]), times((before[2], before[3]), entering))
    state, opened = of_payload(other)
    at_core = plus(state, times(scaled(by_device, opened), at_chip))
    out[0], out[1] = where2(place[1] == (0 if reverse else 1), at_core, at_chip)


def small_call(name, kernel, reverse, shapes, operands, after=()):
    return pl.pallas_call(
        functools.partial(kernel, reverse),
        name=name,
        cost_estimate=taking(1.6),
        out_shape=shapes,
        in_specs=[SMEM] + [VMEM] * (len(operands) - 1) + [ANY] * len(after),
        out_specs=jax.tree.map(lambda _: VMEM, shapes),
        compiler_params=pltpu.CompilerParams(vmem_limit_bytes=8 * MIB),
    )(*operands, *after)


def carried_state(place, mine, powers, reverse, after=(), late=()):
    sign = -1 if reverse else 1
    payload = struct(2 * N + 8, C)
    other = swap(mine, "seq_2", 1)
    chip = small_call("chip_state", chip_kernel, reverse, payload, (place, mine, other, powers))
    got = [
        lax.ppermute(chip, "seq_1", [(i, (i + sign * k) % 4) for i in range(4)]) for k in (1, 2, 3)
    ]
    plane, before = small_call(
        "plane_state",
        plane_kernel,
        reverse,
        (payload, struct(4, N, C)),
        (place, chip, *got, powers),
        after,
    )
    got = [shifted(plane, "seq_0", sign * k) for k in (1, 2, 3)]
    entering = small_call(
        "entering_state",
        enter_kernel,
        reverse,
        struct(2, N, C),
        (place, before, *got, other, powers),
        late,
    )
    return entering


def sum_over(x, axis, *after):
    if lax.axis_size(axis) == 2:
        return x + swap(x, axis, 1)
    got = [swap(x, axis, k) for k in (1, 2, 3)]
    if after:
        got = [tie(g, *after) for g in got]
    return (x + got[0]) + (got[1] + got[2])


def inverse_rms(values):
    return lax.rsqrt(jnp.mean(values * values, axis=-1, keepdims=True) + epsilon)


def nothing(*refs):
    pass


def tie(x, *after, hbm=False):
    shape = struct(*x.shape, dtype=x.dtype)
    if hbm:
        x, shape = in_hbm(x), pltpu.HBM(x.shape, x.dtype)
    return pl.pallas_call(
        nothing,
        name="tie",
        out_shape=shape,
        in_specs=[ANY] * (1 + len(after)),
        out_specs=ANY,
        input_output_aliases={0: 0},
        compiler_params=pltpu.CompilerParams(vmem_limit_bytes=6 * MIB),
    )(x, *after)


WIDE = 1408


def wide_sum_kernel(left_a, l03, r10, l12, r23, left_b, more_b, right, wide, gain, out, token, both, rows_a, rows_b):
    step = pl.program_id(0)

    @pl.when(step == 0)
    def _():
        both[:T] = right[...]
        both[T:] = wide[...].astype(BF16)
        token[...] = jnp.zeros(token.shape, F32)

    def put(*quarters):
        rows_a[T:] = (jnp.concatenate(quarters) * gain[...]).astype(BF16)

    pl.when(step < 2)(lambda: put(l03[:ROWS], l12[:ROWS], l12[ROWS:], l03[ROWS:]))
    pl.when(step >= 2)(lambda: put(r10[ROWS:], r10[:ROWS], r23[:ROWS], r23[ROWS:]))
    rows_a[:T], rows_b[:T], rows_b[T:] = left_a[...], left_b[...], more_b[...]
    out[:, :WIDE] = token_sum(rows_a[...], both[:, :WIDE])
    out[:, WIDE:] = token_sum(rows_b[...], both[:, WIDE:])


def wide_token_sum(left_a, more_a, left_b, more_b, right, wide, gain):
    rows = 512
    column = pl.BlockSpec((T, rows), lambda i: (0, i))
    low = pl.BlockSpec((2 * ROWS, rows), lambda i: (0, jnp.minimum(i, 1)))
    high = pl.BlockSpec((2 * ROWS, rows), lambda i: (0, jnp.maximum(i - 2, 0)))
    width = right.shape[1]
    return pl.pallas_call(
        wide_sum_kernel,
        name="weight_gradients",
        cost_estimate=taking(10),
        grid=(D // rows,),
        out_shape=(pltpu.HBM((D, width), F32), struct(8, 128)),
        in_specs=[column, low, high, low, high, column, column]
        + [VMEM, VMEM, pl.BlockSpec((1, rows), lambda i: (0, i))],
        out_specs=(pl.BlockSpec((rows, width), lambda i: (i, 0)), whole(8, 128)),
        scratch_shapes=[
            pltpu.VMEM((2 * T, width), BF16),
            pltpu.VMEM((2 * T, rows), BF16),
            pltpu.VMEM((2 * T, rows), BF16),
        ],
        compiler_params=pltpu.CompilerParams(vmem_limit_bytes=27 * MIB),
    )(left_a, *more_a, left_b, more_b, right, wide, gain)


ORDERS = {1: (0, 3, 1, 2), 3: (0, 1, 3, 2)}
STREAMS = (("seq_1", 1), ("seq_1", 3), ("seq_0", 1), ("seq_0", 3))


def stream_places(step):
    jz, jy = divmod(step, 4)
    places = []
    for axis, mask in STREAMS:
        order = ORDERS[mask]
        first, second = (jy, jz) if axis == "seq_1" else (jz, jy)
        places.append(order.index(first) * 4 + order.index(second))
    return places


def stream_sum_kernel(
    place,
    left_a,
    more_a,
    left_b,
    more_b,
    right_a,
    wide_a,
    right_b,
    wide_b,
    sums,
    gains_a,
    gains_b,
    *rest,
):
    kept, sent, token, turned = rest[-10:-6], rest[-6:-2], rest[-2], rest[-1]
    token[...] = jnp.zeros(token.shape, F32)
    for s in range(4):
        kept[s][2048 : 2048 + 80] = sums[:, 128 * s : 128 * s + 128]
        for n in range(8):
            row = (gains_a, gains_b)[n // 4]
            at = C * (n % 4) + 128 * s
            kept[s][2128 + n : 2129 + n] = row[:, at : at + 128]
        sent[s][2048:] = kept[s][2048:]
    turned[0:768, 0:T] = right_a[...].T
    turned[768:, 0:T] = right_b[...].T
    turned[0:768, T:] = wide_a[...].astype(BF16).T
    turned[768:, T:] = wide_b[...].astype(BF16).T
    y, z = place[2], place[3]
    for step in range(16):
        jz, jy = divmod(step, 4)
        chunk = (z ^ jz) * 4 + (y ^ jy)
        columns = pl.ds(pl.multiple_of(chunk * 128, 128), 128)
        total_a = dot(turned[0:768, 0:T], left_a[:, columns]) + dot(turned[0:768, T:], more_a[:, columns])
        total_b = dot(turned[768:, 0:T], left_b[:, columns]) + dot(turned[768:, T:], more_b[:, columns])
        for s, at in enumerate(stream_places(step)):
            target = kept[s] if at < 8 else sent[s]
            rows = slice((at % 8) * 256, (at % 8) * 256 + 256)
            target[rows] = total_a[256 * s : 256 * s + 256] if s < 3 else total_b


def stream_token_sum(place, *operands):
    out = pl.pallas_call(
        stream_sum_kernel,
        name="mixer_weight_gradients",
        cost_estimate=taking(7),
        out_shape=(struct(2048 + SMALL, 128),) * 8 + (struct(8, 128),),
        in_specs=[SMEM] + [VMEM] * 11 + [ANY] * (len(operands) - 11),
        out_specs=(VMEM,) * 9,
        scratch_shapes=[pltpu.VMEM((1024, 2 * T), BF16)],
        compiler_params=pltpu.CompilerParams(vmem_limit_bytes=8 * MIB),
    )(place, *operands)
    return out[:4], out[4:8], out[8]


SMALL = 88


def stream_add_kernel(*refs):
    held, got, kept, sent = refs[0:4], refs[4:8], refs[-8:-4], refs[-4:]
    for s in range(4):
        rows = held[s].shape[0] - SMALL
        low = rows // 2
        small = held[s][rows:] + got[s][rows:]
        kept[s][0:low] = held[s][0:low] + got[s][0:low]
        kept[s][low:] = small
        sent[s][0:low] = held[s][low:rows] + got[s][low:rows]
        sent[s][low:] = small


def stream_add(held, got, *after):
    rows = held[0].shape[0] - SMALL
    shape = struct(rows // 2 + SMALL, 128)
    out = pl.pallas_call(
        stream_add_kernel,
        name="stream_add",
        cost_estimate=taking(0.7 + rows / 1000),
        out_shape=[shape] * 8,
        in_specs=[VMEM] * 8 + [ANY] * len(after),
        out_specs=[VMEM] * 8,
        compiler_params=pltpu.CompilerParams(vmem_limit_bytes=6 * MIB),
    )(*held, *got, *after)
    return out[:4], out[4:]


def stream_last_kernel(place, *refs):
    held, got, (own, send, small, gains) = refs[0:4], refs[4:8], refs[-4:]
    first = place[1] == 0
    for s in range(4):
        total = (held[s][0:256] + got[s][0:256]).T
        columns = slice(256 * s, 256 * s + 256)
        own[:, columns] = jnp.where(first, total[:64], total[64:])
        send[:, columns] = jnp.where(first, total[64:], total[:64])
        total = held[s][256:] + got[s][256:]
        small[:, 128 * s : 128 * s + 128] = total[:80]
        gains[:, 128 * s : 128 * s + 128] = total[80:]


def stream_last(place, held, got, *after):
    return pl.pallas_call(
        stream_last_kernel,
        name="stream_last",
        cost_estimate=taking(1.5),
        out_shape=(struct(64, 1024), struct(64, 1024), struct(80, C), struct(8, C)),
        in_specs=[SMEM] + [VMEM] * 8 + [ANY] * len(after),
        out_specs=[VMEM] * 4,
        compiler_params=pltpu.CompilerParams(vmem_limit_bytes=6 * MIB),
    )(place, *held, *got, *after)


def stream_masks(axis, mask):
    other = "seq_0" if axis == "seq_1" else "seq_1"
    return ((axis, mask), (axis, 4 - mask), (other, mask), (other, 4 - mask))


def stream_swap(sent, step):
    return [swap(x, *stream_masks(*STREAMS[s])[step]) for s, x in enumerate(sent)]


def mixer_shares_kernel(place, own, got, small, small_got, *rest):
    grad_in, grad_out, small_sum = rest[-3:]
    first = place[1] == 0
    low = jnp.where(first, own[...], got[...])
    high = jnp.where(first, got[...], own[...])
    for k in range(3):
        columns = slice(256 * k, 256 * k + 256)
        grad_in[k, :, :256], grad_in[k, :, 256:] = low[:, columns], high[:, columns]
    grad_out[:, :256], grad_out[:, 256:] = low[:, 768:], high[:, 768:]
    small_sum[...] = small[...] + small_got[...]


def mixer_shares(place, own, got, small, small_got, *after):
    return pl.pallas_call(
        mixer_shares_kernel,
        name="mixer_shares",
        cost_estimate=taking(1.5),
        out_shape=(struct(3, 64, C), struct(64, C), struct(80, C)),
        in_specs=[SMEM] + [VMEM] * 4 + [ANY] * len(after),
        out_specs=[VMEM] * 3,
        compiler_params=pltpu.CompilerParams(vmem_limit_bytes=6 * MIB),
    )(place, own, got, small, small_got, *after)


def ffn_send_kernel(place, share, *rest):
    own, send = rest[-2:]
    first = place[1] == 0
    low, high = share[:64], share[64:]
    own[...] = jnp.where(first, low, high)
    send[...] = jnp.where(first, high, low)


def ffn_shares_kernel(place, own, got, *rest):
    gate, up, down, token = rest[-4:]
    first = place[1] == 0
    low = jnp.where(first, own[...], got[...])
    high = jnp.where(first, got[...], own[...])
    gate[:, :768], gate[:, 768:] = low[:, :768], high[:, 768:1408]
    up[:, :640], up[:, 640:] = low[:, 768:1408], high[:, :768]
    down[:, :768], down[:, 768:] = low[:, 1408:], high[:, 1408 + 128 :]
    token[...] = jnp.zeros(token.shape, F32)


def ffn_halves(place, share, *after):
    return pl.pallas_call(
        ffn_send_kernel,
        name="ffn_send",
        cost_estimate=taking(1),
        out_shape=(struct(64, 2176),) * 2,
        in_specs=[SMEM, VMEM] + [ANY] * len(after),
        out_specs=[VMEM] * 2,
        compiler_params=pltpu.CompilerParams(vmem_limit_bytes=6 * MIB),
    )(place, share, *after)


def ffn_shares(place, own, got, *after):
    return pl.pallas_call(
        ffn_shares_kernel,
        name="ffn_shares",
        cost_estimate=taking(2),
        out_shape=(struct(64, 1408),) * 3 + (struct(8, 128),),
        in_specs=[SMEM, VMEM, VMEM] + [ANY] * len(after),
        out_specs=[VMEM] * 4,
        compiler_params=pltpu.CompilerParams(vmem_limit_bytes=8 * MIB),
    )(place, own, got, *after)


def norm_kernel(values, gain, *rest):
    out, inverse = rest[-2:]
    v = values[...]
    inverse[...] = inverse_rms(v)
    out[...] = (v * inverse[...] * gain[...]).astype(BF16)


def normed(values, gain, *after):
    rows = 128
    row = pl.BlockSpec((rows, D), lambda i: (i, 0))
    return pl.pallas_call(
        norm_kernel,
        name="normed_in",
        cost_estimate=taking(1.8),
        grid=(values.shape[0] // rows,),
        out_shape=(struct(*values.shape, dtype=BF16), struct(values.shape[0], 1)),
        in_specs=[row, whole(1, D)] + [ANY] * len(after),
        out_specs=(row, pl.BlockSpec((rows, 1), lambda i: (i, 0))),
        compiler_params=pltpu.CompilerParams(vmem_limit_bytes=11 * MIB),
    )(values, gain, *after)


HALF = D // 2


def rows_by_quarter(place, ref):
    return jnp.concatenate([ref[quarter_rows(place[0] ^ q), :] for q in range(4)])


def cotangent_kernel(place, cotangent, w_down, *rest):
    low, grad_hidden = rest[-2:]

    @pl.when(pl.program_id(0) == 0)
    def _():
        for q in range(4):
            low[ROWS * q : ROWS * q + ROWS] = cotangent[quarter_rows(place[0] ^ q), :].astype(BF16)

    grad_hidden[...] = dot_t(low[...], w_down[...])


def cotangent_part(place, cotangent, w_down, *after):
    wide = w_down.shape[0]
    return pl.pallas_call(
        cotangent_kernel,
        name="cotangent_part",
        cost_estimate=taking(4),
        grid=(6,),
        out_shape=(struct(T, D, dtype=BF16), struct(T, wide)),
        in_specs=[SMEM, VMEM, pl.BlockSpec((256, D), lambda i: (i, 0))] + [ANY] * len(after),
        out_specs=(VMEM, pl.BlockSpec((T, 256), lambda i: (0, i))),
        compiler_params=pltpu.CompilerParams(vmem_limit_bytes=9 * MIB),
    )(place, cotangent, w_down, *after)


def out_parts_kernel(place, gated, *rest):
    own, send = rest[-2:]
    first = place[1] == 0
    rows = rows_by_quarter(place, gated).astype(F32)
    low, high = rows[:, :256], rows[:, 256:]
    own[...] = jnp.where(first, low, high).astype(BF16)
    send[...] = jnp.where(first, high, low)


def out_parts(place, gated, *after):
    return pl.pallas_call(
        out_parts_kernel,
        name="out_parts",
        cost_estimate=taking(1),
        out_shape=(struct(T, 256, dtype=BF16), struct(T, 256)),
        in_specs=[SMEM, VMEM] + [ANY] * len(after),
        out_specs=[VMEM] * 2,
        compiler_params=pltpu.CompilerParams(vmem_limit_bytes=7 * MIB),
    )(place, gated, *after)


def owner_kernel(place, rows, *rest):
    rest[-1][...] = rows[...].astype(BF16)


def owner_rows(place, x, *after):
    row = pl.BlockSpec((ROWS, D), lambda i, place: (place[0] ^ i, 0))
    out = pl.BlockSpec((ROWS, D), lambda i, place: (i, 0))
    return pl.pallas_call(
        owner_kernel,
        name="owner_rows",
        cost_estimate=taking(2),
        out_shape=pltpu.HBM((T, D), BF16),
        grid_spec=pltpu.PrefetchScalarGridSpec(
            num_scalar_prefetch=1, grid=(4,), in_specs=[row] + [ANY] * len(after), out_specs=out
        ),
        compiler_params=pltpu.CompilerParams(vmem_limit_bytes=9 * MIB),
    )(place, in_hbm(x), *after)


def branch_other_kernel(place, cotangent, through, out):
    out[...] = (cotangent[...] + through[...]).astype(BF16)


def branch_other_of(place, cotangent, through):
    row = pl.BlockSpec((ROWS, D), lambda i, place: (i, 0))
    return pl.pallas_call(
        branch_other_kernel,
        name="branch_other",
        cost_estimate=taking(2),
        out_shape=struct(T, D, dtype=BF16),
        grid_spec=pltpu.PrefetchScalarGridSpec(
            num_scalar_prefetch=1,
            grid=(4,),
            in_specs=[pl.BlockSpec((ROWS, D), lambda i, place: (place[0] ^ i, 0)), row],
            out_specs=row,
        ),
        compiler_params=pltpu.CompilerParams(vmem_limit_bytes=9 * MIB),
    )(place, in_hbm(cotangent), through)


def middle_kernel(place, left, left_more, right, right_more, hidden, *rest):
    middle, out_left, out_right = rest[-3:]
    low = hidden[:, :HALF] + (left[...] + left_more[...])
    high = hidden[:, HALF:] + (right[...] + right_more[...])
    square = jnp.sum(low * low, axis=-1, keepdims=True) + jnp.sum(high * high, axis=-1, keepdims=True)
    inverse = lax.rsqrt(square * (1.0 / D) + epsilon)
    middle[:, :HALF], middle[:, HALF:] = low, high
    out_left[...], out_right[...] = low * inverse, high * inverse


def norm_back_parts(left, left_more, right, right_more, values, gain):
    grads = (left[...] + left_more[...], right[...] + right_more[...])
    v = (values[:, :HALF], values[:, HALF:])
    g = (gain[:, :HALF], gain[:, HALF:])
    square = sum(jnp.sum(x * x, axis=-1, keepdims=True) for x in v)
    inverse = lax.rsqrt(square * (1.0 / D) + epsilon)
    along = sum(jnp.sum(a * b * c, axis=-1, keepdims=True) for a, b, c in zip(g, grads, v))
    along = inverse * inverse * inverse * (along * (1.0 / D))
    back = [inverse * g[n] * grads[n] - v[n] * along for n in (0, 1)]
    return back, [grads[n] * (v[n] * inverse) for n in (0, 1)]


def norm_back_kernel(left, left_more, right, right_more, values, gain, *rest):
    out_left, out_right, gains = rest[-3:]
    back, weighed = norm_back_parts(left, left_more, right, right_more, values, gain)
    out_left[...], out_right[...] = back
    for n in (0, 1):
        gains[:, HALF * n : HALF * n + HALF] = jnp.sum(weighed[n], axis=0, keepdims=True)


def by_owner_grid(in_specs, out_specs):
    return pltpu.PrefetchScalarGridSpec(
        num_scalar_prefetch=1, grid=(1,), in_specs=in_specs, out_specs=out_specs
    )


MINE = pl.BlockSpec((ROWS, D), lambda i, place: (place[0], 0))


def after_middle(place, pieces, hidden, *after):
    return pl.pallas_call(
        middle_kernel,
        name="middle_and_norm",
        cost_estimate=taking(1.5),
        out_shape=(pltpu.HBM((ROWS, D), F32), struct(ROWS, HALF), struct(ROWS, HALF)),
        grid_spec=by_owner_grid([VMEM] * 4 + [MINE] + [ANY] * len(after), (VMEM,) * 3),
        compiler_params=pltpu.CompilerParams(vmem_limit_bytes=8 * MIB),
    )(place, *pieces, in_hbm(hidden), *after)


def norm_back(pieces, values, gain, *after):
    return pl.pallas_call(
        norm_back_kernel,
        name="norm_back",
        cost_estimate=taking(2),
        out_shape=(struct(ROWS, HALF), struct(ROWS, HALF), struct(1, D)),
        grid=(1,),
        in_specs=[whole(ROWS, HALF)] * 4 + [whole(ROWS, D), whole(1, D)] + [ANY] * len(after),
        out_specs=(VMEM,) * 3,
        compiler_params=pltpu.CompilerParams(vmem_limit_bytes=9 * MIB),
    )(*pieces, values, gain, *after)


def rim_kernel(starts, rows, *rest):
    out = rest[-1]
    at = lax.broadcasted_iota(jnp.int32, (8, D), 0)
    out[...] = jnp.where(at == 6, rows[...] * keep_at(starts, T - 1), rows[...])


def rim_rows_of(starts, hidden, *after):
    return pl.pallas_call(
        rim_kernel,
        name="rim_rows",
        cost_estimate=taking(1),
        grid=(1,),
        out_shape=struct(8, D),
        in_specs=[SMEM, pl.BlockSpec((8, D), lambda i: (T // 8 - 1, 0))] + [ANY] * len(after),
        out_specs=whole(8, D),
        compiler_params=pltpu.CompilerParams(vmem_limit_bytes=6 * MIB),
    )(starts, in_hbm(hidden), *after)


PIECES = ((0, 3), (1, 2), (0, 1), (3, 2))
PIECE_SHAPES = (struct(2 * ROWS, HALF),) * 4


def put_pieces(place, block, total, outs, by_owner=False):
    which, columns = block // 2, slice(512 * (block % 2), 512 * (block % 2) + 512)
    for n in (0, 1):
        out, quarters = outs[2 * which + n], PIECES[2 * which + n]
        for m, q in enumerate(quarters):
            rows = slice(ROWS * q, ROWS * q + ROWS) if by_owner else quarter_rows(place[0] ^ q)
            out[ROWS * m : ROWS * m + ROWS, columns] = total[rows, :]


def split_kernel(compute, by_owner, count, place, *refs):
    *outs, total = refs[-5:]
    for block in range(4):
        total[...] = compute(slice(512 * block, 512 * block + 512), *refs[:count])
        put_pieces(place, block, total, outs, by_owner)


def split_dot(name, compute, by_owner, place, *operands, after=()):
    return pl.pallas_call(
        functools.partial(split_kernel, compute, by_owner, len(operands)),
        name=name,
        cost_estimate=taking(2.5),
        out_shape=PIECE_SHAPES,
        in_specs=[SMEM] + [VMEM] * len(operands) + [ANY] * len(after),
        out_specs=[VMEM] * 4,
        scratch_shapes=[pltpu.VMEM((T, 512), F32)],
        compiler_params=pltpu.CompilerParams(vmem_limit_bytes=8 * MIB),
    )(place, *operands, *after)


def result_kernel(place, hidden, w_down, middle, *rest):
    out, token = rest[-2:]
    token[...] = jnp.zeros(token.shape, F32)
    for block in range(4):
        columns = slice(512 * block, 512 * block + 512)
        total = dot(hidden[...], w_down[:, columns])
        for q in range(4):
            rows = total[ROWS * q : ROWS * q + ROWS]
            out[quarter_rows(place[0] ^ q), columns] = rows + middle[:, columns] if q == 0 else rows


def result_part(place, hidden, w_down, middle, *after):
    return pl.pallas_call(
        result_kernel,
        name="result_part",
        cost_estimate=taking(2.5),
        out_shape=(pltpu.HBM((T, D), F32), struct(8, 128)),
        in_specs=[SMEM] + [VMEM] * 3 + [ANY] * len(after),
        out_specs=(VMEM, VMEM),
        compiler_params=pltpu.CompilerParams(vmem_limit_bytes=10 * MIB),
    )(place, hidden, w_down, middle, *after)


def ffn_kernel(place, *refs):
    parts, refs = refs[:6], refs[6:]
    gain, w_gate, w_up, grad_hidden = refs[:4]
    mid_x, hidden, grad_gate, grad_up, own_all, send_all = refs[-6:]
    for q, (left, right) in enumerate(quarters_of(parts)):
        rows = slice(ROWS * q, ROWS * q + ROWS)
        mid_x[rows, :HALF] = (left * gain[:, :HALF]).astype(BF16)
        mid_x[rows, HALF:] = (right * gain[:, HALF:]).astype(BF16)
    wide = w_gate.shape[1]
    for start in range(0, wide, 256):
        columns = slice(start, min(start + 256, wide))
        gate = dot(mid_x[...], w_gate[:, columns])
        up = dot(mid_x[...], w_up[:, columns])
        sig = 1.0 / (1.0 + jnp.exp(-gate))
        silu = gate * sig
        incoming = grad_hidden[:, columns]
        hidden[:, columns] = (silu * up).astype(BF16)
        grad_gate[:, columns] = (incoming * up * sig * (1.0 + gate * (1.0 - sig))).astype(BF16)
        grad_up[:, columns] = (incoming * silu).astype(BF16)
    first = place[1] == 0

    def halves(columns, low, high):
        a, b = low.astype(F32), high.astype(F32)
        own_all[:, columns] = jnp.where(first, a, b).astype(BF16)
        send_all[:, columns] = jnp.where(first, b, a)

    halves(slice(0, 768), grad_gate[:, :768], grad_up[:, 640:1408])
    halves(slice(768, 1408), grad_up[:, :640], grad_gate[:, 768:1408])
    halves(slice(1408, 2176), hidden[:, :768], hidden[:, 640:1408])


def feed_forward(place, parts, gain, w_gate, w_up, grad_hidden, *after):
    wide = w_gate.shape[1]
    low = struct(T, wide, dtype=BF16)
    return pl.pallas_call(
        ffn_kernel,
        name="feed_forward",
        cost_estimate=taking(7),
        out_shape=(
            struct(T, D, dtype=BF16),
            low,
            low,
            low,
            struct(T, wide + 768, dtype=BF16),
            struct(T, wide + 768),
        ),
        in_specs=[SMEM] + [VMEM] * 10 + [ANY] * len(after),
        out_specs=(VMEM,) * 6,
        compiler_params=pltpu.CompilerParams(vmem_limit_bytes=10 * MIB),
    )(place, *parts, gain, w_gate, w_up, grad_hidden, *after)


def branch_back_kernel(place, *refs):
    parts, cotangent, w_out = refs[:6], *refs[6:8]
    through, branch, grad_gated = refs[-3:]
    for q, (left, right) in enumerate(quarters_of(parts)):
        rows = slice(ROWS * q, ROWS * q + ROWS)
        through[rows, :HALF], through[rows, HALF:] = left, right
    branch[...] = (rows_by_quarter(place, cotangent) + through[...]).astype(BF16)
    back = dot_t(branch[...], w_out[...])
    for q in range(4):
        grad_gated[quarter_rows(place[0] ^ q), :] = back[ROWS * q : ROWS * q + ROWS]


def branch_back(place, parts, cotangent, w_out, *after):
    return pl.pallas_call(
        branch_back_kernel,
        name="branch_back",
        cost_estimate=taking(3),
        out_shape=(struct(T, D), pltpu.HBM((T, D), BF16), struct(T, C)),
        in_specs=[SMEM] + [VMEM] * 8 + [ANY] * len(after),
        out_specs=(VMEM,) * 3,
        compiler_params=pltpu.CompilerParams(vmem_limit_bytes=8 * MIB),
    )(place, *parts, cotangent, w_out, *after)


def finish_kernel(place, starts, grads, rim, *rest):
    low, own, send = rest[-3:]
    first = place[1] == 0
    at = lax.broadcasted_iota(jnp.int32, (8, C), 0)
    for k in range(3):
        turned = jnp.concatenate([jnp.zeros((6, C), F32), rim[k, 0:2]])
        turned = jnp.where(at == 6, turned * keep_at(starts, T - 1), turned)
        low[k, : T - 16] = grads[k, : T - 16].astype(BF16)
        low[k, T - 16 :] = jnp.concatenate(
            [grads[k, T - 16 : T - 8], grads[k, T - 8 :] + turned]
        ).astype(BF16)
        a, b = low[k, :, :256].astype(F32), low[k, :, 256:].astype(F32)
        columns = slice(256 * k, 256 * k + 256)
        own[:, columns] = jnp.where(first, a, b).astype(BF16)
        send[:, columns] = jnp.where(first, b, a)


def finish_projected(place, starts, grads, rim, *after):
    return pl.pallas_call(
        finish_kernel,
        name="finish_projected",
        cost_estimate=taking(1.5),
        out_shape=(struct(3, T, C, dtype=BF16), struct(T, 768, dtype=BF16), struct(T, 768)),
        in_specs=[SMEM, SMEM, VMEM, VMEM] + [ANY] * len(after),
        out_specs=(VMEM,) * 3,
        compiler_params=pltpu.CompilerParams(vmem_limit_bytes=7 * MIB),
    )(place, starts, grads, rim, *after)


def first_kernel(place, grads, hidden, inverse, gain, w_in, cotangent, left, right, *rest):
    out, gains, total = rest[-3:]
    along = jnp.zeros((T, 1), F32)
    for block in range(4):
        columns = slice(512 * block, 512 * block + 512)
        part = sum(dot_t(grads[k], w_in[k, columns, :]) for k in range(3))
        weighed = part * (hidden[:, columns] * inverse[...])
        gains[:, columns] = jnp.sum(weighed, axis=0, keepdims=True)
        along += jnp.sum(weighed * gain[:, columns], axis=1, keepdims=True)
        total[:, columns] = part
    along = inverse[...] * inverse[...] * (along * (1.0 / D))
    mine = quarter_rows(place[0])
    for block in range(4):
        columns = slice(512 * block, 512 * block + 512)
        out[:, columns] = inverse[...] * (gain[:, columns] * total[:, columns]) - hidden[:, columns] * along
        side, own = (left, right)[block // 2], slice(512 * (block % 2), 512 * (block % 2) + 512)
        out[mine, columns] += cotangent[mine, columns] + side[:, own]


def first_back(place, grads, hidden, inverse, gain, w_in, cotangent, left, right, *after):
    return pl.pallas_call(
        first_kernel,
        name="first_back",
        cost_estimate=taking(4),
        out_shape=(pltpu.HBM((T, D), F32), struct(1, D)),
        in_specs=[SMEM] + [VMEM] * 8 + [ANY] * len(after),
        out_specs=[VMEM] * 2,
        scratch_shapes=[pltpu.VMEM((T, D), F32)],
        compiler_params=pltpu.CompilerParams(vmem_limit_bytes=14 * MIB),
    )(place, grads, hidden, inverse, gain, w_in, cotangent, left, right, *after)


def emit_kernel(first, second, *rest):
    first_out, second_out, token = rest[-3:]
    token[...] = jnp.zeros(token.shape, F32)
    first_out[...], second_out[...] = first[...], second[...]


def emit(first, second, *after):
    row = pl.BlockSpec((ROWS, D), lambda i: (i, 0))
    return pl.pallas_call(
        emit_kernel,
        name="emit",
        cost_estimate=taking(3),
        grid=(4,),
        out_shape=(struct(T, D), struct(T, D), struct(8, 128)),
        in_specs=[row, row] + [ANY] * len(after),
        out_specs=(row, row, whole(8, 128)),
        compiler_params=pltpu.CompilerParams(vmem_limit_bytes=9 * MIB),
    )(in_hbm(first), in_hbm(second), *after)


def per_device(
    hidden_in,
    cotangent,
    starts,
    norm_in,
    w_in,
    short_w,
    pole_pairs,
    residues,
    w_out,
    norm_mid,
    w_gate,
    w_up,
    w_down,
):
    place = jnp.stack(
        [lax.axis_index(axis) for axis in ("tp", "seq_2", "seq_1", "seq_0")]
    ).astype(jnp.int32)
    column = starts[:, None]
    gain_in, gain_mid = norm_in[None], norm_mid[None]

    def other_core(x):
        return swap(x, "seq_2", 1)

    rim_rows = rim_rows_of(starts, hidden_in, place, column)
    rim_rows = lax.ppermute(rim_rows, SEQ, [(i, i + 1) for i in range(31)])
    hidden_other = other_core(hidden_in)
    cotangent_other = other_core(cotangent)
    normed_in, inverse_in = normed(hidden_in, gain_in)
    proj, rim, mixed, end, powers = project_and_mix(
        normed_in, rim_rows, gain_in, w_in, short_w, column, starts, pole_pairs
    )

    entering = carried_state(place, end, powers, False)
    signal, gated = signal_of(mixed, starts, pole_pairs, residues, entering)

    branch = split_dot(
        "branch",
        lambda columns, a, b: dot(a[...], b[:, columns]),
        False,
        place,
        gated,
        w_out,
    )
    *history, history_token = history_of(mixed, starts, pole_pairs, entering, branch[1])
    out_right, out_send = out_parts(place, gated, branch[1])
    pieces = scatter_sum(branch, history_token, out_send)
    down_grad, grad_hidden = cotangent_part(place, cotangent, w_down, pieces[0])
    middle, mid_left, mid_right = after_middle(place, pieces, hidden_in, grad_hidden)

    normed_other, _ = normed(hidden_other, gain_in, mid_left)
    down_other = owner_rows(place, cotangent_other, mid_left)
    parts, joined = gather_joined(mid_left, mid_right, in_hbm(normed_other), in_hbm(down_other))
    mid_other = [other_core(x) for x in joined]
    mid_x, hidden, grad_gate, grad_up, own_all, send_all = feed_forward(
        place,
        parts,
        gain_mid,
        w_gate,
        w_up,
        grad_hidden,
        *mid_other,
    )
    mid_other += [other_core(parts[1]), other_core(parts[5])]
    mid_terms = split_dot(
        "mid_terms",
        lambda columns, a, b, c, d: dot_t(a[...], c[columns, :]) + dot_t(b[...], d[columns, :]),
        True,
        place,
        grad_gate,
        grad_up,
        w_gate,
        w_up,
        after=mid_other[2:],
    )

    ffn_sum, ffn_token = wide_token_sum(
        mid_x,
        mid_other,
        down_grad,
        down_other,
        own_all,
        other_core(tie(send_all, mid_terms[1])),
        gain_mid,
    )

    pieces = scatter_sum(mid_terms, ffn_token, shape=in_hbm_struct)
    share_ffn = lax.psum_scatter(
        tie(ffn_sum, pieces[0], hbm=True), ("seq_0", "seq_1"), scatter_dimension=0, tiled=True
    )
    left, left_more, right, right_more = pieces
    through_left, through_right, gains_mid = norm_back(
        (in_hbm(left), left_more, in_hbm(right), right_more), in_hbm(middle), gain_mid
    )
    result, part_token = result_part(place, hidden, w_down, middle, gains_mid)
    through_f, branch_grad, grad_gated = branch_back(
        place, gather_parts(through_left, through_right), cotangent, w_out, part_token
    )

    leaving = adjoint_end(grad_gated, mixed, column, starts, pole_pairs, residues)
    branch_other = branch_other_of(place, cotangent_other, other_core(through_f))
    returning = carried_state(place, leaving, powers, True, after=(in_hbm(branch_other),))
    grad_proj, rim_grad, sums = back(
        grad_gated,
        mixed,
        signal,
        proj,
        rim,
        history,
        short_w,
        column,
        starts,
        pole_pairs,
        residues,
        returning,
    )
    rim_back = lax.ppermute(rim_grad, SEQ, [(i + 1, i) for i in range(31)])

    projected_low, proj_own, proj_send = finish_projected(
        place, starts, grad_proj, rim_back
    )
    proj_wide = other_core(proj_send)
    grad_input, gains_in = first_back(
        place,
        projected_low,
        hidden_in,
        inverse_in,
        gain_in,
        w_in,
        cotangent,
        through_left,
        through_right,
    )
    result, grad_input = lax.psum((result, grad_input), "tp")
    kept, leaving_now, mixer_token = stream_token_sum(
        place,
        normed_in,
        normed_other,
        branch_grad,
        branch_other,
        proj_own,
        proj_wide,
        out_right,
        other_core(out_send),
        sums,
        gains_in,
        gains_mid,
    )
    got = stream_swap(leaving_now, 0)
    kept, leaving_now = stream_add(kept, got)
    got = stream_swap(leaving_now, 1)
    ffn_own, ffn_out = ffn_halves(place, share_ffn, kept[0])
    kept, leaving_now = stream_add(kept, got, ffn_own)
    got = stream_swap(leaving_now, 2)
    share_gate, share_up, share_down, shares_token = ffn_shares(
        place, ffn_own, other_core(ffn_out), kept[0]
    )
    kept, leaving_now = stream_add(kept, got, shares_token)
    got = stream_swap(leaving_now, 3)
    result, grad_input, output_token = emit(result, grad_input, kept[0])
    own, send, small, gains = stream_last(place, kept, got)
    share_in, share_out, small = mixer_shares(
        place, own, other_core(send), small, other_core(small), output_token
    )
    gains = sum_over(sum_over(gains, "tp", output_token), "seq_2")
    return (
        result,
        grad_input,
        gains[0:4].reshape(D),
        share_in,
        small[64:73].reshape(3, 3, C),
        small[0:32].reshape(2, N, C),
        small[32:64].reshape(2, N, C),
        share_out.T,
        gains[4:8].reshape(D),
        share_gate,
        share_up,
        share_down.T,
    )


def solution(mesh):
    split = Mesh(mesh.devices.reshape(4, 4, 2, mesh.shape["tp"]), ("seq_0", "seq_1", "seq_2", "tp"))
    in_specs = (
        P(SEQ, None),
        P(SEQ, None),
        P(SEQ),
        P(),
        P(None, None, "tp"),
        P(None, None, "tp"),
        P(None, None, "tp"),
        P(None, None, "tp"),
        P("tp", None),
        P(),
        P(None, "tp"),
        P(None, "tp"),
        P("tp", None),
    )
    out_specs = (
        P(SEQ, None),
        P(SEQ, None),
        P(),
        P(None, SEQ, "tp"),
        P(None, None, "tp"),
        P(None, None, "tp"),
        P(None, None, "tp"),
        P("tp", SEQ),
        P(),
        P(SEQ, "tp"),
        P(SEQ, "tp"),
        P("tp", SEQ),
    )
    return jax.shard_map(
        per_device, mesh=split, in_specs=in_specs, out_specs=out_specs, check_vma=False
    )
```

```python
import functools

import jax
import jax.numpy as jnp
from jax import lax
from jax.experimental import pallas as pl
from jax.experimental.pallas import tpu as pltpu
from jax.sharding import Mesh
from jax.sharding import PartitionSpec as P

SEQ = ("seq_0", "seq_1", "seq_2")
F32 = jnp.float32
BF16 = jnp.bfloat16
epsilon = 1e-06
MIB = 1 << 20
T, C, N, D = 256, 512, 16, 2048
BLOCK = 32
BLOCKS = T // BLOCK
PARTS = 1
ROWS = 64
VMEM = pl.BlockSpec(memory_space=pltpu.VMEM)
SMEM = pl.BlockSpec(memory_space=pltpu.SMEM)
ANY = pl.BlockSpec(memory_space=pl.ANY)


def in_hbm(x):
    return pltpu.with_memory_space_constraint(x, pltpu.HBM)


def taking(microseconds):
    return pl.CostEstimate(flops=0, bytes_accessed=int(microseconds * 3.0e6), transcendentals=0)


def whole(*shape):
    return pl.BlockSpec(shape, lambda i: (0,) * len(shape))


def struct(*shape, dtype=F32):
    return jax.ShapeDtypeStruct(shape, dtype)


def times(a, b):
    return a[0] * b[0] - a[1] * b[1], a[0] * b[1] + a[1] * b[0]


def plus(a, b):
    return a[0] + b[0], a[1] + b[1]


def where2(flag, a, b):
    return jnp.where(flag, a[0], b[0]), jnp.where(flag, a[1], b[1])


def scaled(a, factor):
    return a[0] * factor, a[1] * factor


def token_sum(a, b):
    return lax.dot_general(a, b, (((0,), (0,)), ((), ())), preferred_element_type=F32)


def dot(a, b):
    return jnp.dot(a, b, preferred_element_type=F32)


def dot_t(a, b):
    return lax.dot_general(a, b, (((1,), (1,)), ((), ())), preferred_element_type=F32)


def scan_groups(groups, starts, base, run, carry, reverse):
    def body(step, kept):
        group = groups - 1 - step if reverse else step
        first = base + group * 8
        marks = starts[first]
        for r in range(1, 8):
            marks = marks + starts[first + r]
        return lax.cond(
            marks > 0, lambda c: run(group, c, True), lambda c: run(group, c, False), kept
        )

    return lax.fori_loop(0, groups, body, carry)


def quarter_rows(quarter):
    return pl.ds(pl.multiple_of(quarter * ROWS, ROWS), ROWS)


def eight(group):
    return pl.ds(pl.multiple_of(group * 8, 8), 8)


def fold(x, y, step):
    at = lax.broadcasted_iota(jnp.int32, x.shape, 0)
    of_x = (at & step) == 0
    return jnp.where(of_x, x, y) + pltpu.roll(jnp.where(of_x, y, x), 8 - step, 0)


def row_sums(parts):
    for step in (1, 2, 4):
        parts = [fold(parts[n], parts[n + 1], step) for n in range(0, len(parts), 2)]
    return parts[0]


def keep_at(starts, token):
    return (1 - starts[token]).astype(F32)


def with_rim(proj, rim, k, rows):
    rows[0:8] = rim[k]
    rows[8:] = proj[k]


def keeps_of(column):
    marks = column[...].astype(F32)
    one = 1.0 - marks
    two = one * jnp.concatenate([jnp.ones((1, 1), F32), one[: T - 1]])
    return one, two, 1.0 - jnp.max(marks, axis=0, keepdims=True)


def project_kernel(values, gain, weights, low, inverse, proj, proj_kept):
    v = values[...]
    inverse[...] = inverse_rms(v)
    low[...] = (v * inverse[...] * gain[...]).astype(BF16)
    for k in range(3):
        proj[k] = dot(low[...], weights[k])
        proj_kept[k] = proj[k]


def project(values, gain, weights):
    return pl.pallas_call(
        project_kernel,
        name="project",
        cost_estimate=taking(3),
        out_shape=(
            struct(T, D, dtype=BF16),
            struct(T, 1),
            struct(3, T, C),
            pltpu.HBM((3, T, C), F32),
        ),
        in_specs=[VMEM] * 3,
        out_specs=[VMEM] * 4,
        compiler_params=pltpu.CompilerParams(vmem_limit_bytes=12 * MIB),
    )(values, gain, weights)


def mix_kernel(proj, rim, gain, weights, taps, column, starts, poles, *refs):
    proj_rim, mixed, end, powers, kept, shifted_rows, driven = refs
    v = rim[...]
    v = v * inverse_rms(v) * gain[...]
    low = jnp.concatenate([v, v]).astype(BF16)
    for k in range(3):
        proj_rim[k] = dot(low, weights[k])[:8]
        kept[k, :T], kept[k, T:] = proj[k], proj_rim[k]
    mix_end(kept, taps, column, starts, poles, mixed, end, powers, shifted_rows, driven)


def mix_end(kept, taps, column, starts, poles, mixed, end, powers, rows, driven):
    one, two, is_open = keeps_of(column)
    for k in range(3):
        rows[0:8], rows[8:] = kept[k, T:], kept[k, :T]
        mixed[k] = (
            taps[k, 0:1] * kept[k, :T]
            + taps[k, 1:2] * (one * rows[7 : 7 + T])
            + taps[k, 2:3] * (two * rows[6 : 6 + T])
        )
    driven[...] = mixed[1] * mixed[2]
    pre, pim = poles[0], poles[1]

    def run(group, state, masked):
        source = driven[eight(group), :]
        re, im = state
        for r in range(8):
            if masked:
                keep = keep_at(starts, group * 8 + r)
                re, im = re * keep, im * keep
            re, im = pre * re - pim * im + source[r : r + 1], pre * im + pim * re
        return re, im

    zero = jnp.zeros((N, C), F32)
    end[0:N], end[N : 2 * N] = scan_groups(T // 8, starts, 0, run, (zero, zero), False)
    end[2 * N :] = jnp.broadcast_to(is_open, (8, C))
    power = (pre, pim)
    for n in range(1, 12):
        power = times(power, power)
        if n in (8, 9, 11):
            at = {8: 0, 9: 2, 11: 4}[n]
            powers[at], powers[at + 1] = power


def mix(proj, rim, gain, weights, taps, column, starts, poles):
    return pl.pallas_call(
        mix_kernel,
        name="mix",
        cost_estimate=taking(5),
        out_shape=(
            struct(3, 8, C),
            pltpu.HBM((3, T, C), F32),
            struct(2 * N + 8, C),
            struct(6, N, C),
        ),
        in_specs=[VMEM] * 6 + [SMEM, VMEM],
        out_specs=(VMEM,) * 4,
        scratch_shapes=[
            pltpu.VMEM((3, T + 8, C), F32),
            pltpu.VMEM((T + 8, C), F32),
            pltpu.VMEM((T, C), F32),
        ],
        compiler_params=pltpu.CompilerParams(vmem_limit_bytes=22 * MIB),
    )(proj, rim, gain, weights, taps, column, starts, poles)


def forward_rows(mixed, starts, poles, block, state, visit, finish=None):
    pre, pim = poles[0], poles[1]
    base = block * BLOCK

    def run(group, kept, masked):
        source = mixed[1, eight(group), :] * mixed[2, eight(group), :]
        re, im = kept
        seen = []
        for r in range(8):
            if masked:
                keep = keep_at(starts, base + group * 8 + r)
                re, im = re * keep, im * keep
            re, im = pre * re - pim * im + source[r : r + 1], pre * im + pim * re
            seen.append(visit(group * 8 + r, re, im))
        if finish:
            finish(group, seen)
        return re, im

    state[0], state[1] = scan_groups(BLOCK // 8, starts, base, run, (state[0], state[1]), False)


def signal_kernel(mixed, starts, poles, residues, first, signal, gated, state):
    block = pl.program_id(0)

    @pl.when(block == 0)
    def _():
        state[...] = first[...]

    qre, qim = residues[0], residues[1]

    def visit(row, re, im):
        weighed = qre * re - qim * im
        return weighed[:8] + weighed[8:]

    def finish(group, seen):
        signal[eight(group), :] = row_sums(seen)

    forward_rows(mixed, starts, poles, block, state, visit, finish)
    gated[...] = (mixed[0] * signal[...]).astype(BF16)


def history_kernel(mixed, starts, poles, first, *rest):
    h0, h1, h2, h3, token, state = rest[-6:]
    block = pl.program_id(0)
    token[...] = jnp.zeros(token.shape, F32)

    @pl.when(block == 0)
    def _():
        state[...] = first[...]

    def visit(row, re, im):
        h0[row], h1[row] = re[:8], re[8:]
        h2[row], h3[row] = im[:8], im[8:]

    forward_rows(mixed, starts, poles, block, state, visit)


def signal_of(mixed, starts, poles, residues, first):
    return pl.pallas_call(
        signal_kernel,
        name="signal",
        cost_estimate=taking(6),
        grid=(BLOCKS,),
        out_shape=(struct(T, C), struct(T, C, dtype=BF16)),
        in_specs=[
            pl.BlockSpec((3, BLOCK, C), lambda i: (0, i, 0)),
            SMEM,
            whole(2, N, C),
            whole(2, N, C),
            whole(2, N, C),
        ],
        out_specs=(pl.BlockSpec((BLOCK, C), lambda i: (i, 0)),) * 2,
        scratch_shapes=[pltpu.VMEM((2, N, C), F32)],
        compiler_params=pltpu.CompilerParams(vmem_limit_bytes=8 * MIB),
    )(mixed, starts, poles, residues, first)


def history_of(mixed, starts, poles, first, *after):
    return pl.pallas_call(
        history_kernel,
        name="state_history",
        cost_estimate=taking(8),
        grid=(BLOCKS,),
        out_shape=(pltpu.HBM((T, 8, C), F32),) * 4 + (struct(8, 128),),
        in_specs=[
            pl.BlockSpec((3, BLOCK, C), lambda i: (0, i, 0)),
            SMEM,
            whole(2, N, C),
            whole(2, N, C),
        ]
        + [ANY] * len(after),
        out_specs=(pl.BlockSpec((BLOCK, 8, C), lambda i: (i, 0, 0)),) * 4 + (whole(8, 128),),
        scratch_shapes=[pltpu.VMEM((2, N, C), F32)],
        compiler_params=pltpu.CompilerParams(vmem_limit_bytes=11 * MIB),
    )(in_hbm(mixed), starts, poles, first, *after)


def adjoint_kernel(grad_gated, query, column, starts, poles, residues, out, grads):
    grads[...] = grad_gated[...] * query[0]
    pre, pim, qre, qim = poles[0], poles[1], residues[0], residues[1]

    def run(group, kept, masked):
        source = grads[eight(group), :]
        re, im = kept
        for r in reversed(range(8)):
            row = source[r : r + 1]
            re, im = row * qre + (pre * re + pim * im), (pre * im - pim * re) - row * qim
            if masked:
                keep = keep_at(starts, group * 8 + r)
                re, im = re * keep, im * keep
        return re, im

    zero = jnp.zeros((N, C), F32)
    out[0:N], out[N : 2 * N] = scan_groups(T // 8, starts, 0, run, (zero, zero), True)
    out[2 * N :] = jnp.broadcast_to(keeps_of(column)[2], (8, C))


def adjoint_end(grad_gated, mixed, column, starts, poles, residues):
    return pl.pallas_call(
        adjoint_kernel,
        name="adjoint_end",
        cost_estimate=taking(4),
        grid=(1,),
        out_shape=struct(2 * N + 8, C),
        in_specs=[
            whole(T, C),
            pl.BlockSpec((1, T, C), lambda i: (0, 0, 0)),
            whole(T, 1),
            SMEM,
            whole(2, N, C),
            whole(2, N, C),
        ],
        out_specs=whole(2 * N + 8, C),
        scratch_shapes=[pltpu.VMEM((T, C), F32)],
        compiler_params=pltpu.CompilerParams(vmem_limit_bytes=9 * MIB),
    )(grad_gated, mixed, column, starts, poles, residues)


def back_kernel(
    grad_gated,
    mixed,
    signal,
    proj,
    proj_rim,
    h0,
    h1,
    h2,
    h3,
    taps,
    column,
    starts,
    poles,
    residues,
    first,
    *rest,
):
    grad_proj, rim, sums, state, driven_grad, mixed_grad, rows_before = rest[-7:]
    step = pl.program_id(0)
    block = BLOCKS - 1 - step

    @pl.when(step == 0)
    def _():
        state[...] = first[...]
        sums[...] = jnp.zeros(sums.shape, F32)

    base = block * BLOCK
    for part in range(PARTS):
        columns = slice(C // PARTS * part, C // PARTS * (part + 1))
        pre, pim = poles[0, :, columns], poles[1, :, columns]
        qre, qim = residues[0, :, columns], residues[1, :, columns]

        def run(group, kept, masked):
            rows = pl.ds(pl.multiple_of(base + group * 8, 8), 8)
            source = grad_gated[rows, columns] * mixed[0, rows, columns]
            re, im, pole_re, pole_im, res_re, res_im = kept
            seen = [None] * 8
            for r in reversed(range(8)):
                row = source[r : r + 1]
                token = group * 8 + r
                sre = jnp.concatenate([h0[token, :, columns], h1[token, :, columns]])
                sim = jnp.concatenate([h2[token, :, columns], h3[token, :, columns]])
                pole_re += re * sre + im * sim
                pole_im += im * sre - re * sim
                res_re += row * sre
                res_im -= row * sim
                re, im = row * qre + (pre * re + pim * im), (pre * im - pim * re) - row * qim
                seen[r] = re[:8] + re[8:]
                if masked:
                    keep = keep_at(starts, base + group * 8 + r)
                    re, im = re * keep, im * keep
            driven_grad[rows, columns] = row_sums(seen)
            return re, im, pole_re, pole_im, res_re, res_im

        zero = jnp.zeros((N, C // PARTS), F32)
        kept = (state[0, :, columns], state[1, :, columns], zero, zero, zero, zero)
        kept = scan_groups(BLOCK // 8, starts, base, run, kept, True)
        state[0, :, columns], state[1, :, columns] = kept[:2]
        for n in range(4):
            sums[N * n : N * n + N, columns] += kept[2 + n]

    @pl.when(step == BLOCKS - 1)
    def _():
        one, two, _ = keeps_of(column)
        mixed_grad[0, 0:T] = grad_gated[...] * signal[...]
        mixed_grad[1, 0:T] = driven_grad[...] * mixed[2]
        mixed_grad[2, 0:T] = driven_grad[...] * mixed[1]
        for k in range(3):
            with_rim(proj, proj_rim, k, rows_before)
            here = mixed_grad[k, 0:T]
            sums[64 + 3 * k : 65 + 3 * k] = jnp.sum(here * proj[k], axis=0, keepdims=True)
            grad_proj[k] = taps[k, 0:1] * here
            here = one * mixed_grad[k, 0:T]
            sums[65 + 3 * k : 66 + 3 * k] = jnp.sum(here * rows_before[7 : 7 + T], axis=0, keepdims=True)
            mixed_grad[k, 0:T] = two * mixed_grad[k, 0:T]
            here = taps[k, 1:2] * here
            grad_proj[k, 0 : T - 1] += here[1:T]
            rim[k] = jnp.zeros((8, C), F32)
            rim[k, 1:2] = here[0:1]
            here = mixed_grad[k, 0:T]
            sums[66 + 3 * k : 67 + 3 * k] = jnp.sum(here * rows_before[6 : 6 + T], axis=0, keepdims=True)
            here = taps[k, 2:3] * here
            grad_proj[k, 0 : T - 2] += here[2:T]
            rim[k, 0:2] += here[0:2]


def back(grad_gated, mixed, signal, proj, proj_rim, history, taps, column, starts, poles, residues, first, *after):
    return pl.pallas_call(
        back_kernel,
        name="adjoint_and_short_back",
        cost_estimate=taking(13),
        grid=(BLOCKS,),
        out_shape=(struct(3, T, C), struct(3, 8, C), struct(80, C)),
        in_specs=[
            whole(T, C),
            whole(3, T, C),
            whole(T, C),
            whole(3, T, C),
            whole(3, 8, C),
        ]
        + [pl.BlockSpec((BLOCK, 8, C), lambda i: (BLOCKS - 1 - i, 0, 0))] * 4
        + [
            whole(3, 3, C),
            whole(T, 1),
            SMEM,
            whole(2, N, C),
            whole(2, N, C),
            whole(2, N, C),
        ]
        + [ANY] * len(after),
        out_specs=(whole(3, T, C), whole(3, 8, C), whole(80, C)),
        scratch_shapes=[
            pltpu.VMEM((2, N, C), F32),
            pltpu.VMEM((T, C), F32),
            pltpu.VMEM((3, T, C), F32),
            pltpu.VMEM((T + 8, C), F32),
        ],
        compiler_params=pltpu.CompilerParams(vmem_limit_bytes=25 * MIB),
    )(
        grad_gated,
        mixed,
        signal,
        proj,
        proj_rim,
        *history,
        taps,
        column,
        starts,
        poles,
        residues,
        first,
        *after,
    )


def swap(value, axis, mask):
    size = lax.axis_size(axis)
    return lax.ppermute(value, axis, [(i, i ^ mask) for i in range(size)])


def shifted(value, axis, steps):
    count = lax.axis_size(axis)
    first, last = max(0, -steps), min(count, count - steps)
    return lax.ppermute(value, axis, [(i, i + steps) for i in range(first, last)])


def pair_add_kernel(left, got_left, right, got_right, *rest):
    left_own, left_next, right_own, right_next = rest[-4:]
    left_own[...] = left[:ROWS] + got_left[:ROWS]
    left_next[...] = left[ROWS:] + got_left[ROWS:]
    right_own[...] = right[:ROWS] + got_right[:ROWS]
    right_next[...] = right[ROWS:] + got_right[ROWS:]


def pair_call(name, kernel, shapes, operands, after):
    return pl.pallas_call(
        kernel,
        name=name,
        cost_estimate=taking(0.8),
        out_shape=shapes,
        in_specs=[VMEM] * len(operands) + [ANY] * len(after),
        out_specs=[VMEM] * len(shapes),
        compiler_params=pltpu.CompilerParams(vmem_limit_bytes=10 * MIB),
    )(*operands, *after)


def scatter_end(pieces, got_left, got_right, *after, shape=struct):
    left_own, left_next, right_own, right_next = pair_call(
        "pair_add",
        pair_add_kernel,
        [shape(ROWS, HALF)] * 4,
        (pieces[0], got_left, pieces[2], got_right),
        after,
    )
    return left_own, swap(left_next, "tp", 3), right_own, swap(right_next, "tp", 1)


def scatter_start(pieces):
    return swap(pieces[1], "tp", 1), swap(pieces[3], "tp", 3)


def in_hbm_struct(*shape):
    return pltpu.HBM(shape, F32)


def scatter_sum(pieces, *after, shape=struct):
    return scatter_end(pieces, *scatter_start(pieces), *after, shape=shape)


def pair_join_kernel(left, left_3, right, right_1, *rest):
    left_03, right_10 = rest[-2:]
    rows = left.shape[0]
    left_03[:rows], left_03[rows:] = left[...], left_3[...]
    right_10[:rows], right_10[rows:] = right_1[...], right[...]


def gather_joined(left, right, *after):
    return joined_parts(left, swap(left, "tp", 3), right, swap(right, "tp", 1), *after)


def joined_parts(left, left_3, right, right_1, *after):
    left_03, right_10 = pair_call(
        "pair_join",
        pair_join_kernel,
        [struct(2 * left.shape[0], HALF)] * 2,
        (left, left_3, right, right_1),
        after,
    )
    parts = left, swap(left_03, "tp", 1), left_3, right, right_1, swap(right_10, "tp", 3)
    return parts, (left_03, right_10)


def gather_parts(left, right, *after):
    return gather_joined(left, right, *after)[0]


def quarters_of(parts):
    left, left_12, left_3, right, right_1, right_23 = parts
    rows = left.shape[0]
    return (
        (left[:rows], right[:rows]),
        (left_12[:rows], right_1[:rows]),
        (left_12[rows:], right_23[:rows]),
        (left_3[:rows], right_23[rows:]),
    )


def of_payload(ref):
    return (ref[0:N], ref[N : 2 * N]), ref[2 * N : 2 * N + 1]


def to_payload(ref, state, is_open):
    ref[0:N], ref[N : 2 * N] = state
    ref[2 * N :] = jnp.broadcast_to(is_open, (8, C))


def power_of(powers, at, reverse):
    return powers[at], -powers[at + 1] if reverse else powers[at + 1]


def chip_kernel(reverse, place, mine, other, powers, out):
    (state, is_open), (state_other, open_other) = of_payload(mine), of_payload(other)
    by_device = power_of(powers, 0, reverse)
    last = place[1] == (0 if reverse else 1)
    earlier = where2(last, state_other, state)
    later = where2(last, state, state_other)
    later_open = jnp.where(last, is_open, open_other)
    chip = plus(later, times(scaled(by_device, later_open), earlier))
    to_payload(out, chip, is_open * open_other)


def plane_kernel(reverse, place, mine, got_1, got_2, got_3, powers, *rest):
    out, before = rest[-2:]
    chip, is_open = of_payload(mine)
    by_chip = power_of(powers, 2, reverse)
    got = {1: of_payload(got_1), 2: of_payload(got_2), 3: of_payload(got_3)}
    y = 3 - place[2] if reverse else place[2]
    one, zero = jnp.ones((N, C), F32), jnp.zeros((N, C), F32)
    entering, weight = (zero, zero), (one, zero)
    for k in (1, 2, 3):
        state, opened = got[k]
        entering = where2(y >= k, plus(entering, times(weight, state)), entering)
        weight = where2(y >= k, times(weight, scaled(by_chip, opened)), weight)
    plane = plus(chip, times(scaled(by_chip, is_open), entering))
    for j in (1, 2, 3):
        state, opened = got[4 - j]
        plane = where2(y + j <= 3, plus(state, times(scaled(by_chip, opened), plane)), plane)
        is_open = is_open * opened
    to_payload(out, plane, is_open)
    before[0], before[1] = entering
    before[2], before[3] = weight


def enter_kernel(reverse, place, before, got_1, got_2, got_3, other, powers, *rest):
    out = rest[-1]
    by_device, by_plane = power_of(powers, 0, reverse), power_of(powers, 4, reverse)
    one, zero = jnp.ones((N, C), F32), jnp.zeros((N, C), F32)
    entering, weight = (zero, zero), (one, zero)
    for ref in (got_1, got_2, got_3):
        state, opened = of_payload(ref)
        entering = plus(entering, times(weight, state))
        weight = times(weight, scaled(by_plane, opened))
    at_chip = plus((before[0], before[1]), times((before[2], before[3]), entering))
    state, opened = of_payload(other)
    at_core = plus(state, times(scaled(by_device, opened), at_chip))
    out[0], out[1] = where2(place[1] == (0 if reverse else 1), at_core, at_chip)


def small_call(name, kernel, reverse, shapes, operands, after=()):
    return pl.pallas_call(
        functools.partial(kernel, reverse),
        name=name,
        cost_estimate=taking(1.6),
        out_shape=shapes,
        in_specs=[SMEM] + [VMEM] * (len(operands) - 1) + [ANY] * len(after),
        out_specs=jax.tree.map(lambda _: VMEM, shapes),
        compiler_params=pltpu.CompilerParams(vmem_limit_bytes=8 * MIB),
    )(*operands, *after)


def carried_state(place, mine, powers, reverse, after=(), late=()):
    sign = -1 if reverse else 1
    payload = struct(2 * N + 8, C)
    other = swap(mine, "seq_2", 1)
    chip = small_call("chip_state", chip_kernel, reverse, payload, (place, mine, other, powers))
    got = [
        lax.ppermute(chip, "seq_1", [(i, (i + sign * k) % 4) for i in range(4)]) for k in (1, 2, 3)
    ]
    plane, before = small_call(
        "plane_state",
        plane_kernel,
        reverse,
        (payload, struct(4, N, C)),
        (place, chip, *got, powers),
        after,
    )
    got = [shifted(plane, "seq_0", sign * k) for k in (1, 2, 3)]
    entering = small_call(
        "entering_state",
        enter_kernel,
        reverse,
        struct(2, N, C),
        (place, before, *got, other, powers),
        late,
    )
    return entering


def sum_over(x, axis, *after):
    if lax.axis_size(axis) == 2:
        return x + swap(x, axis, 1)
    got = [swap(x, axis, k) for k in (1, 2, 3)]
    if after:
        got = [tie(g, *after) for g in got]
    return (x + got[0]) + (got[1] + got[2])


def inverse_rms(values):
    return lax.rsqrt(jnp.mean(values * values, axis=-1, keepdims=True) + epsilon)


def nothing(*refs):
    pass


def tie(x, *after, hbm=False):
    shape = struct(*x.shape, dtype=x.dtype)
    if hbm:
        x, shape = in_hbm(x), pltpu.HBM(x.shape, x.dtype)
    return pl.pallas_call(
        nothing,
        name="tie",
        out_shape=shape,
        in_specs=[ANY] * (1 + len(after)),
        out_specs=ANY,
        input_output_aliases={0: 0},
        compiler_params=pltpu.CompilerParams(vmem_limit_bytes=6 * MIB),
    )(x, *after)


WIDE = 1408


def wide_sum_kernel(left_a, l03, r10, l12, r23, left_b, more_b, right, wide, gain, out, token, both, rows_a, rows_b):
    step = pl.program_id(0)

    @pl.when(step == 0)
    def _():
        both[:T] = right[...]
        both[T:] = wide[...].astype(BF16)
        token[...] = jnp.zeros(token.shape, F32)

    def put(*quarters):
        rows_a[T:] = (jnp.concatenate(quarters) * gain[...]).astype(BF16)

    pl.when(step < 2)(lambda: put(l03[:ROWS], l12[:ROWS], l12[ROWS:], l03[ROWS:]))
    pl.when(step >= 2)(lambda: put(r10[ROWS:], r10[:ROWS], r23[:ROWS], r23[ROWS:]))
    rows_a[:T], rows_b[:T], rows_b[T:] = left_a[...], left_b[...], more_b[...]
    out[:, :WIDE] = token_sum(rows_a[...], both[:, :WIDE])
    out[:, WIDE:] = token_sum(rows_b[...], both[:, WIDE:])


def wide_token_sum(left_a, more_a, left_b, more_b, right, wide, gain):
    rows = 512
    column = pl.BlockSpec((T, rows), lambda i: (0, i))
    low = pl.BlockSpec((2 * ROWS, rows), lambda i: (0, jnp.minimum(i, 1)))
    high = pl.BlockSpec((2 * ROWS, rows), lambda i: (0, jnp.maximum(i - 2, 0)))
    width = right.shape[1]
    return pl.pallas_call(
        wide_sum_kernel,
        name="weight_gradients",
        cost_estimate=taking(10),
        grid=(D // rows,),
        out_shape=(pltpu.HBM((D, width), F32), struct(8, 128)),
        in_specs=[column, low, high, low, high, column, column]
        + [VMEM, VMEM, pl.BlockSpec((1, rows), lambda i: (0, i))],
        out_specs=(pl.BlockSpec((rows, width), lambda i: (i, 0)), whole(8, 128)),
        scratch_shapes=[
            pltpu.VMEM((2 * T, width), BF16),
            pltpu.VMEM((2 * T, rows), BF16),
            pltpu.VMEM((2 * T, rows), BF16),
        ],
        compiler_params=pltpu.CompilerParams(vmem_limit_bytes=27 * MIB),
    )(left_a, *more_a, left_b, more_b, right, wide, gain)


ORDERS = {1: (0, 3, 1, 2), 3: (0, 1, 3, 2)}
STREAMS = (("seq_1", 1), ("seq_1", 3), ("seq_0", 1), ("seq_0", 3))


def stream_places(step):
    jz, jy = divmod(step, 4)
    places = []
    for axis, mask in STREAMS:
        order = ORDERS[mask]
        first, second = (jy, jz) if axis == "seq_1" else (jz, jy)
        places.append(order.index(first) * 4 + order.index(second))
    return places


def stream_sum_kernel(
    place,
    left_a,
    more_a,
    left_b,
    more_b,
    right_a,
    wide_a,
    right_b,
    wide_b,
    sums,
    gains_a,
    gains_b,
    *rest,
):
    kept, sent, token, turned = rest[-10:-6], rest[-6:-2], rest[-2], rest[-1]
    token[...] = jnp.zeros(token.shape, F32)
    for s in range(4):
        kept[s][2048 : 2048 + 80] = sums[:, 128 * s : 128 * s + 128]
        for n in range(8):
            row = (gains_a, gains_b)[n // 4]
            at = C * (n % 4) + 128 * s
            kept[s][2128 + n : 2129 + n] = row[:, at : at + 128]
        sent[s][2048:] = kept[s][2048:]
    turned[0:768, 0:T] = right_a[...].T
    turned[768:, 0:T] = right_b[...].T
    turned[0:768, T:] = wide_a[...].astype(BF16).T
    turned[768:, T:] = wide_b[...].astype(BF16).T
    y, z = place[2], place[3]
    for step in range(16):
        jz, jy = divmod(step, 4)
        chunk = (z ^ jz) * 4 + (y ^ jy)
        columns = pl.ds(pl.multiple_of(chunk * 128, 128), 128)
        total_a = dot(turned[0:768, 0:T], left_a[:, columns]) + dot(turned[0:768, T:], more_a[:, columns])
        total_b = dot(turned[768:, 0:T], left_b[:, columns]) + dot(turned[768:, T:], more_b[:, columns])
        for s, at in enumerate(stream_places(step)):
            target = kept[s] if at < 8 else sent[s]
            rows = slice((at % 8) * 256, (at % 8) * 256 + 256)
            target[rows] = total_a[256 * s : 256 * s + 256] if s < 3 else total_b


def stream_token_sum(place, *operands):
    out = pl.pallas_call(
        stream_sum_kernel,
        name="mixer_weight_gradients",
        cost_estimate=taking(7),
        out_shape=(struct(2048 + SMALL, 128),) * 8 + (struct(8, 128),),
        in_specs=[SMEM] + [VMEM] * 11 + [ANY] * (len(operands) - 11),
        out_specs=(VMEM,) * 9,
        scratch_shapes=[pltpu.VMEM((1024, 2 * T), BF16)],
        compiler_params=pltpu.CompilerParams(vmem_limit_bytes=8 * MIB),
    )(place, *operands)
    return out[:4], out[4:8], out[8]


SMALL = 88


def stream_add_kernel(*refs):
    held, got, kept, sent = refs[0:4], refs[4:8], refs[-8:-4], refs[-4:]
    for s in range(4):
        rows = held[s].shape[0] - SMALL
        low = rows // 2
        small = held[s][rows:] + got[s][rows:]
        kept[s][0:low] = held[s][0:low] + got[s][0:low]
        kept[s][low:] = small
        sent[s][0:low] = held[s][low:rows] + got[s][low:rows]
        sent[s][low:] = small


def stream_add(held, got, *after):
    rows = held[0].shape[0] - SMALL
    shape = struct(rows // 2 + SMALL, 128)
    out = pl.pallas_call(
        stream_add_kernel,
        name="stream_add",
        cost_estimate=taking(0.7 + rows / 1000),
        out_shape=[shape] * 8,
        in_specs=[VMEM] * 8 + [ANY] * len(after),
        out_specs=[VMEM] * 8,
        compiler_params=pltpu.CompilerParams(vmem_limit_bytes=6 * MIB),
    )(*held, *got, *after)
    return out[:4], out[4:]


def stream_last_kernel(place, *refs):
    held, got, (own, send, small, gains) = refs[0:4], refs[4:8], refs[-4:]
    first = place[1] == 0
    for s in range(4):
        total = (held[s][0:256] + got[s][0:256]).T
        columns = slice(256 * s, 256 * s + 256)
        own[:, columns] = jnp.where(first, total[:64], total[64:])
        send[:, columns] = jnp.where(first, total[64:], total[:64])
        total = held[s][256:] + got[s][256:]
        small[:, 128 * s : 128 * s + 128] = total[:80]
        gains[:, 128 * s : 128 * s + 128] = total[80:]


def stream_last(place, held, got, *after):
    return pl.pallas_call(
        stream_last_kernel,
        name="stream_last",
        cost_estimate=taking(1.5),
        out_shape=(struct(64, 1024), struct(64, 1024), struct(80, C), struct(8, C)),
        in_specs=[SMEM] + [VMEM] * 8 + [ANY] * len(after),
        out_specs=[VMEM] * 4,
        compiler_params=pltpu.CompilerParams(vmem_limit_bytes=6 * MIB),
    )(place, *held, *got, *after)


def stream_masks(axis, mask):
    other = "seq_0" if axis == "seq_1" else "seq_1"
    return ((axis, mask), (axis, 4 - mask), (other, mask), (other, 4 - mask))


def stream_swap(sent, step):
    return [swap(x, *stream_masks(*STREAMS[s])[step]) for s, x in enumerate(sent)]


def mixer_shares_kernel(place, own, got, small, small_got, *rest):
    grad_in, grad_out, small_sum = rest[-3:]
    first = place[1] == 0
    low = jnp.where(first, own[...], got[...])
    high = jnp.where(first, got[...], own[...])
    for k in range(3):
        columns = slice(256 * k, 256 * k + 256)
        grad_in[k, :, :256], grad_in[k, :, 256:] = low[:, columns], high[:, columns]
    grad_out[:, :256], grad_out[:, 256:] = low[:, 768:], high[:, 768:]
    small_sum[...] = small[...] + small_got[...]


def mixer_shares(place, own, got, small, small_got, *after):
    return pl.pallas_call(
        mixer_shares_kernel,
        name="mixer_shares",
        cost_estimate=taking(1.5),
        out_shape=(struct(3, 64, C), struct(64, C), struct(80, C)),
        in_specs=[SMEM] + [VMEM] * 4 + [ANY] * len(after),
        out_specs=[VMEM] * 3,
        compiler_params=pltpu.CompilerParams(vmem_limit_bytes=6 * MIB),
    )(place, own, got, small, small_got, *after)


def ffn_send_kernel(place, share, *rest):
    own, send = rest[-2:]
    first = place[1] == 0
    low, high = share[:64], share[64:]
    own[...] = jnp.where(first, low, high)
    send[...] = jnp.where(first, high, low)


def ffn_shares_kernel(place, own, got, *rest):
    gate, up, down, token = rest[-4:]
    first = place[1] == 0
    low = jnp.where(first, own[...], got[...])
    high = jnp.where(first, got[...], own[...])
    gate[:, :768], gate[:, 768:] = low[:, :768], high[:, 768:1408]
    up[:, :640], up[:, 640:] = low[:, 768:1408], high[:, :768]
    down[:, :768], down[:, 768:] = low[:, 1408:], high[:, 1408 + 128 :]
    token[...] = jnp.zeros(token.shape, F32)


def ffn_halves(place, share, *after):
    return pl.pallas_call(
        ffn_send_kernel,
        name="ffn_send",
        cost_estimate=taking(1),
        out_shape=(struct(64, 2176),) * 2,
        in_specs=[SMEM, VMEM] + [ANY] * len(after),
        out_specs=[VMEM] * 2,
        compiler_params=pltpu.CompilerParams(vmem_limit_bytes=6 * MIB),
    )(place, share, *after)


def ffn_shares(place, own, got, *after):
    return pl.pallas_call(
        ffn_shares_kernel,
        name="ffn_shares",
        cost_estimate=taking(2),
        out_shape=(struct(64, 1408),) * 3 + (struct(8, 128),),
        in_specs=[SMEM, VMEM, VMEM] + [ANY] * len(after),
        out_specs=[VMEM] * 4,
        compiler_params=pltpu.CompilerParams(vmem_limit_bytes=8 * MIB),
    )(place, own, got, *after)


def norm_kernel(values, gain, *rest):
    out, inverse = rest[-2:]
    v = values[...]
    inverse[...] = inverse_rms(v)
    out[...] = (v * inverse[...] * gain[...]).astype(BF16)


def normed(values, gain, *after):
    rows = 128
    row = pl.BlockSpec((rows, D), lambda i: (i, 0))
    return pl.pallas_call(
        norm_kernel,
        name="normed_in",
        cost_estimate=taking(1.8),
        grid=(values.shape[0] // rows,),
        out_shape=(struct(*values.shape, dtype=BF16), struct(values.shape[0], 1)),
        in_specs=[row, whole(1, D)] + [ANY] * len(after),
        out_specs=(row, pl.BlockSpec((rows, 1), lambda i: (i, 0))),
        compiler_params=pltpu.CompilerParams(vmem_limit_bytes=11 * MIB),
    )(values, gain, *after)


HALF = D // 2


def rows_by_quarter(place, ref):
    return jnp.concatenate([ref[quarter_rows(place[0] ^ q), :] for q in range(4)])


def cotangent_kernel(place, cotangent, w_down, *rest):
    low, grad_hidden = rest[-2:]

    @pl.when(pl.program_id(0) == 0)
    def _():
        for q in range(4):
            low[ROWS * q : ROWS * q + ROWS] = cotangent[quarter_rows(place[0] ^ q), :].astype(BF16)

    grad_hidden[...] = dot_t(low[...], w_down[...])


def cotangent_part(place, cotangent, w_down, *after):
    wide = w_down.shape[0]
    return pl.pallas_call(
        cotangent_kernel,
        name="cotangent_part",
        cost_estimate=taking(4),
        grid=(6,),
        out_shape=(struct(T, D, dtype=BF16), struct(T, wide)),
        in_specs=[SMEM, VMEM, pl.BlockSpec((256, D), lambda i: (i, 0))] + [ANY] * len(after),
        out_specs=(VMEM, pl.BlockSpec((T, 256), lambda i: (0, i))),
        compiler_params=pltpu.CompilerParams(vmem_limit_bytes=9 * MIB),
    )(place, cotangent, w_down, *after)


def out_parts_kernel(place, gated, *rest):
    own, send = rest[-2:]
    first = place[1] == 0
    rows = rows_by_quarter(place, gated).astype(F32)
    low, high = rows[:, :256], rows[:, 256:]
    own[...] = jnp.where(first, low, high).astype(BF16)
    send[...] = jnp.where(first, high, low)


def out_parts(place, gated, *after):
    return pl.pallas_call(
        out_parts_kernel,
        name="out_parts",
        cost_estimate=taking(1),
        out_shape=(struct(T, 256, dtype=BF16), struct(T, 256)),
        in_specs=[SMEM, VMEM] + [ANY] * len(after),
        out_specs=[VMEM] * 2,
        compiler_params=pltpu.CompilerParams(vmem_limit_bytes=7 * MIB),
    )(place, gated, *after)


def owner_kernel(place, rows, *rest):
    rest[-1][...] = rows[...].astype(BF16)


def owner_rows(place, x, *after):
    row = pl.BlockSpec((ROWS, D), lambda i, place: (place[0] ^ i, 0))
    out = pl.BlockSpec((ROWS, D), lambda i, place: (i, 0))
    return pl.pallas_call(
        owner_kernel,
        name="owner_rows",
        cost_estimate=taking(2),
        out_shape=pltpu.HBM((T, D), BF16),
        grid_spec=pltpu.PrefetchScalarGridSpec(
            num_scalar_prefetch=1, grid=(4,), in_specs=[row] + [ANY] * len(after), out_specs=out
        ),
        compiler_params=pltpu.CompilerParams(vmem_limit_bytes=9 * MIB),
    )(place, in_hbm(x), *after)


def branch_other_kernel(place, cotangent, through, out):
    out[...] = (cotangent[...] + through[...]).astype(BF16)


def branch_other_of(place, cotangent, through):
    row = pl.BlockSpec((ROWS, D), lambda i, place: (i, 0))
    return pl.pallas_call(
        branch_other_kernel,
        name="branch_other",
        cost_estimate=taking(2),
        out_shape=struct(T, D, dtype=BF16),
        grid_spec=pltpu.PrefetchScalarGridSpec(
            num_scalar_prefetch=1,
            grid=(4,),
            in_specs=[pl.BlockSpec((ROWS, D), lambda i, place: (place[0] ^ i, 0)), row],
            out_specs=row,
        ),
        compiler_params=pltpu.CompilerParams(vmem_limit_bytes=9 * MIB),
    )(place, in_hbm(cotangent), through)


def middle_kernel(place, left, left_more, right, right_more, hidden, *rest):
    middle, out_left, out_right = rest[-3:]
    low = hidden[:, :HALF] + (left[...] + left_more[...])
    high = hidden[:, HALF:] + (right[...] + right_more[...])
    square = jnp.sum(low * low, axis=-1, keepdims=True) + jnp.sum(high * high, axis=-1, keepdims=True)
    inverse = lax.rsqrt(square * (1.0 / D) + epsilon)
    middle[:, :HALF], middle[:, HALF:] = low, high
    out_left[...], out_right[...] = low * inverse, high * inverse


def norm_back_parts(left, left_more, right, right_more, values, gain):
    grads = (left[...] + left_more[...], right[...] + right_more[...])
    v = (values[:, :HALF], values[:, HALF:])
    g = (gain[:, :HALF], gain[:, HALF:])
    square = sum(jnp.sum(x * x, axis=-1, keepdims=True) for x in v)
    inverse = lax.rsqrt(square * (1.0 / D) + epsilon)
    along = sum(jnp.sum(a * b * c, axis=-1, keepdims=True) for a, b, c in zip(g, grads, v))
    along = inverse * inverse * inverse * (along * (1.0 / D))
    back = [inverse * g[n] * grads[n] - v[n] * along for n in (0, 1)]
    return back, [grads[n] * (v[n] * inverse) for n in (0, 1)]


def norm_back_kernel(left, left_more, right, right_more, values, gain, *rest):
    out_left, out_right, gains = rest[-3:]
    back, weighed = norm_back_parts(left, left_more, right, right_more, values, gain)
    out_left[...], out_right[...] = back
    for n in (0, 1):
        gains[:, HALF * n : HALF * n + HALF] = jnp.sum(weighed[n], axis=0, keepdims=True)


def by_owner_grid(in_specs, out_specs):
    return pltpu.PrefetchScalarGridSpec(
        num_scalar_prefetch=1, grid=(1,), in_specs=in_specs, out_specs=out_specs
    )


MINE = pl.BlockSpec((ROWS, D), lambda i, place: (place[0], 0))


def after_middle(place, pieces, hidden, *after):
    return pl.pallas_call(
        middle_kernel,
        name="middle_and_norm",
        cost_estimate=taking(1.5),
        out_shape=(pltpu.HBM((ROWS, D), F32), struct(ROWS, HALF), struct(ROWS, HALF)),
        grid_spec=by_owner_grid([VMEM] * 4 + [MINE] + [ANY] * len(after), (VMEM,) * 3),
        compiler_params=pltpu.CompilerParams(vmem_limit_bytes=8 * MIB),
    )(place, *pieces, in_hbm(hidden), *after)


def norm_back(pieces, values, gain, *after):
    return pl.pallas_call(
        norm_back_kernel,
        name="norm_back",
        cost_estimate=taking(2),
        out_shape=(struct(ROWS, HALF), struct(ROWS, HALF), struct(1, D)),
        grid=(1,),
        in_specs=[whole(ROWS, HALF)] * 4 + [whole(ROWS, D), whole(1, D)] + [ANY] * len(after),
        out_specs=(VMEM,) * 3,
        compiler_params=pltpu.CompilerParams(vmem_limit_bytes=9 * MIB),
    )(*pieces, values, gain, *after)


def rim_kernel(starts, rows, *rest):
    out = rest[-1]
    at = lax.broadcasted_iota(jnp.int32, (8, D), 0)
    out[...] = jnp.where(at == 6, rows[...] * keep_at(starts, T - 1), rows[...])


def rim_rows_of(starts, hidden, *after):
    return pl.pallas_call(
        rim_kernel,
        name="rim_rows",
        cost_estimate=taking(1),
        grid=(1,),
        out_shape=struct(8, D),
        in_specs=[SMEM, pl.BlockSpec((8, D), lambda i: (T // 8 - 1, 0))] + [ANY] * len(after),
        out_specs=whole(8, D),
        compiler_params=pltpu.CompilerParams(vmem_limit_bytes=6 * MIB),
    )(starts, in_hbm(hidden), *after)


PIECES = ((0, 3), (1, 2), (0, 1), (3, 2))
PIECE_SHAPES = (struct(2 * ROWS, HALF),) * 4


def put_pieces(place, block, total, outs, by_owner=False):
    which, columns = block // 2, slice(512 * (block % 2), 512 * (block % 2) + 512)
    for n in (0, 1):
        out, quarters = outs[2 * which + n], PIECES[2 * which + n]
        for m, q in enumerate(quarters):
            rows = slice(ROWS * q, ROWS * q + ROWS) if by_owner else quarter_rows(place[0] ^ q)
            out[ROWS * m : ROWS * m + ROWS, columns] = total[rows, :]


def split_kernel(compute, by_owner, count, place, *refs):
    *outs, total = refs[-5:]
    for block in range(4):
        total[...] = compute(slice(512 * block, 512 * block + 512), *refs[:count])
        put_pieces(place, block, total, outs, by_owner)


def split_dot(name, compute, by_owner, place, *operands, after=()):
    return pl.pallas_call(
        functools.partial(split_kernel, compute, by_owner, len(operands)),
        name=name,
        cost_estimate=taking(2.5),
        out_shape=PIECE_SHAPES,
        in_specs=[SMEM] + [VMEM] * len(operands) + [ANY] * len(after),
        out_specs=[VMEM] * 4,
        scratch_shapes=[pltpu.VMEM((T, 512), F32)],
        compiler_params=pltpu.CompilerParams(vmem_limit_bytes=8 * MIB),
    )(place, *operands, *after)


def result_kernel(place, hidden, w_down, middle, *rest):
    out, token = rest[-2:]
    token[...] = jnp.zeros(token.shape, F32)
    for block in range(4):
        columns = slice(512 * block, 512 * block + 512)
        total = dot(hidden[...], w_down[:, columns])
        for q in range(4):
            rows = total[ROWS * q : ROWS * q + ROWS]
            out[quarter_rows(place[0] ^ q), columns] = rows + middle[:, columns] if q == 0 else rows


def result_part(place, hidden, w_down, middle, *after):
    return pl.pallas_call(
        result_kernel,
        name="result_part",
        cost_estimate=taking(2.5),
        out_shape=(pltpu.HBM((T, D), F32), struct(8, 128)),
        in_specs=[SMEM] + [VMEM] * 3 + [ANY] * len(after),
        out_specs=(VMEM, VMEM),
        compiler_params=pltpu.CompilerParams(vmem_limit_bytes=10 * MIB),
    )(place, hidden, w_down, middle, *after)


def ffn_kernel(place, *refs):
    parts, refs = refs[:6], refs[6:]
    gain, w_gate, w_up, grad_hidden = refs[:4]
    mid_x, hidden, grad_gate, grad_up, own_all, send_all = refs[-6:]
    for q, (left, right) in enumerate(quarters_of(parts)):
        rows = slice(ROWS * q, ROWS * q + ROWS)
        mid_x[rows, :HALF] = (left * gain[:, :HALF]).astype(BF16)
        mid_x[rows, HALF:] = (right * gain[:, HALF:]).astype(BF16)
    wide = w_gate.shape[1]
    for start in range(0, wide, 256):
        columns = slice(start, min(start + 256, wide))
        gate = dot(mid_x[...], w_gate[:, columns])
        up = dot(mid_x[...], w_up[:, columns])
        sig = 1.0 / (1.0 + jnp.exp(-gate))
        silu = gate * sig
        incoming = grad_hidden[:, columns]
        hidden[:, columns] = (silu * up).astype(BF16)
        grad_gate[:, columns] = (incoming * up * sig * (1.0 + gate * (1.0 - sig))).astype(BF16)
        grad_up[:, columns] = (incoming * silu).astype(BF16)
    first = place[1] == 0

    def halves(columns, low, high):
        a, b = low.astype(F32), high.astype(F32)
        own_all[:, columns] = jnp.where(first, a, b).astype(BF16)
        send_all[:, columns] = jnp.where(first, b, a)

    halves(slice(0, 768), grad_gate[:, :768], grad_up[:, 640:1408])
    halves(slice(768, 1408), grad_up[:, :640], grad_gate[:, 768:1408])
    halves(slice(1408, 2176), hidden[:, :768], hidden[:, 640:1408])


def feed_forward(place, parts, gain, w_gate, w_up, grad_hidden, *after):
    wide = w_gate.shape[1]
    low = struct(T, wide, dtype=BF16)
    return pl.pallas_call(
        ffn_kernel,
        name="feed_forward",
        cost_estimate=taking(7),
        out_shape=(
            struct(T, D, dtype=BF16),
            low,
            low,
            low,
            struct(T, wide + 768, dtype=BF16),
            struct(T, wide + 768),
        ),
        in_specs=[SMEM] + [VMEM] * 10 + [ANY] * len(after),
        out_specs=(VMEM,) * 6,
        compiler_params=pltpu.CompilerParams(vmem_limit_bytes=10 * MIB),
    )(place, *parts, gain, w_gate, w_up, grad_hidden, *after)


def branch_back_kernel(place, *refs):
    parts, cotangent, w_out = refs[:6], *refs[6:8]
    through, branch, grad_gated = refs[-3:]
    for q, (left, right) in enumerate(quarters_of(parts)):
        rows = slice(ROWS * q, ROWS * q + ROWS)
        through[rows, :HALF], through[rows, HALF:] = left, right
    branch[...] = (rows_by_quarter(place, cotangent) + through[...]).astype(BF16)
    back = dot_t(branch[...], w_out[...])
    for q in range(4):
        grad_gated[quarter_rows(place[0] ^ q), :] = back[ROWS * q : ROWS * q + ROWS]


def branch_back(place, parts, cotangent, w_out, *after):
    return pl.pallas_call(
        branch_back_kernel,
        name="branch_back",
        cost_estimate=taking(3),
        out_shape=(struct(T, D), pltpu.HBM((T, D), BF16), struct(T, C)),
        in_specs=[SMEM] + [VMEM] * 8 + [ANY] * len(after),
        out_specs=(VMEM,) * 3,
        compiler_params=pltpu.CompilerParams(vmem_limit_bytes=8 * MIB),
    )(place, *parts, cotangent, w_out, *after)


def finish_kernel(place, starts, grads, rim, *rest):
    low, own, send = rest[-3:]
    first = place[1] == 0
    at = lax.broadcasted_iota(jnp.int32, (8, C), 0)
    for k in range(3):
        turned = jnp.concatenate([jnp.zeros((6, C), F32), rim[k, 0:2]])
        turned = jnp.where(at == 6, turned * keep_at(starts, T - 1), turned)
        low[k, : T - 16] = grads[k, : T - 16].astype(BF16)
        low[k, T - 16 :] = jnp.concatenate(
            [grads[k, T - 16 : T - 8], grads[k, T - 8 :] + turned]
        ).astype(BF16)
        a, b = low[k, :, :256].astype(F32), low[k, :, 256:].astype(F32)
        columns = slice(256 * k, 256 * k + 256)
        own[:, columns] = jnp.where(first, a, b).astype(BF16)
        send[:, columns] = jnp.where(first, b, a)


def finish_projected(place, starts, grads, rim, *after):
    return pl.pallas_call(
        finish_kernel,
        name="finish_projected",
        cost_estimate=taking(1.5),
        out_shape=(struct(3, T, C, dtype=BF16), pltpu.HBM((T, 768), BF16), struct(T, 768)),
        in_specs=[SMEM, SMEM, VMEM, VMEM] + [ANY] * len(after),
        out_specs=(VMEM,) * 3,
        compiler_params=pltpu.CompilerParams(vmem_limit_bytes=7 * MIB),
    )(place, starts, grads, rim, *after)


def first_kernel(place, grads, hidden, inverse, gain, w_in, cotangent, left, right, *rest):
    out, gains, total = rest[-3:]
    along = jnp.zeros((T, 1), F32)
    for block in range(4):
        columns = slice(512 * block, 512 * block + 512)
        part = sum(dot_t(grads[k], w_in[k, columns, :]) for k in range(3))
        weighed = part * (hidden[:, columns] * inverse[...])
        gains[:, columns] = jnp.sum(weighed, axis=0, keepdims=True)
        along += jnp.sum(weighed * gain[:, columns], axis=1, keepdims=True)
        total[:, columns] = part
    along = inverse[...] * inverse[...] * (along * (1.0 / D))
    mine = quarter_rows(place[0])
    for block in range(4):
        columns = slice(512 * block, 512 * block + 512)
        out[:, columns] = inverse[...] * (gain[:, columns] * total[:, columns]) - hidden[:, columns] * along
        side, own = (left, right)[block // 2], slice(512 * (block % 2), 512 * (block % 2) + 512)
        out[mine, columns] += cotangent[mine, columns] + side[:, own]


def first_back(place, grads, hidden, inverse, gain, w_in, cotangent, left, right, *after):
    return pl.pallas_call(
        first_kernel,
        name="first_back",
        cost_estimate=taking(4),
        out_shape=(pltpu.HBM((T, D), F32), struct(1, D)),
        in_specs=[SMEM] + [VMEM] * 8 + [ANY] * len(after),
        out_specs=[VMEM] * 2,
        scratch_shapes=[pltpu.VMEM((T, D), F32)],
        compiler_params=pltpu.CompilerParams(vmem_limit_bytes=14 * MIB),
    )(place, grads, hidden, inverse, gain, w_in, cotangent, left, right, *after)


def emit_kernel(first, second, *rest):
    first_out, second_out, token = rest[-3:]
    token[...] = jnp.zeros(token.shape, F32)
    first_out[...], second_out[...] = first[...], second[...]


def emit(first, second, *after):
    row = pl.BlockSpec((ROWS, D), lambda i: (i, 0))
    return pl.pallas_call(
        emit_kernel,
        name="emit",
        cost_estimate=taking(3),
        grid=(4,),
        out_shape=(struct(T, D), struct(T, D), struct(8, 128)),
        in_specs=[row, row] + [ANY] * len(after),
        out_specs=(row, row, whole(8, 128)),
        compiler_params=pltpu.CompilerParams(vmem_limit_bytes=9 * MIB),
    )(in_hbm(first), in_hbm(second), *after)


def per_device(
    hidden_in,
    cotangent,
    starts,
    norm_in,
    w_in,
    short_w,
    pole_pairs,
    residues,
    w_out,
    norm_mid,
    w_gate,
    w_up,
    w_down,
):
    place = jnp.stack(
        [lax.axis_index(axis) for axis in ("tp", "seq_2", "seq_1", "seq_0")]
    ).astype(jnp.int32)
    column = starts[:, None]
    gain_in, gain_mid = norm_in[None], norm_mid[None]

    def other_core(x):
        return swap(x, "seq_2", 1)

    rim_rows = rim_rows_of(starts, hidden_in, place, column)
    rim_rows = lax.ppermute(rim_rows, SEQ, [(i, i + 1) for i in range(31)])
    hidden_other = other_core(hidden_in)
    cotangent_other = other_core(cotangent)
    normed_in, inverse_in, proj_now, proj = project(hidden_in, gain_in, w_in)
    rim, mixed, end, powers = mix(
        proj_now, rim_rows, gain_in, w_in, short_w, column, starts, pole_pairs
    )
    entering = carried_state(place, end, powers, False)
    signal, gated = signal_of(mixed, starts, pole_pairs, residues, entering)

    branch = split_dot(
        "branch",
        lambda columns, a, b: dot(a[...], b[:, columns]),
        False,
        place,
        gated,
        w_out,
    )
    *history, history_token = history_of(mixed, starts, pole_pairs, entering, branch[1])
    out_right, out_send = out_parts(place, gated, branch[1])
    pieces = scatter_sum(branch, history_token, out_send)
    down_grad, grad_hidden = cotangent_part(place, cotangent, w_down, pieces[0])
    middle, mid_left, mid_right = after_middle(place, pieces, hidden_in, grad_hidden)

    normed_other, _ = normed(hidden_other, gain_in, mid_left)
    down_other = owner_rows(place, cotangent_other, mid_left)
    parts, joined = gather_joined(mid_left, mid_right, in_hbm(normed_other), in_hbm(down_other))
    mid_other = [other_core(x) for x in joined]
    mid_x, hidden, grad_gate, grad_up, own_all, send_all = feed_forward(
        place,
        parts,
        gain_mid,
        w_gate,
        w_up,
        grad_hidden,
        *mid_other,
    )
    mid_other += [other_core(parts[1]), other_core(parts[5])]
    mid_terms = split_dot(
        "mid_terms",
        lambda columns, a, b, c, d: dot_t(a[...], c[columns, :]) + dot_t(b[...], d[columns, :]),
        True,
        place,
        grad_gate,
        grad_up,
        w_gate,
        w_up,
        after=mid_other[2:],
    )

    ffn_sum, ffn_token = wide_token_sum(
        mid_x,
        mid_other,
        down_grad,
        down_other,
        own_all,
        other_core(tie(send_all, mid_terms[1])),
        gain_mid,
    )

    pieces = scatter_sum(mid_terms, ffn_token, shape=in_hbm_struct)
    share_ffn = lax.psum_scatter(
        tie(ffn_sum, pieces[0], hbm=True), ("seq_0", "seq_1"), scatter_dimension=0, tiled=True
    )
    left, left_more, right, right_more = pieces
    through_left, through_right, gains_mid = norm_back(
        (in_hbm(left), left_more, in_hbm(right), right_more), in_hbm(middle), gain_mid
    )
    result, part_token = result_part(place, hidden, w_down, middle, gains_mid)
    through_f, branch_grad, grad_gated = branch_back(
        place, gather_parts(through_left, through_right), cotangent, w_out, part_token
    )

    leaving = adjoint_end(grad_gated, mixed, column, starts, pole_pairs, residues)
    branch_other = branch_other_of(place, cotangent_other, other_core(through_f))
    returning = carried_state(place, leaving, powers, True, after=(in_hbm(branch_other),))
    grad_proj, rim_grad, sums = back(
        grad_gated,
        mixed,
        signal,
        proj,
        rim,
        history,
        short_w,
        column,
        starts,
        pole_pairs,
        residues,
        returning,
    )
    rim_back = lax.ppermute(rim_grad, SEQ, [(i + 1, i) for i in range(31)])

    projected_low, proj_own, proj_send = finish_projected(
        place, starts, grad_proj, rim_back
    )
    proj_wide = other_core(proj_send)
    grad_input, gains_in = first_back(
        place,
        projected_low,
        hidden_in,
        inverse_in,
        gain_in,
        w_in,
        cotangent,
        through_left,
        through_right,
    )
    result, grad_input = lax.psum((result, grad_input), "tp")
    kept, leaving_now, mixer_token = stream_token_sum(
        place,
        normed_in,
        normed_other,
        branch_grad,
        branch_other,
        proj_own,
        proj_wide,
        out_right,
        other_core(out_send),
        sums,
        gains_in,
        gains_mid,
    )
    got = stream_swap(leaving_now, 0)
    kept, leaving_now = stream_add(kept, got)
    got = stream_swap(leaving_now, 1)
    ffn_own, ffn_out = ffn_halves(place, share_ffn, kept[0])
    kept, leaving_now = stream_add(kept, got, ffn_own)
    got = stream_swap(leaving_now, 2)
    share_gate, share_up, share_down, shares_token = ffn_shares(
        place, ffn_own, other_core(ffn_out), kept[0]
    )
    kept, leaving_now = stream_add(kept, got, shares_token)
    got = stream_swap(leaving_now, 3)
    result, grad_input, output_token = emit(result, grad_input, kept[0])
    own, send, small, gains = stream_last(place, kept, got, output_token)
    share_in, share_out, small = mixer_shares(
        place, own, other_core(send), small, other_core(small)
    )
    gains = sum_over(sum_over(gains, "tp"), "seq_2")
    return (
        result,
        grad_input,
        gains[0:4].reshape(D),
        share_in,
        small[64:73].reshape(3, 3, C),
        small[0:32].reshape(2, N, C),
        small[32:64].reshape(2, N, C),
        share_out.T,
        gains[4:8].reshape(D),
        share_gate,
        share_up,
        share_down.T,
    )


def solution(mesh):
    split = Mesh(mesh.devices.reshape(4, 4, 2, mesh.shape["tp"]), ("seq_0", "seq_1", "seq_2", "tp"))
    in_specs = (
        P(SEQ, None),
        P(SEQ, None),
        P(SEQ),
        P(),
        P(None, None, "tp"),
        P(None, None, "tp"),
        P(None, None, "tp"),
        P(None, None, "tp"),
        P("tp", None),
        P(),
        P(None, "tp"),
        P(None, "tp"),
        P("tp", None),
    )
    out_specs = (
        P(SEQ, None),
        P(SEQ, None),
        P(),
        P(None, SEQ, "tp"),
        P(None, None, "tp"),
        P(None, None, "tp"),
        P(None, None, "tp"),
        P("tp", SEQ),
        P(),
        P(SEQ, "tp"),
        P(SEQ, "tp"),
        P("tp", SEQ),
    )
    return jax.shard_map(
        per_device, mesh=split, in_specs=in_specs, out_specs=out_specs, check_vma=False
    )
```

```python
import functools

import jax
import jax.numpy as jnp
from jax import lax
from jax.experimental import pallas as pl
from jax.experimental.pallas import tpu as pltpu
from jax.sharding import Mesh
from jax.sharding import PartitionSpec as P

SEQ = ("seq_0", "seq_1", "seq_2")
F32 = jnp.float32
BF16 = jnp.bfloat16
epsilon = 1e-06
MIB = 1 << 20
T, C, N, D = 256, 512, 16, 2048
BLOCK = 32
BLOCKS = T // BLOCK
PARTS = 1
ROWS = 64
VMEM = pl.BlockSpec(memory_space=pltpu.VMEM)
SMEM = pl.BlockSpec(memory_space=pltpu.SMEM)
ANY = pl.BlockSpec(memory_space=pl.ANY)


def in_hbm(x):
    return pltpu.with_memory_space_constraint(x, pltpu.HBM)


def taking(microseconds):
    return pl.CostEstimate(flops=0, bytes_accessed=int(microseconds * 3.0e6), transcendentals=0)


def whole(*shape):
    return pl.BlockSpec(shape, lambda i: (0,) * len(shape))


def struct(*shape, dtype=F32):
    return jax.ShapeDtypeStruct(shape, dtype)


def times(a, b):
    return a[0] * b[0] - a[1] * b[1], a[0] * b[1] + a[1] * b[0]


def plus(a, b):
    return a[0] + b[0], a[1] + b[1]


def where2(flag, a, b):
    return jnp.where(flag, a[0], b[0]), jnp.where(flag, a[1], b[1])


def scaled(a, factor):
    return a[0] * factor, a[1] * factor


def token_sum(a, b):
    return lax.dot_general(a, b, (((0,), (0,)), ((), ())), preferred_element_type=F32)


def dot(a, b):
    return jnp.dot(a, b, preferred_element_type=F32)


def dot_t(a, b):
    return lax.dot_general(a, b, (((1,), (1,)), ((), ())), preferred_element_type=F32)


def scan_groups(groups, starts, base, run, carry, reverse):
    def body(step, kept):
        group = groups - 1 - step if reverse else step
        first = base + group * 8
        marks = starts[first]
        for r in range(1, 8):
            marks = marks + starts[first + r]
        return lax.cond(
            marks > 0, lambda c: run(group, c, True), lambda c: run(group, c, False), kept
        )

    return lax.fori_loop(0, groups, body, carry)


def quarter_rows(quarter):
    return pl.ds(pl.multiple_of(quarter * ROWS, ROWS), ROWS)


def eight(group):
    return pl.ds(pl.multiple_of(group * 8, 8), 8)


def fold(x, y, step):
    at = lax.broadcasted_iota(jnp.int32, x.shape, 0)
    of_x = (at & step) == 0
    return jnp.where(of_x, x, y) + pltpu.roll(jnp.where(of_x, y, x), 8 - step, 0)


def row_sums(parts):
    for step in (1, 2, 4):
        parts = [fold(parts[n], parts[n + 1], step) for n in range(0, len(parts), 2)]
    return parts[0]


def keep_at(starts, token):
    return (1 - starts[token]).astype(F32)


def with_rim(proj, rim, k, rows):
    rows[0:8] = rim[k]
    rows[8:] = proj[k]


def keeps_of(column):
    marks = column[...].astype(F32)
    one = 1.0 - marks
    two = one * jnp.concatenate([jnp.ones((1, 1), F32), one[: T - 1]])
    return one, two, 1.0 - jnp.max(marks, axis=0, keepdims=True)


def project_kernel(values, gain, weights, low, inverse, proj, proj_kept):
    v = values[...]
    inverse[...] = inverse_rms(v)
    low[...] = (v * inverse[...] * gain[...]).astype(BF16)
    for k in range(3):
        proj[k] = dot(low[...], weights[k])
        proj_kept[k] = proj[k]


def project(values, gain, weights):
    return pl.pallas_call(
        project_kernel,
        name="project",
        cost_estimate=taking(3),
        out_shape=(
            struct(T, D, dtype=BF16),
            struct(T, 1),
            struct(3, T, C),
            pltpu.HBM((3, T, C), F32),
        ),
        in_specs=[VMEM] * 3,
        out_specs=[VMEM] * 4,
        compiler_params=pltpu.CompilerParams(vmem_limit_bytes=12 * MIB),
    )(values, gain, weights)


def mix_kernel(proj, rim, gain, weights, taps, column, starts, poles, *refs):
    proj_rim, mixed, end, powers, kept, shifted_rows, driven = refs
    v = rim[...]
    v = v * inverse_rms(v) * gain[...]
    low = jnp.concatenate([v, v]).astype(BF16)
    for k in range(3):
        proj_rim[k] = dot(low, weights[k])[:8]
        kept[k, :T], kept[k, T:] = proj[k], proj_rim[k]
    mix_end(kept, taps, column, starts, poles, mixed, end, powers, shifted_rows, driven)


def mix_end(kept, taps, column, starts, poles, mixed, end, powers, rows, driven):
    one, two, is_open = keeps_of(column)
    for k in range(3):
        rows[0:8], rows[8:] = kept[k, T:], kept[k, :T]
        mixed[k] = (
            taps[k, 0:1] * kept[k, :T]
            + taps[k, 1:2] * (one * rows[7 : 7 + T])
            + taps[k, 2:3] * (two * rows[6 : 6 + T])
        )
    driven[...] = mixed[1] * mixed[2]
    pre, pim = poles[0], poles[1]

    def run(group, state, masked):
        source = driven[eight(group), :]
        re, im = state
        for r in range(8):
            if masked:
                keep = keep_at(starts, group * 8 + r)
                re, im = re * keep, im * keep
            re, im = pre * re - pim * im + source[r : r + 1], pre * im + pim * re
        return re, im

    zero = jnp.zeros((N, C), F32)
    end[0:N], end[N : 2 * N] = scan_groups(T // 8, starts, 0, run, (zero, zero), False)
    end[2 * N :] = jnp.broadcast_to(is_open, (8, C))
    power = (pre, pim)
    for n in range(1, 12):
        power = times(power, power)
        if n in (8, 9, 11):
            at = {8: 0, 9: 2, 11: 4}[n]
            powers[at], powers[at + 1] = power


def mix(proj, rim, gain, weights, taps, column, starts, poles):
    return pl.pallas_call(
        mix_kernel,
        name="mix",
        cost_estimate=taking(5),
        out_shape=(
            struct(3, 8, C),
            pltpu.HBM((3, T, C), F32),
            struct(2 * N + 8, C),
            struct(6, N, C),
        ),
        in_specs=[VMEM] * 6 + [SMEM, VMEM],
        out_specs=(VMEM,) * 4,
        scratch_shapes=[
            pltpu.VMEM((3, T + 8, C), F32),
            pltpu.VMEM((T + 8, C), F32),
            pltpu.VMEM((T, C), F32),
        ],
        compiler_params=pltpu.CompilerParams(vmem_limit_bytes=22 * MIB),
    )(proj, rim, gain, weights, taps, column, starts, poles)


def forward_rows(mixed, starts, poles, block, state, visit, finish=None):
    pre, pim = poles[0], poles[1]
    base = block * BLOCK

    def run(group, kept, masked):
        source = mixed[1, eight(group), :] * mixed[2, eight(group), :]
        re, im = kept
        seen = []
        for r in range(8):
            if masked:
                keep = keep_at(starts, base + group * 8 + r)
                re, im = re * keep, im * keep
            re, im = pre * re - pim * im + source[r : r + 1], pre * im + pim * re
            seen.append(visit(group * 8 + r, re, im))
        if finish:
            finish(group, seen)
        return re, im

    state[0], state[1] = scan_groups(BLOCK // 8, starts, base, run, (state[0], state[1]), False)


def signal_kernel(mixed, starts, poles, residues, first, signal, gated, state):
    block = pl.program_id(0)

    @pl.when(block == 0)
    def _():
        state[...] = first[...]

    qre, qim = residues[0], residues[1]

    def visit(row, re, im):
        weighed = qre * re - qim * im
        return weighed[:8] + weighed[8:]

    def finish(group, seen):
        signal[eight(group), :] = row_sums(seen)

    forward_rows(mixed, starts, poles, block, state, visit, finish)
    gated[...] = (mixed[0] * signal[...]).astype(BF16)


def history_kernel(mixed, starts, poles, first, *rest):
    h0, h1, h2, h3, token, state = rest[-6:]
    block = pl.program_id(0)
    token[...] = jnp.zeros(token.shape, F32)

    @pl.when(block == 0)
    def _():
        state[...] = first[...]

    def visit(row, re, im):
        h0[row], h1[row] = re[:8], re[8:]
        h2[row], h3[row] = im[:8], im[8:]

    forward_rows(mixed, starts, poles, block, state, visit)


def signal_of(mixed, starts, poles, residues, first):
    return pl.pallas_call(
        signal_kernel,
        name="signal",
        cost_estimate=taking(6),
        grid=(BLOCKS,),
        out_shape=(struct(T, C), struct(T, C, dtype=BF16)),
        in_specs=[
            pl.BlockSpec((3, BLOCK, C), lambda i: (0, i, 0)),
            SMEM,
            whole(2, N, C),
            whole(2, N, C),
            whole(2, N, C),
        ],
        out_specs=(pl.BlockSpec((BLOCK, C), lambda i: (i, 0)),) * 2,
        scratch_shapes=[pltpu.VMEM((2, N, C), F32)],
        compiler_params=pltpu.CompilerParams(vmem_limit_bytes=8 * MIB),
    )(mixed, starts, poles, residues, first)


def history_of(mixed, starts, poles, first, *after):
    return pl.pallas_call(
        history_kernel,
        name="state_history",
        cost_estimate=taking(8),
        grid=(BLOCKS,),
        out_shape=(pltpu.HBM((T, 8, C), F32),) * 4 + (struct(8, 128),),
        in_specs=[
            pl.BlockSpec((3, BLOCK, C), lambda i: (0, i, 0)),
            SMEM,
            whole(2, N, C),
            whole(2, N, C),
        ]
        + [ANY] * len(after),
        out_specs=(pl.BlockSpec((BLOCK, 8, C), lambda i: (i, 0, 0)),) * 4 + (whole(8, 128),),
        scratch_shapes=[pltpu.VMEM((2, N, C), F32)],
        compiler_params=pltpu.CompilerParams(vmem_limit_bytes=11 * MIB),
    )(in_hbm(mixed), starts, poles, first, *after)


def adjoint_kernel(grad_gated, query, column, starts, poles, residues, out, grads):
    grads[...] = grad_gated[...] * query[0]
    pre, pim, qre, qim = poles[0], poles[1], residues[0], residues[1]

    def run(group, kept, masked):
        source = grads[eight(group), :]
        re, im = kept
        for r in reversed(range(8)):
            row = source[r : r + 1]
            re, im = row * qre + (pre * re + pim * im), (pre * im - pim * re) - row * qim
            if masked:
                keep = keep_at(starts, group * 8 + r)
                re, im = re * keep, im * keep
        return re, im

    zero = jnp.zeros((N, C), F32)
    out[0:N], out[N : 2 * N] = scan_groups(T // 8, starts, 0, run, (zero, zero), True)
    out[2 * N :] = jnp.broadcast_to(keeps_of(column)[2], (8, C))


def adjoint_end(grad_gated, mixed, column, starts, poles, residues):
    return pl.pallas_call(
        adjoint_kernel,
        name="adjoint_end",
        cost_estimate=taking(4),
        grid=(1,),
        out_shape=struct(2 * N + 8, C),
        in_specs=[
            whole(T, C),
            pl.BlockSpec((1, T, C), lambda i: (0, 0, 0)),
            whole(T, 1),
            SMEM,
            whole(2, N, C),
            whole(2, N, C),
        ],
        out_specs=whole(2 * N + 8, C),
        scratch_shapes=[pltpu.VMEM((T, C), F32)],
        compiler_params=pltpu.CompilerParams(vmem_limit_bytes=9 * MIB),
    )(grad_gated, mixed, column, starts, poles, residues)


def back_kernel(
    grad_gated,
    mixed,
    signal,
    proj,
    proj_rim,
    h0,
    h1,
    h2,
    h3,
    taps,
    column,
    starts,
    poles,
    residues,
    first,
    *rest,
):
    grad_proj, rim, sums, state, driven_grad, mixed_grad, rows_before = rest[-7:]
    step = pl.program_id(0)
    block = BLOCKS - 1 - step

    @pl.when(step == 0)
    def _():
        state[...] = first[...]
        sums[...] = jnp.zeros(sums.shape, F32)

    base = block * BLOCK
    for part in range(PARTS):
        columns = slice(C // PARTS * part, C // PARTS * (part + 1))
        pre, pim = poles[0, :, columns], poles[1, :, columns]
        qre, qim = residues[0, :, columns], residues[1, :, columns]

        def run(group, kept, masked):
            rows = pl.ds(pl.multiple_of(base + group * 8, 8), 8)
            source = grad_gated[rows, columns] * mixed[0, rows, columns]
            re, im, pole_re, pole_im, res_re, res_im = kept
            seen = [None] * 8
            for r in reversed(range(8)):
                row = source[r : r + 1]
                token = group * 8 + r
                sre = jnp.concatenate([h0[token, :, columns], h1[token, :, columns]])
                sim = jnp.concatenate([h2[token, :, columns], h3[token, :, columns]])
                pole_re += re * sre + im * sim
                pole_im += im * sre - re * sim
                res_re += row * sre
                res_im -= row * sim
                re, im = row * qre + (pre * re + pim * im), (pre * im - pim * re) - row * qim
                seen[r] = re[:8] + re[8:]
                if masked:
                    keep = keep_at(starts, base + group * 8 + r)
                    re, im = re * keep, im * keep
            driven_grad[rows, columns] = row_sums(seen)
            return re, im, pole_re, pole_im, res_re, res_im

        zero = jnp.zeros((N, C // PARTS), F32)
        kept = (state[0, :, columns], state[1, :, columns], zero, zero, zero, zero)
        kept = scan_groups(BLOCK // 8, starts, base, run, kept, True)
        state[0, :, columns], state[1, :, columns] = kept[:2]
        for n in range(4):
            sums[N * n : N * n + N, columns] += kept[2 + n]

    @pl.when(step == BLOCKS - 1)
    def _():
        one, two, _ = keeps_of(column)
        mixed_grad[0, 0:T] = grad_gated[...] * signal[...]
        mixed_grad[1, 0:T] = driven_grad[...] * mixed[2]
        mixed_grad[2, 0:T] = driven_grad[...] * mixed[1]
        for k in range(3):
            with_rim(proj, proj_rim, k, rows_before)
            here = mixed_grad[k, 0:T]
            sums[64 + 3 * k : 65 + 3 * k] = jnp.sum(here * proj[k], axis=0, keepdims=True)
            grad_proj[k] = taps[k, 0:1] * here
            here = one * mixed_grad[k, 0:T]
            sums[65 + 3 * k : 66 + 3 * k] = jnp.sum(here * rows_before[7 : 7 + T], axis=0, keepdims=True)
            mixed_grad[k, 0:T] = two * mixed_grad[k, 0:T]
            here = taps[k, 1:2] * here
            grad_proj[k, 0 : T - 1] += here[1:T]
            rim[k] = jnp.zeros((8, C), F32)
            rim[k, 1:2] = here[0:1]
            here = mixed_grad[k, 0:T]
            sums[66 + 3 * k : 67 + 3 * k] = jnp.sum(here * rows_before[6 : 6 + T], axis=0, keepdims=True)
            here = taps[k, 2:3] * here
            grad_proj[k, 0 : T - 2] += here[2:T]
            rim[k, 0:2] += here[0:2]


def back(grad_gated, mixed, signal, proj, proj_rim, history, taps, column, starts, poles, residues, first, *after):
    return pl.pallas_call(
        back_kernel,
        name="adjoint_and_short_back",
        cost_estimate=taking(13),
        grid=(BLOCKS,),
        out_shape=(struct(3, T, C), struct(3, 8, C), struct(80, C)),
        in_specs=[
            whole(T, C),
            whole(3, T, C),
            whole(T, C),
            whole(3, T, C),
            whole(3, 8, C),
        ]
        + [pl.BlockSpec((BLOCK, 8, C), lambda i: (BLOCKS - 1 - i, 0, 0))] * 4
        + [
            whole(3, 3, C),
            whole(T, 1),
            SMEM,
            whole(2, N, C),
            whole(2, N, C),
            whole(2, N, C),
        ]
        + [ANY] * len(after),
        out_specs=(whole(3, T, C), whole(3, 8, C), whole(80, C)),
        scratch_shapes=[
            pltpu.VMEM((2, N, C), F32),
            pltpu.VMEM((T, C), F32),
            pltpu.VMEM((3, T, C), F32),
            pltpu.VMEM((T + 8, C), F32),
        ],
        compiler_params=pltpu.CompilerParams(vmem_limit_bytes=25 * MIB),
    )(
        grad_gated,
        mixed,
        signal,
        proj,
        proj_rim,
        *history,
        taps,
        column,
        starts,
        poles,
        residues,
        first,
        *after,
    )


def swap(value, axis, mask):
    size = lax.axis_size(axis)
    return lax.ppermute(value, axis, [(i, i ^ mask) for i in range(size)])


def shifted(value, axis, steps):
    count = lax.axis_size(axis)
    first, last = max(0, -steps), min(count, count - steps)
    return lax.ppermute(value, axis, [(i, i + steps) for i in range(first, last)])


def pair_add_kernel(left, got_left, right, got_right, *rest):
    left_own, left_next, right_own, right_next = rest[-4:]
    left_own[...] = left[:ROWS] + got_left[:ROWS]
    left_next[...] = left[ROWS:] + got_left[ROWS:]
    right_own[...] = right[:ROWS] + got_right[:ROWS]
    right_next[...] = right[ROWS:] + got_right[ROWS:]


def pair_call(name, kernel, shapes, operands, after):
    return pl.pallas_call(
        kernel,
        name=name,
        cost_estimate=taking(0.8),
        out_shape=shapes,
        in_specs=[VMEM] * len(operands) + [ANY] * len(after),
        out_specs=[VMEM] * len(shapes),
        compiler_params=pltpu.CompilerParams(vmem_limit_bytes=10 * MIB),
    )(*operands, *after)


def scatter_end(pieces, got_left, got_right, *after, shape=struct):
    left_own, left_next, right_own, right_next = pair_call(
        "pair_add",
        pair_add_kernel,
        [shape(ROWS, HALF)] * 4,
        (pieces[0], got_left, pieces[2], got_right),
        after,
    )
    return left_own, swap(left_next, "tp", 3), right_own, swap(right_next, "tp", 1)


def scatter_start(pieces):
    return swap(pieces[1], "tp", 1), swap(pieces[3], "tp", 3)


def in_hbm_struct(*shape):
    return pltpu.HBM(shape, F32)


def scatter_sum(pieces, *after, shape=struct):
    return scatter_end(pieces, *scatter_start(pieces), *after, shape=shape)


def pair_join_kernel(left, left_3, right, right_1, *rest):
    left_03, right_10 = rest[-2:]
    rows = left.shape[0]
    left_03[:rows], left_03[rows:] = left[...], left_3[...]
    right_10[:rows], right_10[rows:] = right_1[...], right[...]


def gather_joined(left, right, *after):
    return joined_parts(left, swap(left, "tp", 3), right, swap(right, "tp", 1), *after)


def joined_parts(left, left_3, right, right_1, *after):
    left_03, right_10 = pair_call(
        "pair_join",
        pair_join_kernel,
        [struct(2 * left.shape[0], HALF)] * 2,
        (left, left_3, right, right_1),
        after,
    )
    parts = left, swap(left_03, "tp", 1), left_3, right, right_1, swap(right_10, "tp", 3)
    return parts, (left_03, right_10)


def gather_parts(left, right, *after):
    return gather_joined(left, right, *after)[0]


def quarters_of(parts):
    left, left_12, left_3, right, right_1, right_23 = parts
    rows = left.shape[0]
    return (
        (left[:rows], right[:rows]),
        (left_12[:rows], right_1[:rows]),
        (left_12[rows:], right_23[:rows]),
        (left_3[:rows], right_23[rows:]),
    )


def of_payload(ref):
    return (ref[0:N], ref[N : 2 * N]), ref[2 * N : 2 * N + 1]


def to_payload(ref, state, is_open):
    ref[0:N], ref[N : 2 * N] = state
    ref[2 * N :] = jnp.broadcast_to(is_open, (8, C))


def power_of(powers, at, reverse):
    return powers[at], -powers[at + 1] if reverse else powers[at + 1]


def chip_kernel(reverse, place, mine, other, powers, out):
    (state, is_open), (state_other, open_other) = of_payload(mine), of_payload(other)
    by_device = power_of(powers, 0, reverse)
    last = place[1] == (0 if reverse else 1)
    earlier = where2(last, state_other, state)
    later = where2(last, state, state_other)
    later_open = jnp.where(last, is_open, open_other)
    chip = plus(later, times(scaled(by_device, later_open), earlier))
    to_payload(out, chip, is_open * open_other)


def plane_kernel(reverse, place, mine, got_1, got_2, got_3, powers, *rest):
    out, before = rest[-2:]
    chip, is_open = of_payload(mine)
    by_chip = power_of(powers, 2, reverse)
    got = {1: of_payload(got_1), 2: of_payload(got_2), 3: of_payload(got_3)}
    y = 3 - place[2] if reverse else place[2]
    one, zero = jnp.ones((N, C), F32), jnp.zeros((N, C), F32)
    entering, weight = (zero, zero), (one, zero)
    for k in (1, 2, 3):
        state, opened = got[k]
        entering = where2(y >= k, plus(entering, times(weight, state)), entering)
        weight = where2(y >= k, times(weight, scaled(by_chip, opened)), weight)
    plane = plus(chip, times(scaled(by_chip, is_open), entering))
    for j in (1, 2, 3):
        state, opened = got[4 - j]
        plane = where2(y + j <= 3, plus(state, times(scaled(by_chip, opened), plane)), plane)
        is_open = is_open * opened
    to_payload(out, plane, is_open)
    before[0], before[1] = entering
    before[2], before[3] = weight


def enter_kernel(reverse, place, before, got_1, got_2, got_3, other, powers, *rest):
    out = rest[-1]
    by_device, by_plane = power_of(powers, 0, reverse), power_of(powers, 4, reverse)
    one, zero = jnp.ones((N, C), F32), jnp.zeros((N, C), F32)
    entering, weight = (zero, zero), (one, zero)
    for ref in (got_1, got_2, got_3):
        state, opened = of_payload(ref)
        entering = plus(entering, times(weight, state))
        weight = times(weight, scaled(by_plane, opened))
    at_chip = plus((before[0], before[1]), times((before[2], before[3]), entering))
    state, opened = of_payload(other)
    at_core = plus(state, times(scaled(by_device, opened), at_chip))
    out[0], out[1] = where2(place[1] == (0 if reverse else 1), at_core, at_chip)


def small_call(name, kernel, reverse, shapes, operands, after=()):
    return pl.pallas_call(
        functools.partial(kernel, reverse),
        name=name,
        cost_estimate=taking(1.6),
        out_shape=shapes,
        in_specs=[SMEM] + [VMEM] * (len(operands) - 1) + [ANY] * len(after),
        out_specs=jax.tree.map(lambda _: VMEM, shapes),
        compiler_params=pltpu.CompilerParams(vmem_limit_bytes=8 * MIB),
    )(*operands, *after)


def carried_state(place, mine, powers, reverse, after=(), late=()):
    sign = -1 if reverse else 1
    payload = struct(2 * N + 8, C)
    other = swap(mine, "seq_2", 1)
    chip = small_call("chip_state", chip_kernel, reverse, payload, (place, mine, other, powers))
    got = [
        lax.ppermute(chip, "seq_1", [(i, (i + sign * k) % 4) for i in range(4)]) for k in (1, 2, 3)
    ]
    plane, before = small_call(
        "plane_state",
        plane_kernel,
        reverse,
        (payload, struct(4, N, C)),
        (place, chip, *got, powers),
        after,
    )
    got = [shifted(plane, "seq_0", sign * k) for k in (1, 2, 3)]
    entering = small_call(
        "entering_state",
        enter_kernel,
        reverse,
        struct(2, N, C),
        (place, before, *got, other, powers),
        late,
    )
    return entering


def sum_over(x, axis, *after):
    if lax.axis_size(axis) == 2:
        return x + swap(x, axis, 1)
    got = [swap(x, axis, k) for k in (1, 2, 3)]
    if after:
        got = [tie(g, *after) for g in got]
    return (x + got[0]) + (got[1] + got[2])


def inverse_rms(values):
    return lax.rsqrt(jnp.mean(values * values, axis=-1, keepdims=True) + epsilon)


def nothing(*refs):
    pass


def tie(x, *after, hbm=False):
    shape = struct(*x.shape, dtype=x.dtype)
    if hbm:
        x, shape = in_hbm(x), pltpu.HBM(x.shape, x.dtype)
    return pl.pallas_call(
        nothing,
        name="tie",
        out_shape=shape,
        in_specs=[ANY] * (1 + len(after)),
        out_specs=ANY,
        input_output_aliases={0: 0},
        compiler_params=pltpu.CompilerParams(vmem_limit_bytes=6 * MIB),
    )(x, *after)


WIDE = 1408


def wide_sum_kernel(left_a, l03, r10, l12, r23, left_b, more_b, right, wide, gain, out, token, both, rows_a, rows_b):
    step = pl.program_id(0)

    @pl.when(step == 0)
    def _():
        both[:T] = right[...]
        both[T:] = wide[...].astype(BF16)
        token[...] = jnp.zeros(token.shape, F32)

    def put(*quarters):
        rows_a[T:] = (jnp.concatenate(quarters) * gain[...]).astype(BF16)

    pl.when(step < 2)(lambda: put(l03[:ROWS], l12[:ROWS], l12[ROWS:], l03[ROWS:]))
    pl.when(step >= 2)(lambda: put(r10[ROWS:], r10[:ROWS], r23[:ROWS], r23[ROWS:]))
    rows_a[:T], rows_b[:T], rows_b[T:] = left_a[...], left_b[...], more_b[...]
    out[:, :WIDE] = token_sum(rows_a[...], both[:, :WIDE])
    out[:, WIDE:] = token_sum(rows_b[...], both[:, WIDE:])


def wide_token_sum(left_a, more_a, left_b, more_b, right, wide, gain):
    rows = 512
    column = pl.BlockSpec((T, rows), lambda i: (0, i))
    low = pl.BlockSpec((2 * ROWS, rows), lambda i: (0, jnp.minimum(i, 1)))
    high = pl.BlockSpec((2 * ROWS, rows), lambda i: (0, jnp.maximum(i - 2, 0)))
    width = right.shape[1]
    return pl.pallas_call(
        wide_sum_kernel,
        name="weight_gradients",
        cost_estimate=taking(10),
        grid=(D // rows,),
        out_shape=(pltpu.HBM((D, width), F32), struct(8, 128)),
        in_specs=[column, low, high, low, high, column, column]
        + [VMEM, VMEM, pl.BlockSpec((1, rows), lambda i: (0, i))],
        out_specs=(pl.BlockSpec((rows, width), lambda i: (i, 0)), whole(8, 128)),
        scratch_shapes=[
            pltpu.VMEM((2 * T, width), BF16),
            pltpu.VMEM((2 * T, rows), BF16),
            pltpu.VMEM((2 * T, rows), BF16),
        ],
        compiler_params=pltpu.CompilerParams(vmem_limit_bytes=21 * MIB),
    )(left_a, *more_a, left_b, more_b, right, wide, gain)


ORDERS = {1: (0, 3, 1, 2), 3: (0, 1, 3, 2)}
STREAMS = (("seq_1", 1), ("seq_1", 3), ("seq_0", 1), ("seq_0", 3))


def stream_places(step):
    jz, jy = divmod(step, 4)
    places = []
    for axis, mask in STREAMS:
        order = ORDERS[mask]
        first, second = (jy, jz) if axis == "seq_1" else (jz, jy)
        places.append(order.index(first) * 4 + order.index(second))
    return places


def stream_sum_kernel(
    place,
    left_a,
    more_a,
    left_b,
    more_b,
    right_a,
    wide_a,
    right_b,
    wide_b,
    sums,
    gains_a,
    gains_b,
    *rest,
):
    kept, sent, token, turned = rest[-10:-6], rest[-6:-2], rest[-2], rest[-1]
    token[...] = jnp.zeros(token.shape, F32)
    for s in range(4):
        kept[s][2048 : 2048 + 80] = sums[:, 128 * s : 128 * s + 128]
        for n in range(8):
            row = (gains_a, gains_b)[n // 4]
            at = C * (n % 4) + 128 * s
            kept[s][2128 + n : 2129 + n] = row[:, at : at + 128]
        sent[s][2048:] = kept[s][2048:]
    turned[0:768, 0:T] = right_a[...].T
    turned[768:, 0:T] = right_b[...].T
    turned[0:768, T:] = wide_a[...].astype(BF16).T
    turned[768:, T:] = wide_b[...].astype(BF16).T
    y, z = place[2], place[3]
    for step in range(16):
        jz, jy = divmod(step, 4)
        chunk = (z ^ jz) * 4 + (y ^ jy)
        columns = pl.ds(pl.multiple_of(chunk * 128, 128), 128)
        total_a = dot(turned[0:768, 0:T], left_a[:, columns]) + dot(turned[0:768, T:], more_a[:, columns])
        total_b = dot(turned[768:, 0:T], left_b[:, columns]) + dot(turned[768:, T:], more_b[:, columns])
        for s, at in enumerate(stream_places(step)):
            target = kept[s] if at < 8 else sent[s]
            rows = slice((at % 8) * 256, (at % 8) * 256 + 256)
            target[rows] = total_a[256 * s : 256 * s + 256] if s < 3 else total_b


def stream_token_sum(place, *operands):
    out = pl.pallas_call(
        stream_sum_kernel,
        name="mixer_weight_gradients",
        cost_estimate=taking(7),
        out_shape=(struct(2048 + SMALL, 128),) * 8 + (struct(8, 128),),
        in_specs=[SMEM] + [VMEM] * 11 + [ANY] * (len(operands) - 11),
        out_specs=(VMEM,) * 9,
        scratch_shapes=[pltpu.VMEM((1024, 2 * T), BF16)],
        compiler_params=pltpu.CompilerParams(vmem_limit_bytes=8 * MIB),
    )(place, *operands)
    return out[:4], out[4:8], out[8]


SMALL = 88


def stream_add_kernel(*refs):
    held, got, kept, sent = refs[0:4], refs[4:8], refs[-8:-4], refs[-4:]
    for s in range(4):
        rows = held[s].shape[0] - SMALL
        low = rows // 2
        small = held[s][rows:] + got[s][rows:]
        kept[s][0:low] = held[s][0:low] + got[s][0:low]
        kept[s][low:] = small
        sent[s][0:low] = held[s][low:rows] + got[s][low:rows]
        sent[s][low:] = small


def stream_add(held, got, *after):
    rows = held[0].shape[0] - SMALL
    shape = struct(rows // 2 + SMALL, 128)
    out = pl.pallas_call(
        stream_add_kernel,
        name="stream_add",
        cost_estimate=taking(0.7 + rows / 1000),
        out_shape=[shape] * 8,
        in_specs=[VMEM] * 8 + [ANY] * len(after),
        out_specs=[VMEM] * 8,
        compiler_params=pltpu.CompilerParams(vmem_limit_bytes=6 * MIB),
    )(*held, *got, *after)
    return out[:4], out[4:]


def stream_last_kernel(place, *refs):
    held, got, (own, send, small, gains) = refs[0:4], refs[4:8], refs[-4:]
    first = place[1] == 0
    for s in range(4):
        total = (held[s][0:256] + got[s][0:256]).T
        columns = slice(256 * s, 256 * s + 256)
        own[:, columns] = jnp.where(first, total[:64], total[64:])
        send[:, columns] = jnp.where(first, total[64:], total[:64])
        total = held[s][256:] + got[s][256:]
        small[:, 128 * s : 128 * s + 128] = total[:80]
        gains[:, 128 * s : 128 * s + 128] = total[80:]


def stream_last(place, held, got, *after):
    return pl.pallas_call(
        stream_last_kernel,
        name="stream_last",
        cost_estimate=taking(1.5),
        out_shape=(struct(64, 1024), struct(64, 1024), struct(80, C), struct(8, C)),
        in_specs=[SMEM] + [VMEM] * 8 + [ANY] * len(after),
        out_specs=[VMEM] * 4,
        compiler_params=pltpu.CompilerParams(vmem_limit_bytes=6 * MIB),
    )(place, *held, *got, *after)


def stream_masks(axis, mask):
    other = "seq_0" if axis == "seq_1" else "seq_1"
    return ((axis, mask), (axis, 4 - mask), (other, mask), (other, 4 - mask))


def stream_swap(sent, step):
    return [swap(x, *stream_masks(*STREAMS[s])[step]) for s, x in enumerate(sent)]


def mixer_shares_kernel(place, own, got, small, small_got, *rest):
    grad_in, grad_out, small_sum = rest[-3:]
    first = place[1] == 0
    low = jnp.where(first, own[...], got[...])
    high = jnp.where(first, got[...], own[...])
    for k in range(3):
        columns = slice(256 * k, 256 * k + 256)
        grad_in[k, :, :256], grad_in[k, :, 256:] = low[:, columns], high[:, columns]
    grad_out[:, :256], grad_out[:, 256:] = low[:, 768:], high[:, 768:]
    small_sum[...] = small[...] + small_got[...]


def mixer_shares(place, own, got, small, small_got, *after):
    return pl.pallas_call(
        mixer_shares_kernel,
        name="mixer_shares",
        cost_estimate=taking(1.5),
        out_shape=(struct(3, 64, C), struct(64, C), struct(80, C)),
        in_specs=[SMEM] + [VMEM] * 4 + [ANY] * len(after),
        out_specs=[VMEM] * 3,
        compiler_params=pltpu.CompilerParams(vmem_limit_bytes=6 * MIB),
    )(place, own, got, small, small_got, *after)


def ffn_send_kernel(place, share, *rest):
    own, send = rest[-2:]
    first = place[1] == 0
    low, high = share[:64], share[64:]
    own[...] = jnp.where(first, low, high)
    send[...] = jnp.where(first, high, low)


def ffn_shares_kernel(place, own, got, *rest):
    gate, up, down, token = rest[-4:]
    first = place[1] == 0
    low = jnp.where(first, own[...], got[...])
    high = jnp.where(first, got[...], own[...])
    gate[:, :768], gate[:, 768:] = low[:, :768], high[:, 768:1408]
    up[:, :640], up[:, 640:] = low[:, 768:1408], high[:, :768]
    down[:, :768], down[:, 768:] = low[:, 1408:], high[:, 1408 + 128 :]
    token[...] = jnp.zeros(token.shape, F32)


def ffn_halves(place, share, *after):
    return pl.pallas_call(
        ffn_send_kernel,
        name="ffn_send",
        cost_estimate=taking(1),
        out_shape=(struct(64, 2176),) * 2,
        in_specs=[SMEM, VMEM] + [ANY] * len(after),
        out_specs=[VMEM] * 2,
        compiler_params=pltpu.CompilerParams(vmem_limit_bytes=6 * MIB),
    )(place, share, *after)


def ffn_shares(place, own, got, *after):
    return pl.pallas_call(
        ffn_shares_kernel,
        name="ffn_shares",
        cost_estimate=taking(2),
        out_shape=(struct(64, 1408),) * 3 + (struct(8, 128),),
        in_specs=[SMEM, VMEM, VMEM] + [ANY] * len(after),
        out_specs=[VMEM] * 4,
        compiler_params=pltpu.CompilerParams(vmem_limit_bytes=8 * MIB),
    )(place, own, got, *after)


def norm_kernel(values, gain, *rest):
    out, inverse = rest[-2:]
    v = values[...]
    inverse[...] = inverse_rms(v)
    out[...] = (v * inverse[...] * gain[...]).astype(BF16)


def normed(values, gain, *after):
    rows = 128
    row = pl.BlockSpec((rows, D), lambda i: (i, 0))
    return pl.pallas_call(
        norm_kernel,
        name="normed_in",
        cost_estimate=taking(1.8),
        grid=(values.shape[0] // rows,),
        out_shape=(struct(*values.shape, dtype=BF16), struct(values.shape[0], 1)),
        in_specs=[row, whole(1, D)] + [ANY] * len(after),
        out_specs=(row, pl.BlockSpec((rows, 1), lambda i: (i, 0))),
        compiler_params=pltpu.CompilerParams(vmem_limit_bytes=11 * MIB),
    )(values, gain, *after)


HALF = D // 2


def rows_by_quarter(place, ref):
    return jnp.concatenate([ref[quarter_rows(place[0] ^ q), :] for q in range(4)])


def cotangent_kernel(place, cotangent, w_down, *rest):
    low, grad_hidden = rest[-2:]

    @pl.when(pl.program_id(0) == 0)
    def _():
        for q in range(4):
            low[ROWS * q : ROWS * q + ROWS] = cotangent[quarter_rows(place[0] ^ q), :].astype(BF16)

    grad_hidden[...] = dot_t(low[...], w_down[...])


def cotangent_part(place, cotangent, w_down, *after):
    wide = w_down.shape[0]
    return pl.pallas_call(
        cotangent_kernel,
        name="cotangent_part",
        cost_estimate=taking(4),
        grid=(6,),
        out_shape=(struct(T, D, dtype=BF16), struct(T, wide)),
        in_specs=[SMEM, VMEM, pl.BlockSpec((256, D), lambda i: (i, 0))] + [ANY] * len(after),
        out_specs=(VMEM, pl.BlockSpec((T, 256), lambda i: (0, i))),
        compiler_params=pltpu.CompilerParams(vmem_limit_bytes=9 * MIB),
    )(place, cotangent, w_down, *after)


def out_parts_kernel(place, gated, *rest):
    own, send = rest[-2:]
    first = place[1] == 0
    rows = rows_by_quarter(place, gated).astype(F32)
    low, high = rows[:, :256], rows[:, 256:]
    own[...] = jnp.where(first, low, high).astype(BF16)
    send[...] = jnp.where(first, high, low)


def out_parts(place, gated, *after):
    return pl.pallas_call(
        out_parts_kernel,
        name="out_parts",
        cost_estimate=taking(1),
        out_shape=(struct(T, 256, dtype=BF16), struct(T, 256)),
        in_specs=[SMEM, VMEM] + [ANY] * len(after),
        out_specs=[VMEM] * 2,
        compiler_params=pltpu.CompilerParams(vmem_limit_bytes=7 * MIB),
    )(place, gated, *after)


def owner_kernel(place, rows, *rest):
    rest[-1][...] = rows[...].astype(BF16)


def owner_rows(place, x, *after):
    row = pl.BlockSpec((ROWS, D), lambda i, place: (place[0] ^ i, 0))
    out = pl.BlockSpec((ROWS, D), lambda i, place: (i, 0))
    return pl.pallas_call(
        owner_kernel,
        name="owner_rows",
        cost_estimate=taking(2),
        out_shape=pltpu.HBM((T, D), BF16),
        grid_spec=pltpu.PrefetchScalarGridSpec(
            num_scalar_prefetch=1, grid=(4,), in_specs=[row] + [ANY] * len(after), out_specs=out
        ),
        compiler_params=pltpu.CompilerParams(vmem_limit_bytes=9 * MIB),
    )(place, in_hbm(x), *after)


def branch_other_kernel(place, cotangent, through, out):
    out[...] = (cotangent[...] + through[...]).astype(BF16)


def branch_other_of(place, cotangent, through):
    row = pl.BlockSpec((ROWS, D), lambda i, place: (i, 0))
    return pl.pallas_call(
        branch_other_kernel,
        name="branch_other",
        cost_estimate=taking(2),
        out_shape=struct(T, D, dtype=BF16),
        grid_spec=pltpu.PrefetchScalarGridSpec(
            num_scalar_prefetch=1,
            grid=(4,),
            in_specs=[pl.BlockSpec((ROWS, D), lambda i, place: (place[0] ^ i, 0)), row],
            out_specs=row,
        ),
        compiler_params=pltpu.CompilerParams(vmem_limit_bytes=9 * MIB),
    )(place, in_hbm(cotangent), through)


def middle_kernel(place, left, left_more, right, right_more, hidden, *rest):
    middle, out_left, out_right = rest[-3:]
    low = hidden[:, :HALF] + (left[...] + left_more[...])
    high = hidden[:, HALF:] + (right[...] + right_more[...])
    square = jnp.sum(low * low, axis=-1, keepdims=True) + jnp.sum(high * high, axis=-1, keepdims=True)
    inverse = lax.rsqrt(square * (1.0 / D) + epsilon)
    middle[:, :HALF], middle[:, HALF:] = low, high
    out_left[...], out_right[...] = low * inverse, high * inverse


def norm_back_parts(left, left_more, right, right_more, values, gain):
    grads = (left[...] + left_more[...], right[...] + right_more[...])
    v = (values[:, :HALF], values[:, HALF:])
    g = (gain[:, :HALF], gain[:, HALF:])
    square = sum(jnp.sum(x * x, axis=-1, keepdims=True) for x in v)
    inverse = lax.rsqrt(square * (1.0 / D) + epsilon)
    along = sum(jnp.sum(a * b * c, axis=-1, keepdims=True) for a, b, c in zip(g, grads, v))
    along = inverse * inverse * inverse * (along * (1.0 / D))
    back = [inverse * g[n] * grads[n] - v[n] * along for n in (0, 1)]
    return back, [grads[n] * (v[n] * inverse) for n in (0, 1)]


def norm_back_kernel(left, left_more, right, right_more, values, gain, *rest):
    out_left, out_right, gains = rest[-3:]
    back, weighed = norm_back_parts(left, left_more, right, right_more, values, gain)
    out_left[...], out_right[...] = back
    for n in (0, 1):
        gains[:, HALF * n : HALF * n + HALF] = jnp.sum(weighed[n], axis=0, keepdims=True)


def by_owner_grid(in_specs, out_specs):
    return pltpu.PrefetchScalarGridSpec(
        num_scalar_prefetch=1, grid=(1,), in_specs=in_specs, out_specs=out_specs
    )


MINE = pl.BlockSpec((ROWS, D), lambda i, place: (place[0], 0))


def after_middle(place, pieces, hidden, *after):
    return pl.pallas_call(
        middle_kernel,
        name="middle_and_norm",
        cost_estimate=taking(1.5),
        out_shape=(pltpu.HBM((ROWS, D), F32), struct(ROWS, HALF), struct(ROWS, HALF)),
        grid_spec=by_owner_grid([VMEM] * 4 + [MINE] + [ANY] * len(after), (VMEM,) * 3),
        compiler_params=pltpu.CompilerParams(vmem_limit_bytes=8 * MIB),
    )(place, *pieces, in_hbm(hidden), *after)


def norm_back(pieces, values, gain, *after):
    return pl.pallas_call(
        norm_back_kernel,
        name="norm_back",
        cost_estimate=taking(2),
        out_shape=(struct(ROWS, HALF), struct(ROWS, HALF), struct(1, D)),
        grid=(1,),
        in_specs=[whole(ROWS, HALF)] * 4 + [whole(ROWS, D), whole(1, D)] + [ANY] * len(after),
        out_specs=(VMEM,) * 3,
        compiler_params=pltpu.CompilerParams(vmem_limit_bytes=9 * MIB),
    )(*pieces, values, gain, *after)


def rim_kernel(starts, rows, *rest):
    out = rest[-1]
    at = lax.broadcasted_iota(jnp.int32, (8, D), 0)
    out[...] = jnp.where(at == 6, rows[...] * keep_at(starts, T - 1), rows[...])


def rim_rows_of(starts, hidden, weights, *after):
    return pl.pallas_call(
        rim_kernel,
        name="rim_rows",
        cost_estimate=taking(1),
        grid=(1,),
        out_shape=struct(8, D),
        in_specs=[SMEM, pl.BlockSpec((8, D), lambda i: (T // 8 - 1, 0)), VMEM] + [ANY] * len(after),
        out_specs=whole(8, D),
        compiler_params=pltpu.CompilerParams(vmem_limit_bytes=6 * MIB),
    )(starts, in_hbm(hidden), weights, *after)


PIECES = ((0, 3), (1, 2), (0, 1), (3, 2))
PIECE_SHAPES = (struct(2 * ROWS, HALF),) * 4


def put_pieces(place, block, total, outs, by_owner=False):
    which, columns = block // 2, slice(512 * (block % 2), 512 * (block % 2) + 512)
    for n in (0, 1):
        out, quarters = outs[2 * which + n], PIECES[2 * which + n]
        for m, q in enumerate(quarters):
            rows = slice(ROWS * q, ROWS * q + ROWS) if by_owner else quarter_rows(place[0] ^ q)
            out[ROWS * m : ROWS * m + ROWS, columns] = total[rows, :]


def split_kernel(compute, by_owner, count, place, *refs):
    *outs, total = refs[-5:]
    for block in range(4):
        total[...] = compute(slice(512 * block, 512 * block + 512), *refs[:count])
        put_pieces(place, block, total, outs, by_owner)


def split_dot(name, compute, by_owner, place, *operands, after=()):
    return pl.pallas_call(
        functools.partial(split_kernel, compute, by_owner, len(operands)),
        name=name,
        cost_estimate=taking(2.5),
        out_shape=PIECE_SHAPES,
        in_specs=[SMEM] + [VMEM] * len(operands) + [ANY] * len(after),
        out_specs=[VMEM] * 4,
        scratch_shapes=[pltpu.VMEM((T, 512), F32)],
        compiler_params=pltpu.CompilerParams(vmem_limit_bytes=8 * MIB),
    )(place, *operands, *after)


def result_kernel(place, hidden, w_down, middle, *rest):
    out, token = rest[-2:]
    token[...] = jnp.zeros(token.shape, F32)
    for block in range(4):
        columns = slice(512 * block, 512 * block + 512)
        total = dot(hidden[...], w_down[:, columns])
        for q in range(4):
            rows = total[ROWS * q : ROWS * q + ROWS]
            out[quarter_rows(place[0] ^ q), columns] = rows + middle[:, columns] if q == 0 else rows


def result_part(place, hidden, w_down, middle, *after):
    return pl.pallas_call(
        result_kernel,
        name="result_part",
        cost_estimate=taking(2.5),
        out_shape=(pltpu.HBM((T, D), F32), struct(8, 128)),
        in_specs=[SMEM] + [VMEM] * 3 + [ANY] * len(after),
        out_specs=(VMEM, VMEM),
        compiler_params=pltpu.CompilerParams(vmem_limit_bytes=10 * MIB),
    )(place, hidden, w_down, middle, *after)


def ffn_kernel(place, *refs):
    parts, refs = refs[:6], refs[6:]
    gain, w_gate, w_up, grad_hidden = refs[:4]
    mid_x, hidden, grad_gate, grad_up, own_all, send_all = refs[-6:]
    for q, (left, right) in enumerate(quarters_of(parts)):
        rows = slice(ROWS * q, ROWS * q + ROWS)
        mid_x[rows, :HALF] = (left * gain[:, :HALF]).astype(BF16)
        mid_x[rows, HALF:] = (right * gain[:, HALF:]).astype(BF16)
    wide = w_gate.shape[1]
    for start in range(0, wide, 256):
        columns = slice(start, min(start + 256, wide))
        gate = dot(mid_x[...], w_gate[:, columns])
        up = dot(mid_x[...], w_up[:, columns])
        sig = 1.0 / (1.0 + jnp.exp(-gate))
        silu = gate * sig
        incoming = grad_hidden[:, columns]
        hidden[:, columns] = (silu * up).astype(BF16)
        grad_gate[:, columns] = (incoming * up * sig * (1.0 + gate * (1.0 - sig))).astype(BF16)
        grad_up[:, columns] = (incoming * silu).astype(BF16)
    first = place[1] == 0

    def halves(columns, low, high):
        a, b = low.astype(F32), high.astype(F32)
        own_all[:, columns] = jnp.where(first, a, b).astype(BF16)
        send_all[:, columns] = jnp.where(first, b, a)

    halves(slice(0, 768), grad_gate[:, :768], grad_up[:, 640:1408])
    halves(slice(768, 1408), grad_up[:, :640], grad_gate[:, 768:1408])
    halves(slice(1408, 2176), hidden[:, :768], hidden[:, 640:1408])


def feed_forward(place, parts, gain, w_gate, w_up, grad_hidden, *after):
    wide = w_gate.shape[1]
    low = struct(T, wide, dtype=BF16)
    return pl.pallas_call(
        ffn_kernel,
        name="feed_forward",
        cost_estimate=taking(7),
        out_shape=(
            struct(T, D, dtype=BF16),
            low,
            low,
            low,
            struct(T, wide + 768, dtype=BF16),
            struct(T, wide + 768),
        ),
        in_specs=[SMEM] + [VMEM] * 10 + [ANY] * len(after),
        out_specs=(VMEM,) * 6,
        compiler_params=pltpu.CompilerParams(vmem_limit_bytes=10 * MIB),
    )(place, *parts, gain, w_gate, w_up, grad_hidden, *after)


def branch_back_kernel(place, *refs):
    parts, cotangent, w_out = refs[:6], *refs[6:8]
    through, branch, grad_gated = refs[-3:]
    for q, (left, right) in enumerate(quarters_of(parts)):
        rows = slice(ROWS * q, ROWS * q + ROWS)
        through[rows, :HALF], through[rows, HALF:] = left, right
    branch[...] = (rows_by_quarter(place, cotangent) + through[...]).astype(BF16)
    back = dot_t(branch[...], w_out[...])
    for q in range(4):
        grad_gated[quarter_rows(place[0] ^ q), :] = back[ROWS * q : ROWS * q + ROWS]


def branch_back(place, parts, cotangent, w_out, *after):
    return pl.pallas_call(
        branch_back_kernel,
        name="branch_back",
        cost_estimate=taking(3),
        out_shape=(struct(T, D), pltpu.HBM((T, D), BF16), struct(T, C)),
        in_specs=[SMEM] + [VMEM] * 8 + [ANY] * len(after),
        out_specs=(VMEM,) * 3,
        compiler_params=pltpu.CompilerParams(vmem_limit_bytes=8 * MIB),
    )(place, *parts, cotangent, w_out, *after)


def finish_kernel(place, starts, grads, rim, *rest):
    low, own, send = rest[-3:]
    first = place[1] == 0
    at = lax.broadcasted_iota(jnp.int32, (8, C), 0)
    for k in range(3):
        turned = jnp.concatenate([jnp.zeros((6, C), F32), rim[k, 0:2]])
        turned = jnp.where(at == 6, turned * keep_at(starts, T - 1), turned)
        low[k, : T - 16] = grads[k, : T - 16].astype(BF16)
        low[k, T - 16 :] = jnp.concatenate(
            [grads[k, T - 16 : T - 8], grads[k, T - 8 :] + turned]
        ).astype(BF16)
        a, b = low[k, :, :256].astype(F32), low[k, :, 256:].astype(F32)
        columns = slice(256 * k, 256 * k + 256)
        own[:, columns] = jnp.where(first, a, b).astype(BF16)
        send[:, columns] = jnp.where(first, b, a)


def finish_projected(place, starts, grads, rim, *after):
    return pl.pallas_call(
        finish_kernel,
        name="finish_projected",
        cost_estimate=taking(1.5),
        out_shape=(struct(3, T, C, dtype=BF16), pltpu.HBM((T, 768), BF16), struct(T, 768)),
        in_specs=[SMEM, SMEM, VMEM, VMEM] + [ANY] * len(after),
        out_specs=(VMEM,) * 3,
        compiler_params=pltpu.CompilerParams(vmem_limit_bytes=7 * MIB),
    )(place, starts, grads, rim, *after)


def first_kernel(place, grads, hidden, inverse, gain, w_in, cotangent, left, right, *rest):
    out, gains, total = rest[-3:]
    along = jnp.zeros((T, 1), F32)
    for block in range(4):
        columns = slice(512 * block, 512 * block + 512)
        part = sum(dot_t(grads[k], w_in[k, columns, :]) for k in range(3))
        weighed = part * (hidden[:, columns] * inverse[...])
        gains[:, columns] = jnp.sum(weighed, axis=0, keepdims=True)
        along += jnp.sum(weighed * gain[:, columns], axis=1, keepdims=True)
        total[:, columns] = part
    along = inverse[...] * inverse[...] * (along * (1.0 / D))
    mine = quarter_rows(place[0])
    for block in range(4):
        columns = slice(512 * block, 512 * block + 512)
        out[:, columns] = inverse[...] * (gain[:, columns] * total[:, columns]) - hidden[:, columns] * along
        side, own = (left, right)[block // 2], slice(512 * (block % 2), 512 * (block % 2) + 512)
        out[mine, columns] += cotangent[mine, columns] + side[:, own]


def first_back(place, grads, hidden, inverse, gain, w_in, cotangent, left, right, *after):
    return pl.pallas_call(
        first_kernel,
        name="first_back",
        cost_estimate=taking(4),
        out_shape=(pltpu.HBM((T, D), F32), struct(1, D)),
        in_specs=[SMEM] + [VMEM] * 8 + [ANY] * len(after),
        out_specs=[VMEM] * 2,
        scratch_shapes=[pltpu.VMEM((T, D), F32)],
        compiler_params=pltpu.CompilerParams(vmem_limit_bytes=14 * MIB),
    )(place, grads, hidden, inverse, gain, w_in, cotangent, left, right, *after)


def emit_kernel(first, second, *rest):
    first_out, second_out, token = rest[-3:]
    token[...] = jnp.zeros(token.shape, F32)
    first_out[...], second_out[...] = first[...], second[...]


def emit(first, second, *after):
    row = pl.BlockSpec((ROWS, D), lambda i: (i, 0))
    return pl.pallas_call(
        emit_kernel,
        name="emit",
        cost_estimate=taking(3),
        grid=(4,),
        out_shape=(struct(T, D), struct(T, D), struct(8, 128)),
        in_specs=[row, row] + [ANY] * len(after),
        out_specs=(row, row, whole(8, 128)),
        compiler_params=pltpu.CompilerParams(vmem_limit_bytes=9 * MIB),
    )(in_hbm(first), in_hbm(second), *after)


def per_device(
    hidden_in,
    cotangent,
    starts,
    norm_in,
    w_in,
    short_w,
    pole_pairs,
    residues,
    w_out,
    norm_mid,
    w_gate,
    w_up,
    w_down,
):
    place = jnp.stack(
        [lax.axis_index(axis) for axis in ("tp", "seq_2", "seq_1", "seq_0")]
    ).astype(jnp.int32)
    column = starts[:, None]
    gain_in, gain_mid = norm_in[None], norm_mid[None]

    def other_core(x):
        return swap(x, "seq_2", 1)

    rim_rows = rim_rows_of(starts, hidden_in, w_in, place, column)
    rim_rows = lax.ppermute(rim_rows, SEQ, [(i, i + 1) for i in range(31)])
    hidden_other = other_core(hidden_in)
    cotangent_other = other_core(cotangent)
    normed_in, inverse_in, proj_now, proj = project(hidden_in, gain_in, w_in)
    rim, mixed, end, powers = mix(
        proj_now, rim_rows, gain_in, w_in, short_w, column, starts, pole_pairs
    )
    entering = carried_state(place, end, powers, False)
    signal, gated = signal_of(mixed, starts, pole_pairs, residues, entering)

    branch = split_dot(
        "branch",
        lambda columns, a, b: dot(a[...], b[:, columns]),
        False,
        place,
        gated,
        w_out,
    )
    *history, history_token = history_of(mixed, starts, pole_pairs, entering, branch[1])
    out_right, out_send = out_parts(place, gated, branch[1])
    pieces = scatter_sum(branch, history_token, out_send)
    down_grad, grad_hidden = cotangent_part(place, cotangent, w_down, pieces[0])
    middle, mid_left, mid_right = after_middle(place, pieces, hidden_in, grad_hidden)

    normed_other, _ = normed(hidden_other, gain_in, mid_left)
    down_other = owner_rows(place, cotangent_other, mid_left)
    parts, joined = gather_joined(mid_left, mid_right, in_hbm(normed_other), in_hbm(down_other))
    mid_other = [other_core(x) for x in joined]
    mid_x, hidden, grad_gate, grad_up, own_all, send_all = feed_forward(
        place,
        parts,
        gain_mid,
        w_gate,
        w_up,
        grad_hidden,
        *mid_other,
    )
    mid_other += [other_core(parts[1]), other_core(parts[5])]
    mid_terms = split_dot(
        "mid_terms",
        lambda columns, a, b, c, d: dot_t(a[...], c[columns, :]) + dot_t(b[...], d[columns, :]),
        True,
        place,
        grad_gate,
        grad_up,
        w_gate,
        w_up,
        after=mid_other[2:],
    )

    ffn_sum, ffn_token = wide_token_sum(
        mid_x,
        mid_other,
        down_grad,
        down_other,
        own_all,
        other_core(tie(send_all, mid_terms[1])),
        gain_mid,
    )

    pieces = scatter_sum(mid_terms, ffn_token, shape=in_hbm_struct)
    share_ffn = lax.psum_scatter(
        tie(ffn_sum, pieces[0], hbm=True), ("seq_0", "seq_1"), scatter_dimension=0, tiled=True
    )
    left, left_more, right, right_more = pieces
    through_left, through_right, gains_mid = norm_back(
        (in_hbm(left), left_more, in_hbm(right), right_more), in_hbm(middle), gain_mid
    )
    result, part_token = result_part(place, hidden, w_down, middle, gains_mid)
    through_f, branch_grad, grad_gated = branch_back(
        place, gather_parts(through_left, through_right), cotangent, w_out, part_token
    )

    leaving = adjoint_end(grad_gated, mixed, column, starts, pole_pairs, residues)
    branch_other = branch_other_of(place, cotangent_other, other_core(through_f))
    returning = carried_state(place, leaving, powers, True, after=(in_hbm(branch_other),))
    grad_proj, rim_grad, sums = back(
        grad_gated,
        mixed,
        signal,
        proj,
        rim,
        history,
        short_w,
        column,
        starts,
        pole_pairs,
        residues,
        returning,
    )
    rim_back = lax.ppermute(rim_grad, SEQ, [(i + 1, i) for i in range(31)])

    projected_low, proj_own, proj_send = finish_projected(
        place, starts, grad_proj, rim_back
    )
    proj_wide = other_core(proj_send)
    grad_input, gains_in = first_back(
        place,
        projected_low,
        hidden_in,
        inverse_in,
        gain_in,
        w_in,
        cotangent,
        through_left,
        through_right,
    )
    result, grad_input = lax.psum((result, grad_input), "tp")
    kept, leaving_now, mixer_token = stream_token_sum(
        place,
        normed_in,
        normed_other,
        branch_grad,
        branch_other,
        proj_own,
        proj_wide,
        out_right,
        other_core(out_send),
        sums,
        gains_in,
        gains_mid,
    )
    got = stream_swap(leaving_now, 0)
    kept, leaving_now = stream_add(kept, got)
    got = stream_swap(leaving_now, 1)
    ffn_own, ffn_out = ffn_halves(place, share_ffn, kept[0])
    kept, leaving_now = stream_add(kept, got, ffn_own)
    got = stream_swap(leaving_now, 2)
    share_gate, share_up, share_down, shares_token = ffn_shares(
        place, ffn_own, other_core(ffn_out), kept[0]
    )
    kept, leaving_now = stream_add(kept, got, shares_token)
    got = stream_swap(leaving_now, 3)
    result, grad_input, output_token = emit(result, grad_input, kept[0])
    own, send, small, gains = stream_last(place, kept, got, output_token)
    share_in, share_out, small = mixer_shares(
        place, own, other_core(send), small, other_core(small)
    )
    gains = sum_over(sum_over(gains, "tp"), "seq_2")
    return (
        result,
        grad_input,
        gains[0:4].reshape(D),
        share_in,
        small[64:73].reshape(3, 3, C),
        small[0:32].reshape(2, N, C),
        small[32:64].reshape(2, N, C),
        share_out.T,
        gains[4:8].reshape(D),
        share_gate,
        share_up,
        share_down.T,
    )


def solution(mesh):
    split = Mesh(mesh.devices.reshape(4, 4, 2, mesh.shape["tp"]), ("seq_0", "seq_1", "seq_2", "tp"))
    in_specs = (
        P(SEQ, None),
        P(SEQ, None),
        P(SEQ),
        P(),
        P(None, None, "tp"),
        P(None, None, "tp"),
        P(None, None, "tp"),
        P(None, None, "tp"),
        P("tp", None),
        P(),
        P(None, "tp"),
        P(None, "tp"),
        P("tp", None),
    )
    out_specs = (
        P(SEQ, None),
        P(SEQ, None),
        P(),
        P(None, SEQ, "tp"),
        P(None, None, "tp"),
        P(None, None, "tp"),
        P(None, None, "tp"),
        P("tp", SEQ),
        P(),
        P(SEQ, "tp"),
        P(SEQ, "tp"),
        P("tp", SEQ),
    )
    return jax.shard_map(
        per_device, mesh=split, in_specs=in_specs, out_specs=out_specs, check_vma=False
    )
```

```python
import functools

import jax
import jax.numpy as jnp
from jax import lax
from jax.experimental import pallas as pl
from jax.experimental.pallas import tpu as pltpu
from jax.sharding import Mesh
from jax.sharding import PartitionSpec as P

SEQ = ("seq_0", "seq_1", "seq_2")
F32 = jnp.float32
BF16 = jnp.bfloat16
epsilon = 1e-06
MIB = 1 << 20
T, C, N, D = 256, 512, 16, 2048
BLOCK = 32
BLOCKS = T // BLOCK
PARTS = 1
ROWS = 64
VMEM = pl.BlockSpec(memory_space=pltpu.VMEM)
SMEM = pl.BlockSpec(memory_space=pltpu.SMEM)
ANY = pl.BlockSpec(memory_space=pl.ANY)


def in_hbm(x):
    return pltpu.with_memory_space_constraint(x, pltpu.HBM)


def taking(microseconds):
    return pl.CostEstimate(flops=0, bytes_accessed=int(microseconds * 3.0e6), transcendentals=0)


def whole(*shape):
    return pl.BlockSpec(shape, lambda i: (0,) * len(shape))


def struct(*shape, dtype=F32):
    return jax.ShapeDtypeStruct(shape, dtype)


def times(a, b):
    return a[0] * b[0] - a[1] * b[1], a[0] * b[1] + a[1] * b[0]


def plus(a, b):
    return a[0] + b[0], a[1] + b[1]


def where2(flag, a, b):
    return jnp.where(flag, a[0], b[0]), jnp.where(flag, a[1], b[1])


def scaled(a, factor):
    return a[0] * factor, a[1] * factor


def token_sum(a, b):
    return lax.dot_general(a, b, (((0,), (0,)), ((), ())), preferred_element_type=F32)


def dot(a, b):
    return jnp.dot(a, b, preferred_element_type=F32)


def dot_t(a, b):
    return lax.dot_general(a, b, (((1,), (1,)), ((), ())), preferred_element_type=F32)


def scan_groups(groups, starts, base, run, carry, reverse):
    def body(step, kept):
        group = groups - 1 - step if reverse else step
        first = base + group * 8
        marks = starts[first]
        for r in range(1, 8):
            marks = marks + starts[first + r]
        return lax.cond(
            marks > 0, lambda c: run(group, c, True), lambda c: run(group, c, False), kept
        )

    return lax.fori_loop(0, groups, body, carry)


def quarter_rows(quarter):
    return pl.ds(pl.multiple_of(quarter * ROWS, ROWS), ROWS)


def eight(group):
    return pl.ds(pl.multiple_of(group * 8, 8), 8)


def fold(x, y, step):
    at = lax.broadcasted_iota(jnp.int32, x.shape, 0)
    of_x = (at & step) == 0
    return jnp.where(of_x, x, y) + pltpu.roll(jnp.where(of_x, y, x), 8 - step, 0)


def row_sums(parts):
    for step in (1, 2, 4):
        parts = [fold(parts[n], parts[n + 1], step) for n in range(0, len(parts), 2)]
    return parts[0]


def keep_at(starts, token):
    return (1 - starts[token]).astype(F32)


def with_rim(proj, rim, k, rows):
    rows[0:8] = rim[k]
    rows[8:] = proj[k]


def keeps_of(column):
    marks = column[...].astype(F32)
    one = 1.0 - marks
    two = one * jnp.concatenate([jnp.ones((1, 1), F32), one[: T - 1]])
    return one, two, 1.0 - jnp.max(marks, axis=0, keepdims=True)


def project_kernel(values, gain, weights, low, inverse, proj, proj_kept):
    v = values[...]
    inverse[...] = inverse_rms(v)
    low[...] = (v * inverse[...] * gain[...]).astype(BF16)
    for k in range(3):
        proj[k] = dot(low[...], weights[k])
        proj_kept[k] = proj[k]


def project(values, gain, weights):
    return pl.pallas_call(
        project_kernel,
        name="project",
        cost_estimate=taking(3),
        out_shape=(
            struct(T, D, dtype=BF16),
            struct(T, 1),
            struct(3, T, C),
            pltpu.HBM((3, T, C), F32),
        ),
        in_specs=[VMEM] * 3,
        out_specs=[VMEM] * 4,
        compiler_params=pltpu.CompilerParams(vmem_limit_bytes=12 * MIB),
    )(values, gain, weights)


def mix_kernel(proj, rim, gain, weights, taps, column, starts, poles, *refs):
    proj_rim, mixed, end, powers, kept, shifted_rows, driven = refs
    v = rim[...]
    v = v * inverse_rms(v) * gain[...]
    low = jnp.concatenate([v, v]).astype(BF16)
    for k in range(3):
        proj_rim[k] = dot(low, weights[k])[:8]
        kept[k, :T], kept[k, T:] = proj[k], proj_rim[k]
    mix_end(kept, taps, column, starts, poles, mixed, end, powers, shifted_rows, driven)


def mix_end(kept, taps, column, starts, poles, mixed, end, powers, rows, driven):
    one, two, is_open = keeps_of(column)
    for k in range(3):
        rows[0:8], rows[8:] = kept[k, T:], kept[k, :T]
        mixed[k] = (
            taps[k, 0:1] * kept[k, :T]
            + taps[k, 1:2] * (one * rows[7 : 7 + T])
            + taps[k, 2:3] * (two * rows[6 : 6 + T])
        )
    driven[...] = mixed[1] * mixed[2]
    pre, pim = poles[0], poles[1]

    def run(group, state, masked):
        source = driven[eight(group), :]
        re, im = state
        for r in range(8):
            if masked:
                keep = keep_at(starts, group * 8 + r)
                re, im = re * keep, im * keep
            re, im = pre * re - pim * im + source[r : r + 1], pre * im + pim * re
        return re, im

    zero = jnp.zeros((N, C), F32)
    end[0:N], end[N : 2 * N] = scan_groups(T // 8, starts, 0, run, (zero, zero), False)
    end[2 * N :] = jnp.broadcast_to(is_open, (8, C))
    power = (pre, pim)
    for n in range(1, 12):
        power = times(power, power)
        if n in (8, 9, 11):
            at = {8: 0, 9: 2, 11: 4}[n]
            powers[at], powers[at + 1] = power


def mix(proj, rim, gain, weights, taps, column, starts, poles):
    return pl.pallas_call(
        mix_kernel,
        name="mix",
        cost_estimate=taking(5),
        out_shape=(
            struct(3, 8, C),
            pltpu.HBM((3, T, C), F32),
            struct(2 * N + 8, C),
            struct(6, N, C),
        ),
        in_specs=[VMEM] * 6 + [SMEM, VMEM],
        out_specs=(VMEM,) * 4,
        scratch_shapes=[
            pltpu.VMEM((3, T + 8, C), F32),
            pltpu.VMEM((T + 8, C), F32),
            pltpu.VMEM((T, C), F32),
        ],
        compiler_params=pltpu.CompilerParams(vmem_limit_bytes=22 * MIB),
    )(proj, rim, gain, weights, taps, column, starts, poles)


def forward_rows(mixed, starts, poles, block, state, visit, finish=None):
    pre, pim = poles[0], poles[1]
    base = block * BLOCK

    def run(group, kept, masked):
        source = mixed[1, eight(group), :] * mixed[2, eight(group), :]
        re, im = kept
        seen = []
        for r in range(8):
            if masked:
                keep = keep_at(starts, base + group * 8 + r)
                re, im = re * keep, im * keep
            re, im = pre * re - pim * im + source[r : r + 1], pre * im + pim * re
            seen.append(visit(group * 8 + r, re, im))
        if finish:
            finish(group, seen)
        return re, im

    state[0], state[1] = scan_groups(BLOCK // 8, starts, base, run, (state[0], state[1]), False)


def signal_kernel(mixed, starts, poles, residues, first, signal, gated, state):
    block = pl.program_id(0)

    @pl.when(block == 0)
    def _():
        state[...] = first[...]

    qre, qim = residues[0], residues[1]

    def visit(row, re, im):
        weighed = qre * re - qim * im
        return weighed[:8] + weighed[8:]

    def finish(group, seen):
        signal[eight(group), :] = row_sums(seen)

    forward_rows(mixed, starts, poles, block, state, visit, finish)
    gated[...] = (mixed[0] * signal[...]).astype(BF16)


def history_kernel(mixed, starts, poles, first, *rest):
    h0, h1, h2, h3, token, state = rest[-6:]
    block = pl.program_id(0)
    token[...] = jnp.zeros(token.shape, F32)

    @pl.when(block == 0)
    def _():
        state[...] = first[...]

    def visit(row, re, im):
        h0[row], h1[row] = re[:8], re[8:]
        h2[row], h3[row] = im[:8], im[8:]

    forward_rows(mixed, starts, poles, block, state, visit)


def signal_of(mixed, starts, poles, residues, first):
    return pl.pallas_call(
        signal_kernel,
        name="signal",
        cost_estimate=taking(6),
        grid=(BLOCKS,),
        out_shape=(struct(T, C), struct(T, C, dtype=BF16)),
        in_specs=[
            pl.BlockSpec((3, BLOCK, C), lambda i: (0, i, 0)),
            SMEM,
            whole(2, N, C),
            whole(2, N, C),
            whole(2, N, C),
        ],
        out_specs=(pl.BlockSpec((BLOCK, C), lambda i: (i, 0)),) * 2,
        scratch_shapes=[pltpu.VMEM((2, N, C), F32)],
        compiler_params=pltpu.CompilerParams(vmem_limit_bytes=8 * MIB),
    )(mixed, starts, poles, residues, first)


def history_of(mixed, starts, poles, first, *after):
    return pl.pallas_call(
        history_kernel,
        name="state_history",
        cost_estimate=taking(8),
        grid=(BLOCKS,),
        out_shape=(pltpu.HBM((T, 8, C), F32),) * 4 + (struct(8, 128),),
        in_specs=[
            pl.BlockSpec((3, BLOCK, C), lambda i: (0, i, 0)),
            SMEM,
            whole(2, N, C),
            whole(2, N, C),
        ]
        + [ANY] * len(after),
        out_specs=(pl.BlockSpec((BLOCK, 8, C), lambda i: (i, 0, 0)),) * 4 + (whole(8, 128),),
        scratch_shapes=[pltpu.VMEM((2, N, C), F32)],
        compiler_params=pltpu.CompilerParams(vmem_limit_bytes=11 * MIB),
    )(in_hbm(mixed), starts, poles, first, *after)


def adjoint_kernel(grad_gated, query, column, starts, poles, residues, out, grads):
    grads[...] = grad_gated[...] * query[0]
    pre, pim, qre, qim = poles[0], poles[1], residues[0], residues[1]

    def run(group, kept, masked):
        source = grads[eight(group), :]
        re, im = kept
        for r in reversed(range(8)):
            row = source[r : r + 1]
            re, im = row * qre + (pre * re + pim * im), (pre * im - pim * re) - row * qim
            if masked:
                keep = keep_at(starts, group * 8 + r)
                re, im = re * keep, im * keep
        return re, im

    zero = jnp.zeros((N, C), F32)
    out[0:N], out[N : 2 * N] = scan_groups(T // 8, starts, 0, run, (zero, zero), True)
    out[2 * N :] = jnp.broadcast_to(keeps_of(column)[2], (8, C))


def adjoint_end(grad_gated, mixed, column, starts, poles, residues):
    return pl.pallas_call(
        adjoint_kernel,
        name="adjoint_end",
        cost_estimate=taking(4),
        grid=(1,),
        out_shape=struct(2 * N + 8, C),
        in_specs=[
            whole(T, C),
            pl.BlockSpec((1, T, C), lambda i: (0, 0, 0)),
            whole(T, 1),
            SMEM,
            whole(2, N, C),
            whole(2, N, C),
        ],
        out_specs=whole(2 * N + 8, C),
        scratch_shapes=[pltpu.VMEM((T, C), F32)],
        compiler_params=pltpu.CompilerParams(vmem_limit_bytes=9 * MIB),
    )(grad_gated, mixed, column, starts, poles, residues)


def back_kernel(
    grad_gated,
    mixed,
    signal,
    proj,
    proj_rim,
    h0,
    h1,
    h2,
    h3,
    taps,
    column,
    starts,
    poles,
    residues,
    first,
    *rest,
):
    grad_proj, rim, sums, state, driven_grad, mixed_grad, rows_before = rest[-7:]
    step = pl.program_id(0)
    block = BLOCKS - 1 - step

    @pl.when(step == 0)
    def _():
        state[...] = first[...]
        sums[...] = jnp.zeros(sums.shape, F32)

    base = block * BLOCK
    for part in range(PARTS):
        columns = slice(C // PARTS * part, C // PARTS * (part + 1))
        pre, pim = poles[0, :, columns], poles[1, :, columns]
        qre, qim = residues[0, :, columns], residues[1, :, columns]

        def run(group, kept, masked):
            rows = pl.ds(pl.multiple_of(base + group * 8, 8), 8)
            source = grad_gated[rows, columns] * mixed[0, rows, columns]
            re, im, pole_re, pole_im, res_re, res_im = kept
            seen = [None] * 8
            for r in reversed(range(8)):
                row = source[r : r + 1]
                token = group * 8 + r
                sre = jnp.concatenate([h0[token, :, columns], h1[token, :, columns]])
                sim = jnp.concatenate([h2[token, :, columns], h3[token, :, columns]])
                pole_re += re * sre + im * sim
                pole_im += im * sre - re * sim
                res_re += row * sre
                res_im -= row * sim
                re, im = row * qre + (pre * re + pim * im), (pre * im - pim * re) - row * qim
                seen[r] = re[:8] + re[8:]
                if masked:
                    keep = keep_at(starts, base + group * 8 + r)
                    re, im = re * keep, im * keep
            driven_grad[rows, columns] = row_sums(seen)
            return re, im, pole_re, pole_im, res_re, res_im

        zero = jnp.zeros((N, C // PARTS), F32)
        kept = (state[0, :, columns], state[1, :, columns], zero, zero, zero, zero)
        kept = scan_groups(BLOCK // 8, starts, base, run, kept, True)
        state[0, :, columns], state[1, :, columns] = kept[:2]
        for n in range(4):
            sums[N * n : N * n + N, columns] += kept[2 + n]

    @pl.when(step == BLOCKS - 1)
    def _():
        one, two, _ = keeps_of(column)
        mixed_grad[0, 0:T] = grad_gated[...] * signal[...]
        mixed_grad[1, 0:T] = driven_grad[...] * mixed[2]
        mixed_grad[2, 0:T] = driven_grad[...] * mixed[1]
        for k in range(3):
            with_rim(proj, proj_rim, k, rows_before)
            here = mixed_grad[k, 0:T]
            sums[64 + 3 * k : 65 + 3 * k] = jnp.sum(here * proj[k], axis=0, keepdims=True)
            grad_proj[k] = taps[k, 0:1] * here
            here = one * mixed_grad[k, 0:T]
            sums[65 + 3 * k : 66 + 3 * k] = jnp.sum(here * rows_before[7 : 7 + T], axis=0, keepdims=True)
            mixed_grad[k, 0:T] = two * mixed_grad[k, 0:T]
            here = taps[k, 1:2] * here
            grad_proj[k, 0 : T - 1] += here[1:T]
            rim[k] = jnp.zeros((8, C), F32)
            rim[k, 1:2] = here[0:1]
            here = mixed_grad[k, 0:T]
            sums[66 + 3 * k : 67 + 3 * k] = jnp.sum(here * rows_before[6 : 6 + T], axis=0, keepdims=True)
            here = taps[k, 2:3] * here
            grad_proj[k, 0 : T - 2] += here[2:T]
            rim[k, 0:2] += here[0:2]


def back(grad_gated, mixed, signal, proj, proj_rim, history, taps, column, starts, poles, residues, first, *after):
    return pl.pallas_call(
        back_kernel,
        name="adjoint_and_short_back",
        cost_estimate=taking(13),
        grid=(BLOCKS,),
        out_shape=(struct(3, T, C), struct(3, 8, C), struct(80, C)),
        in_specs=[
            whole(T, C),
            whole(3, T, C),
            whole(T, C),
            whole(3, T, C),
            whole(3, 8, C),
        ]
        + [pl.BlockSpec((BLOCK, 8, C), lambda i: (BLOCKS - 1 - i, 0, 0))] * 4
        + [
            whole(3, 3, C),
            whole(T, 1),
            SMEM,
            whole(2, N, C),
            whole(2, N, C),
            whole(2, N, C),
        ]
        + [ANY] * len(after),
        out_specs=(whole(3, T, C), whole(3, 8, C), whole(80, C)),
        scratch_shapes=[
            pltpu.VMEM((2, N, C), F32),
            pltpu.VMEM((T, C), F32),
            pltpu.VMEM((3, T, C), F32),
            pltpu.VMEM((T + 8, C), F32),
        ],
        compiler_params=pltpu.CompilerParams(vmem_limit_bytes=25 * MIB),
    )(
        grad_gated,
        mixed,
        signal,
        proj,
        proj_rim,
        *history,
        taps,
        column,
        starts,
        poles,
        residues,
        first,
        *after,
    )


def swap(value, axis, mask):
    size = lax.axis_size(axis)
    return lax.ppermute(value, axis, [(i, i ^ mask) for i in range(size)])


def shifted(value, axis, steps):
    count = lax.axis_size(axis)
    first, last = max(0, -steps), min(count, count - steps)
    return lax.ppermute(value, axis, [(i, i + steps) for i in range(first, last)])


def pair_add_kernel(left, got_left, right, got_right, *rest):
    left_own, left_next, right_own, right_next = rest[-4:]
    left_own[...] = left[:ROWS] + got_left[:ROWS]
    left_next[...] = left[ROWS:] + got_left[ROWS:]
    right_own[...] = right[:ROWS] + got_right[:ROWS]
    right_next[...] = right[ROWS:] + got_right[ROWS:]


def pair_call(name, kernel, shapes, operands, after):
    return pl.pallas_call(
        kernel,
        name=name,
        cost_estimate=taking(0.8),
        out_shape=shapes,
        in_specs=[VMEM] * len(operands) + [ANY] * len(after),
        out_specs=[VMEM] * len(shapes),
        compiler_params=pltpu.CompilerParams(vmem_limit_bytes=10 * MIB),
    )(*operands, *after)


def scatter_end(pieces, got_left, got_right, *after, shape=struct):
    left_own, left_next, right_own, right_next = pair_call(
        "pair_add",
        pair_add_kernel,
        [shape(ROWS, HALF)] * 4,
        (pieces[0], got_left, pieces[2], got_right),
        after,
    )
    return left_own, swap(left_next, "tp", 3), right_own, swap(right_next, "tp", 1)


def scatter_start(pieces):
    return swap(pieces[1], "tp", 1), swap(pieces[3], "tp", 3)


def in_hbm_struct(*shape):
    return pltpu.HBM(shape, F32)


def scatter_sum(pieces, *after, shape=struct):
    return scatter_end(pieces, *scatter_start(pieces), *after, shape=shape)


def pair_join_kernel(left, left_3, right, right_1, *rest):
    left_03, right_10 = rest[-2:]
    rows = left.shape[0]
    left_03[:rows], left_03[rows:] = left[...], left_3[...]
    right_10[:rows], right_10[rows:] = right_1[...], right[...]


def gather_joined(left, right, *after):
    return joined_parts(left, swap(left, "tp", 3), right, swap(right, "tp", 1), *after)


def joined_parts(left, left_3, right, right_1, *after):
    left_03, right_10 = pair_call(
        "pair_join",
        pair_join_kernel,
        [struct(2 * left.shape[0], HALF)] * 2,
        (left, left_3, right, right_1),
        after,
    )
    parts = left, swap(left_03, "tp", 1), left_3, right, right_1, swap(right_10, "tp", 3)
    return parts, (left_03, right_10)


def gather_parts(left, right, *after):
    return gather_joined(left, right, *after)[0]


def quarters_of(parts):
    left, left_12, left_3, right, right_1, right_23 = parts
    rows = left.shape[0]
    return (
        (left[:rows], right[:rows]),
        (left_12[:rows], right_1[:rows]),
        (left_12[rows:], right_23[:rows]),
        (left_3[:rows], right_23[rows:]),
    )


def of_payload(ref):
    return (ref[0:N], ref[N : 2 * N]), ref[2 * N : 2 * N + 1]


def to_payload(ref, state, is_open):
    ref[0:N], ref[N : 2 * N] = state
    ref[2 * N :] = jnp.broadcast_to(is_open, (8, C))


def power_of(powers, at, reverse):
    return powers[at], -powers[at + 1] if reverse else powers[at + 1]


def chip_kernel(reverse, place, mine, other, powers, out):
    (state, is_open), (state_other, open_other) = of_payload(mine), of_payload(other)
    by_device = power_of(powers, 0, reverse)
    last = place[1] == (0 if reverse else 1)
    earlier = where2(last, state_other, state)
    later = where2(last, state, state_other)
    later_open = jnp.where(last, is_open, open_other)
    chip = plus(later, times(scaled(by_device, later_open), earlier))
    to_payload(out, chip, is_open * open_other)


def plane_kernel(reverse, place, mine, got_1, got_2, got_3, powers, *rest):
    out, before = rest[-2:]
    chip, is_open = of_payload(mine)
    by_chip = power_of(powers, 2, reverse)
    got = {1: of_payload(got_1), 2: of_payload(got_2), 3: of_payload(got_3)}
    y = 3 - place[2] if reverse else place[2]
    one, zero = jnp.ones((N, C), F32), jnp.zeros((N, C), F32)
    entering, weight = (zero, zero), (one, zero)
    for k in (1, 2, 3):
        state, opened = got[k]
        entering = where2(y >= k, plus(entering, times(weight, state)), entering)
        weight = where2(y >= k, times(weight, scaled(by_chip, opened)), weight)
    plane = plus(chip, times(scaled(by_chip, is_open), entering))
    for j in (1, 2, 3):
        state, opened = got[4 - j]
        plane = where2(y + j <= 3, plus(state, times(scaled(by_chip, opened), plane)), plane)
        is_open = is_open * opened
    to_payload(out, plane, is_open)
    before[0], before[1] = entering
    before[2], before[3] = weight


def enter_kernel(reverse, place, before, got_1, got_2, got_3, other, powers, *rest):
    out = rest[-1]
    by_device, by_plane = power_of(powers, 0, reverse), power_of(powers, 4, reverse)
    one, zero = jnp.ones((N, C), F32), jnp.zeros((N, C), F32)
    entering, weight = (zero, zero), (one, zero)
    for ref in (got_1, got_2, got_3):
        state, opened = of_payload(ref)
        entering = plus(entering, times(weight, state))
        weight = times(weight, scaled(by_plane, opened))
    at_chip = plus((before[0], before[1]), times((before[2], before[3]), entering))
    state, opened = of_payload(other)
    at_core = plus(state, times(scaled(by_device, opened), at_chip))
    out[0], out[1] = where2(place[1] == (0 if reverse else 1), at_core, at_chip)


def small_call(name, kernel, reverse, shapes, operands, after=()):
    return pl.pallas_call(
        functools.partial(kernel, reverse),
        name=name,
        cost_estimate=taking(1.6),
        out_shape=shapes,
        in_specs=[SMEM] + [VMEM] * (len(operands) - 1) + [ANY] * len(after),
        out_specs=jax.tree.map(lambda _: VMEM, shapes),
        compiler_params=pltpu.CompilerParams(vmem_limit_bytes=8 * MIB),
    )(*operands, *after)


def carried_state(place, mine, powers, reverse, after=(), late=()):
    sign = -1 if reverse else 1
    payload = struct(2 * N + 8, C)
    other = swap(mine, "seq_2", 1)
    chip = small_call("chip_state", chip_kernel, reverse, payload, (place, mine, other, powers))
    got = [
        lax.ppermute(chip, "seq_1", [(i, (i + sign * k) % 4) for i in range(4)]) for k in (1, 2, 3)
    ]
    plane, before = small_call(
        "plane_state",
        plane_kernel,
        reverse,
        (payload, struct(4, N, C)),
        (place, chip, *got, powers),
        after,
    )
    got = [shifted(plane, "seq_0", sign * k) for k in (1, 2, 3)]
    entering = small_call(
        "entering_state",
        enter_kernel,
        reverse,
        struct(2, N, C),
        (place, before, *got, other, powers),
        late,
    )
    return entering


def sum_over(x, axis, *after):
    if lax.axis_size(axis) == 2:
        return x + swap(x, axis, 1)
    got = [swap(x, axis, k) for k in (1, 2, 3)]
    if after:
        got = [tie(g, *after) for g in got]
    return (x + got[0]) + (got[1] + got[2])


def inverse_rms(values):
    return lax.rsqrt(jnp.mean(values * values, axis=-1, keepdims=True) + epsilon)


def nothing(*refs):
    pass


def tie(x, *after, hbm=False):
    shape = struct(*x.shape, dtype=x.dtype)
    if hbm:
        x, shape = in_hbm(x), pltpu.HBM(x.shape, x.dtype)
    return pl.pallas_call(
        nothing,
        name="tie",
        out_shape=shape,
        in_specs=[ANY] * (1 + len(after)),
        out_specs=ANY,
        input_output_aliases={0: 0},
        compiler_params=pltpu.CompilerParams(vmem_limit_bytes=6 * MIB),
    )(x, *after)


WIDE = 1408


def wide_sum_kernel(left_a, l03, r10, l12, r23, left_b, more_b, right, wide, gain, out, token, both, rows_a, rows_b):
    step = pl.program_id(0)

    @pl.when(step == 0)
    def _():
        both[:T] = right[...]
        both[T:] = wide[...].astype(BF16)
        token[...] = jnp.zeros(token.shape, F32)

    def put(*quarters):
        rows_a[T:] = (jnp.concatenate(quarters) * gain[...]).astype(BF16)

    pl.when(step < 2)(lambda: put(l03[:ROWS], l12[:ROWS], l12[ROWS:], l03[ROWS:]))
    pl.when(step >= 2)(lambda: put(r10[ROWS:], r10[:ROWS], r23[:ROWS], r23[ROWS:]))
    rows_a[:T], rows_b[:T], rows_b[T:] = left_a[...], left_b[...], more_b[...]
    out[:, :WIDE] = token_sum(rows_a[...], both[:, :WIDE])
    out[:, WIDE:] = token_sum(rows_b[...], both[:, WIDE:])


def wide_token_sum(left_a, more_a, left_b, more_b, right, wide, gain):
    rows = 512
    column = pl.BlockSpec((T, rows), lambda i: (0, i))
    low = pl.BlockSpec((2 * ROWS, rows), lambda i: (0, jnp.minimum(i, 1)))
    high = pl.BlockSpec((2 * ROWS, rows), lambda i: (0, jnp.maximum(i - 2, 0)))
    width = right.shape[1]
    return pl.pallas_call(
        wide_sum_kernel,
        name="weight_gradients",
        cost_estimate=taking(10),
        grid=(D // rows,),
        out_shape=(pltpu.HBM((D, width), F32), struct(8, 128)),
        in_specs=[column, low, high, low, high, column, column]
        + [VMEM, VMEM, pl.BlockSpec((1, rows), lambda i: (0, i))],
        out_specs=(pl.BlockSpec((rows, width), lambda i: (i, 0)), whole(8, 128)),
        scratch_shapes=[
            pltpu.VMEM((2 * T, width), BF16),
            pltpu.VMEM((2 * T, rows), BF16),
            pltpu.VMEM((2 * T, rows), BF16),
        ],
        compiler_params=pltpu.CompilerParams(vmem_limit_bytes=21 * MIB),
    )(left_a, *more_a, left_b, more_b, right, wide, gain)


ORDERS = {1: (0, 3, 1, 2), 3: (0, 1, 3, 2)}
STREAMS = (("seq_1", 1), ("seq_1", 3), ("seq_0", 1), ("seq_0", 3))


def stream_places(step):
    jz, jy = divmod(step, 4)
    places = []
    for axis, mask in STREAMS:
        order = ORDERS[mask]
        first, second = (jy, jz) if axis == "seq_1" else (jz, jy)
        places.append(order.index(first) * 4 + order.index(second))
    return places


def stream_sum_kernel(
    place,
    left_a,
    more_a,
    left_b,
    more_b,
    right_a,
    wide_a,
    right_b,
    wide_b,
    sums,
    gains_a,
    gains_b,
    *rest,
):
    kept, sent, token, turned = rest[-10:-6], rest[-6:-2], rest[-2], rest[-1]
    token[...] = jnp.zeros(token.shape, F32)
    for s in range(4):
        kept[s][2048 : 2048 + 80] = sums[:, 128 * s : 128 * s + 128]
        for n in range(8):
            row = (gains_a, gains_b)[n // 4]
            at = C * (n % 4) + 128 * s
            kept[s][2128 + n : 2129 + n] = row[:, at : at + 128]
        sent[s][2048:] = kept[s][2048:]
    turned[0:768, 0:T] = right_a[...].T
    turned[768:, 0:T] = right_b[...].T
    turned[0:768, T:] = wide_a[...].astype(BF16).T
    turned[768:, T:] = wide_b[...].astype(BF16).T
    y, z = place[2], place[3]
    for step in range(16):
        jz, jy = divmod(step, 4)
        chunk = (z ^ jz) * 4 + (y ^ jy)
        columns = pl.ds(pl.multiple_of(chunk * 128, 128), 128)
        total_a = dot(turned[0:768, 0:T], left_a[:, columns]) + dot(turned[0:768, T:], more_a[:, columns])
        total_b = dot(turned[768:, 0:T], left_b[:, columns]) + dot(turned[768:, T:], more_b[:, columns])
        for s, at in enumerate(stream_places(step)):
            target = kept[s] if at < 8 else sent[s]
            rows = slice((at % 8) * 256, (at % 8) * 256 + 256)
            target[rows] = total_a[256 * s : 256 * s + 256] if s < 3 else total_b


def stream_token_sum(place, *operands):
    out = pl.pallas_call(
        stream_sum_kernel,
        name="mixer_weight_gradients",
        cost_estimate=taking(7),
        out_shape=(struct(2048 + SMALL, 128),) * 8 + (struct(8, 128),),
        in_specs=[SMEM] + [VMEM] * 11 + [ANY] * (len(operands) - 11),
        out_specs=(VMEM,) * 9,
        scratch_shapes=[pltpu.VMEM((1024, 2 * T), BF16)],
        compiler_params=pltpu.CompilerParams(vmem_limit_bytes=8 * MIB),
    )(place, *operands)
    return out[:4], out[4:8], out[8]


SMALL = 88


def stream_add_kernel(*refs):
    held, got, kept, sent = refs[0:4], refs[4:8], refs[-8:-4], refs[-4:]
    for s in range(4):
        rows = held[s].shape[0] - SMALL
        low = rows // 2
        small = held[s][rows:] + got[s][rows:]
        kept[s][0:low] = held[s][0:low] + got[s][0:low]
        kept[s][low:] = small
        sent[s][0:low] = held[s][low:rows] + got[s][low:rows]
        sent[s][low:] = small


def stream_add(held, got, *after):
    rows = held[0].shape[0] - SMALL
    shape = struct(rows // 2 + SMALL, 128)
    out = pl.pallas_call(
        stream_add_kernel,
        name="stream_add",
        cost_estimate=taking(0.7 + rows / 1000),
        out_shape=[shape] * 8,
        in_specs=[VMEM] * 8 + [ANY] * len(after),
        out_specs=[VMEM] * 8,
        compiler_params=pltpu.CompilerParams(vmem_limit_bytes=6 * MIB),
    )(*held, *got, *after)
    return out[:4], out[4:]


def stream_last_kernel(place, *refs):
    held, got, (own, send, small, gains) = refs[0:4], refs[4:8], refs[-4:]
    first = place[1] == 0
    for s in range(4):
        total = (held[s][0:256] + got[s][0:256]).T
        columns = slice(256 * s, 256 * s + 256)
        own[:, columns] = jnp.where(first, total[:64], total[64:])
        send[:, columns] = jnp.where(first, total[64:], total[:64])
        total = held[s][256:] + got[s][256:]
        small[:, 128 * s : 128 * s + 128] = total[:80]
        gains[:, 128 * s : 128 * s + 128] = total[80:]


def stream_last(place, held, got, *after):
    return pl.pallas_call(
        stream_last_kernel,
        name="stream_last",
        cost_estimate=taking(1.5),
        out_shape=(struct(64, 1024), struct(64, 1024), struct(80, C), struct(8, C)),
        in_specs=[SMEM] + [VMEM] * 8 + [ANY] * len(after),
        out_specs=[VMEM] * 4,
        compiler_params=pltpu.CompilerParams(vmem_limit_bytes=6 * MIB),
    )(place, *held, *got, *after)


def stream_masks(axis, mask):
    other = "seq_0" if axis == "seq_1" else "seq_1"
    return ((axis, mask), (axis, 4 - mask), (other, mask), (other, 4 - mask))


def stream_swap(sent, step):
    return [swap(x, *stream_masks(*STREAMS[s])[step]) for s, x in enumerate(sent)]


def mixer_shares_kernel(place, own, got, small, small_got, *rest):
    grad_in, grad_out, small_sum = rest[-3:]
    first = place[1] == 0
    low = jnp.where(first, own[...], got[...])
    high = jnp.where(first, got[...], own[...])
    for k in range(3):
        columns = slice(256 * k, 256 * k + 256)
        grad_in[k, :, :256], grad_in[k, :, 256:] = low[:, columns], high[:, columns]
    grad_out[:, :256], grad_out[:, 256:] = low[:, 768:], high[:, 768:]
    small_sum[...] = small[...] + small_got[...]


def mixer_shares(place, own, got, small, small_got, *after):
    return pl.pallas_call(
        mixer_shares_kernel,
        name="mixer_shares",
        cost_estimate=taking(1.5),
        out_shape=(struct(3, 64, C), struct(64, C), struct(80, C)),
        in_specs=[SMEM] + [VMEM] * 4 + [ANY] * len(after),
        out_specs=[VMEM] * 3,
        compiler_params=pltpu.CompilerParams(vmem_limit_bytes=6 * MIB),
    )(place, own, got, small, small_got, *after)


def ffn_send_kernel(place, share, *rest):
    own, send = rest[-2:]
    first = place[1] == 0
    low, high = share[:64], share[64:]
    own[...] = jnp.where(first, low, high)
    send[...] = jnp.where(first, high, low)


def ffn_shares_kernel(place, own, got, *rest):
    gate, up, down, token = rest[-4:]
    first = place[1] == 0
    low = jnp.where(first, own[...], got[...])
    high = jnp.where(first, got[...], own[...])
    gate[:, :768], gate[:, 768:] = low[:, :768], high[:, 768:1408]
    up[:, :640], up[:, 640:] = low[:, 768:1408], high[:, :768]
    down[:, :768], down[:, 768:] = low[:, 1408:], high[:, 1408 + 128 :]
    token[...] = jnp.zeros(token.shape, F32)


def ffn_halves(place, share, *after):
    return pl.pallas_call(
        ffn_send_kernel,
        name="ffn_send",
        cost_estimate=taking(1),
        out_shape=(struct(64, 2176),) * 2,
        in_specs=[SMEM, VMEM] + [ANY] * len(after),
        out_specs=[VMEM] * 2,
        compiler_params=pltpu.CompilerParams(vmem_limit_bytes=6 * MIB),
    )(place, share, *after)


def ffn_shares(place, own, got, *after):
    return pl.pallas_call(
        ffn_shares_kernel,
        name="ffn_shares",
        cost_estimate=taking(2),
        out_shape=(struct(64, 1408),) * 3 + (struct(8, 128),),
        in_specs=[SMEM, VMEM, VMEM] + [ANY] * len(after),
        out_specs=[VMEM] * 4,
        compiler_params=pltpu.CompilerParams(vmem_limit_bytes=8 * MIB),
    )(place, own, got, *after)


def norm_kernel(values, gain, *rest):
    out, inverse = rest[-2:]
    v = values[...]
    inverse[...] = inverse_rms(v)
    out[...] = (v * inverse[...] * gain[...]).astype(BF16)


def normed(values, gain, *after):
    rows = 128
    row = pl.BlockSpec((rows, D), lambda i: (i, 0))
    return pl.pallas_call(
        norm_kernel,
        name="normed_in",
        cost_estimate=taking(1.8),
        grid=(values.shape[0] // rows,),
        out_shape=(struct(*values.shape, dtype=BF16), struct(values.shape[0], 1)),
        in_specs=[row, whole(1, D)] + [ANY] * len(after),
        out_specs=(row, pl.BlockSpec((rows, 1), lambda i: (i, 0))),
        compiler_params=pltpu.CompilerParams(vmem_limit_bytes=11 * MIB),
    )(values, gain, *after)


HALF = D // 2


def rows_by_quarter(place, ref):
    return jnp.concatenate([ref[quarter_rows(place[0] ^ q), :] for q in range(4)])


def cotangent_kernel(place, cotangent, w_down, *rest):
    low, grad_hidden = rest[-2:]

    @pl.when(pl.program_id(0) == 0)
    def _():
        for q in range(4):
            low[ROWS * q : ROWS * q + ROWS] = cotangent[quarter_rows(place[0] ^ q), :].astype(BF16)

    grad_hidden[...] = dot_t(low[...], w_down[...])


def cotangent_part(place, cotangent, w_down, *after):
    wide = w_down.shape[0]
    return pl.pallas_call(
        cotangent_kernel,
        name="cotangent_part",
        cost_estimate=taking(4),
        grid=(6,),
        out_shape=(struct(T, D, dtype=BF16), struct(T, wide)),
        in_specs=[SMEM, VMEM, pl.BlockSpec((256, D), lambda i: (i, 0))] + [ANY] * len(after),
        out_specs=(VMEM, pl.BlockSpec((T, 256), lambda i: (0, i))),
        compiler_params=pltpu.CompilerParams(vmem_limit_bytes=9 * MIB),
    )(place, cotangent, w_down, *after)


def out_parts_kernel(place, gated, *rest):
    own, send = rest[-2:]
    first = place[1] == 0
    rows = rows_by_quarter(place, gated).astype(F32)
    low, high = rows[:, :256], rows[:, 256:]
    own[...] = jnp.where(first, low, high).astype(BF16)
    send[...] = jnp.where(first, high, low)


def out_parts(place, gated, *after):
    return pl.pallas_call(
        out_parts_kernel,
        name="out_parts",
        cost_estimate=taking(1),
        out_shape=(struct(T, 256, dtype=BF16), struct(T, 256)),
        in_specs=[SMEM, VMEM] + [ANY] * len(after),
        out_specs=[VMEM] * 2,
        compiler_params=pltpu.CompilerParams(vmem_limit_bytes=7 * MIB),
    )(place, gated, *after)


def owner_kernel(place, rows, *rest):
    rest[-1][...] = rows[...].astype(BF16)


def owner_rows(place, x, *after):
    row = pl.BlockSpec((ROWS, D), lambda i, place: (place[0] ^ i, 0))
    out = pl.BlockSpec((ROWS, D), lambda i, place: (i, 0))
    return pl.pallas_call(
        owner_kernel,
        name="owner_rows",
        cost_estimate=taking(2),
        out_shape=pltpu.HBM((T, D), BF16),
        grid_spec=pltpu.PrefetchScalarGridSpec(
            num_scalar_prefetch=1, grid=(4,), in_specs=[row] + [ANY] * len(after), out_specs=out
        ),
        compiler_params=pltpu.CompilerParams(vmem_limit_bytes=9 * MIB),
    )(place, in_hbm(x), *after)


def branch_other_kernel(place, cotangent, through, out):
    out[...] = (cotangent[...] + through[...]).astype(BF16)


def branch_other_of(place, cotangent, through):
    row = pl.BlockSpec((ROWS, D), lambda i, place: (i, 0))
    return pl.pallas_call(
        branch_other_kernel,
        name="branch_other",
        cost_estimate=taking(2),
        out_shape=struct(T, D, dtype=BF16),
        grid_spec=pltpu.PrefetchScalarGridSpec(
            num_scalar_prefetch=1,
            grid=(4,),
            in_specs=[pl.BlockSpec((ROWS, D), lambda i, place: (place[0] ^ i, 0)), row],
            out_specs=row,
        ),
        compiler_params=pltpu.CompilerParams(vmem_limit_bytes=9 * MIB),
    )(place, in_hbm(cotangent), through)


def middle_kernel(place, left, left_more, right, right_more, hidden, *rest):
    middle, out_left, out_right = rest[-3:]
    low = hidden[:, :HALF] + (left[...] + left_more[...])
    high = hidden[:, HALF:] + (right[...] + right_more[...])
    square = jnp.sum(low * low, axis=-1, keepdims=True) + jnp.sum(high * high, axis=-1, keepdims=True)
    inverse = lax.rsqrt(square * (1.0 / D) + epsilon)
    middle[:, :HALF], middle[:, HALF:] = low, high
    out_left[...], out_right[...] = low * inverse, high * inverse


def norm_back_parts(left, left_more, right, right_more, values, gain):
    grads = (left[...] + left_more[...], right[...] + right_more[...])
    v = (values[:, :HALF], values[:, HALF:])
    g = (gain[:, :HALF], gain[:, HALF:])
    square = sum(jnp.sum(x * x, axis=-1, keepdims=True) for x in v)
    inverse = lax.rsqrt(square * (1.0 / D) + epsilon)
    along = sum(jnp.sum(a * b * c, axis=-1, keepdims=True) for a, b, c in zip(g, grads, v))
    along = inverse * inverse * inverse * (along * (1.0 / D))
    back = [inverse * g[n] * grads[n] - v[n] * along for n in (0, 1)]
    return back, [grads[n] * (v[n] * inverse) for n in (0, 1)]


def norm_back_kernel(left, left_more, right, right_more, values, gain, *rest):
    out_left, out_right, gains = rest[-3:]
    back, weighed = norm_back_parts(left, left_more, right, right_more, values, gain)
    out_left[...], out_right[...] = back
    for n in (0, 1):
        gains[:, HALF * n : HALF * n + HALF] = jnp.sum(weighed[n], axis=0, keepdims=True)


def by_owner_grid(in_specs, out_specs):
    return pltpu.PrefetchScalarGridSpec(
        num_scalar_prefetch=1, grid=(1,), in_specs=in_specs, out_specs=out_specs
    )


MINE = pl.BlockSpec((ROWS, D), lambda i, place: (place[0], 0))


def after_middle(place, pieces, hidden, *after):
    return pl.pallas_call(
        middle_kernel,
        name="middle_and_norm",
        cost_estimate=taking(1.5),
        out_shape=(pltpu.HBM((ROWS, D), F32), struct(ROWS, HALF), struct(ROWS, HALF)),
        grid_spec=by_owner_grid([VMEM] * 4 + [MINE] + [ANY] * len(after), (VMEM,) * 3),
        compiler_params=pltpu.CompilerParams(vmem_limit_bytes=8 * MIB),
    )(place, *pieces, in_hbm(hidden), *after)


def norm_back(pieces, values, gain, *after):
    return pl.pallas_call(
        norm_back_kernel,
        name="norm_back",
        cost_estimate=taking(2),
        out_shape=(struct(ROWS, HALF), struct(ROWS, HALF), struct(1, D)),
        grid=(1,),
        in_specs=[whole(ROWS, HALF)] * 4 + [whole(ROWS, D), whole(1, D)] + [ANY] * len(after),
        out_specs=(VMEM,) * 3,
        compiler_params=pltpu.CompilerParams(vmem_limit_bytes=9 * MIB),
    )(*pieces, values, gain, *after)


def rim_kernel(starts, rows, *rest):
    out = rest[-1]
    at = lax.broadcasted_iota(jnp.int32, (8, D), 0)
    out[...] = jnp.where(at == 6, rows[...] * keep_at(starts, T - 1), rows[...])


def rim_rows_of(starts, hidden, weights, *after):
    return pl.pallas_call(
        rim_kernel,
        name="rim_rows",
        cost_estimate=taking(1),
        grid=(1,),
        out_shape=struct(8, D),
        in_specs=[SMEM, pl.BlockSpec((8, D), lambda i: (T // 8 - 1, 0)), VMEM] + [ANY] * len(after),
        out_specs=whole(8, D),
        compiler_params=pltpu.CompilerParams(vmem_limit_bytes=6 * MIB),
    )(starts, in_hbm(hidden), weights, *after)


PIECES = ((0, 3), (1, 2), (0, 1), (3, 2))
PIECE_SHAPES = (struct(2 * ROWS, HALF),) * 4


def put_pieces(place, block, total, outs, by_owner=False):
    which, columns = block // 2, slice(512 * (block % 2), 512 * (block % 2) + 512)
    for n in (0, 1):
        out, quarters = outs[2 * which + n], PIECES[2 * which + n]
        for m, q in enumerate(quarters):
            rows = slice(ROWS * q, ROWS * q + ROWS) if by_owner else quarter_rows(place[0] ^ q)
            out[ROWS * m : ROWS * m + ROWS, columns] = total[rows, :]


def split_kernel(compute, by_owner, count, place, *refs):
    *outs, total = refs[-5:]
    for block in range(4):
        total[...] = compute(slice(512 * block, 512 * block + 512), *refs[:count])
        put_pieces(place, block, total, outs, by_owner)


def split_dot(name, compute, by_owner, place, *operands, after=()):
    return pl.pallas_call(
        functools.partial(split_kernel, compute, by_owner, len(operands)),
        name=name,
        cost_estimate=taking(2.5),
        out_shape=PIECE_SHAPES,
        in_specs=[SMEM] + [VMEM] * len(operands) + [ANY] * len(after),
        out_specs=[VMEM] * 4,
        scratch_shapes=[pltpu.VMEM((T, 512), F32)],
        compiler_params=pltpu.CompilerParams(vmem_limit_bytes=8 * MIB),
    )(place, *operands, *after)


def result_kernel(place, hidden, w_down, middle, *rest):
    out, token = rest[-2:]
    token[...] = jnp.zeros(token.shape, F32)
    for block in range(4):
        columns = slice(512 * block, 512 * block + 512)
        total = dot(hidden[...], w_down[:, columns])
        for q in range(4):
            rows = total[ROWS * q : ROWS * q + ROWS]
            out[quarter_rows(place[0] ^ q), columns] = rows + middle[:, columns] if q == 0 else rows


def result_part(place, hidden, w_down, middle, *after):
    return pl.pallas_call(
        result_kernel,
        name="result_part",
        cost_estimate=taking(2.5),
        out_shape=(pltpu.HBM((T, D), F32), struct(8, 128)),
        in_specs=[SMEM] + [VMEM] * 3 + [ANY] * len(after),
        out_specs=(VMEM, VMEM),
        compiler_params=pltpu.CompilerParams(vmem_limit_bytes=10 * MIB),
    )(place, hidden, w_down, middle, *after)


def ffn_kernel(place, *refs):
    parts, refs = refs[:6], refs[6:]
    gain, w_gate, w_up, grad_hidden = refs[:4]
    mid_x, hidden, grad_gate, grad_up, own_all, send_all = refs[-6:]
    for q, (left, right) in enumerate(quarters_of(parts)):
        rows = slice(ROWS * q, ROWS * q + ROWS)
        mid_x[rows, :HALF] = (left * gain[:, :HALF]).astype(BF16)
        mid_x[rows, HALF:] = (right * gain[:, HALF:]).astype(BF16)
    wide = w_gate.shape[1]
    for start in range(0, wide, 256):
        columns = slice(start, min(start + 256, wide))
        gate = dot(mid_x[...], w_gate[:, columns])
        up = dot(mid_x[...], w_up[:, columns])
        sig = 1.0 / (1.0 + jnp.exp(-gate))
        silu = gate * sig
        incoming = grad_hidden[:, columns]
        hidden[:, columns] = (silu * up).astype(BF16)
        grad_gate[:, columns] = (incoming * up * sig * (1.0 + gate * (1.0 - sig))).astype(BF16)
        grad_up[:, columns] = (incoming * silu).astype(BF16)
    first = place[1] == 0

    def halves(columns, low, high):
        a, b = low.astype(F32), high.astype(F32)
        own_all[:, columns] = jnp.where(first, a, b).astype(BF16)
        send_all[:, columns] = jnp.where(first, b, a)

    halves(slice(0, 768), grad_gate[:, :768], grad_up[:, 640:1408])
    halves(slice(768, 1408), grad_up[:, :640], grad_gate[:, 768:1408])
    halves(slice(1408, 2176), hidden[:, :768], hidden[:, 640:1408])


def feed_forward(place, parts, gain, w_gate, w_up, grad_hidden, *after):
    wide = w_gate.shape[1]
    low = struct(T, wide, dtype=BF16)
    return pl.pallas_call(
        ffn_kernel,
        name="feed_forward",
        cost_estimate=taking(7),
        out_shape=(
            struct(T, D, dtype=BF16),
            low,
            low,
            low,
            struct(T, wide + 768, dtype=BF16),
            struct(T, wide + 768),
        ),
        in_specs=[SMEM] + [VMEM] * 10 + [ANY] * len(after),
        out_specs=(VMEM,) * 6,
        compiler_params=pltpu.CompilerParams(vmem_limit_bytes=10 * MIB),
    )(place, *parts, gain, w_gate, w_up, grad_hidden, *after)


def branch_back_kernel(place, *refs):
    parts, cotangent, w_out = refs[:6], *refs[6:8]
    through, branch, grad_gated = refs[-3:]
    for q, (left, right) in enumerate(quarters_of(parts)):
        rows = slice(ROWS * q, ROWS * q + ROWS)
        through[rows, :HALF], through[rows, HALF:] = left, right
    branch[...] = (rows_by_quarter(place, cotangent) + through[...]).astype(BF16)
    back = dot_t(branch[...], w_out[...])
    for q in range(4):
        grad_gated[quarter_rows(place[0] ^ q), :] = back[ROWS * q : ROWS * q + ROWS]


def branch_back(place, parts, cotangent, w_out, *after):
    return pl.pallas_call(
        branch_back_kernel,
        name="branch_back",
        cost_estimate=taking(3),
        out_shape=(struct(T, D), pltpu.HBM((T, D), BF16), struct(T, C)),
        in_specs=[SMEM] + [VMEM] * 8 + [ANY] * len(after),
        out_specs=(VMEM,) * 3,
        compiler_params=pltpu.CompilerParams(vmem_limit_bytes=8 * MIB),
    )(place, *parts, cotangent, w_out, *after)


def finish_kernel(place, starts, grads, rim, *rest):
    low, own, send = rest[-3:]
    first = place[1] == 0
    at = lax.broadcasted_iota(jnp.int32, (8, C), 0)
    for k in range(3):
        turned = jnp.concatenate([jnp.zeros((6, C), F32), rim[k, 0:2]])
        turned = jnp.where(at == 6, turned * keep_at(starts, T - 1), turned)
        low[k, : T - 16] = grads[k, : T - 16].astype(BF16)
        low[k, T - 16 :] = jnp.concatenate(
            [grads[k, T - 16 : T - 8], grads[k, T - 8 :] + turned]
        ).astype(BF16)
        a, b = low[k, :, :256].astype(F32), low[k, :, 256:].astype(F32)
        columns = slice(256 * k, 256 * k + 256)
        own[:, columns] = jnp.where(first, a, b).astype(BF16)
        send[:, columns] = jnp.where(first, b, a)


def finish_projected(place, starts, grads, rim, *after):
    return pl.pallas_call(
        finish_kernel,
        name="finish_projected",
        cost_estimate=taking(1.5),
        out_shape=(struct(3, T, C, dtype=BF16), pltpu.HBM((T, 768), BF16), struct(T, 768)),
        in_specs=[SMEM, SMEM, VMEM, VMEM] + [ANY] * len(after),
        out_specs=(VMEM,) * 3,
        compiler_params=pltpu.CompilerParams(vmem_limit_bytes=7 * MIB),
    )(place, starts, grads, rim, *after)


def first_kernel(place, grads, hidden, inverse, gain, w_in, cotangent, left, right, *rest):
    out, gains, total = rest[-3:]
    along = jnp.zeros((T, 1), F32)
    for block in range(4):
        columns = slice(512 * block, 512 * block + 512)
        part = sum(dot_t(grads[k], w_in[k, columns, :]) for k in range(3))
        weighed = part * (hidden[:, columns] * inverse[...])
        gains[:, columns] = jnp.sum(weighed, axis=0, keepdims=True)
        along += jnp.sum(weighed * gain[:, columns], axis=1, keepdims=True)
        total[:, columns] = part
    along = inverse[...] * inverse[...] * (along * (1.0 / D))
    mine = quarter_rows(place[0])
    for block in range(4):
        columns = slice(512 * block, 512 * block + 512)
        out[:, columns] = inverse[...] * (gain[:, columns] * total[:, columns]) - hidden[:, columns] * along
        side, own = (left, right)[block // 2], slice(512 * (block % 2), 512 * (block % 2) + 512)
        out[mine, columns] += cotangent[mine, columns] + side[:, own]


def first_back(place, grads, hidden, inverse, gain, w_in, cotangent, left, right, *after):
    return pl.pallas_call(
        first_kernel,
        name="first_back",
        cost_estimate=taking(4),
        out_shape=(pltpu.HBM((T, D), F32), struct(1, D)),
        in_specs=[SMEM] + [VMEM] * 8 + [ANY] * len(after),
        out_specs=[VMEM] * 2,
        scratch_shapes=[pltpu.VMEM((T, D), F32)],
        compiler_params=pltpu.CompilerParams(vmem_limit_bytes=14 * MIB),
    )(place, grads, hidden, inverse, gain, w_in, cotangent, left, right, *after)


def emit_kernel(first, second, *rest):
    first_out, second_out, token = rest[-3:]
    token[...] = jnp.zeros(token.shape, F32)
    first_out[...], second_out[...] = first[...], second[...]


def emit(first, second, *after):
    row = pl.BlockSpec((ROWS, D), lambda i: (i, 0))
    return pl.pallas_call(
        emit_kernel,
        name="emit",
        cost_estimate=taking(3),
        grid=(4,),
        out_shape=(struct(T, D), struct(T, D), struct(8, 128)),
        in_specs=[row, row] + [ANY] * len(after),
        out_specs=(row, row, whole(8, 128)),
        compiler_params=pltpu.CompilerParams(vmem_limit_bytes=9 * MIB),
    )(in_hbm(first), in_hbm(second), *after)


def per_device(
    hidden_in,
    cotangent,
    starts,
    norm_in,
    w_in,
    short_w,
    pole_pairs,
    residues,
    w_out,
    norm_mid,
    w_gate,
    w_up,
    w_down,
):
    place = jnp.stack(
        [lax.axis_index(axis) for axis in ("tp", "seq_2", "seq_1", "seq_0")]
    ).astype(jnp.int32)
    column = starts[:, None]
    gain_in, gain_mid = norm_in[None], norm_mid[None]

    def other_core(x):
        return swap(x, "seq_2", 1)

    rim_rows = rim_rows_of(starts, hidden_in, w_in, place, column)
    rim_rows = lax.ppermute(rim_rows, SEQ, [(i, i + 1) for i in range(31)])
    hidden_other = other_core(hidden_in)
    cotangent_other = other_core(cotangent)
    normed_in, inverse_in, proj_now, proj = project(hidden_in, gain_in, w_in)
    rim, mixed, end, powers = mix(
        proj_now, rim_rows, gain_in, w_in, short_w, column, starts, pole_pairs
    )
    entering = carried_state(place, end, powers, False)
    signal, gated = signal_of(mixed, starts, pole_pairs, residues, entering)

    branch = split_dot(
        "branch",
        lambda columns, a, b: dot(a[...], b[:, columns]),
        False,
        place,
        gated,
        w_out,
    )
    *history, history_token = history_of(mixed, starts, pole_pairs, entering, branch[1])
    out_right, out_send = out_parts(place, gated, branch[1])
    out_wide = other_core(out_send)
    pieces = scatter_sum(branch, history_token, in_hbm(out_wide))
    down_grad, grad_hidden = cotangent_part(place, cotangent, w_down, pieces[0])
    middle, mid_left, mid_right = after_middle(place, pieces, hidden_in, grad_hidden)

    normed_other, _ = normed(hidden_other, gain_in, mid_left)
    down_other = owner_rows(place, cotangent_other, mid_left)
    parts, joined = gather_joined(mid_left, mid_right, in_hbm(normed_other), in_hbm(down_other))
    mid_other = [other_core(x) for x in joined]
    mid_x, hidden, grad_gate, grad_up, own_all, send_all = feed_forward(
        place,
        parts,
        gain_mid,
        w_gate,
        w_up,
        grad_hidden,
        *mid_other,
    )
    mid_other += [other_core(parts[1]), other_core(parts[5])]
    mid_terms = split_dot(
        "mid_terms",
        lambda columns, a, b, c, d: dot_t(a[...], c[columns, :]) + dot_t(b[...], d[columns, :]),
        True,
        place,
        grad_gate,
        grad_up,
        w_gate,
        w_up,
        after=mid_other[2:],
    )

    ffn_sum, ffn_token = wide_token_sum(
        mid_x,
        mid_other,
        down_grad,
        down_other,
        own_all,
        other_core(tie(send_all, mid_terms[1])),
        gain_mid,
    )

    pieces = scatter_sum(mid_terms, ffn_token, shape=in_hbm_struct)
    share_ffn = lax.psum_scatter(
        tie(ffn_sum, pieces[0], hbm=True), ("seq_0", "seq_1"), scatter_dimension=0, tiled=True
    )
    left, left_more, right, right_more = pieces
    through_left, through_right, gains_mid = norm_back(
        (in_hbm(left), left_more, in_hbm(right), right_more), in_hbm(middle), gain_mid
    )
    result, part_token = result_part(place, hidden, w_down, middle, gains_mid)
    through_f, branch_grad, grad_gated = branch_back(
        place, gather_parts(through_left, through_right), cotangent, w_out, part_token
    )

    leaving = adjoint_end(grad_gated, mixed, column, starts, pole_pairs, residues)
    branch_other = branch_other_of(place, cotangent_other, other_core(through_f))
    returning = carried_state(place, leaving, powers, True, after=(in_hbm(branch_other),))
    grad_proj, rim_grad, sums = back(
        grad_gated,
        mixed,
        signal,
        proj,
        rim,
        history,
        short_w,
        column,
        starts,
        pole_pairs,
        residues,
        returning,
    )
    rim_back = lax.ppermute(rim_grad, SEQ, [(i + 1, i) for i in range(31)])

    projected_low, proj_own, proj_send = finish_projected(
        place, starts, grad_proj, rim_back
    )
    proj_wide = other_core(proj_send)
    grad_input, gains_in = first_back(
        place,
        projected_low,
        hidden_in,
        inverse_in,
        gain_in,
        w_in,
        cotangent,
        through_left,
        through_right,
    )
    result, grad_input = lax.psum((result, grad_input), "tp")
    kept, leaving_now, mixer_token = stream_token_sum(
        place,
        normed_in,
        normed_other,
        branch_grad,
        branch_other,
        proj_own,
        proj_wide,
        out_right,
        out_wide,
        sums,
        gains_in,
        gains_mid,
    )
    got = stream_swap(leaving_now, 0)
    kept, leaving_now = stream_add(kept, got)
    got = stream_swap(leaving_now, 1)
    ffn_own, ffn_out = ffn_halves(place, share_ffn, kept[0])
    kept, leaving_now = stream_add(kept, got, ffn_own)
    got = stream_swap(leaving_now, 2)
    share_gate, share_up, share_down, shares_token = ffn_shares(
        place, ffn_own, other_core(ffn_out), kept[0]
    )
    kept, leaving_now = stream_add(kept, got, shares_token)
    got = stream_swap(leaving_now, 3)
    result, grad_input, output_token = emit(result, grad_input, kept[0])
    own, send, small, gains = stream_last(place, kept, got, output_token)
    share_in, share_out, small = mixer_shares(
        place, own, other_core(send), small, other_core(small)
    )
    gains = sum_over(sum_over(gains, "tp"), "seq_2")
    return (
        result,
        grad_input,
        gains[0:4].reshape(D),
        share_in,
        small[64:73].reshape(3, 3, C),
        small[0:32].reshape(2, N, C),
        small[32:64].reshape(2, N, C),
        share_out.T,
        gains[4:8].reshape(D),
        share_gate,
        share_up,
        share_down.T,
    )


def solution(mesh):
    split = Mesh(mesh.devices.reshape(4, 4, 2, mesh.shape["tp"]), ("seq_0", "seq_1", "seq_2", "tp"))
    in_specs = (
        P(SEQ, None),
        P(SEQ, None),
        P(SEQ),
        P(),
        P(None, None, "tp"),
        P(None, None, "tp"),
        P(None, None, "tp"),
        P(None, None, "tp"),
        P("tp", None),
        P(),
        P(None, "tp"),
        P(None, "tp"),
        P("tp", None),
    )
    out_specs = (
        P(SEQ, None),
        P(SEQ, None),
        P(),
        P(None, SEQ, "tp"),
        P(None, None, "tp"),
        P(None, None, "tp"),
        P(None, None, "tp"),
        P("tp", SEQ),
        P(),
        P(SEQ, "tp"),
        P(SEQ, "tp"),
        P("tp", SEQ),
    )
    return jax.shard_map(
        per_device, mesh=split, in_specs=in_specs, out_specs=out_specs, check_vma=False
    )
```
